32 devices in a mesh: frames: 4 (over x, core), mp: 8 (over z, y).
Axes of the slice: x: 2, y: 2, z: 4, core: 2. Of those that a mesh axis runs over, the one named last changes fastest.
Arguments:
- inputs: bfloat16 [1536, 16, 1024], P(('frames', 'mp')), may hold values from -6 to 6
- counts: int32 [4], P('frames'), may hold values from 96 to 384, as said below
- norm_gains: float32 [2, 16, 1024], replicated, may hold values from 0.5 to 1.5
- in_weight: bfloat16 [16, 3, 1024, 1024], P(None, None, None, 'mp'), may hold values from -0.1875 to 0.1875
- out_weight: bfloat16 [16, 1024, 1024], P(None, 'mp'), may hold values from -0.5 to 0.5
- gate_up: bfloat16 [16, 2, 1024, 4096], P(None, None, None, 'mp'), may hold values from -0.1875 to 0.1875
- down_weight: bfloat16 [16, 4096, 1024], P(None, 'mp'), may hold values from -0.09375 to 0.09375
- cotangent: bfloat16 [1536, 16, 1024], P(('frames', 'mp')), may hold values from -6 to 6
Outputs:
- output: bfloat16 [1536, 16, 1024], P(('frames', 'mp'))
- input_grad: bfloat16 [1536, 16, 1024], P(('frames', 'mp'))
- grad_in_weight: float32 [16, 3, 1024, 1024], P(None, None, 'frames', 'mp')
- grad_out_weight: float32 [16, 1024, 1024], P(None, 'mp', 'frames')
- grad_gate_up: float32 [16, 2, 1024, 4096], P(None, None, 'frames', 'mp')
- grad_down: float32 [16, 4096, 1024], P(None, 'mp', 'frames')
- grad_gains: float32 [2, 16, 1024], P(None, None, 'frames')
The draws below stay inside these ranges and needn't reach their ends.
Inputs may be any that keep to these rules, and one draw needn't show every extreme that they name: counts[i] valid frames start each block of 384 frames; at least one block is completely valid.
All inputs are finite; a program needn't handle non-finite values.
Results may differ from the reference program's by a relative error of at most 0.014.
Values may be sent and summed in bfloat16 or wider, within the bound.
A program may use at most 384 MiB of HBM per device.

```python
import math
import jax
import jax.numpy as jnp
from jax import lax

D = 1024
HEADS = 16
HDIM = 64
FF = 4096
P_SIZE = 16
GROUP_FRAMES = 384
DH = 1024
FRAMES = 1536
N_FRAMES = 4


def draw_counts(key, part):
    key = jax.random.fold_in(key, 7)
    first, second = jax.random.split(key)
    base = jax.random.randint(first, (N_FRAMES,), GROUP_FRAMES // 4, GROUP_FRAMES + 1)
    chosen = jax.random.randint(second, (), 0, N_FRAMES)
    return jnp.where(jnp.arange(N_FRAMES) == chosen, GROUP_FRAMES, base).astype(jnp.int32)


def strengthened(values, own_key, source, target, blocks, factor):
    owner, partner = [(jnp.arange(values.shape[axis_at]) // (values.shape[axis_at] // blocks)).reshape([-1 if axis == axis_at else 1 for axis in range(values.ndim)]) for axis_at in (source, target)]
    chosen = jax.random.permutation(own_key, blocks)[partner]
    strong = (owner == chosen) | (owner == (partner + blocks // 2) % blocks)
    return jnp.where(strong, factor * values, values)


def level_of(rng, shape, cuts, least, top_value):
    def one(position, shards_of):
        draws = jax.random.uniform(jax.random.fold_in(jax.random.fold_in(rng, 6), position), (shards_of,), jnp.float32, least / len(cuts), top_value / len(cuts))
        return jnp.repeat(jnp.exp(draws), shape[position] // shards_of).reshape((-1,) + (1,) * (len(shape) - position - 1))

    gain = one(*cuts[0])
    for cut in cuts[1:]:
        gain = gain * one(*cut)
    return gain


def bell_draw(stream_key, shape, width, limit, cuts=(), dtype=jnp.bfloat16):
    loudness = level_of(stream_key, shape, cuts, -0.22, 0.18) if cuts else 1.0
    values = jax.random.normal(stream_key, shape, jnp.float32) * width * loudness
    return jnp.minimum(jnp.maximum(values, -limit), limit).astype(dtype)


def bell_draw_with(key, extent, scale, limit, cuts, heavy, kind=jnp.bfloat16):
    drawn = scale * jax.random.normal(key, extent, jnp.float32)
    if cuts:
        drawn = drawn * level_of(key, extent, cuts, -0.22, 0.18)
    return jnp.clip(strengthened(drawn, jax.random.fold_in(key, 3), *heavy), -limit, limit).astype(kind)


def setup_inputs(seed: int = 0) -> dict:
    key_of = jax.random.split(jax.random.key(seed), 9)
    return {
        "inputs": bell_draw(key_of[0], (FRAMES, P_SIZE, D), 1.0, 6.0, ((0, 32),)),
        "counts": draw_counts(jax.random.fold_in(key_of[8], 71), 0),
        "norm_gains": jnp.clip(1.0 + 0.1 * jax.random.normal(key_of[2], (2, P_SIZE, D), jnp.float32), 0.5, 1.5),
        "in_weight": bell_draw(key_of[3], (P_SIZE, 3, D, DH), D ** -0.5, 0.1875, ((3, 8),)),
        "out_weight": bell_draw(key_of[4], (P_SIZE, DH, D), (DH // 8) ** -0.5, 0.5, ((1, 8),)),
        "gate_up": bell_draw(key_of[5], (P_SIZE, 2, D, FF), D ** -0.5, 0.1875, ((3, 8),)),
        "down_weight": bell_draw(key_of[6], (P_SIZE, FF, D), FF ** -0.5, 0.09375, ((1, 8),)),
        "cotangent": bell_draw_with(key_of[7], (FRAMES, P_SIZE, D), 1.0, 6.0, ((0, 32),), (0, 2, 32, 2.75)),
    }


@jax.custom_vjp
def low(v):
    return lax.optimization_barrier(v.astype(jnp.bfloat16)).astype(jnp.float32)

@jax.custom_vjp
def low_back(v):
    return v

def low_keep(v):
    return (low(v), None)

def low_pass(kept, grad):
    return (grad,)

def back_keep(v):
    return (v, None)

def back_low(kept, grad):
    return (low(grad),)
low.defvjp(low_keep, low_pass)
low_back.defvjp(back_keep, back_low)
epsilon = 1e-05
highest = lax.Precision.HIGHEST

def inverse_rms(values):
    return lax.rsqrt(lax.optimization_barrier(jnp.mean(values * values, axis=-1, keepdims=True)) + epsilon)

def reference(inputs, counts, norm_gains, in_weight, out_weight, gate_up, down_weight, cotangent):
    frame_ids = jnp.arange(FRAMES)
    valid = (frame_ids % GROUP_FRAMES < counts[frame_ids // GROUP_FRAMES]).astype(jnp.float32)
    block = math.gcd(FRAMES, 256)
    nblocks = FRAMES // block
    mask_blocks = valid.reshape(nblocks, block)
    causal = jnp.arange(P_SIZE)[:, None] >= jnp.arange(P_SIZE)[None, :]
    scale = HDIM ** (-0.5)

    def forward(residual, gains, w_in, w_out, w_gate, w_down):

        def one_block(pair):
            rows, mask = pair
            weight = mask[:, None, None]
            attn_in = low(rows * inverse_rms(rows) * gains[0])
            projected = jnp.einsum('fpd,pcde->fpce', attn_in, w_in, precision=highest)
            projected = low(low_back(projected)).reshape(block, P_SIZE, 3, HEADS, HDIM)
            queries, keys, values = (projected[:, :, 0], projected[:, :, 1], projected[:, :, 2])
            logits = low_back(jnp.einsum('fphe,fqhe->fhpq', queries, keys, precision=highest) * scale)
            logits = jnp.where(causal, logits, -1e+30)
            top = lax.optimization_barrier(jnp.max(logits, axis=-1, keepdims=True))
            expo = jnp.exp(logits - top)
            probs = low(expo / lax.optimization_barrier(jnp.sum(expo, axis=-1, keepdims=True)))
            mixed = jnp.einsum('fhpq,fqhe->fphe', probs, values, precision=highest)
            mixed = low(low_back(mixed)).reshape(block, P_SIZE, DH)
            attn = jnp.einsum('fpe,ped->fpd', mixed, w_out, precision=highest)
            hmid = rows + weight * low_back(attn)
            ffn_in = low(hmid * inverse_rms(hmid) * gains[1])
            pair_out = low_back(jnp.einsum('fpd,pcdk->fpck', ffn_in, w_gate, precision=highest))
            act = low(jax.nn.silu(pair_out[:, :, 0]) * pair_out[:, :, 1])
            ffn = jnp.einsum('fpk,pkd->fpd', act, w_down, precision=highest)
            return hmid + weight * low_back(ffn)
        stacked = lax.map(jax.checkpoint(one_block), (residual.reshape(nblocks, block, P_SIZE, D), mask_blocks))
        return stacked.reshape(FRAMES, P_SIZE, D)
    primal = (inputs.astype(jnp.float32), norm_gains.astype(jnp.float32), in_weight.astype(jnp.float32), out_weight.astype(jnp.float32), gate_up.astype(jnp.float32), down_weight.astype(jnp.float32))
    result, pullback = jax.vjp(forward, *primal)
    grads = pullback(cotangent.astype(jnp.float32))
    return (result.astype(jnp.bfloat16), grads[0].astype(jnp.bfloat16), grads[2], grads[3], grads[4], grads[5], grads[1])
```

```python
import functools
import math

import jax
import jax.numpy as jnp
from jax import lax
from jax.experimental import pallas as pl
from jax.experimental.pallas import tpu as pltpu
from jax.sharding import PartitionSpec as P

HDIM = 64
EPSILON = 1e-05
Z_CHIPS = 4
FRAME_BLOCK = 16
CHUNKS = 4
VMEM_BYTES = 56 * 1024 * 1024

f32 = jnp.float32
bf16 = jnp.bfloat16


class Line:
    def __init__(self, total, n, stride):
        self.n = n
        self.stride = stride
        self.starts = [i for i in range(total) if (i // stride) % n == 0]

    def up(self, low, high):
        return [(s + i * self.stride, s + (i + 1) * self.stride) for s in self.starts for i in range(low, high)]

    def down(self, low, high):
        return [(s + (i + 1) * self.stride, s + i * self.stride) for s in self.starts for i in range(low, high)]

    def gather(self, own):
        n = self.n
        if n == 1:
            return [own]
        if n == 2:
            return [own, lax.ppermute(own, "mp", self.up(0, 1) + self.down(0, 1))]
        ups, downs = [own], [own]
        for k in range(1, n):
            ups.append(lax.ppermute(ups[-1], "mp", self.up(k - 1, n - 1)))
            downs.append(lax.ppermute(downs[-1], "mp", self.down(0, n - k)))
        return [own] + [ups[k] + downs[n - k] for k in range(1, n)]

    def reduce(self, term):
        n = self.n
        if n == 1:
            return [term(0)]
        if n == 2:
            return [term(0), lax.ppermute(term(1).astype(bf16), "mp", self.up(0, 1) + self.down(0, 1)).astype(f32)]
        up = down = None
        for s in range(1, n):
            send_up = term(s) if up is None else term(s) + up.astype(f32)
            send_down = term(n - s) if down is None else term(n - s) + down.astype(f32)
            up = lax.ppermute(send_up.astype(bf16), "mp", self.up(0, min(s, n - 1)))
            down = lax.ppermute(send_down.astype(bf16), "mp", self.down(n - 1 - s, n - 1))
        return [term(0), up.astype(f32), down.astype(f32)]


class Group:
    def __init__(self, size):
        self.nz = math.gcd(size, Z_CHIPS)
        self.ny = size // self.nz
        self.z = Line(size, self.nz, self.ny)
        self.y = Line(size, self.ny, 1)

    def gather(self, own, z_first):
        if z_first:
            column = jnp.stack(self.z.gather(own), axis=1)
            return jnp.stack(self.y.gather(column), axis=1)
        row = jnp.stack(self.y.gather(own), axis=1)
        return jnp.stack(self.z.gather(row), axis=2)

    def reduce(self, parts, z_first):
        if not z_first:
            if self.ny == 2:
                got = lax.ppermute(parts[1], "mp", self.y.up(0, 1) + self.y.down(0, 1))
                columns = [parts[0], got]

                def term(k):
                    return columns[0][:, k].astype(f32) + columns[1][:, k].astype(f32)

            else:
                terms = self.y.reduce(lambda k: parts[k].astype(f32))

                def term(k):
                    return sum(t[:, k] for t in terms)

            return sum(self.z.reduce(term))

        def row(k):
            return jnp.stack([part[:, k] for part in parts], axis=1).astype(f32)

        terms = self.z.reduce(row)
        return sum(self.y.reduce(lambda k: sum(t[:, k] for t in terms)))


def frames_sum(keep, send, size):
    step = 1
    while True:
        got = lax.ppermute(send, "frames", [(i, i ^ step) for i in range(size)])
        total = keep.astype(f32) + got.astype(f32)
        step *= 2
        if step == size:
            return total[:, 0]
        keep, send = total[:, 0::2], total[:, 1::2].astype(send.dtype)


def dot(a, b, dims):
    return lax.dot_general(a, b, (dims, ((), ())), preferred_element_type=f32)


NN = ((1,), (0,))
NT = ((1,), (1,))
TN = ((0,), (0,))


def params():
    return pltpu.CompilerParams(vmem_limit_bytes=VMEM_BYTES)


def cost(flops, nbytes):
    return pl.CostEstimate(flops=int(flops), bytes_accessed=int(nbytes), transcendentals=0)


def qkv_kernel(x_ref, w_ref, q_ref, k_ref, v_ref):
    x = x_ref[0]
    for c, out in enumerate((q_ref, k_ref, v_ref)):
        out[0] = dot(x, w_ref[0, c], NN).astype(bf16)


def qkv(x, weight, base):
    count, rows, depth = x.shape
    width = weight.shape[-1]
    out = jax.ShapeDtypeStruct((count, rows, width), bf16)
    return pl.pallas_call(
        qkv_kernel,
        grid=(count,),
        in_specs=[
            pl.BlockSpec((1, rows, depth), lambda i: (i, 0, 0)),
            pl.BlockSpec((1, 3, depth, width), lambda i: (base + i, 0, 0, 0)),
        ],
        out_specs=[pl.BlockSpec((1, rows, width), lambda i: (i, 0, 0))] * 3,
        out_shape=[out] * 3,
        compiler_params=params(),
        cost_estimate=cost(6 * count * rows * depth * width, 2 * count * depth * (rows + 3 * width)),
        name="qkv",
    )(x, weight)


def head_masks(rows, width):
    lane = lax.broadcasted_iota(jnp.int32, (rows, width), 1)
    return [(lane >= h * HDIM) & (lane < (h + 1) * HDIM) for h in range(width // HDIM)]


def attention_mask(count, base, columns):
    rows = count * FRAME_BLOCK
    row = lax.broadcasted_iota(jnp.int32, (rows, columns), 0)
    column = lax.broadcasted_iota(jnp.int32, (rows, columns), 1)
    same = (row % FRAME_BLOCK) == (column % FRAME_BLOCK)
    return same & (column // FRAME_BLOCK <= row // FRAME_BLOCK + base)


def block_of(refs, rows):
    pieces = [ref[:, rows, :] for ref in refs]
    pieces = [p.reshape(p.shape[0] * p.shape[1], p.shape[2]) for p in pieces]
    return pieces[0] if len(pieces) == 1 else jnp.concatenate(pieces, axis=0)


def softmax(scores):
    top = jnp.max(scores, axis=-1, keepdims=True)
    raised = jnp.exp(scores - top)
    return raised / jnp.sum(raised, axis=-1, keepdims=True)


def pick(masks, values):
    out = values[0]
    for mask, value in zip(masks[1:], values[1:]):
        out = jnp.where(mask, value, out)
    return out


def attend_kernel(base, n_kv, ny, q_ref, *refs):
    k_refs, v_refs = refs[:n_kv], refs[n_kv : 2 * n_kv]
    w_ref = refs[2 * n_kv]
    mixed_ref = refs[2 * n_kv + 1]
    part_refs = refs[2 * n_kv + 2 :]
    count, rows, width = q_ref.shape
    columns = sum(ref.shape[0] for ref in k_refs) * FRAME_BLOCK
    step = pl.program_id(0)

    @pl.when(step == 0)
    def _():
        heads = head_masks(count * FRAME_BLOCK, width)
        allowed = attention_mask(count, base, columns)

        def one(b):
            at = pl.ds(pl.multiple_of(b * FRAME_BLOCK, FRAME_BLOCK), FRAME_BLOCK)
            queries = block_of([q_ref], at) * HDIM ** (-0.5)
            keys, values = block_of(k_refs, at), block_of(v_refs, at)
            outs = []
            for head in heads:
                mine = jnp.where(head, queries, jnp.zeros_like(queries))
                scores = jnp.where(allowed, dot(mine, keys, NT), -1e30)
                outs.append(dot(softmax(scores).astype(bf16), values, NN))
            mixed_ref[:, at, :] = pick(heads, outs).astype(bf16).reshape(count, FRAME_BLOCK, width)

        lax.fori_loop(0, rows // FRAME_BLOCK, lambda b, c: (one(b), c)[1], 0, unroll=4)

    out = dot(mixed_ref[step], w_ref[0], NN)
    span = rows // ny
    for y, part in enumerate(part_refs):
        part[0] = out[y * span : (y + 1) * span].astype(bf16)


def attend(q, ks, vs, weight, base, ny):
    count, rows, width = q.shape
    depth = weight.shape[-1]
    whole = pl.BlockSpec((count, rows, width), lambda i: (0, 0, 0))
    part = jax.ShapeDtypeStruct((count, rows // ny, depth), bf16)
    n_kv = len(ks)
    return pl.pallas_call(
        functools.partial(attend_kernel, base, n_kv, ny),
        grid=(count,),
        in_specs=[whole] * (1 + 2 * n_kv) + [pl.BlockSpec((1, width, depth), lambda i: (base + i, 0, 0))],
        out_specs=[whole] + [pl.BlockSpec((1, rows // ny, depth), lambda i: (i, 0, 0))] * ny,
        out_shape=[jax.ShapeDtypeStruct(q.shape, bf16)] + [part] * ny,
        compiler_params=params(),
        cost_estimate=cost(4 * count * rows * depth * width, 2 * count * rows * (depth + (2 + 2 * n_kv) * width)),
        name="attend",
    )(q, *ks, *vs, weight)


def gradient_pieces(size, depth):
    return size if size > 1 and (depth // size) % 128 == 0 else 1


def piece_at(piece, mine, span):
    return pl.ds(pl.multiple_of((piece ^ mine) * span, span), span)


def ffn_kernel(ny, pieces, mine_ref, x_ref, g_ref, gu_ref, dn_ref, *refs):
    outs, backs = refs[:ny], refs[ny : 2 * ny]
    gain_ref = refs[2 * ny]
    grads = refs[2 * ny + 1 :]
    rows, depth = x_ref.shape[1:]
    span = rows // ny
    x, g = x_ref[0], g_ref[0]
    gate = dot(x, gu_ref[0, 0], NN)
    up = dot(x, gu_ref[0, 1], NN)
    grad_act = dot(g, dn_ref[0], NT)
    sigma = 1.0 / (1.0 + jnp.exp(-gate))
    silu = gate * sigma
    act = (silu * up).astype(bf16)
    grad_gate = (grad_act * up * sigma * (1.0 + gate * (1.0 - sigma))).astype(bf16)
    grad_up = (grad_act * silu).astype(bf16)
    out = dot(act, dn_ref[0], NN)
    for y in range(ny):
        outs[y][0] = out[y * span : (y + 1) * span].astype(bf16)
    back = dot(grad_gate, gu_ref[0, 0], NT) + dot(grad_up, gu_ref[0, 1], NT)
    for y in range(ny):
        backs[y][0] = back[y * span : (y + 1) * span].astype(bf16)
    gain_ref[0] = jnp.sum(back * x.astype(f32), axis=0, keepdims=True)
    if pieces == 1:
        grads[0][0, 0] = dot(x, grad_gate, TN).astype(bf16)
        grads[0][0, 1] = dot(x, grad_up, TN).astype(bf16)
        grads[1][0] = dot(act, g, TN).astype(bf16)
        return
    mine = mine_ref[0]
    width = depth // pieces
    for r in range(pieces):
        at = piece_at(r, mine, width)
        gu_out, dn_out = grads[r % 2], grads[2 + r % 2]
        columns = x_ref[0, :, at]
        gu_out[0, r // 2, 0] = dot(columns, grad_gate, TN).astype(bf16)
        gu_out[0, r // 2, 1] = dot(columns, grad_up, TN).astype(bf16)
        dn_out[0, r // 2] = dot(act, g_ref[0, :, at], TN).astype(bf16)


def split_specs(shape, pieces, axis):
    if pieces == 1:
        block = (1,) + shape[1:]
        return [pl.BlockSpec(block, lambda i: (i,) + (0,) * (len(block) - 1))], [jax.ShapeDtypeStruct(shape, bf16)]
    rest = list(shape[1:])
    rest[axis - 1] //= pieces
    block = (1, pieces // 2) + tuple(rest)
    spec = pl.BlockSpec(block, lambda i: (i,) + (0,) * (len(block) - 1))
    return [spec] * 2, [jax.ShapeDtypeStruct((shape[0],) + block[1:], bf16)] * 2


def ffn(x, g, gate_up, down, base, ny, frames, mine):
    count, rows, depth = x.shape
    width = down.shape[1]
    pieces = gradient_pieces(frames, depth)
    part = jax.ShapeDtypeStruct((count, rows // ny, depth), bf16)
    part_spec = pl.BlockSpec((1, rows // ny, depth), lambda i: (i, 0, 0))
    row_spec = pl.BlockSpec((1, rows, depth), lambda i: (i, 0, 0))
    gu_specs, gu_shapes = split_specs((count, 2, depth, width), pieces, 2)
    dn_specs, dn_shapes = split_specs((count, width, depth), pieces, 2)
    out = pl.pallas_call(
        functools.partial(ffn_kernel, ny, pieces),
        grid=(count,),
        in_specs=[
            pl.BlockSpec(memory_space=pltpu.SMEM),
            row_spec,
            row_spec,
            pl.BlockSpec((1, 2, depth, width), lambda i: (base + i, 0, 0, 0)),
            pl.BlockSpec((1, width, depth), lambda i: (base + i, 0, 0)),
        ],
        out_specs=[part_spec] * (2 * ny) + [pl.BlockSpec((1, 1, depth), lambda i: (i, 0, 0))] + gu_specs + dn_specs,
        out_shape=[part] * (2 * ny) + [jax.ShapeDtypeStruct((count, 1, depth), f32)] + gu_shapes + dn_shapes,
        compiler_params=params(),
        cost_estimate=cost(18 * count * rows * depth * width, 2 * count * depth * (4 * rows + 6 * width)),
        name="ffn",
    )(mine, x, g, gate_up, down)
    n = len(gu_specs)
    return out[:ny], out[ny : 2 * ny], out[2 * ny], out[2 * ny + 1 : 2 * ny + 1 + n], out[2 * ny + 1 + n :]


def attend_back_kernel(base, n_kv, first, ny, pieces, mine_ref, ga_ref, gp_ref, x_ref, q_ref, *refs):
    refs = list(refs)

    def take(n):
        got = refs[:n]
        del refs[:n]
        return got

    k_refs, v_refs = take(n_kv), take(n_kv)
    (mixed_ref, ow_all_ref, iw_ref) = take(3)
    dk_in = dv_in = ()
    if not first:
        dk_in, dv_in = take(n_kv), take(n_kv)
    part_refs = take(ny)
    (gain_ref,) = take(1)
    n_out = 1 if pieces == 1 else 2
    iw_grads, ow_grads = take(n_out), take(n_out)
    dk_out, dv_out = take(n_kv - 1), take(n_kv - 1)
    gmixed_ref, gproj_ref = take(2)
    count, rows, width = q_ref.shape
    columns = n_kv * count * FRAME_BLOCK
    block = count * FRAME_BLOCK
    step = pl.program_id(0)

    @pl.when(step == 0)
    def _():
        for p in range(count):
            gmixed_ref[p] = dot(ga_ref[p], ow_all_ref[p], NT).astype(bf16)
        heads = head_masks(block, width)
        allowed = attention_mask(count, base, columns)
        factor = HDIM ** (-0.5)

        def one(b):
            at = pl.ds(pl.multiple_of(b * FRAME_BLOCK, FRAME_BLOCK), FRAME_BLOCK)
            queries = block_of([q_ref], at) * factor
            grad_mixed = block_of([gmixed_ref], at)
            keys, values = block_of(k_refs, at), block_of(v_refs, at)
            dqs, dk, dv = [], None, None
            for head in heads:
                my_q = jnp.where(head, queries, jnp.zeros_like(queries))
                my_g = jnp.where(head, grad_mixed, jnp.zeros_like(grad_mixed))
                probs = softmax(jnp.where(allowed, dot(my_q, keys, NT), -1e30))
                grad_probs = dot(my_g, values, NT)
                weighted = probs * grad_probs
                grad_scores = (weighted - probs * jnp.sum(weighted, axis=-1, keepdims=True)).astype(bf16)
                dqs.append(dot(grad_scores, keys, NN))
                more_k = dot(grad_scores, my_q, TN)
                more_v = dot(probs.astype(bf16), my_g, TN)
                dk = more_k if dk is None else dk + more_k
                dv = more_v if dv is None else dv + more_v
            gproj_ref[:, 0, at, :] = (pick(heads, dqs) * factor).astype(bf16).reshape(count, FRAME_BLOCK, width)
            for c, total, earlier, later in ((1, dk, dk_in, dk_out), (2, dv, dv_in, dv_out)):
                for j in range(n_kv):
                    piece = total[j * block : (j + 1) * block].reshape(count, FRAME_BLOCK, width)
                    if not first:
                        piece = piece + earlier[j][:, at, :]
                    if j < n_kv - 1:
                        later[j][:, at, :] = piece
                    else:
                        gproj_ref[:, c, at, :] = piece.astype(bf16)

        lax.fori_loop(0, rows // FRAME_BLOCK, lambda b, c: (one(b), c)[1], 0, unroll=2)

    grads = [gproj_ref[step, c] for c in range(3)]
    back = dot(grads[0], iw_ref[0, 0], NT) + dot(grads[1], iw_ref[0, 1], NT) + dot(grads[2], iw_ref[0, 2], NT)
    span = rows // ny
    for y, part in enumerate(part_refs):
        part[0] = back[y * span : (y + 1) * span].astype(bf16)
    gain_ref[0] = jnp.sum(back * x_ref[0].astype(f32), axis=0, keepdims=True)
    mixed = mixed_ref[0]
    if pieces == 1:
        for c in range(3):
            iw_grads[0][0, c] = dot(x_ref[0], grads[c], TN).astype(bf16)
        ow_grads[0][0] = dot(mixed, gp_ref[0], TN).astype(bf16)
        return
    mine = mine_ref[0]
    depth = x_ref.shape[2]
    for r in range(pieces):
        at = piece_at(r, mine, depth // pieces)
        columns = x_ref[0, :, at]
        for c in range(3):
            iw_grads[r % 2][0, r // 2, c] = dot(columns, grads[c], TN).astype(bf16)
        ow_grads[r % 2][0, r // 2] = dot(mixed, gp_ref[0, :, at], TN).astype(bf16)


def attend_back(grad_rows, x, q, ks, vs, mixed, out_weight, in_weight, dks, dvs, base, ny, frames, mine):
    count, rows, depth = x.shape
    width = q.shape[-1]
    pieces = gradient_pieces(frames, depth)
    n_kv = len(ks)
    first = not dks
    whole = pl.BlockSpec((count, rows, width), lambda i: (0, 0, 0))
    row_spec = pl.BlockSpec((1, rows, depth), lambda i: (i, 0, 0))
    chunk = base // count
    part = jax.ShapeDtypeStruct((count, rows // ny, depth), bf16)
    part_spec = pl.BlockSpec((1, rows // ny, depth), lambda i: (i, 0, 0))
    iw_specs, iw_shapes = split_specs((count, 3, depth, width), pieces, 2)
    ow_specs, ow_shapes = split_specs((count, width, depth), pieces, 2)
    total = jax.ShapeDtypeStruct((count, rows, width), f32)
    out = pl.pallas_call(
        functools.partial(attend_back_kernel, base, n_kv, first, ny, pieces),
        grid=(count,),
        in_specs=[
            pl.BlockSpec(memory_space=pltpu.SMEM),
            pl.BlockSpec((count, rows, depth), lambda i: (0, 0, 0)),
            row_spec,
            row_spec,
        ]
        + [whole] * (1 + 2 * n_kv)
        + [
            pl.BlockSpec((1, rows, width), lambda i: (i, 0, 0)),
            pl.BlockSpec((count, width, depth), lambda i: (chunk, 0, 0)),
            pl.BlockSpec((1, 3, depth, width), lambda i: (base + i, 0, 0, 0)),
        ]
        + [whole] * (len(dks) + len(dvs)),
        out_specs=[part_spec] * ny
        + [pl.BlockSpec((1, 1, depth), lambda i: (i, 0, 0))]
        + iw_specs
        + ow_specs
        + [whole] * (2 * (n_kv - 1)),
        out_shape=[part] * ny
        + [jax.ShapeDtypeStruct((count, 1, depth), f32)]
        + iw_shapes
        + ow_shapes
        + [total] * (2 * (n_kv - 1)),
        scratch_shapes=[pltpu.VMEM((count, rows, width), bf16), pltpu.VMEM((count, 3, rows, width), bf16)],
        compiler_params=params(),
        cost_estimate=cost(16 * count * rows * depth * width, 2 * count * rows * (4 * depth + 8 * n_kv * width)),
        name="attend_back",
    )(mine, grad_rows, grad_rows, x, q, *ks, *vs, mixed, out_weight, in_weight, *dks, *dvs)
    out = list(out)
    n = len(iw_specs)
    parts, gain = out[:ny], out[ny]
    iw, ow = out[ny + 1 : ny + 1 + n], out[ny + 1 + n : ny + 1 + 2 * n]
    rest = out[ny + 1 + 2 * n :]
    return parts, gain, iw, ow, rest[: n_kv - 1], rest[n_kv - 1 :]


def inverse_rms(values):
    return lax.rsqrt(jnp.mean(values * values, axis=-1, keepdims=True) + EPSILON)


def norm_back(grad_normed, normed, factor, gain):
    scaled = grad_normed * gain
    return factor * (scaled - normed * jnp.mean(scaled * normed, axis=-1, keepdims=True))


def body(inputs, counts, norm_gains, in_weight, out_weight, gate_up, down_weight, cotangent):
    frames, group_size = lax.axis_size("frames"), lax.axis_size("mp")
    group = Group(group_size)
    ny, nz = group.ny, group.nz
    local, positions, depth = inputs.shape
    rows = local * group_size
    size = positions // CHUNKS
    ids = lax.axis_index("mp") * local + jnp.arange(local)
    mask = (ids < counts[0]).astype(f32)[None, :, None]
    mine = lax.axis_index("frames").astype(jnp.int32)[None]
    x_major = jnp.swapaxes(inputs, 0, 1)
    g_major = jnp.swapaxes(cotangent, 0, 1)
    gains = norm_gains[:, :, None, :]

    def at(c):
        return slice(c * size, (c + 1) * size)

    def gathered(own, z_first):
        return group.gather(own, z_first).reshape(size, rows, depth)

    def reduced(parts, z_first):
        return group.reduce([p.reshape(size, nz, local, depth) for p in parts], z_first)

    def summed(grads):
        if len(grads) == 1:
            return lax.psum_scatter(grads[0], "frames", scatter_dimension=grads[0].ndim - 1, tiled=True).astype(f32)
        return frames_sum(grads[0], grads[1], frames)

    def summed_middle(grads):
        if len(grads) == 1:
            return lax.psum_scatter(grads[0], "frames", scatter_dimension=2, tiled=True).astype(f32)
        return frames_sum(grads[0], grads[1], frames)

    order = list(range(CHUNKS))[::-1]
    attn_in, qs, ks, vs = {}, {}, {}, {}
    for c in order:
        residual = x_major[at(c)].astype(f32)
        own = (residual * inverse_rms(residual) * gains[0, at(c)]).astype(bf16)
        attn_in[c] = gathered(own, True)
        qs[c], ks[c], vs[c] = qkv(attn_in[c], in_weight, c * size)

    outputs, input_grads = {}, {}
    g_in, g_out, g_gu, g_dn, gain_terms = {}, {}, {}, {}, {}
    dks, dvs = [], []
    for c in order:
        base = c * size
        gain_first, gain_second = gains[0, at(c)], gains[1, at(c)]
        residual = x_major[at(c)].astype(f32)
        gy = g_major[at(c)].astype(f32)
        grad_rows = gathered((mask * gy).astype(bf16), c % 2 == 0)
        earlier_k, earlier_v = [ks[j] for j in range(c + 1)], [vs[j] for j in range(c + 1)]
        mixed, *parts = attend(qs[c], earlier_k, earlier_v, out_weight, base, ny)
        hmid = residual + mask * reduced(parts, False)
        scale_second = inverse_rms(hmid)
        normed_second = hmid * scale_second
        ffn_rows = gathered((normed_second * gain_second).astype(bf16), True)
        out_parts, back_parts, gain_back, grad_gu, grad_dn = ffn(
            ffn_rows, grad_rows, gate_up, down_weight, base, ny, frames, mine
        )
        grad_ffn_in = reduced(back_parts, False)
        grad_mid = gy + norm_back(grad_ffn_in, normed_second, scale_second, gain_second)
        grad_attn = gathered((mask * grad_mid).astype(bf16), True)
        outputs[c] = (hmid + mask * reduced(out_parts, True)).astype(bf16)
        back, gain_front, grad_iw, grad_ow, dks, dvs = attend_back(
            grad_attn, attn_in[c], qs[c], earlier_k, earlier_v, mixed, out_weight, in_weight,
            dks, dvs, base, ny, frames, mine,
        )
        grad_attn_in = reduced(back, c % 2 == 1)
        scale_first = inverse_rms(residual)
        input_grads[c] = (
            grad_mid + norm_back(grad_attn_in, residual * scale_first, scale_first, gain_first)
        ).astype(bf16)
        gain_terms[c] = jnp.stack([gain_front[:, 0] / norm_gains[0, at(c)], gain_back[:, 0] / norm_gains[1, at(c)]])
        g_gu[c], g_dn[c] = summed_middle(grad_gu), summed(grad_dn)
        g_in[c], g_out[c] = summed_middle(grad_iw), summed(grad_ow)

    def joined(pieces, axis=0):
        return jnp.concatenate([pieces[c] for c in range(CHUNKS)], axis=axis)

    terms = lax.psum_scatter(joined(gain_terms, 1), "frames", scatter_dimension=2, tiled=True)
    step = 1
    while step < group_size:
        terms = terms + lax.ppermute(terms, "mp", [(i, i ^ step) for i in range(group_size)])
        step *= 2
    return (
        jnp.swapaxes(joined(outputs), 0, 1),
        jnp.swapaxes(joined(input_grads), 0, 1),
        joined(g_in),
        joined(g_out),
        joined(g_gu),
        joined(g_dn),
        terms,
    )


def solution(mesh):
    placed = (
        P(("frames", "mp"), None, None),
        P("frames"),
        P(),
        P(None, None, None, "mp"),
        P(None, "mp", None),
        P(None, None, None, "mp"),
        P(None, "mp", None),
        P(("frames", "mp"), None, None),
    )
    return jax.shard_map(
        body,
        mesh=mesh,
        in_specs=placed,
        out_specs=(
            P(("frames", "mp"), None, None),
            P(("frames", "mp"), None, None),
            P(None, None, "frames", "mp"),
            P(None, "mp", "frames"),
            P(None, None, "frames", "mp"),
            P(None, "mp", "frames"),
            P(None, None, "frames"),
        ),
        check_vma=False,
    )
```

```python
import functools
import math

import jax
import jax.numpy as jnp
from jax import lax
from jax.experimental import pallas as pl
from jax.experimental.pallas import tpu as pltpu
from jax.sharding import PartitionSpec as P

HDIM = 64
EPSILON = 1e-05
Z_CHIPS = 4
FRAME_BLOCK = 16
CHUNKS = 4
VMEM_BYTES = 56 * 1024 * 1024
KERNEL_VMEM_BYTES = 63 * 1024 * 1024

f32 = jnp.float32
bf16 = jnp.bfloat16


class Line:
    def __init__(self, total, n, stride):
        self.n = n
        self.stride = stride
        self.starts = [i for i in range(total) if (i // stride) % n == 0]

    def up(self, low, high):
        return [(s + i * self.stride, s + (i + 1) * self.stride) for s in self.starts for i in range(low, high)]

    def down(self, low, high):
        return [(s + (i + 1) * self.stride, s + i * self.stride) for s in self.starts for i in range(low, high)]

    def gather(self, own):
        n = self.n
        if n == 1:
            return [own]
        if n == 2:
            return [own, lax.ppermute(own, "mp", self.up(0, 1) + self.down(0, 1))]
        ups, downs = [own], [own]
        for k in range(1, n):
            ups.append(lax.ppermute(ups[-1], "mp", self.up(k - 1, n - 1)))
            downs.append(lax.ppermute(downs[-1], "mp", self.down(0, n - k)))
        return [own] + [ups[k] + downs[n - k] for k in range(1, n)]

    def reduce(self, term):
        n = self.n
        if n == 1:
            return [term(0)]
        if n == 2:
            return [term(0), lax.ppermute(term(1).astype(bf16), "mp", self.up(0, 1) + self.down(0, 1)).astype(f32)]
        up = down = None
        for s in range(1, n):
            send_up = term(s) if up is None else term(s) + up.astype(f32)
            send_down = term(n - s) if down is None else term(n - s) + down.astype(f32)
            up = lax.ppermute(send_up.astype(bf16), "mp", self.up(0, min(s, n - 1)))
            down = lax.ppermute(send_down.astype(bf16), "mp", self.down(n - 1 - s, n - 1))
        return [term(0), up.astype(f32), down.astype(f32)]


class Group:
    def __init__(self, size):
        self.nz = math.gcd(size, Z_CHIPS)
        self.ny = size // self.nz
        self.z = Line(size, self.nz, self.ny)
        self.y = Line(size, self.ny, 1)

    def gather(self, own, z_first):
        if z_first:
            column = jnp.stack(self.z.gather(own), axis=1)
            return jnp.stack(self.y.gather(column), axis=1)
        row = jnp.stack(self.y.gather(own), axis=1)
        return jnp.stack(self.z.gather(row), axis=2)

    def reduce(self, parts, z_first):
        if not z_first:
            if self.ny == 2:
                got = lax.ppermute(parts[1], "mp", self.y.up(0, 1) + self.y.down(0, 1))
                columns = [parts[0], got]

                def term(k):
                    return columns[0][:, k].astype(f32) + columns[1][:, k].astype(f32)

            else:
                terms = self.y.reduce(lambda k: parts[k].astype(f32))

                def term(k):
                    return sum(t[:, k] for t in terms)

            return sum(self.z.reduce(term))

        def row(k):
            return jnp.stack([part[:, k] for part in parts], axis=1).astype(f32)

        terms = self.z.reduce(row)
        return sum(self.y.reduce(lambda k: sum(t[:, k] for t in terms)))


def frames_sum(keep, send, size):
    step = 1
    while True:
        got = lax.ppermute(send, "frames", [(i, i ^ step) for i in range(size)])
        total = keep.astype(f32) + got.astype(f32)
        step *= 2
        if step == size:
            return total[:, 0]
        keep, send = total[:, 0::2], total[:, 1::2].astype(send.dtype)


def dot(a, b, dims):
    return lax.dot_general(a, b, (dims, ((), ())), preferred_element_type=f32)


NN = ((1,), (0,))
NT = ((1,), (1,))
TN = ((0,), (0,))


def params():
    return pltpu.CompilerParams(vmem_limit_bytes=VMEM_BYTES)


def cost(flops, nbytes):
    return pl.CostEstimate(flops=int(flops), bytes_accessed=int(nbytes), transcendentals=0)


def qkv_kernel(x_ref, w_ref, q_ref, k_ref, v_ref):
    x = x_ref[0]
    for c, out in enumerate((q_ref, k_ref, v_ref)):
        out[0] = dot(x, w_ref[0, c], NN).astype(bf16)


def qkv(x, weight, base):
    count, rows, depth = x.shape
    width = weight.shape[-1]
    out = jax.ShapeDtypeStruct((count, rows, width), bf16)
    return pl.pallas_call(
        qkv_kernel,
        grid=(count,),
        in_specs=[
            pl.BlockSpec((1, rows, depth), lambda i: (i, 0, 0)),
            pl.BlockSpec((1, 3, depth, width), lambda i: (base + i, 0, 0, 0)),
        ],
        out_specs=[pl.BlockSpec((1, rows, width), lambda i: (i, 0, 0))] * 3,
        out_shape=[out] * 3,
        compiler_params=params(),
        cost_estimate=cost(6 * count * rows * depth * width, 2 * count * depth * (rows + 3 * width)),
        name="qkv",
    )(x, weight)


def head_masks(rows, width):
    lane = lax.broadcasted_iota(jnp.int32, (rows, width), 1)
    return [(lane >= h * HDIM) & (lane < (h + 1) * HDIM) for h in range(width // HDIM)]


def attention_mask(count, base, columns):
    rows = count * FRAME_BLOCK
    row = lax.broadcasted_iota(jnp.int32, (rows, columns), 0)
    column = lax.broadcasted_iota(jnp.int32, (rows, columns), 1)
    same = (row % FRAME_BLOCK) == (column % FRAME_BLOCK)
    return same & (column // FRAME_BLOCK <= row // FRAME_BLOCK + base)


def block_of(refs, rows):
    pieces = [ref[:, rows, :] for ref in refs]
    pieces = [p.reshape(p.shape[0] * p.shape[1], p.shape[2]) for p in pieces]
    return pieces[0] if len(pieces) == 1 else jnp.concatenate(pieces, axis=0)


def softmax(scores):
    top = jnp.max(scores, axis=-1, keepdims=True)
    raised = jnp.exp(scores - top)
    return raised / jnp.sum(raised, axis=-1, keepdims=True)


def pick(masks, values):
    out = values[0]
    for mask, value in zip(masks[1:], values[1:]):
        out = jnp.where(mask, value, out)
    return out


def attend_kernel(base, n_kv, ny, q_ref, *refs):
    k_refs, v_refs = refs[:n_kv], refs[n_kv : 2 * n_kv]
    w_ref = refs[2 * n_kv]
    mixed_ref = refs[2 * n_kv + 1]
    part_refs = refs[2 * n_kv + 2 :]
    count, rows, width = q_ref.shape
    columns = sum(ref.shape[0] for ref in k_refs) * FRAME_BLOCK
    step = pl.program_id(0)

    @pl.when(step == 0)
    def _():
        heads = head_masks(count * FRAME_BLOCK, width)
        allowed = attention_mask(count, base, columns)

        def one(b):
            at = pl.ds(pl.multiple_of(b * FRAME_BLOCK, FRAME_BLOCK), FRAME_BLOCK)
            queries = block_of([q_ref], at) * HDIM ** (-0.5)
            keys, values = block_of(k_refs, at), block_of(v_refs, at)
            outs = []
            for head in heads:
                mine = jnp.where(head, queries, jnp.zeros_like(queries))
                scores = jnp.where(allowed, dot(mine, keys, NT), -1e30)
                outs.append(dot(softmax(scores).astype(bf16), values, NN))
            mixed_ref[:, at, :] = pick(heads, outs).astype(bf16).reshape(count, FRAME_BLOCK, width)

        lax.fori_loop(0, rows // FRAME_BLOCK, lambda b, c: (one(b), c)[1], 0, unroll=4)

    out = dot(mixed_ref[step], w_ref[0], NN)
    span = rows // ny
    for y, part in enumerate(part_refs):
        part[0] = out[y * span : (y + 1) * span].astype(bf16)


def attend(q, ks, vs, weight, base, ny):
    count, rows, width = q.shape
    depth = weight.shape[-1]
    whole = pl.BlockSpec((count, rows, width), lambda i: (0, 0, 0))
    part = jax.ShapeDtypeStruct((count, rows // ny, depth), bf16)
    n_kv = len(ks)
    return pl.pallas_call(
        functools.partial(attend_kernel, base, n_kv, ny),
        grid=(count,),
        in_specs=[whole] * (1 + 2 * n_kv) + [pl.BlockSpec((1, width, depth), lambda i: (base + i, 0, 0))],
        out_specs=[whole] + [pl.BlockSpec((1, rows // ny, depth), lambda i: (i, 0, 0))] * ny,
        out_shape=[jax.ShapeDtypeStruct(q.shape, bf16)] + [part] * ny,
        compiler_params=params(),
        cost_estimate=cost(4 * count * rows * depth * width, 2 * count * rows * (depth + (2 + 2 * n_kv) * width)),
        name="attend",
    )(q, *ks, *vs, weight)


def gradient_pieces(size, depth):
    return size if size > 1 and (depth // size) % 128 == 0 else 1


def piece_at(piece, mine, span):
    return pl.ds(pl.multiple_of((piece ^ mine) * span, span), span)


def ffn_kernel(ny, pieces, mine_ref, x_ref, g_ref, gu_ref, dn_ref, *refs):
    outs, backs = refs[:ny], refs[ny : 2 * ny]
    gain_ref = refs[2 * ny]
    grads = refs[2 * ny + 1 :]
    rows, depth = x_ref.shape[1:]
    span = rows // ny
    x, g = x_ref[0], g_ref[0]
    gate = dot(x, gu_ref[0, 0], NN)
    up = dot(x, gu_ref[0, 1], NN)
    grad_act = dot(g, dn_ref[0], NT)
    sigma = 1.0 / (1.0 + jnp.exp(-gate))
    silu = gate * sigma
    act = (silu * up).astype(bf16)
    grad_gate = (grad_act * up * sigma * (1.0 + gate * (1.0 - sigma))).astype(bf16)
    grad_up = (grad_act * silu).astype(bf16)
    out = dot(act, dn_ref[0], NN)
    for y in range(ny):
        outs[y][0] = out[y * span : (y + 1) * span].astype(bf16)
    back = dot(grad_gate, gu_ref[0, 0], NT) + dot(grad_up, gu_ref[0, 1], NT)
    for y in range(ny):
        backs[y][0] = back[y * span : (y + 1) * span].astype(bf16)
    gain_ref[0] = jnp.sum(back * x.astype(f32), axis=0, keepdims=True)
    if pieces == 1:
        grads[0][0, 0] = dot(x, grad_gate, TN).astype(bf16)
        grads[0][0, 1] = dot(x, grad_up, TN).astype(bf16)
        grads[1][0] = dot(act, g, TN).astype(bf16)
        return
    mine = mine_ref[0]
    width = depth // pieces
    for r in range(pieces):
        at = piece_at(r, mine, width)
        gu_out, dn_out = grads[r % 2], grads[2 + r % 2]
        columns = x_ref[0, :, at]
        gu_out[0, r // 2, 0] = dot(columns, grad_gate, TN).astype(bf16)
        gu_out[0, r // 2, 1] = dot(columns, grad_up, TN).astype(bf16)
        dn_out[0, r // 2] = dot(act, g_ref[0, :, at], TN).astype(bf16)


def split_specs(shape, pieces, axis):
    if pieces == 1:
        block = (1,) + shape[1:]
        return [pl.BlockSpec(block, lambda i: (i,) + (0,) * (len(block) - 1))], [jax.ShapeDtypeStruct(shape, bf16)]
    rest = list(shape[1:])
    rest[axis - 1] //= pieces
    block = (1, pieces // 2) + tuple(rest)
    spec = pl.BlockSpec(block, lambda i: (i,) + (0,) * (len(block) - 1))
    return [spec] * 2, [jax.ShapeDtypeStruct((shape[0],) + block[1:], bf16)] * 2


def ffn(x, g, gate_up, down, base, ny, frames, mine):
    count, rows, depth = x.shape
    width = down.shape[1]
    pieces = gradient_pieces(frames, depth)
    part = jax.ShapeDtypeStruct((count, rows // ny, depth), bf16)
    part_spec = pl.BlockSpec((1, rows // ny, depth), lambda i: (i, 0, 0))
    row_spec = pl.BlockSpec((1, rows, depth), lambda i: (i, 0, 0))
    gu_specs, gu_shapes = split_specs((count, 2, depth, width), pieces, 2)
    dn_specs, dn_shapes = split_specs((count, width, depth), pieces, 2)
    out = pl.pallas_call(
        functools.partial(ffn_kernel, ny, pieces),
        grid=(count,),
        in_specs=[
            pl.BlockSpec(memory_space=pltpu.SMEM),
            row_spec,
            row_spec,
            pl.BlockSpec((1, 2, depth, width), lambda i: (base + i, 0, 0, 0)),
            pl.BlockSpec((1, width, depth), lambda i: (base + i, 0, 0)),
        ],
        out_specs=[part_spec] * (2 * ny) + [pl.BlockSpec((1, 1, depth), lambda i: (i, 0, 0))] + gu_specs + dn_specs,
        out_shape=[part] * (2 * ny) + [jax.ShapeDtypeStruct((count, 1, depth), f32)] + gu_shapes + dn_shapes,
        compiler_params=params(),
        cost_estimate=cost(18 * count * rows * depth * width, 2 * count * depth * (4 * rows + 6 * width)),
        name="ffn",
    )(mine, x, g, gate_up, down)
    n = len(gu_specs)
    return out[:ny], out[ny : 2 * ny], out[2 * ny], out[2 * ny + 1 : 2 * ny + 1 + n], out[2 * ny + 1 + n :]


def attend_back_kernel(base, n_kv, first, ny, pieces, mine_ref, ga_ref, gp_ref, x_ref, q_ref, *refs):
    refs = list(refs)

    def take(n):
        got = refs[:n]
        del refs[:n]
        return got

    k_refs, v_refs = take(n_kv), take(n_kv)
    (mixed_ref, ow_all_ref, iw_ref) = take(3)
    dk_in = dv_in = ()
    if not first:
        dk_in, dv_in = take(n_kv), take(n_kv)
    part_refs = take(ny)
    (gain_ref,) = take(1)
    n_out = 1 if pieces == 1 else 2
    iw_grads, ow_grads = take(n_out), take(n_out)
    dk_out, dv_out = take(n_kv - 1), take(n_kv - 1)
    gmixed_ref, gproj_ref = take(2)
    count, rows, width = q_ref.shape
    columns = n_kv * count * FRAME_BLOCK
    block = count * FRAME_BLOCK
    step = pl.program_id(0)

    @pl.when(step == 0)
    def _():
        for p in range(count):
            gmixed_ref[p] = dot(ga_ref[p], ow_all_ref[p], NT).astype(bf16)
        heads = head_masks(block, width)
        allowed = attention_mask(count, base, columns)
        factor = HDIM ** (-0.5)

        def one(b):
            at = pl.ds(pl.multiple_of(b * FRAME_BLOCK, FRAME_BLOCK), FRAME_BLOCK)
            queries = block_of([q_ref], at) * factor
            grad_mixed = block_of([gmixed_ref], at)
            keys, values = block_of(k_refs, at), block_of(v_refs, at)
            dqs, dk, dv = [], None, None
            for head in heads:
                my_q = jnp.where(head, queries, jnp.zeros_like(queries))
                my_g = jnp.where(head, grad_mixed, jnp.zeros_like(grad_mixed))
                probs = softmax(jnp.where(allowed, dot(my_q, keys, NT), -1e30))
                grad_probs = dot(my_g, values, NT)
                weighted = probs * grad_probs
                grad_scores = (weighted - probs * jnp.sum(weighted, axis=-1, keepdims=True)).astype(bf16)
                dqs.append(dot(grad_scores, keys, NN))
                more_k = dot(grad_scores, my_q, TN)
                more_v = dot(probs.astype(bf16), my_g, TN)
                dk = more_k if dk is None else dk + more_k
                dv = more_v if dv is None else dv + more_v
            gproj_ref[:, 0, at, :] = (pick(heads, dqs) * factor).astype(bf16).reshape(count, FRAME_BLOCK, width)
            for c, total, earlier, later in ((1, dk, dk_in, dk_out), (2, dv, dv_in, dv_out)):
                for j in range(n_kv):
                    piece = total[j * block : (j + 1) * block].reshape(count, FRAME_BLOCK, width)
                    if not first:
                        piece = piece + earlier[j][:, at, :]
                    if j < n_kv - 1:
                        later[j][:, at, :] = piece
                    else:
                        gproj_ref[:, c, at, :] = piece.astype(bf16)

        lax.fori_loop(0, rows // FRAME_BLOCK, lambda b, c: (one(b), c)[1], 0, unroll=2)

    grads = [gproj_ref[step, c] for c in range(3)]
    back = dot(grads[0], iw_ref[0, 0], NT) + dot(grads[1], iw_ref[0, 1], NT) + dot(grads[2], iw_ref[0, 2], NT)
    span = rows // ny
    for y, part in enumerate(part_refs):
        part[0] = back[y * span : (y + 1) * span].astype(bf16)
    gain_ref[0] = jnp.sum(back * x_ref[0].astype(f32), axis=0, keepdims=True)
    mixed = mixed_ref[0]
    if pieces == 1:
        for c in range(3):
            iw_grads[0][0, c] = dot(x_ref[0], grads[c], TN).astype(bf16)
        ow_grads[0][0] = dot(mixed, gp_ref[0], TN).astype(bf16)
        return
    mine = mine_ref[0]
    depth = x_ref.shape[2]
    for r in range(pieces):
        at = piece_at(r, mine, depth // pieces)
        columns = x_ref[0, :, at]
        for c in range(3):
            iw_grads[r % 2][0, r // 2, c] = dot(columns, grads[c], TN).astype(bf16)
        ow_grads[r % 2][0, r // 2] = dot(mixed, gp_ref[0, :, at], TN).astype(bf16)


def attend_back(grad_rows, x, q, ks, vs, mixed, out_weight, in_weight, dks, dvs, base, ny, frames, mine):
    count, rows, depth = x.shape
    width = q.shape[-1]
    pieces = gradient_pieces(frames, depth)
    n_kv = len(ks)
    first = not dks
    whole = pl.BlockSpec((count, rows, width), lambda i: (0, 0, 0))
    row_spec = pl.BlockSpec((1, rows, depth), lambda i: (i, 0, 0))
    chunk = base // count
    part = jax.ShapeDtypeStruct((count, rows // ny, depth), bf16)
    part_spec = pl.BlockSpec((1, rows // ny, depth), lambda i: (i, 0, 0))
    iw_specs, iw_shapes = split_specs((count, 3, depth, width), pieces, 2)
    ow_specs, ow_shapes = split_specs((count, width, depth), pieces, 2)
    total = jax.ShapeDtypeStruct((count, rows, width), f32)
    out = pl.pallas_call(
        functools.partial(attend_back_kernel, base, n_kv, first, ny, pieces),
        grid=(count,),
        in_specs=[
            pl.BlockSpec(memory_space=pltpu.SMEM),
            pl.BlockSpec((count, rows, depth), lambda i: (0, 0, 0)),
            row_spec,
            row_spec,
        ]
        + [whole] * (1 + 2 * n_kv)
        + [
            pl.BlockSpec((1, rows, width), lambda i: (i, 0, 0)),
            pl.BlockSpec((count, width, depth), lambda i: (chunk, 0, 0)),
            pl.BlockSpec((1, 3, depth, width), lambda i: (base + i, 0, 0, 0)),
        ]
        + [whole] * (len(dks) + len(dvs)),
        out_specs=[part_spec] * ny
        + [pl.BlockSpec((1, 1, depth), lambda i: (i, 0, 0))]
        + iw_specs
        + ow_specs
        + [whole] * (2 * (n_kv - 1)),
        out_shape=[part] * ny
        + [jax.ShapeDtypeStruct((count, 1, depth), f32)]
        + iw_shapes
        + ow_shapes
        + [total] * (2 * (n_kv - 1)),
        scratch_shapes=[pltpu.VMEM((count, rows, width), bf16), pltpu.VMEM((count, 3, rows, width), bf16)],
        compiler_params=params(),
        cost_estimate=cost(16 * count * rows * depth * width, 2 * count * rows * (4 * depth + 8 * n_kv * width)),
        name="attend_back",
    )(mine, grad_rows, grad_rows, x, q, *ks, *vs, mixed, out_weight, in_weight, *dks, *dvs)
    out = list(out)
    n = len(iw_specs)
    parts, gain = out[:ny], out[ny]
    iw, ow = out[ny + 1 : ny + 1 + n], out[ny + 1 + n : ny + 1 + 2 * n]
    rest = out[ny + 1 + 2 * n :]
    return parts, gain, iw, ow, rest[: n_kv - 1], rest[n_kv - 1 :]


def inverse_rms(values):
    return lax.rsqrt(jnp.mean(values * values, axis=-1, keepdims=True) + EPSILON)


def norm_back(grad_normed, normed, factor, gain):
    scaled = grad_normed * gain
    return factor * (scaled - normed * jnp.mean(scaled * normed, axis=-1, keepdims=True))


def body(inputs, counts, norm_gains, in_weight, out_weight, gate_up, down_weight, cotangent):
    frames, group_size = lax.axis_size("frames"), lax.axis_size("mp")
    group = Group(group_size)
    ny, nz = group.ny, group.nz
    local, positions, depth = inputs.shape
    rows = local * group_size
    size = positions // CHUNKS
    ids = lax.axis_index("mp") * local + jnp.arange(local)
    mask = (ids < counts[0]).astype(f32)[None, :, None]
    mine = lax.axis_index("frames").astype(jnp.int32)[None]
    x_major = jnp.swapaxes(inputs, 0, 1)
    g_major = jnp.swapaxes(cotangent, 0, 1)
    gains = norm_gains[:, :, None, :]

    def at(c):
        return slice(c * size, (c + 1) * size)

    def gathered(own, z_first):
        return group.gather(own, z_first).reshape(size, rows, depth)

    def reduced(parts, z_first):
        return group.reduce([p.reshape(size, nz, local, depth) for p in parts], z_first)

    def summed(grads):
        if len(grads) == 1:
            return lax.psum_scatter(grads[0], "frames", scatter_dimension=grads[0].ndim - 1, tiled=True).astype(f32)
        return frames_sum(grads[0], grads[1], frames)

    def summed_middle(grads):
        if len(grads) == 1:
            return lax.psum_scatter(grads[0], "frames", scatter_dimension=2, tiled=True).astype(f32)
        return frames_sum(grads[0], grads[1], frames)

    order = list(range(CHUNKS))[::-1]
    attn_in, qs, ks, vs = {}, {}, {}, {}
    for c in order:
        residual = x_major[at(c)].astype(f32)
        own = (residual * inverse_rms(residual) * gains[0, at(c)]).astype(bf16)
        attn_in[c] = gathered(own, True)
        qs[c], ks[c], vs[c] = qkv(attn_in[c], in_weight, c * size)

    outputs, input_grads = {}, {}
    g_in, g_out, g_gu, g_dn, gain_terms = {}, {}, {}, {}, {}
    dks, dvs = [], []
    for c in order:
        base = c * size
        gain_first, gain_second = gains[0, at(c)], gains[1, at(c)]
        residual = x_major[at(c)].astype(f32)
        gy = g_major[at(c)].astype(f32)
        grad_rows = gathered((mask * gy).astype(bf16), c % 2 == 0)
        earlier_k, earlier_v = [ks[j] for j in range(c + 1)], [vs[j] for j in range(c + 1)]
        mixed, *parts = attend(qs[c], earlier_k, earlier_v, out_weight, base, ny)
        hmid = residual + mask * reduced(parts, False)
        scale_second = inverse_rms(hmid)
        normed_second = hmid * scale_second
        ffn_rows = gathered((normed_second * gain_second).astype(bf16), True)
        out_parts, back_parts, gain_back, grad_gu, grad_dn = ffn(
            ffn_rows, grad_rows, gate_up, down_weight, base, ny, frames, mine
        )
        grad_ffn_in = reduced(back_parts, False)
        grad_mid = gy + norm_back(grad_ffn_in, normed_second, scale_second, gain_second)
        grad_attn = gathered((mask * grad_mid).astype(bf16), True)
        outputs[c] = (hmid + mask * reduced(out_parts, True)).astype(bf16)
        back, gain_front, grad_iw, grad_ow, dks, dvs = attend_back(
            grad_attn, attn_in[c], qs[c], earlier_k, earlier_v, mixed, out_weight, in_weight,
            dks, dvs, base, ny, frames, mine,
        )
        grad_attn_in = reduced(back, c % 2 == 1)
        scale_first = inverse_rms(residual)
        input_grads[c] = (
            grad_mid + norm_back(grad_attn_in, residual * scale_first, scale_first, gain_first)
        ).astype(bf16)
        gain_terms[c] = jnp.stack([gain_front[:, 0] / norm_gains[0, at(c)], gain_back[:, 0] / norm_gains[1, at(c)]])
        g_gu[c], g_dn[c] = summed_middle(grad_gu), summed(grad_dn)
        g_in[c], g_out[c] = summed_middle(grad_iw), summed(grad_ow)

    def joined(pieces, axis=0):
        return jnp.concatenate([pieces[c] for c in range(CHUNKS)], axis=axis)

    terms = lax.psum_scatter(joined(gain_terms, 1), "frames", scatter_dimension=2, tiled=True)
    step = 1
    while step < group_size:
        terms = terms + lax.ppermute(terms, "mp", [(i, i ^ step) for i in range(group_size)])
        step *= 2
    return (
        jnp.swapaxes(joined(outputs), 0, 1),
        jnp.swapaxes(joined(input_grads), 0, 1),
        joined(g_in),
        joined(g_out),
        joined(g_gu),
        joined(g_dn),
        terms,
    )


MESH = pl.DeviceIdType.MESH
ZN, YN = 4, 2


def fits(frames, group_size, local, positions, depth, width, hidden):
    return (
        frames == 4
        and group_size == ZN * YN
        and local % 16 == 0
        and positions == 16
        and width % 128 == 0
        and (depth // frames) % 128 == 0
        and hidden % 128 == 0
    )


class Place:
    def __init__(self):
        self.m = lax.axis_index("mp")
        self.f = lax.axis_index("frames")
        self.z = self.m // YN
        self.ids = {
            "y": ("mp", self.m ^ 1),
            "up": ("mp", self.m + YN),
            "down": ("mp", self.m - YN),
            "core": ("frames", self.f ^ 1),
            "x": ("frames", self.f ^ 2),
        }

    def device(self, way):
        axis, index = self.ids[way]
        return {axis: index}

    def copy(self, src, dst, send, recv, way):
        return pltpu.make_async_remote_copy(
            src_ref=src, dst_ref=dst, send_sem=send, recv_sem=recv, device_id=self.device(way), device_id_type=MESH
        )


def when(condition, run):
    pl.when(condition)(run)


def wait_got(dst, send, recv, place):
    place.copy(dst, dst, send, recv, "y").wait_recv()


class GatherZ:
    def __init__(self, place, g, send, recv):
        self.place, self.g, self.send, self.recv = place, g, send, recv

    def site(self, number, way, src, dst):
        return self.place.copy(
            self.g.at[src[0], src[1]],
            self.g.at[dst[0], dst[1]],
            self.send.at[number],
            self.recv.at[dst[0] * 2 + dst[1]],
            way,
        )

    def up(self, k):
        return self.site(k - 1, "up", (k - 1, 0), (k, 0))

    def down(self, k):
        return self.site(2 + k, "down", ((5 - k) % 4, 0), (4 - k, 0))

    def across(self, k):
        return self.site(6 + k, "y", (k, 0), (k, 1))

    def got(self, k, y):
        wait_got(self.g.at[k, y], self.send.at[0], self.recv.at[k * 2 + y], self.place)

    def t1(self):
        z = self.place.z
        when(z < 3, lambda: self.up(1).start())
        when(z > 0, lambda: self.down(1).start())
        self.across(0).start()

    def t2(self):
        z = self.place.z

        def low():
            self.got(1, 0)
            when(z < 3, lambda: self.up(2).start())
            self.across(1).start()

        def high():
            self.got(3, 0)
            when(z > 0, lambda: self.down(2).start())
            self.across(3).start()

        when(z >= 1, low)
        when(z <= 2, high)
        when(z < 3, lambda: self.up(1).wait_send())
        when(z > 0, lambda: self.down(1).wait_send())
        self.across(0).wait_send()

    def t3(self):
        z = self.place.z
        self.got(2, 0)
        when(z == 2, lambda: self.up(3).start())
        when(z == 1, lambda: self.down(3).start())
        self.across(2).start()
        when((z >= 1) & (z < 3), lambda: self.up(2).wait_send())
        when((z <= 2) & (z > 0), lambda: self.down(2).wait_send())
        when(z >= 1, lambda: self.across(1).wait_send())
        when(z <= 2, lambda: self.across(3).wait_send())

    def t4(self):
        z = self.place.z

        def bottom():
            self.got(1, 0)
            self.across(1).start()

        def top():
            self.got(3, 0)
            self.across(3).start()

        when(z == 0, bottom)
        when(z == 3, top)
        when(z == 2, lambda: self.up(3).wait_send())
        when(z == 1, lambda: self.down(3).wait_send())
        self.across(2).wait_send()

    def done(self):
        z = self.place.z
        for k in range(4):
            self.got(k, 1)
        when(z == 0, lambda: self.across(1).wait_send())
        when(z == 3, lambda: self.across(3).wait_send())


class GatherY:
    def __init__(self, place, g, send, recv):
        self.place, self.g, self.send, self.recv = place, g, send, recv

    def site(self, number, way, src, dst):
        return self.place.copy(self.g.at[src], self.g.at[dst], self.send.at[number], self.recv.at[dst], way)

    def up(self, k):
        return self.site(k - 1, "up", k - 1, k)

    def down(self, k):
        return self.site(2 + k, "down", (5 - k) % 4, 4 - k)

    def across(self):
        return self.place.copy(self.g.at[0, 0], self.g.at[0, 1], self.send.at[6], self.recv.at[4], "y")

    def got(self, k):
        wait_got(self.g.at[k], self.send.at[0], self.recv.at[k], self.place)

    def t1(self):
        self.across().start()

    def t2(self):
        z = self.place.z
        wait_got(self.g.at[0, 1], self.send.at[0], self.recv.at[4], self.place)
        when(z < 3, lambda: self.up(1).start())
        when(z > 0, lambda: self.down(1).start())
        self.across().wait_send()

    def t3(self):
        z = self.place.z

        def low():
            self.got(1)
            when(z < 3, lambda: self.up(2).start())

        def high():
            self.got(3)
            when(z > 0, lambda: self.down(2).start())

        when(z >= 1, low)
        when(z <= 2, high)
        when(z < 3, lambda: self.up(1).wait_send())
        when(z > 0, lambda: self.down(1).wait_send())

    def t4(self):
        z = self.place.z
        self.got(2)
        when(z == 2, lambda: self.up(3).start())
        when(z == 1, lambda: self.down(3).start())
        when((z >= 1) & (z < 3), lambda: self.up(2).wait_send())
        when((z <= 2) & (z > 0), lambda: self.down(2).wait_send())

    def done(self):
        z = self.place.z
        when(z == 0, lambda: self.got(1))
        when(z == 3, lambda: self.got(3))
        when(z == 2, lambda: self.up(3).wait_send())
        when(z == 1, lambda: self.down(3).wait_send())


def up_to_f32(condition, ref):
    return jnp.where(condition, ref[...].astype(f32), 0.0)


class ReduceY:
    def __init__(self, place, part, over, ups, downs, send, recv):
        self.place, self.part, self.over, self.ups, self.downs = place, part, over, ups, downs
        self.send, self.recv = send, recv

    def across(self):
        return self.place.copy(self.part.at[:, 1], self.over, self.send.at[0], self.recv.at[0], "y")

    def up(self, s):
        return self.place.copy(
            self.part.at[s, 0], self.ups.at[s - 1], self.send.at[2 * s - 1], self.recv.at[s], "up"
        )

    def down(self, s):
        return self.place.copy(
            self.part.at[4 - s, 0], self.downs.at[s - 1], self.send.at[2 * s], self.recv.at[3 + s], "down"
        )

    def got_up(self, s):
        wait_got(self.ups.at[s - 1], self.send.at[0], self.recv.at[s], self.place)

    def got_down(self, s):
        wait_got(self.downs.at[s - 1], self.send.at[0], self.recv.at[3 + s], self.place)

    def local(self, k):
        return self.part[k, 0].astype(f32) + self.over[k].astype(f32)

    def store(self, k, value):
        self.part[k, 0] = value.astype(bf16)

    def t1(self):
        self.across().start()

    def t2(self):
        z = self.place.z
        wait_got(self.over, self.send.at[0], self.recv.at[0], self.place)

        def bottom():
            self.store(1, self.local(1))
            self.up(1).start()

        def top():
            self.store(3, self.local(3))
            self.down(1).start()

        when(z == 0, bottom)
        when(z == 3, top)
        self.across().wait_send()

    def t3(self):
        z = self.place.z
        when(z == 1, lambda: self.got_up(1))
        when(z == 2, lambda: self.got_down(1))
        self.store(
            2, self.local(2) + up_to_f32(z == 1, self.ups.at[0]) + up_to_f32(z == 2, self.downs.at[0])
        )
        when(z <= 1, lambda: self.up(2).start())
        when(z >= 2, lambda: self.down(2).start())
        when(z == 0, lambda: self.up(1).wait_send())
        when(z == 3, lambda: self.down(1).wait_send())

    def t4(self):
        z = self.place.z

        def low():
            when(z >= 1, lambda: self.got_up(2))
            self.store(3, self.local(3) + up_to_f32(z >= 1, self.ups.at[1]))
            self.up(3).start()

        def high():
            when(z <= 2, lambda: self.got_down(2))
            self.store(1, self.local(1) + up_to_f32(z <= 2, self.downs.at[1]))
            self.down(3).start()

        when(z <= 2, low)
        when(z >= 1, high)
        when(z <= 1, lambda: self.up(2).wait_send())
        when(z >= 2, lambda: self.down(2).wait_send())

    def done(self):
        z = self.place.z
        when(z >= 1, lambda: self.got_up(3))
        when(z <= 2, lambda: self.got_down(3))
        when(z <= 2, lambda: self.up(3).wait_send())
        when(z >= 1, lambda: self.down(3).wait_send())

    def total(self):
        z = self.place.z
        return self.local(0) + up_to_f32(z >= 1, self.ups.at[2]) + up_to_f32(z <= 2, self.downs.at[2])


class ReduceZ:
    def __init__(self, place, part, over, ups, downs, send, recv):
        self.place, self.part, self.over, self.ups, self.downs = place, part, over, ups, downs
        self.send, self.recv = send, recv

    def across(self):
        return self.place.copy(self.part.at[0, 1], self.over, self.send.at[0], self.recv.at[0], "y")

    def up(self, s):
        return self.place.copy(self.part.at[s], self.ups.at[s - 1], self.send.at[2 * s - 1], self.recv.at[s], "up")

    def down(self, s):
        return self.place.copy(
            self.part.at[4 - s], self.downs.at[s - 1], self.send.at[2 * s], self.recv.at[3 + s], "down"
        )

    got_up = ReduceY.got_up
    got_down = ReduceY.got_down

    def add(self, k, *more):
        value = self.part[k].astype(f32)
        for term in more:
            value = value + term
        self.part[k] = value.astype(bf16)

    def t1(self):
        z = self.place.z
        when(z == 0, lambda: self.up(1).start())
        when(z == 3, lambda: self.down(1).start())

    def t2(self):
        z = self.place.z

        def low():
            self.got_up(1)
            self.add(2, self.ups[0].astype(f32))

        def high():
            self.got_down(1)
            self.add(2, self.downs[0].astype(f32))

        when(z == 1, low)
        when(z == 2, high)
        when(z <= 1, lambda: self.up(2).start())
        when(z >= 2, lambda: self.down(2).start())
        when(z == 0, lambda: self.up(1).wait_send())
        when(z == 3, lambda: self.down(1).wait_send())

    def t3(self):
        z = self.place.z

        def low():
            self.got_up(2)
            self.add(3, self.ups[1].astype(f32))

        def high():
            self.got_down(2)
            self.add(1, self.downs[1].astype(f32))

        when((z >= 1) & (z <= 2), low)
        when((z >= 1) & (z <= 2), high)
        when(z <= 2, lambda: self.up(3).start())
        when(z >= 1, lambda: self.down(3).start())
        when(z <= 1, lambda: self.up(2).wait_send())
        when(z >= 2, lambda: self.down(2).wait_send())

    def t4(self):
        z = self.place.z
        when(z >= 1, lambda: self.got_up(3))
        when(z <= 2, lambda: self.got_down(3))
        value = self.part[0, 1].astype(f32)
        value = value + up_to_f32(z >= 1, self.ups.at[2, 1]) + up_to_f32(z <= 2, self.downs.at[2, 1])
        self.part[0, 1] = value.astype(bf16)
        self.across().start()
        when(z <= 2, lambda: self.up(3).wait_send())
        when(z >= 1, lambda: self.down(3).wait_send())

    def done(self):
        wait_got(self.over, self.send.at[0], self.recv.at[0], self.place)
        self.across().wait_send()

    def total(self):
        z = self.place.z
        value = self.part[0, 0].astype(f32) + self.over[...].astype(f32)
        return value + up_to_f32(z >= 1, self.ups.at[2, 0]) + up_to_f32(z <= 2, self.downs.at[2, 0])


class FramesSum:
    def __init__(self, place, sent, kept, from_core, from_x, sems, free, number):
        self.place, self.sent, self.kept, self.from_core, self.from_x = place, sent, kept, from_core, from_x
        self.sems, self.free, self.number = sems, free, number

    def core(self, j):
        return self.place.copy(self.sent[j], self.from_core[j], self.sems.at[0, j], self.sems.at[1, j], "core")

    def x(self, j):
        return self.place.copy(self.kept[j].at[1], self.from_x[j], self.sems.at[2, j], self.sems.at[3, j], "x")

    def out(self, j, outs, p):
        return pltpu.make_async_copy(self.kept[j].at[0], outs[j].at[p], self.sems.at[4, j])

    def start(self, later):
        def credit():
            pl.semaphore_wait(self.free.at[2 * self.number], 1)

        when(later, credit)
        for j in range(2):
            self.core(j).start()

    def middle(self, later):
        for j in range(2):
            self.core(j).wait_recv()

        def credit():
            pl.semaphore_wait(self.free.at[2 * self.number + 1], 1)

        when(later, credit)
        for j in range(2):
            kept, got = self.kept[j], self.from_core[j]
            kept[1] = (kept[1].astype(f32) + got[1].astype(f32)).astype(bf16)
            self.x(j).start()
        for j in range(2):
            self.core(j).wait_send()

    def finish(self, outs, p, more):
        for j in range(2):
            self.x(j).wait_recv()
            kept = self.kept[j]
            total = kept[0].astype(f32) + self.from_core[j][0].astype(f32) + self.from_x[j][...].astype(f32)
            kept[0] = total.astype(bf16)
            self.out(j, outs, p).start()

        def credit():
            for k, way in enumerate(("core", "x")):
                pl.semaphore_signal(
                    self.free.at[2 * self.number + k], inc=1, device_id=self.place.device(way), device_id_type=MESH
                )

        when(more, credit)
        for j in range(2):
            self.x(j).wait_send()

    def drained(self, outs, p):
        for j in range(2):
            self.out(j, outs, p).wait()


def layer_kernel(
    x_ref, cot_ref, mask_ref, gains_ref, in_w, out_w, gu_w, dn_w,
    out_hbm, ingrad_hbm, gu_hbm, dn_hbm, iw_hbm, ow_hbm, gain_ref, rows_hbm,
    g_ffn, g_cot, g_att, p_attn, p_gin, p_ffn, p_back,
    over_attn, over_gin, over_ffn, over_back, ups_attn, ups_gin, ups_ffn, ups_back,
    downs_attn, downs_gin, downs_ffn, downs_back,
    q_s, k_s, v_s, mixed_s, dk_s, dv_s, sc, dp,
    gu_v, dn_v, owa_v, owe_v, iw_v, xb,
    act_s, gg_s, gup_s, gmixed_s, gproj_s, hmid_s, ghmid_s, stage,
    gu_sent, gu_kept, gu_core, gu_x, dn_sent, dn_kept, dn_core, dn_x,
    iw_sent, iw_kept, iw_core, iw_x, ow_sent, ow_kept, ow_core, ow_x,
    sem_first, sem_first_got, sem_gather, sem_gather_got, sem_reduce, sem_reduce_got,
    sem_grad_ffn, sem_grad_att, sem_local, credits, free,
):
    place = Place()
    z, f = place.z, place.f
    positions, local, depth = x_ref.shape
    rows = ZN * YN * local
    last = positions - 1
    width = q_s.shape[-1]
    hidden = dn_v.shape[0]
    half = rows // 2
    quarter = depth // 4
    mask = mask_ref[...]
    scale = HDIM ** (-0.5)

    barrier = pltpu.get_barrier_semaphore()

    def greet(way):
        pl.semaphore_signal(barrier, inc=1, device_id=place.device(way), device_id_type=MESH)

    for way in ("y", "core", "x"):
        greet(way)
    when(z < 3, lambda: greet("up"))
    when(z > 0, lambda: greet("down"))
    pl.semaphore_wait(barrier, 3 + (z < 3).astype(jnp.int32) + (z > 0).astype(jnp.int32))

    def load(src, dst, number):
        return pltpu.make_async_copy(src, dst, sem_local.at[number])

    def load_owa(p):
        return load(out_w.at[p], owa_v, 0)

    def load_owe(p):
        return load(out_w.at[p], owe_v, 1)

    def load_iw(p, slot):
        return load(in_w.at[p], iw_v.at[slot], 2 + slot)

    def load_gu(p):
        return load(gu_w.at[p], gu_v, 4)

    def load_dn(p):
        return load(dn_w.at[p], dn_v, 5)

    def load_rows(p, dst, number):
        return load(rows_hbm.at[p // 4, :, :, (p % 4) // 2, p % 2], dst, number)

    groups = positions // 4

    def normalise(p, c):
        residual = x_ref[p].astype(f32)
        value = residual * inverse_rms(residual) * gains_ref[0, p]
        g_att[p // 8, (p % 8) // 2, p % 2] = value.astype(bf16)
        return c

    def own_rows(g):
        return load(g_att.at[g // 2, pl.ds((g % 2) * 2, 2)], rows_hbm.at[g, 0, 0], 10 + g)

    firsts = [
        GatherZ(place, rows_hbm.at[g], sem_first.at[g], sem_first_got.at[g]) for g in range(groups)
    ]
    for g in range(groups):
        lax.fori_loop(4 * g, 4 * g + 4, normalise, 0)
        own_rows(g).start()
        own_rows(g).wait()
        firsts[g].t1()
    load_owa(last).start()
    load_gu(last).start()
    load_dn(last).start()
    load_iw(0, 0).start()
    dk_s[...] = jnp.zeros_like(dk_s)
    dv_s[...] = jnp.zeros_like(dv_s)

    def project(p, c):
        slot = lax.rem(p, 2)
        load_rows(p, g_ffn.at[slot], 6 + slot).wait()
        load_iw(p, slot).wait()

        @pl.when(lax.rem(p, 4) < 3)
        def _():
            load_rows(p + 1, g_ffn.at[1 - slot], 7 - slot).start()

        @pl.when(p < last)
        def _():
            load_iw(p + 1, 1 - slot).start()

        block = g_ffn[slot].reshape(rows, depth)
        q_s[p] = (dot(block, iw_v[slot, 0], NN).astype(bf16) * scale).astype(bf16)
        k_s[p] = dot(block, iw_v[slot, 1], NN).astype(bf16)
        v_s[p] = dot(block, iw_v[slot, 2], NN).astype(bf16)
        return c

    for g in range(groups):
        firsts[g].t2()
    for g in range(groups):
        firsts[g].t3()
    for g in range(groups):
        firsts[g].t4()
    for g in range(groups):
        firsts[g].done()
        load_rows(4 * g, g_ffn.at[0], 6).start()
        lax.fori_loop(4 * g, 4 * g + 4, project, 0)
    load_owe(last).start()
    load_iw(last, 0).start()
    load_rows(last, xb, 8).start()

    row = lax.broadcasted_iota(jnp.int32, (2 * width, width), 0)
    column = lax.broadcasted_iota(jnp.int32, (2 * width, width), 1)
    ones = jnp.where((row % width) // HDIM == column // HDIM, 1.0, 0.0).astype(bf16)

    def per_head(product):
        high = product.astype(bf16)
        low = (product - high.astype(f32)).astype(bf16)
        return dot(jnp.concatenate([high, low], axis=1), ones, NN)

    def scores_of(p, q, at):
        def two(jj, top):
            first = per_head(q * k_s[2 * jj, at].astype(f32))
            second = per_head(q * k_s[2 * jj + 1, at].astype(f32))
            second = jnp.where(2 * jj + 1 <= p, second, -1e30)
            sc[2 * jj], sc[2 * jj + 1] = first, second
            return jnp.maximum(top, jnp.maximum(first, second))

        return lax.fori_loop(0, p // 2 + 1, two, jnp.full((half, width), -1e30, f32))

    def attend_one(p):
        pairs = p // 2 + 1
        for part in range(2):
            at = pl.ds(part * half, half)
            q = q_s[p, at].astype(f32)
            top = scores_of(p, q, at)

            def raise_two(jj, total):
                for t in range(2):
                    raised = jnp.exp(sc[2 * jj + t] - top)
                    sc[2 * jj + t] = raised
                    total = total + raised
                return total

            total = lax.fori_loop(0, pairs, raise_two, jnp.zeros((half, width), f32))
            factor = 1.0 / total

            def mix_two(jj, out):
                for t in range(2):
                    probs = (sc[2 * jj + t] * factor).astype(bf16).astype(f32)
                    out = out + probs * v_s[2 * jj + t, at].astype(f32)
                return out

            out = lax.fori_loop(0, pairs, mix_two, jnp.zeros((half, width), f32))
            mixed_s[p, at] = out.astype(bf16)

    def attend_back_one(p):
        pairs = p // 2 + 1
        for part in range(2):
            at = pl.ds(part * half, half)
            q = q_s[p, at].astype(f32)
            g = gmixed_s[at].astype(f32)
            top = scores_of(p, q, at)

            def raise_two(jj, carry):
                total, weighted = carry
                for t in range(2):
                    raised = jnp.exp(sc[2 * jj + t] - top)
                    sc[2 * jj + t] = raised
                    grad_probs = per_head(g * v_s[2 * jj + t, at].astype(f32))
                    dp[2 * jj + t] = grad_probs
                    total = total + raised
                    weighted = weighted + raised * grad_probs
                return total, weighted

            zero = jnp.zeros((half, width), f32)
            total, weighted = lax.fori_loop(0, pairs, raise_two, (zero, zero))
            factor = 1.0 / total
            centre = weighted * factor

            def back_two(jj, dq):
                for t in range(2):
                    j = 2 * jj + t
                    probs = sc[j] * factor
                    grad = (probs * (dp[j] - centre)).astype(bf16).astype(f32)
                    dq = dq + grad * k_s[j, at].astype(f32)
                    dk_s[j, at] = dk_s[j, at] + grad * q
                    dv_s[j, at] = dv_s[j, at] + probs.astype(bf16).astype(f32) * g
                return dq

            dq = lax.fori_loop(0, pairs, back_two, zero)
            gproj_s[0, at] = (dq * scale).astype(bf16)
        gproj_s[1] = dk_s[p].astype(bf16)
        gproj_s[2] = dv_s[p].astype(bf16)

    blocks = (ZN, YN, local, depth)
    grad_ffn = FramesSum(
        place, (gu_sent, dn_sent), (gu_kept, dn_kept), (gu_core, dn_core), (gu_x, dn_x), sem_grad_ffn, free, 0
    )
    grad_att = FramesSum(
        place, (iw_sent, ow_sent), (iw_kept, ow_kept), (iw_core, ow_core), (iw_x, ow_x), sem_grad_att, free, 1
    )
    ffn_outs, att_outs = (gu_hbm, dn_hbm), (iw_hbm, ow_hbm)

    def step(s, c):
        now = lax.rem(s, 2)
        then = 1 - now

        def valid(delay):
            return (s >= delay) & (s <= last + delay)

        def pos(delay):
            return last - (s - delay)

        def ring(delay):
            return lax.rem(s - delay + 8, 4)

        gather_ffn = GatherZ(place, g_ffn.at[now], sem_gather.at[0], sem_gather_got.at[0, now])
        gather_cot = GatherY(place, g_cot.at[now], sem_gather.at[1], sem_gather_got.at[1, now])
        gather_att = GatherY(place, g_att.at[now], sem_gather.at[2], sem_gather_got.at[2, now])

        def reducing(kind, part, over, ups, downs, number, which):
            return kind(
                place, part, over.at[which], ups.at[which], downs.at[which],
                sem_reduce.at[number], sem_reduce_got.at[number, which],
            )

        attn_now = reducing(ReduceY, p_attn, over_attn, ups_attn, downs_attn, 0, now)
        attn_then = reducing(ReduceY, p_attn, over_attn, ups_attn, downs_attn, 0, then)
        gin_now = reducing(ReduceY, p_gin, over_gin, ups_gin, downs_gin, 1, now)
        gin_then = reducing(ReduceY, p_gin, over_gin, ups_gin, downs_gin, 1, then)
        ffn_now = reducing(ReduceZ, p_ffn.at[now], over_ffn, ups_ffn, downs_ffn, 2, now)
        ffn_then = reducing(ReduceZ, p_ffn.at[then], over_ffn, ups_ffn, downs_ffn, 2, then)
        back_now = reducing(ReduceY, p_back.at[now], over_back, ups_back, downs_back, 3, now)
        back_then = reducing(ReduceY, p_back.at[then], over_back, ups_back, downs_back, 3, then)

        @pl.when(s >= 1)
        def _():
            pl.semaphore_wait(credits.at[0], 1)
            when(z > 0, lambda: pl.semaphore_wait(credits.at[1], 1))
            when(z < 3, lambda: pl.semaphore_wait(credits.at[2], 1))

        @pl.when(valid(1))
        def _():
            p = pos(1)
            g_cot[now, 0, 0] = (mask * cot_ref[p].astype(f32)).astype(bf16)
            gather_cot.t1()
            attn_then.done()
            hmid = x_ref[p].astype(f32) + mask * attn_then.total()
            hmid_s[ring(1)] = hmid
            g_ffn[now, 0, 0] = (hmid * inverse_rms(hmid) * gains_ref[1, p]).astype(bf16)
            gather_ffn.t1()

        @pl.when(valid(3))
        def _():
            p = pos(3)
            gin_then.done()
            hmid = hmid_s[ring(3)]
            factor = inverse_rms(hmid)
            grad = cot_ref[p].astype(f32) + norm_back(gin_then.total(), hmid * factor, factor, gains_ref[1, p])
            ghmid_s[ring(3)] = grad
            g_att[now, 0, 0] = (mask * grad).astype(bf16)
            gather_att.t1()

        @pl.when(valid(0))
        def _():
            p = pos(0)
            attend_one(p)
            load_owa(p).wait()
            p_attn[...] = dot(mixed_s[p], owa_v[...], NN).astype(bf16).reshape(blocks)
            attn_now.t1()
            when(s < last, lambda: load_owa(p - 1).start())

        when(valid(1), gather_cot.t2)
        when(valid(1), gather_ffn.t2)
        when(valid(3), gather_att.t2)
        when(valid(3), ffn_then.t3)
        when(valid(5), back_then.t2)

        @pl.when(valid(2))
        def _():
            p = pos(2)
            load_gu(p).wait()
            load_dn(p).wait()
            x = g_ffn[then].reshape(rows, depth)
            g = g_cot[then].reshape(rows, depth)
            for h in range(2):
                at = slice(h * hidden // 2, (h + 1) * hidden // 2)
                gate = dot(x, gu_v[0, :, at], NN)
                up = dot(x, gu_v[1, :, at], NN)
                grad_act = dot(g, dn_v[at], NT)
                sigma = 1.0 / (1.0 + jnp.exp(-gate))
                silu = gate * sigma
                act_s[:, at] = (silu * up).astype(bf16)
                gg_s[:, at] = (grad_act * up * sigma * (1.0 + gate * (1.0 - sigma))).astype(bf16)
                gup_s[:, at] = (grad_act * silu).astype(bf16)
            back = dot(gg_s[...], gu_v[0], NT) + dot(gup_s[...], gu_v[1], NT)
            p_gin[...] = back.astype(bf16).reshape(blocks)
            gin_now.t1()
            gain_ref[1, p] = jnp.sum(back * x.astype(f32), axis=0, keepdims=True)
            p_ffn[now] = dot(act_s[...], dn_v[...], NN).astype(bf16).reshape(blocks)
            ffn_now.t1()

            @pl.when(s < last + 2)
            def _():
                load_gu(p - 1).start()
                load_dn(p - 1).start()

        when(valid(1), gather_cot.t3)
        when(valid(1), gather_ffn.t3)
        when(valid(3), gather_att.t3)
        when(valid(0), attn_now.t2)
        when(valid(3), ffn_then.t4)
        when(valid(5), back_then.t3)
        when(valid(3), lambda: grad_ffn.finish(ffn_outs, pos(3), s < last + 3))

        @pl.when(valid(4))
        def _():
            p = pos(4)
            load_owe(p).wait()
            load_iw(p, 0).wait()
            load_rows(p, xb, 8).wait()
            gmixed_s[...] = dot(g_att[then].reshape(rows, depth), owe_v[...], NT).astype(bf16)
            attend_back_one(p)
            back = dot(gproj_s[0], iw_v[0, 0], NT)
            back = back + dot(gproj_s[1], iw_v[0, 1], NT)
            back = back + dot(gproj_s[2], iw_v[0, 2], NT)
            p_back[now] = back.astype(bf16).reshape(blocks)
            back_now.t1()
            gain_ref[0, p] = jnp.sum(back * xb[...].reshape(rows, depth).astype(f32), axis=0, keepdims=True)

        when(valid(1), gather_cot.t4)
        when(valid(1), gather_ffn.t4)
        when(valid(3), gather_att.t4)
        when(valid(0), attn_now.t3)
        when(valid(2), gin_now.t2)
        when(valid(2), ffn_now.t2)
        when(valid(5), back_then.t4)

        def out_copy(p):
            return pltpu.make_async_copy(stage.at[0], out_hbm.at[p], sem_local.at[14])

        def ingrad_copy(p):
            return pltpu.make_async_copy(stage.at[1], ingrad_hbm.at[p], sem_local.at[15])

        @pl.when(valid(3))
        def _():
            ffn_then.done()
            stage[0] = (hmid_s[ring(3)] + mask * ffn_then.total()).astype(bf16)
            out_copy(pos(3)).start()

        @pl.when(valid(3))
        def _():
            grad_ffn.drained(ffn_outs, pos(3))

        @pl.when(valid(2))
        def _():
            for r in range(4):
                at = piece_at(r, f, quarter)
                gu_to, dn_to = (gu_kept, dn_kept) if r % 2 == 0 else (gu_sent, dn_sent)
                columns = g_ffn[then, :, :, :, at].reshape(rows, quarter)
                gu_to[r // 2, 0] = dot(columns, gg_s[...], TN).astype(bf16)
                gu_to[r // 2, 1] = dot(columns, gup_s[...], TN).astype(bf16)
                dn_to[r // 2] = dot(act_s[...], g_cot[then, :, :, :, at].reshape(rows, quarter), TN).astype(bf16)
            grad_ffn.start(s > 2)

        when(valid(0), attn_now.t4)
        when(valid(2), gin_now.t3)

        @pl.when(valid(5))
        def _():
            p = pos(5)
            back_then.done()
            residual = x_ref[p].astype(f32)
            factor = inverse_rms(residual)
            grad = norm_back(back_then.total(), residual * factor, factor, gains_ref[0, p])
            stage[1] = (ghmid_s[ring(5)] + grad).astype(bf16)
            ingrad_copy(p).start()
            grad_att.finish(att_outs, p, s < last + 5)
            grad_att.drained(att_outs, p)

        @pl.when(valid(4))
        def _():
            p = pos(4)
            for r in range(4):
                at = piece_at(r, f, quarter)
                iw_to, ow_to = (iw_kept, ow_kept) if r % 2 == 0 else (iw_sent, ow_sent)
                columns = xb[:, :, :, at].reshape(rows, quarter)
                for j in range(3):
                    iw_to[r // 2, j] = dot(columns, gproj_s[j], TN).astype(bf16)
                ow_to[r // 2] = dot(mixed_s[p], g_att[then, :, :, :, at].reshape(rows, quarter), TN).astype(bf16)
            grad_att.start(s > 4)

            @pl.when(s < last + 4)
            def _():
                load_owe(p - 1).start()
                load_iw(p - 1, 0).start()
                load_rows(p - 1, xb, 8).start()

        @pl.when(s < last + 5)
        def _():
            def tell(number, way):
                pl.semaphore_signal(credits.at[number], inc=1, device_id=place.device(way), device_id_type=MESH)

            tell(0, "y")
            when(z < 3, lambda: tell(1, "up"))
            when(z > 0, lambda: tell(2, "down"))

        when(valid(2), lambda: grad_ffn.middle(s > 2))
        when(valid(2), gin_now.t4)
        when(valid(1), gather_cot.done)
        when(valid(1), gather_ffn.done)
        when(valid(3), gather_att.done)
        when(valid(4), lambda: grad_att.middle(s > 4))
        when(valid(3), lambda: out_copy(pos(3)).wait())
        when(valid(5), lambda: ingrad_copy(pos(5)).wait())
        return c

    lax.fori_loop(0, positions + 5, step, 0)


def layer(x, cot, mask, gains, in_weight, out_weight, gate_up, down):
    positions, local, depth = x.shape
    width, hidden = out_weight.shape[1], down.shape[1]
    rows = ZN * YN * local
    quarter = depth // 4
    block = (local, depth)
    groups = positions // 4

    def vm(*shape, dtype=bf16):
        return pltpu.VMEM(shape, dtype)

    def hbm(*shape, dtype=bf16):
        return jax.ShapeDtypeStruct(shape, dtype)

    everything = (ZN, YN) + block
    scratch = (
        [vm(2, *everything)] * 3
        + [vm(*everything)] * 2
        + [vm(2, *everything)] * 2
        + [vm(2, ZN, *block)] * 2
        + [vm(2, *block), vm(2, ZN, *block)]
        + [vm(2, 3, *block), vm(2, 3, *block), vm(2, 3, YN, *block), vm(2, 3, *block)] * 2
        + [vm(positions, rows, width)] * 4
        + [vm(positions, rows, width, dtype=f32)] * 2
        + [vm(positions, rows // 2, width, dtype=f32)] * 2
        + [vm(2, depth, hidden), vm(hidden, depth), vm(width, depth), vm(width, depth)]
        + [vm(2, 3, depth, width), vm(*everything)]
        + [vm(rows, hidden)] * 3
        + [vm(rows, width), vm(3, rows, width)]
        + [vm(4, *block, dtype=f32)] * 2
        + [vm(2, *block)]
        + [vm(2, 2, quarter, hidden)] * 3
        + [vm(2, quarter, hidden)]
        + [vm(2, hidden, quarter)] * 3
        + [vm(hidden, quarter)]
        + [vm(2, 3, quarter, width)] * 3
        + [vm(3, quarter, width)]
        + [vm(2, width, quarter)] * 3
        + [vm(width, quarter)]
        + [
            pltpu.SemaphoreType.DMA((groups, 10)),
            pltpu.SemaphoreType.DMA((groups, 8)),
            pltpu.SemaphoreType.DMA((3, 10)),
            pltpu.SemaphoreType.DMA((3, 2, 8)),
            pltpu.SemaphoreType.DMA((4, 7)),
            pltpu.SemaphoreType.DMA((4, 2, 7)),
            pltpu.SemaphoreType.DMA((5, 2)),
            pltpu.SemaphoreType.DMA((5, 2)),
            pltpu.SemaphoreType.DMA((16,)),
            pltpu.SemaphoreType.REGULAR((3,)),
            pltpu.SemaphoreType.REGULAR((4,)),
        ]
    )
    in_vmem = pl.BlockSpec(memory_space=pltpu.VMEM)
    anywhere = pl.BlockSpec(memory_space=pl.ANY)
    return pl.pallas_call(
        layer_kernel,
        in_specs=[in_vmem] * 4 + [anywhere] * 4,
        out_specs=[anywhere] * 6 + [in_vmem, anywhere],
        out_shape=[
            hbm(positions, *block),
            hbm(positions, *block),
            hbm(positions, 2, quarter, hidden),
            hbm(positions, hidden, quarter),
            hbm(positions, 3, quarter, width),
            hbm(positions, width, quarter),
            hbm(2, positions, 1, depth, dtype=f32),
            hbm(groups, ZN, YN, 2, 2, *block),
        ],
        scratch_shapes=scratch,
        compiler_params=pltpu.CompilerParams(
            collective_id=0, has_side_effects=True, vmem_limit_bytes=KERNEL_VMEM_BYTES
        ),
        name="layer",
    )(x, cot, mask, gains, in_weight, out_weight, gate_up, down)


def body_in_one(inputs, counts, norm_gains, in_weight, out_weight, gate_up, down_weight, cotangent):
    group_size = lax.axis_size("mp")
    local = inputs.shape[0]
    ids = lax.axis_index("mp") * local + jnp.arange(local)
    mask = (ids < counts[0]).astype(f32)[:, None]
    output, input_grad, g_gu, g_dn, g_in, g_out, gain_sums, _ = layer(
        jnp.swapaxes(inputs, 0, 1),
        jnp.swapaxes(cotangent, 0, 1),
        mask,
        norm_gains[:, :, None, :],
        in_weight,
        out_weight,
        gate_up,
        down_weight,
    )
    terms = gain_sums[:, :, 0] / norm_gains
    terms = lax.psum_scatter(terms, "frames", scatter_dimension=2, tiled=True)
    step = 1
    while step < group_size:
        terms = terms + lax.ppermute(terms, "mp", [(i, i ^ step) for i in range(group_size)])
        step *= 2
    return (
        jnp.swapaxes(output, 0, 1),
        jnp.swapaxes(input_grad, 0, 1),
        g_in.astype(f32),
        g_out.astype(f32),
        g_gu.astype(f32),
        g_dn.astype(f32),
        terms,
    )


def solution(mesh):
    placed = (
        P(("frames", "mp"), None, None),
        P("frames"),
        P(),
        P(None, None, None, "mp"),
        P(None, "mp", None),
        P(None, None, None, "mp"),
        P(None, "mp", None),
        P(("frames", "mp"), None, None),
    )
    def local_body(*args):
        frames, group_size = lax.axis_size("frames"), lax.axis_size("mp")
        local, positions, depth = args[0].shape
        width, hidden = args[4].shape[1], args[6].shape[1]
        one = fits(frames, group_size, local, positions, depth, width, hidden)
        return (body_in_one if one else body)(*args)

    return jax.shard_map(
        local_body,
        mesh=mesh,
        in_specs=placed,
        out_specs=(
            P(("frames", "mp"), None, None),
            P(("frames", "mp"), None, None),
            P(None, None, "frames", "mp"),
            P(None, "mp", "frames"),
            P(None, None, "frames", "mp"),
            P(None, "mp", "frames"),
            P(None, None, "frames"),
        ),
        check_vma=False,
    )
```

```python
import functools
import math

import jax
import jax.numpy as jnp
from jax import lax
from jax.experimental import pallas as pl
from jax.experimental.pallas import tpu as pltpu
from jax.sharding import PartitionSpec as P

HDIM = 64
EPSILON = 1e-05
Z_CHIPS = 4
FRAME_BLOCK = 16
CHUNKS = 4
VMEM_BYTES = 56 * 1024 * 1024
KERNEL_VMEM_BYTES = 63 * 1024 * 1024

f32 = jnp.float32
bf16 = jnp.bfloat16


class Line:
    def __init__(self, total, n, stride):
        self.n = n
        self.stride = stride
        self.starts = [i for i in range(total) if (i // stride) % n == 0]

    def up(self, low, high):
        return [(s + i * self.stride, s + (i + 1) * self.stride) for s in self.starts for i in range(low, high)]

    def down(self, low, high):
        return [(s + (i + 1) * self.stride, s + i * self.stride) for s in self.starts for i in range(low, high)]

    def gather(self, own):
        n = self.n
        if n == 1:
            return [own]
        if n == 2:
            return [own, lax.ppermute(own, "mp", self.up(0, 1) + self.down(0, 1))]
        ups, downs = [own], [own]
        for k in range(1, n):
            ups.append(lax.ppermute(ups[-1], "mp", self.up(k - 1, n - 1)))
            downs.append(lax.ppermute(downs[-1], "mp", self.down(0, n - k)))
        return [own] + [ups[k] + downs[n - k] for k in range(1, n)]

    def reduce(self, term):
        n = self.n
        if n == 1:
            return [term(0)]
        if n == 2:
            return [term(0), lax.ppermute(term(1).astype(bf16), "mp", self.up(0, 1) + self.down(0, 1)).astype(f32)]
        up = down = None
        for s in range(1, n):
            send_up = term(s) if up is None else term(s) + up.astype(f32)
            send_down = term(n - s) if down is None else term(n - s) + down.astype(f32)
            up = lax.ppermute(send_up.astype(bf16), "mp", self.up(0, min(s, n - 1)))
            down = lax.ppermute(send_down.astype(bf16), "mp", self.down(n - 1 - s, n - 1))
        return [term(0), up.astype(f32), down.astype(f32)]


class Group:
    def __init__(self, size):
        self.nz = math.gcd(size, Z_CHIPS)
        self.ny = size // self.nz
        self.z = Line(size, self.nz, self.ny)
        self.y = Line(size, self.ny, 1)

    def gather(self, own, z_first):
        if z_first:
            column = jnp.stack(self.z.gather(own), axis=1)
            return jnp.stack(self.y.gather(column), axis=1)
        row = jnp.stack(self.y.gather(own), axis=1)
        return jnp.stack(self.z.gather(row), axis=2)

    def reduce(self, parts, z_first):
        if not z_first:
            if self.ny == 2:
                got = lax.ppermute(parts[1], "mp", self.y.up(0, 1) + self.y.down(0, 1))
                columns = [parts[0], got]

                def term(k):
                    return columns[0][:, k].astype(f32) + columns[1][:, k].astype(f32)

            else:
                terms = self.y.reduce(lambda k: parts[k].astype(f32))

                def term(k):
                    return sum(t[:, k] for t in terms)

            return sum(self.z.reduce(term))

        def row(k):
            return jnp.stack([part[:, k] for part in parts], axis=1).astype(f32)

        terms = self.z.reduce(row)
        return sum(self.y.reduce(lambda k: sum(t[:, k] for t in terms)))


def frames_sum(keep, send, size):
    step = 1
    while True:
        got = lax.ppermute(send, "frames", [(i, i ^ step) for i in range(size)])
        total = keep.astype(f32) + got.astype(f32)
        step *= 2
        if step == size:
            return total[:, 0]
        keep, send = total[:, 0::2], total[:, 1::2].astype(send.dtype)


def dot(a, b, dims):
    return lax.dot_general(a, b, (dims, ((), ())), preferred_element_type=f32)


NN = ((1,), (0,))
NT = ((1,), (1,))
TN = ((0,), (0,))


def params():
    return pltpu.CompilerParams(vmem_limit_bytes=VMEM_BYTES)


def cost(flops, nbytes):
    return pl.CostEstimate(flops=int(flops), bytes_accessed=int(nbytes), transcendentals=0)


def qkv_kernel(x_ref, w_ref, q_ref, k_ref, v_ref):
    x = x_ref[0]
    for c, out in enumerate((q_ref, k_ref, v_ref)):
        out[0] = dot(x, w_ref[0, c], NN).astype(bf16)


def qkv(x, weight, base):
    count, rows, depth = x.shape
    width = weight.shape[-1]
    out = jax.ShapeDtypeStruct((count, rows, width), bf16)
    return pl.pallas_call(
        qkv_kernel,
        grid=(count,),
        in_specs=[
            pl.BlockSpec((1, rows, depth), lambda i: (i, 0, 0)),
            pl.BlockSpec((1, 3, depth, width), lambda i: (base + i, 0, 0, 0)),
        ],
        out_specs=[pl.BlockSpec((1, rows, width), lambda i: (i, 0, 0))] * 3,
        out_shape=[out] * 3,
        compiler_params=params(),
        cost_estimate=cost(6 * count * rows * depth * width, 2 * count * depth * (rows + 3 * width)),
        name="qkv",
    )(x, weight)


def head_masks(rows, width):
    lane = lax.broadcasted_iota(jnp.int32, (rows, width), 1)
    return [(lane >= h * HDIM) & (lane < (h + 1) * HDIM) for h in range(width // HDIM)]


def attention_mask(count, base, columns):
    rows = count * FRAME_BLOCK
    row = lax.broadcasted_iota(jnp.int32, (rows, columns), 0)
    column = lax.broadcasted_iota(jnp.int32, (rows, columns), 1)
    same = (row % FRAME_BLOCK) == (column % FRAME_BLOCK)
    return same & (column // FRAME_BLOCK <= row // FRAME_BLOCK + base)


def block_of(refs, rows):
    pieces = [ref[:, rows, :] for ref in refs]
    pieces = [p.reshape(p.shape[0] * p.shape[1], p.shape[2]) for p in pieces]
    return pieces[0] if len(pieces) == 1 else jnp.concatenate(pieces, axis=0)


def softmax(scores):
    top = jnp.max(scores, axis=-1, keepdims=True)
    raised = jnp.exp(scores - top)
    return raised / jnp.sum(raised, axis=-1, keepdims=True)


def pick(masks, values):
    out = values[0]
    for mask, value in zip(masks[1:], values[1:]):
        out = jnp.where(mask, value, out)
    return out


def attend_kernel(base, n_kv, ny, q_ref, *refs):
    k_refs, v_refs = refs[:n_kv], refs[n_kv : 2 * n_kv]
    w_ref = refs[2 * n_kv]
    mixed_ref = refs[2 * n_kv + 1]
    part_refs = refs[2 * n_kv + 2 :]
    count, rows, width = q_ref.shape
    columns = sum(ref.shape[0] for ref in k_refs) * FRAME_BLOCK
    step = pl.program_id(0)

    @pl.when(step == 0)
    def _():
        heads = head_masks(count * FRAME_BLOCK, width)
        allowed = attention_mask(count, base, columns)

        def one(b):
            at = pl.ds(pl.multiple_of(b * FRAME_BLOCK, FRAME_BLOCK), FRAME_BLOCK)
            queries = block_of([q_ref], at) * HDIM ** (-0.5)
            keys, values = block_of(k_refs, at), block_of(v_refs, at)
            outs = []
            for head in heads:
                mine = jnp.where(head, queries, jnp.zeros_like(queries))
                scores = jnp.where(allowed, dot(mine, keys, NT), -1e30)
                outs.append(dot(softmax(scores).astype(bf16), values, NN))
            mixed_ref[:, at, :] = pick(heads, outs).astype(bf16).reshape(count, FRAME_BLOCK, width)

        lax.fori_loop(0, rows // FRAME_BLOCK, lambda b, c: (one(b), c)[1], 0, unroll=4)

    out = dot(mixed_ref[step], w_ref[0], NN)
    span = rows // ny
    for y, part in enumerate(part_refs):
        part[0] = out[y * span : (y + 1) * span].astype(bf16)


def attend(q, ks, vs, weight, base, ny):
    count, rows, width = q.shape
    depth = weight.shape[-1]
    whole = pl.BlockSpec((count, rows, width), lambda i: (0, 0, 0))
    part = jax.ShapeDtypeStruct((count, rows // ny, depth), bf16)
    n_kv = len(ks)
    return pl.pallas_call(
        functools.partial(attend_kernel, base, n_kv, ny),
        grid=(count,),
        in_specs=[whole] * (1 + 2 * n_kv) + [pl.BlockSpec((1, width, depth), lambda i: (base + i, 0, 0))],
        out_specs=[whole] + [pl.BlockSpec((1, rows // ny, depth), lambda i: (i, 0, 0))] * ny,
        out_shape=[jax.ShapeDtypeStruct(q.shape, bf16)] + [part] * ny,
        compiler_params=params(),
        cost_estimate=cost(4 * count * rows * depth * width, 2 * count * rows * (depth + (2 + 2 * n_kv) * width)),
        name="attend",
    )(q, *ks, *vs, weight)


def gradient_pieces(size, depth):
    return size if size > 1 and (depth // size) % 128 == 0 else 1


def piece_at(piece, mine, span):
    return pl.ds(pl.multiple_of((piece ^ mine) * span, span), span)


def ffn_kernel(ny, pieces, mine_ref, x_ref, g_ref, gu_ref, dn_ref, *refs):
    outs, backs = refs[:ny], refs[ny : 2 * ny]
    gain_ref = refs[2 * ny]
    grads = refs[2 * ny + 1 :]
    rows, depth = x_ref.shape[1:]
    span = rows // ny
    x, g = x_ref[0], g_ref[0]
    gate = dot(x, gu_ref[0, 0], NN)
    up = dot(x, gu_ref[0, 1], NN)
    grad_act = dot(g, dn_ref[0], NT)
    sigma = 1.0 / (1.0 + jnp.exp(-gate))
    silu = gate * sigma
    act = (silu * up).astype(bf16)
    grad_gate = (grad_act * up * sigma * (1.0 + gate * (1.0 - sigma))).astype(bf16)
    grad_up = (grad_act * silu).astype(bf16)
    out = dot(act, dn_ref[0], NN)
    for y in range(ny):
        outs[y][0] = out[y * span : (y + 1) * span].astype(bf16)
    back = dot(grad_gate, gu_ref[0, 0], NT) + dot(grad_up, gu_ref[0, 1], NT)
    for y in range(ny):
        backs[y][0] = back[y * span : (y + 1) * span].astype(bf16)
    gain_ref[0] = jnp.sum(back * x.astype(f32), axis=0, keepdims=True)
    if pieces == 1:
        grads[0][0, 0] = dot(x, grad_gate, TN).astype(bf16)
        grads[0][0, 1] = dot(x, grad_up, TN).astype(bf16)
        grads[1][0] = dot(act, g, TN).astype(bf16)
        return
    mine = mine_ref[0]
    width = depth // pieces
    for r in range(pieces):
        at = piece_at(r, mine, width)
        gu_out, dn_out = grads[r % 2], grads[2 + r % 2]
        columns = x_ref[0, :, at]
        gu_out[0, r // 2, 0] = dot(columns, grad_gate, TN).astype(bf16)
        gu_out[0, r // 2, 1] = dot(columns, grad_up, TN).astype(bf16)
        dn_out[0, r // 2] = dot(act, g_ref[0, :, at], TN).astype(bf16)


def split_specs(shape, pieces, axis):
    if pieces == 1:
        block = (1,) + shape[1:]
        return [pl.BlockSpec(block, lambda i: (i,) + (0,) * (len(block) - 1))], [jax.ShapeDtypeStruct(shape, bf16)]
    rest = list(shape[1:])
    rest[axis - 1] //= pieces
    block = (1, pieces // 2) + tuple(rest)
    spec = pl.BlockSpec(block, lambda i: (i,) + (0,) * (len(block) - 1))
    return [spec] * 2, [jax.ShapeDtypeStruct((shape[0],) + block[1:], bf16)] * 2


def ffn(x, g, gate_up, down, base, ny, frames, mine):
    count, rows, depth = x.shape
    width = down.shape[1]
    pieces = gradient_pieces(frames, depth)
    part = jax.ShapeDtypeStruct((count, rows // ny, depth), bf16)
    part_spec = pl.BlockSpec((1, rows // ny, depth), lambda i: (i, 0, 0))
    row_spec = pl.BlockSpec((1, rows, depth), lambda i: (i, 0, 0))
    gu_specs, gu_shapes = split_specs((count, 2, depth, width), pieces, 2)
    dn_specs, dn_shapes = split_specs((count, width, depth), pieces, 2)
    out = pl.pallas_call(
        functools.partial(ffn_kernel, ny, pieces),
        grid=(count,),
        in_specs=[
            pl.BlockSpec(memory_space=pltpu.SMEM),
            row_spec,
            row_spec,
            pl.BlockSpec((1, 2, depth, width), lambda i: (base + i, 0, 0, 0)),
            pl.BlockSpec((1, width, depth), lambda i: (base + i, 0, 0)),
        ],
        out_specs=[part_spec] * (2 * ny) + [pl.BlockSpec((1, 1, depth), lambda i: (i, 0, 0))] + gu_specs + dn_specs,
        out_shape=[part] * (2 * ny) + [jax.ShapeDtypeStruct((count, 1, depth), f32)] + gu_shapes + dn_shapes,
        compiler_params=params(),
        cost_estimate=cost(18 * count * rows * depth * width, 2 * count * depth * (4 * rows + 6 * width)),
        name="ffn",
    )(mine, x, g, gate_up, down)
    n = len(gu_specs)
    return out[:ny], out[ny : 2 * ny], out[2 * ny], out[2 * ny + 1 : 2 * ny + 1 + n], out[2 * ny + 1 + n :]


def attend_back_kernel(base, n_kv, first, ny, pieces, mine_ref, ga_ref, gp_ref, x_ref, q_ref, *refs):
    refs = list(refs)

    def take(n):
        got = refs[:n]
        del refs[:n]
        return got

    k_refs, v_refs = take(n_kv), take(n_kv)
    (mixed_ref, ow_all_ref, iw_ref) = take(3)
    dk_in = dv_in = ()
    if not first:
        dk_in, dv_in = take(n_kv), take(n_kv)
    part_refs = take(ny)
    (gain_ref,) = take(1)
    n_out = 1 if pieces == 1 else 2
    iw_grads, ow_grads = take(n_out), take(n_out)
    dk_out, dv_out = take(n_kv - 1), take(n_kv - 1)
    gmixed_ref, gproj_ref = take(2)
    count, rows, width = q_ref.shape
    columns = n_kv * count * FRAME_BLOCK
    block = count * FRAME_BLOCK
    step = pl.program_id(0)

    @pl.when(step == 0)
    def _():
        for p in range(count):
            gmixed_ref[p] = dot(ga_ref[p], ow_all_ref[p], NT).astype(bf16)
        heads = head_masks(block, width)
        allowed = attention_mask(count, base, columns)
        factor = HDIM ** (-0.5)

        def one(b):
            at = pl.ds(pl.multiple_of(b * FRAME_BLOCK, FRAME_BLOCK), FRAME_BLOCK)
            queries = block_of([q_ref], at) * factor
            grad_mixed = block_of([gmixed_ref], at)
            keys, values = block_of(k_refs, at), block_of(v_refs, at)
            dqs, dk, dv = [], None, None
            for head in heads:
                my_q = jnp.where(head, queries, jnp.zeros_like(queries))
                my_g = jnp.where(head, grad_mixed, jnp.zeros_like(grad_mixed))
                probs = softmax(jnp.where(allowed, dot(my_q, keys, NT), -1e30))
                grad_probs = dot(my_g, values, NT)
                weighted = probs * grad_probs
                grad_scores = (weighted - probs * jnp.sum(weighted, axis=-1, keepdims=True)).astype(bf16)
                dqs.append(dot(grad_scores, keys, NN))
                more_k = dot(grad_scores, my_q, TN)
                more_v = dot(probs.astype(bf16), my_g, TN)
                dk = more_k if dk is None else dk + more_k
                dv = more_v if dv is None else dv + more_v
            gproj_ref[:, 0, at, :] = (pick(heads, dqs) * factor).astype(bf16).reshape(count, FRAME_BLOCK, width)
            for c, total, earlier, later in ((1, dk, dk_in, dk_out), (2, dv, dv_in, dv_out)):
                for j in range(n_kv):
                    piece = total[j * block : (j + 1) * block].reshape(count, FRAME_BLOCK, width)
                    if not first:
                        piece = piece + earlier[j][:, at, :]
                    if j < n_kv - 1:
                        later[j][:, at, :] = piece
                    else:
                        gproj_ref[:, c, at, :] = piece.astype(bf16)

        lax.fori_loop(0, rows // FRAME_BLOCK, lambda b, c: (one(b), c)[1], 0, unroll=2)

    grads = [gproj_ref[step, c] for c in range(3)]
    back = dot(grads[0], iw_ref[0, 0], NT) + dot(grads[1], iw_ref[0, 1], NT) + dot(grads[2], iw_ref[0, 2], NT)
    span = rows // ny
    for y, part in enumerate(part_refs):
        part[0] = back[y * span : (y + 1) * span].astype(bf16)
    gain_ref[0] = jnp.sum(back * x_ref[0].astype(f32), axis=0, keepdims=True)
    mixed = mixed_ref[0]
    if pieces == 1:
        for c in range(3):
            iw_grads[0][0, c] = dot(x_ref[0], grads[c], TN).astype(bf16)
        ow_grads[0][0] = dot(mixed, gp_ref[0], TN).astype(bf16)
        return
    mine = mine_ref[0]
    depth = x_ref.shape[2]
    for r in range(pieces):
        at = piece_at(r, mine, depth // pieces)
        columns = x_ref[0, :, at]
        for c in range(3):
            iw_grads[r % 2][0, r // 2, c] = dot(columns, grads[c], TN).astype(bf16)
        ow_grads[r % 2][0, r // 2] = dot(mixed, gp_ref[0, :, at], TN).astype(bf16)


def attend_back(grad_rows, x, q, ks, vs, mixed, out_weight, in_weight, dks, dvs, base, ny, frames, mine):
    count, rows, depth = x.shape
    width = q.shape[-1]
    pieces = gradient_pieces(frames, depth)
    n_kv = len(ks)
    first = not dks
    whole = pl.BlockSpec((count, rows, width), lambda i: (0, 0, 0))
    row_spec = pl.BlockSpec((1, rows, depth), lambda i: (i, 0, 0))
    chunk = base // count
    part = jax.ShapeDtypeStruct((count, rows // ny, depth), bf16)
    part_spec = pl.BlockSpec((1, rows // ny, depth), lambda i: (i, 0, 0))
    iw_specs, iw_shapes = split_specs((count, 3, depth, width), pieces, 2)
    ow_specs, ow_shapes = split_specs((count, width, depth), pieces, 2)
    total = jax.ShapeDtypeStruct((count, rows, width), f32)
    out = pl.pallas_call(
        functools.partial(attend_back_kernel, base, n_kv, first, ny, pieces),
        grid=(count,),
        in_specs=[
            pl.BlockSpec(memory_space=pltpu.SMEM),
            pl.BlockSpec((count, rows, depth), lambda i: (0, 0, 0)),
            row_spec,
            row_spec,
        ]
        + [whole] * (1 + 2 * n_kv)
        + [
            pl.BlockSpec((1, rows, width), lambda i: (i, 0, 0)),
            pl.BlockSpec((count, width, depth), lambda i: (chunk, 0, 0)),
            pl.BlockSpec((1, 3, depth, width), lambda i: (base + i, 0, 0, 0)),
        ]
        + [whole] * (len(dks) + len(dvs)),
        out_specs=[part_spec] * ny
        + [pl.BlockSpec((1, 1, depth), lambda i: (i, 0, 0))]
        + iw_specs
        + ow_specs
        + [whole] * (2 * (n_kv - 1)),
        out_shape=[part] * ny
        + [jax.ShapeDtypeStruct((count, 1, depth), f32)]
        + iw_shapes
        + ow_shapes
        + [total] * (2 * (n_kv - 1)),
        scratch_shapes=[pltpu.VMEM((count, rows, width), bf16), pltpu.VMEM((count, 3, rows, width), bf16)],
        compiler_params=params(),
        cost_estimate=cost(16 * count * rows * depth * width, 2 * count * rows * (4 * depth + 8 * n_kv * width)),
        name="attend_back",
    )(mine, grad_rows, grad_rows, x, q, *ks, *vs, mixed, out_weight, in_weight, *dks, *dvs)
    out = list(out)
    n = len(iw_specs)
    parts, gain = out[:ny], out[ny]
    iw, ow = out[ny + 1 : ny + 1 + n], out[ny + 1 + n : ny + 1 + 2 * n]
    rest = out[ny + 1 + 2 * n :]
    return parts, gain, iw, ow, rest[: n_kv - 1], rest[n_kv - 1 :]


def inverse_rms(values):
    return lax.rsqrt(jnp.mean(values * values, axis=-1, keepdims=True) + EPSILON)


def norm_back(grad_normed, normed, factor, gain):
    scaled = grad_normed * gain
    return factor * (scaled - normed * jnp.mean(scaled * normed, axis=-1, keepdims=True))


def body(inputs, counts, norm_gains, in_weight, out_weight, gate_up, down_weight, cotangent):
    frames, group_size = lax.axis_size("frames"), lax.axis_size("mp")
    group = Group(group_size)
    ny, nz = group.ny, group.nz
    local, positions, depth = inputs.shape
    rows = local * group_size
    size = positions // CHUNKS
    ids = lax.axis_index("mp") * local + jnp.arange(local)
    mask = (ids < counts[0]).astype(f32)[None, :, None]
    mine = lax.axis_index("frames").astype(jnp.int32)[None]
    x_major = jnp.swapaxes(inputs, 0, 1)
    g_major = jnp.swapaxes(cotangent, 0, 1)
    gains = norm_gains[:, :, None, :]

    def at(c):
        return slice(c * size, (c + 1) * size)

    def gathered(own, z_first):
        return group.gather(own, z_first).reshape(size, rows, depth)

    def reduced(parts, z_first):
        return group.reduce([p.reshape(size, nz, local, depth) for p in parts], z_first)

    def summed(grads):
        if len(grads) == 1:
            return lax.psum_scatter(grads[0], "frames", scatter_dimension=grads[0].ndim - 1, tiled=True).astype(f32)
        return frames_sum(grads[0], grads[1], frames)

    def summed_middle(grads):
        if len(grads) == 1:
            return lax.psum_scatter(grads[0], "frames", scatter_dimension=2, tiled=True).astype(f32)
        return frames_sum(grads[0], grads[1], frames)

    order = list(range(CHUNKS))[::-1]
    attn_in, qs, ks, vs = {}, {}, {}, {}
    for c in order:
        residual = x_major[at(c)].astype(f32)
        own = (residual * inverse_rms(residual) * gains[0, at(c)]).astype(bf16)
        attn_in[c] = gathered(own, True)
        qs[c], ks[c], vs[c] = qkv(attn_in[c], in_weight, c * size)

    outputs, input_grads = {}, {}
    g_in, g_out, g_gu, g_dn, gain_terms = {}, {}, {}, {}, {}
    dks, dvs = [], []
    for c in order:
        base = c * size
        gain_first, gain_second = gains[0, at(c)], gains[1, at(c)]
        residual = x_major[at(c)].astype(f32)
        gy = g_major[at(c)].astype(f32)
        grad_rows = gathered((mask * gy).astype(bf16), c % 2 == 0)
        earlier_k, earlier_v = [ks[j] for j in range(c + 1)], [vs[j] for j in range(c + 1)]
        mixed, *parts = attend(qs[c], earlier_k, earlier_v, out_weight, base, ny)
        hmid = residual + mask * reduced(parts, False)
        scale_second = inverse_rms(hmid)
        normed_second = hmid * scale_second
        ffn_rows = gathered((normed_second * gain_second).astype(bf16), True)
        out_parts, back_parts, gain_back, grad_gu, grad_dn = ffn(
            ffn_rows, grad_rows, gate_up, down_weight, base, ny, frames, mine
        )
        grad_ffn_in = reduced(back_parts, False)
        grad_mid = gy + norm_back(grad_ffn_in, normed_second, scale_second, gain_second)
        grad_attn = gathered((mask * grad_mid).astype(bf16), True)
        outputs[c] = (hmid + mask * reduced(out_parts, True)).astype(bf16)
        back, gain_front, grad_iw, grad_ow, dks, dvs = attend_back(
            grad_attn, attn_in[c], qs[c], earlier_k, earlier_v, mixed, out_weight, in_weight,
            dks, dvs, base, ny, frames, mine,
        )
        grad_attn_in = reduced(back, c % 2 == 1)
        scale_first = inverse_rms(residual)
        input_grads[c] = (
            grad_mid + norm_back(grad_attn_in, residual * scale_first, scale_first, gain_first)
        ).astype(bf16)
        gain_terms[c] = jnp.stack([gain_front[:, 0] / norm_gains[0, at(c)], gain_back[:, 0] / norm_gains[1, at(c)]])
        g_gu[c], g_dn[c] = summed_middle(grad_gu), summed(grad_dn)
        g_in[c], g_out[c] = summed_middle(grad_iw), summed(grad_ow)

    def joined(pieces, axis=0):
        return jnp.concatenate([pieces[c] for c in range(CHUNKS)], axis=axis)

    terms = lax.psum_scatter(joined(gain_terms, 1), "frames", scatter_dimension=2, tiled=True)
    step = 1
    while step < group_size:
        terms = terms + lax.ppermute(terms, "mp", [(i, i ^ step) for i in range(group_size)])
        step *= 2
    return (
        jnp.swapaxes(joined(outputs), 0, 1),
        jnp.swapaxes(joined(input_grads), 0, 1),
        joined(g_in),
        joined(g_out),
        joined(g_gu),
        joined(g_dn),
        terms,
    )


MESH = pl.DeviceIdType.MESH
ZN, YN = 4, 2


def fits(frames, group_size, local, positions, depth, width, hidden):
    return (
        frames == 4
        and group_size == ZN * YN
        and local % 16 == 0
        and positions == 16
        and width % 128 == 0
        and (depth // frames) % 128 == 0
        and hidden % 128 == 0
    )


class Place:
    def __init__(self):
        self.m = lax.axis_index("mp")
        self.f = lax.axis_index("frames")
        self.z = self.m // YN
        self.ids = {
            "y": ("mp", self.m ^ 1),
            "up": ("mp", self.m + YN),
            "down": ("mp", self.m - YN),
            "core": ("frames", self.f ^ 1),
            "x": ("frames", self.f ^ 2),
            "pair": ("mp", self.m ^ YN),
            "far": ("mp", self.m ^ (2 * YN)),
        }

    def device(self, way):
        axis, index = self.ids[way]
        return {axis: index}

    def copy(self, src, dst, send, recv, way):
        return pltpu.make_async_remote_copy(
            src_ref=src, dst_ref=dst, send_sem=send, recv_sem=recv, device_id=self.device(way), device_id_type=MESH
        )


def when(condition, run):
    pl.when(condition)(run)


def wait_got(dst, send, recv, place):
    place.copy(dst, dst, send, recv, "y").wait_recv()


class GatherZ:
    def __init__(self, place, g, send, recv):
        self.place, self.g, self.send, self.recv = place, g, send, recv

    def site(self, number, way, src, dst):
        return self.place.copy(
            self.g.at[src[0], src[1]],
            self.g.at[dst[0], dst[1]],
            self.send.at[number],
            self.recv.at[dst[0] * 2 + dst[1]],
            way,
        )

    def up(self, k):
        return self.site(k - 1, "up", (k - 1, 0), (k, 0))

    def down(self, k):
        return self.site(2 + k, "down", ((5 - k) % 4, 0), (4 - k, 0))

    def across(self, k):
        return self.site(6 + k, "y", (k, 0), (k, 1))

    def got(self, k, y):
        wait_got(self.g.at[k, y], self.send.at[0], self.recv.at[k * 2 + y], self.place)

    def t1(self):
        z = self.place.z
        when(z < 3, lambda: self.up(1).start())
        when(z > 0, lambda: self.down(1).start())
        self.across(0).start()

    def t2(self):
        z = self.place.z

        def low():
            self.got(1, 0)
            when(z < 3, lambda: self.up(2).start())
            self.across(1).start()

        def high():
            self.got(3, 0)
            when(z > 0, lambda: self.down(2).start())
            self.across(3).start()

        when(z >= 1, low)
        when(z <= 2, high)

    def t3(self):
        z = self.place.z
        self.got(2, 0)
        when(z == 2, lambda: self.up(3).start())
        when(z == 1, lambda: self.down(3).start())
        self.across(2).start()

    def t4(self):
        z = self.place.z

        def bottom():
            self.got(1, 0)
            self.across(1).start()

        def top():
            self.got(3, 0)
            self.across(3).start()

        when(z == 0, bottom)
        when(z == 3, top)

    def done(self):
        z = self.place.z
        for k in range(4):
            self.got(k, 1)
        when(z < 3, lambda: self.up(1).wait_send())
        when(z > 0, lambda: self.down(1).wait_send())
        when((z >= 1) & (z < 3), lambda: self.up(2).wait_send())
        when((z >= 1) & (z < 3), lambda: self.down(2).wait_send())
        when(z == 2, lambda: self.up(3).wait_send())
        when(z == 1, lambda: self.down(3).wait_send())
        for k in range(4):
            self.across(k).wait_send()


class GatherY:
    def __init__(self, place, g, send, recv):
        self.place, self.g, self.send, self.recv = place, g, send, recv

    def site(self, number, way, src, dst):
        return self.place.copy(self.g.at[src], self.g.at[dst], self.send.at[number], self.recv.at[dst], way)

    def up(self, k):
        return self.site(k - 1, "up", k - 1, k)

    def down(self, k):
        return self.site(2 + k, "down", (5 - k) % 4, 4 - k)

    def across(self):
        return self.place.copy(self.g.at[0, 0], self.g.at[0, 1], self.send.at[6], self.recv.at[4], "y")

    def got(self, k):
        wait_got(self.g.at[k], self.send.at[0], self.recv.at[k], self.place)

    def t1(self):
        self.across().start()

    def t2(self):
        z = self.place.z
        wait_got(self.g.at[0, 1], self.send.at[0], self.recv.at[4], self.place)
        when(z < 3, lambda: self.up(1).start())
        when(z > 0, lambda: self.down(1).start())

    def t3(self):
        z = self.place.z

        def low():
            self.got(1)
            when(z < 3, lambda: self.up(2).start())

        def high():
            self.got(3)
            when(z > 0, lambda: self.down(2).start())

        when(z >= 1, low)
        when(z <= 2, high)

    def t4(self):
        z = self.place.z
        self.got(2)
        when(z == 2, lambda: self.up(3).start())
        when(z == 1, lambda: self.down(3).start())

    def done(self):
        z = self.place.z
        when(z == 0, lambda: self.got(1))
        when(z == 3, lambda: self.got(3))
        when(z < 3, lambda: self.up(1).wait_send())
        when(z > 0, lambda: self.down(1).wait_send())
        when((z >= 1) & (z < 3), lambda: self.up(2).wait_send())
        when((z >= 1) & (z < 3), lambda: self.down(2).wait_send())
        when(z == 2, lambda: self.up(3).wait_send())
        when(z == 1, lambda: self.down(3).wait_send())
        self.across().wait_send()


def up_to_f32(condition, ref):
    return jnp.where(condition, ref[...].astype(f32), 0.0)


class ReduceY:
    def __init__(self, place, part, over, ups, downs, send, recv):
        self.place, self.part, self.over, self.ups, self.downs = place, part, over, ups, downs
        self.send, self.recv = send, recv

    def across(self, k):
        return self.place.copy(self.part.at[k, 1], self.over.at[k], self.send.at[6 + k], self.recv.at[7 + k], "y")

    def up(self, s):
        return self.place.copy(
            self.part.at[s, 0], self.ups.at[s - 1], self.send.at[2 * s - 2], self.recv.at[s], "up"
        )

    def down(self, s):
        return self.place.copy(
            self.part.at[4 - s, 0], self.downs.at[s - 1], self.send.at[2 * s - 1], self.recv.at[3 + s], "down"
        )

    def got_over(self, k):
        wait_got(self.over.at[k], self.send.at[0], self.recv.at[7 + k], self.place)

    def got_up(self, s):
        wait_got(self.ups.at[s - 1], self.send.at[0], self.recv.at[s], self.place)

    def got_down(self, s):
        wait_got(self.downs.at[s - 1], self.send.at[0], self.recv.at[3 + s], self.place)

    def local(self, k):
        return self.part[k, 0].astype(f32) + self.over[k].astype(f32)

    def store(self, k, value):
        self.part[k, 0] = value.astype(bf16)

    def t1(self):
        for k in (1, 3, 2, 0):
            self.across(k).start()

    def t2(self):
        z = self.place.z

        def bottom():
            self.got_over(1)
            self.store(1, self.local(1))
            self.up(1).start()

        def top():
            self.got_over(3)
            self.store(3, self.local(3))
            self.down(1).start()

        when(z == 0, bottom)
        when(z == 3, top)

    def t3(self):
        z = self.place.z
        self.got_over(2)
        when(z == 1, lambda: self.got_up(1))
        when(z == 2, lambda: self.got_down(1))
        self.store(
            2, self.local(2) + up_to_f32(z == 1, self.ups.at[0]) + up_to_f32(z == 2, self.downs.at[0])
        )
        when(z <= 1, lambda: self.up(2).start())
        when(z >= 2, lambda: self.down(2).start())

    def t4(self):
        z = self.place.z

        def low():
            self.got_over(3)
            when(z >= 1, lambda: self.got_up(2))
            self.store(3, self.local(3) + up_to_f32(z >= 1, self.ups.at[1]))
            self.up(3).start()

        def high():
            self.got_over(1)
            when(z <= 2, lambda: self.got_down(2))
            self.store(1, self.local(1) + up_to_f32(z <= 2, self.downs.at[1]))
            self.down(3).start()

        when(z <= 2, low)
        when(z >= 1, high)

    def done(self):
        z = self.place.z
        self.got_over(0)
        when(z >= 1, lambda: self.got_up(3))
        when(z <= 2, lambda: self.got_down(3))
        when(z == 0, lambda: self.up(1).wait_send())
        when(z == 3, lambda: self.down(1).wait_send())
        when(z <= 1, lambda: self.up(2).wait_send())
        when(z >= 2, lambda: self.down(2).wait_send())
        when(z <= 2, lambda: self.up(3).wait_send())
        when(z >= 1, lambda: self.down(3).wait_send())
        for k in range(4):
            self.across(k).wait_send()

    def total(self):
        z = self.place.z
        return self.local(0) + up_to_f32(z >= 1, self.ups.at[2]) + up_to_f32(z <= 2, self.downs.at[2])


class ReduceZ:
    def __init__(self, place, part, over, ups, downs, send, recv):
        self.place, self.part, self.over, self.ups, self.downs = place, part, over, ups, downs
        self.send, self.recv = send, recv

    def across(self):
        return self.place.copy(self.part.at[0, 1], self.over, self.send.at[0], self.recv.at[0], "y")

    def up(self, s):
        return self.place.copy(self.part.at[s], self.ups.at[s - 1], self.send.at[2 * s - 1], self.recv.at[s], "up")

    def down(self, s):
        return self.place.copy(
            self.part.at[4 - s], self.downs.at[s - 1], self.send.at[2 * s], self.recv.at[3 + s], "down"
        )

    got_up = ReduceY.got_up
    got_down = ReduceY.got_down

    def add(self, k, *more):
        value = self.part[k].astype(f32)
        for term in more:
            value = value + term
        self.part[k] = value.astype(bf16)

    def t1(self):
        z = self.place.z
        when(z == 0, lambda: self.up(1).start())
        when(z == 3, lambda: self.down(1).start())

    def t2(self):
        z = self.place.z

        def low():
            self.got_up(1)
            self.add(2, self.ups[0].astype(f32))

        def high():
            self.got_down(1)
            self.add(2, self.downs[0].astype(f32))

        when(z == 1, low)
        when(z == 2, high)
        when(z <= 1, lambda: self.up(2).start())
        when(z >= 2, lambda: self.down(2).start())

    def t3(self):
        z = self.place.z

        def low():
            self.got_up(2)
            self.add(3, self.ups[1].astype(f32))

        def high():
            self.got_down(2)
            self.add(1, self.downs[1].astype(f32))

        when((z >= 1) & (z <= 2), low)
        when((z >= 1) & (z <= 2), high)
        when(z <= 2, lambda: self.up(3).start())
        when(z >= 1, lambda: self.down(3).start())

    def t4(self):
        z = self.place.z
        when(z >= 1, lambda: self.got_up(3))
        when(z <= 2, lambda: self.got_down(3))
        value = self.part[0, 1].astype(f32)
        value = value + up_to_f32(z >= 1, self.ups.at[2, 1]) + up_to_f32(z <= 2, self.downs.at[2, 1])
        self.part[0, 1] = value.astype(bf16)
        self.across().start()

    def done(self):
        wait_got(self.over, self.send.at[0], self.recv.at[0], self.place)
        z = self.place.z
        when(z == 0, lambda: self.up(1).wait_send())
        when(z == 3, lambda: self.down(1).wait_send())
        when(z <= 1, lambda: self.up(2).wait_send())
        when(z >= 2, lambda: self.down(2).wait_send())
        when(z <= 2, lambda: self.up(3).wait_send())
        when(z >= 1, lambda: self.down(3).wait_send())
        self.across().wait_send()

    def total(self):
        z = self.place.z
        value = self.part[0, 0].astype(f32) + self.over[...].astype(f32)
        return value + up_to_f32(z >= 1, self.ups.at[2, 0]) + up_to_f32(z <= 2, self.downs.at[2, 0])


class FramesSum:
    def __init__(self, place, sent, kept, from_core, from_x, sems, free, number):
        self.place, self.sent, self.kept, self.from_core, self.from_x = place, sent, kept, from_core, from_x
        self.sems, self.free, self.number = sems, free, number

    def core(self, j):
        return self.place.copy(self.sent[j], self.from_core[j], self.sems.at[0, j], self.sems.at[1, j], "core")

    def x(self, j):
        return self.place.copy(self.kept[j].at[1], self.from_x[j], self.sems.at[2, j], self.sems.at[3, j], "x")

    def out(self, j, outs, p):
        return pltpu.make_async_copy(self.kept[j].at[0], outs[j].at[p], self.sems.at[4, j])

    def start(self, later):
        def credit():
            pl.semaphore_wait(self.free.at[2 * self.number], 1)

        when(later, credit)
        for j in range(2):
            self.core(j).start()

    def middle(self, later):
        for j in range(2):
            self.core(j).wait_recv()

        def credit():
            pl.semaphore_wait(self.free.at[2 * self.number + 1], 1)

        when(later, credit)
        for j in range(2):
            kept, got = self.kept[j], self.from_core[j]
            kept[1] = (kept[1].astype(f32) + got[1].astype(f32)).astype(bf16)
            self.x(j).start()
        for j in range(2):
            self.core(j).wait_send()

    def finish(self, outs, p, more):
        for j in range(2):
            self.x(j).wait_recv()
            kept = self.kept[j]
            total = kept[0].astype(f32) + self.from_core[j][0].astype(f32) + self.from_x[j][...].astype(f32)
            kept[0] = total.astype(bf16)
            self.out(j, outs, p).start()

        def credit():
            for k, way in enumerate(("core", "x")):
                pl.semaphore_signal(
                    self.free.at[2 * self.number + k], inc=1, device_id=self.place.device(way), device_id_type=MESH
                )

        when(more, credit)
        for j in range(2):
            self.x(j).wait_send()

    def drained(self, outs, p):
        for j in range(2):
            self.out(j, outs, p).wait()


COT_GATHER = GatherZ
FFN_GATHER = GatherY
ATT_GATHER = GatherY
ATTN_REDUCE = ReduceY
GIN_REDUCE = ReduceY
FFN_REDUCE = ReduceZ
BACK_REDUCE = ReduceY

SCHEDULE = (
    ("Fm", 3), ("RF3", 3), ("RA5", 1), ("RG5", 3), ("AC1", 0), ("RB4", 5), ("A", 0), ("AF2", 1),
    ("C", 2), ("AG2", 3), ("Ef", 5), ("AC2", 0), ("RA2", 0), ("RF4", 3), ("AF3", 1), ("E", 4),
    ("AC3", 0), ("RA3", 0), ("AG3", 3), ("RA4", 0), ("RG2", 2), ("Eg", 4), ("AC5", 1), ("Ff", 3),
    ("AF4", 1), ("RG3", 2), ("Em", 4), ("RF2", 2), ("Cg", 2), ("RB2", 4), ("RG4", 2), ("AG4", 3),
    ("AC4", 0), ("RB5", 5), ("RF5", 3), ("K", 0), ("RB3", 4),
)


class GainSum:
    def __init__(self, place, pieces, got, send, recv):
        self.place, self.pieces, self.got, self.send, self.recv = place, pieces, got, send, recv

    def hop(self, k):
        ways = ("core", "x", "y", "pair", "far")
        sources = (self.pieces.at[1], self.pieces.at[0].at[1], self.pieces.at[0].at[0])
        src = sources[min(k, 2)]
        if k == 0:
            dst = self.got.at[pl.ds(0, 2)]
        else:
            dst = self.got.at[k + 1]
        return self.place.copy(src, dst, self.send.at[k], self.recv.at[k], ways[k])

    def start(self):
        self.hop(0).start()

    def next(self, k):
        self.hop(k).wait()
        if k == 0:
            self.pieces[0] = self.pieces[0] + self.got[0:2]
        else:
            self.pieces[0, 0] = self.pieces[0, 0] + self.got[k + 1]
        if k < 4:
            self.hop(k + 1).start()


def layer_kernel(
    x_ref, cot_ref, mask_ref, gains_ref, masked_cot, in_w, out_w, gu_w, dn_w,
    out_hbm, ingrad_hbm, gu_hbm, dn_hbm, iw_hbm, ow_hbm, gain_out, rows_hbm, cot_hbm,
    g_ffn, g_att, cot_v, p_attn, p_gin, p_ffn, p_back,
    over_attn, over_gin, over_ffn, over_back, ups_attn, ups_gin, ups_ffn, ups_back,
    downs_attn, downs_gin, downs_ffn, downs_back,
    q_s, k_s, v_s, mixed_s, dk_s, dv_s, sc, dp,
    gu_v, dn_v, owa_v, owe_v, iw_v, xb,
    act_s, gg_s, gup_s, gmixed_s, gproj_s, hmid_s, ghmid_s, stage, gain_s, gain_pieces, gain_got,
    gu_sent, gu_kept, gu_core, gu_x, dn_sent, dn_kept, dn_core, dn_x,
    iw_sent, iw_kept, iw_core, iw_x, ow_sent, ow_kept, ow_core, ow_x,
    sem_first, sem_first_got, sem_gather, sem_gather_got, sem_reduce, sem_reduce_got,
    sem_grad_ffn, sem_grad_att, sem_gain, sem_local, credits, free,
):
    place = Place()
    z, f = place.z, place.f
    positions, local, depth = x_ref.shape
    rows = ZN * YN * local
    last = positions - 1
    width = q_s.shape[-1]
    hidden = dn_v.shape[0]
    half = rows // 2
    quarter = depth // 4
    mask = mask_ref[...]
    scale = HDIM ** (-0.5)
    pairs_of = positions // 2

    def load(src, dst, number):
        return pltpu.make_async_copy(src, dst, sem_local.at[number])

    def load_owa(p):
        return load(out_w.at[p], owa_v, 0)

    def load_owe(p):
        return load(out_w.at[p], owe_v, 1)

    def load_iw(p, slot):
        return load(in_w.at[p], iw_v.at[slot], 2 + slot)

    def load_gu(p):
        return load(gu_w.at[p], gu_v, 4)

    def load_dn(p):
        return load(dn_w.at[p], dn_v, 5)

    def load_rows(p, dst, number):
        return load(rows_hbm.at[p // 4, :, :, (p % 4) // 2, p % 2], dst, number)

    def load_cot(p):
        return load(cot_hbm.at[p // 2, :, :, p % 2], cot_v, 9)

    def own_cot(j):
        return load(masked_cot.at[j], cot_hbm.at[j, 0, 0], 16 + j)

    for j in range(pairs_of):
        own_cot(j).start()

    barrier = pltpu.get_barrier_semaphore()

    def greet(way):
        pl.semaphore_signal(barrier, inc=1, device_id=place.device(way), device_id_type=MESH)

    for way in ("y", "core", "x", "far"):
        greet(way)
    when(z < 3, lambda: greet("up"))
    when(z > 0, lambda: greet("down"))
    pl.semaphore_wait(barrier, 4 + (z < 3).astype(jnp.int32) + (z > 0).astype(jnp.int32))

    groups = positions // 4

    def gain_of(which, p):
        return gains_ref[which, pl.ds(p, 1), :]

    def normalise(p, c):
        residual = x_ref[p].astype(f32)
        value = residual * inverse_rms(residual) * gain_of(0, p)
        g_att[p // 8, (p % 8) // 2, p % 2] = value.astype(bf16)
        return c

    def own_rows(g):
        return load(g_att.at[g // 2, pl.ds((g % 2) * 2, 2)], rows_hbm.at[g, 0, 0], 10 + g)

    def first_kind(g):
        return GatherY if g == groups - 1 else GatherZ

    firsts = [
        first_kind(g)(place, rows_hbm.at[g], sem_first.at[g], sem_first_got.at[g]) for g in range(groups)
    ]

    def cot_gather(j, which):
        return COT_GATHER(place, cot_hbm.at[pairs_of - 1 - j], sem_gather.at[2, which], sem_gather_got.at[2, which])

    first_cot = cot_gather(0, 0)
    for g in range(groups):
        lax.fori_loop(4 * g, 4 * g + 4, normalise, 0)
        own_rows(g).start()
        own_rows(g).wait()
        firsts[g].t1()
    for j in range(pairs_of):
        own_cot(j).wait()
    first_cot.t1()
    load_owa(last).start()
    load_gu(last).start()
    load_dn(last).start()
    load_iw(0, 0).start()
    dk_s[...] = jnp.zeros_like(dk_s)
    dv_s[...] = jnp.zeros_like(dv_s)

    def project(p, c):
        slot = lax.rem(p, 2)
        load_rows(p, g_ffn.at[slot], 6 + slot).wait()
        load_iw(p, slot).wait()

        @pl.when(lax.rem(p, 4) < 3)
        def _():
            load_rows(p + 1, g_ffn.at[1 - slot], 7 - slot).start()

        @pl.when(p < last)
        def _():
            load_iw(p + 1, 1 - slot).start()

        block = g_ffn[slot].reshape(rows, depth)
        q_s[p] = (dot(block, iw_v[slot, 0], NN).astype(bf16) * scale).astype(bf16)
        k_s[p] = dot(block, iw_v[slot, 1], NN).astype(bf16)
        v_s[p] = dot(block, iw_v[slot, 2], NN).astype(bf16)
        return c

    for g in range(groups):
        firsts[g].t2()
    first_cot.t2()
    for g in range(groups):
        firsts[g].t3()
    first_cot.t3()
    for g in range(groups):
        firsts[g].t4()
    first_cot.t4()
    for g in range(groups):
        firsts[g].done()
        load_rows(4 * g, g_ffn.at[0], 6).start()
        lax.fori_loop(4 * g, 4 * g + 4, project, 0)
    first_cot.done()
    load_cot(last).start()
    load_owe(last).start()
    load_iw(last, 0).start()
    load_rows(last, xb, 8).start()

    row = lax.broadcasted_iota(jnp.int32, (2 * width, width), 0)
    column = lax.broadcasted_iota(jnp.int32, (2 * width, width), 1)
    ones = jnp.where((row % width) // HDIM == column // HDIM, 1.0, 0.0).astype(bf16)

    def per_head(product):
        high = product.astype(bf16)
        low = (product - high.astype(f32)).astype(bf16)
        return dot(jnp.concatenate([high, low], axis=1), ones, NN)

    def scores_of(p, q, at):
        def two(jj, top):
            first = per_head(q * k_s[2 * jj, at].astype(f32))
            second = per_head(q * k_s[2 * jj + 1, at].astype(f32))
            second = jnp.where(2 * jj + 1 <= p, second, -1e30)
            sc[2 * jj], sc[2 * jj + 1] = first, second
            return jnp.maximum(top, jnp.maximum(first, second))

        return lax.fori_loop(0, p // 2 + 1, two, jnp.full((half, width), -1e30, f32))

    def attend_one(p):
        pairs = p // 2 + 1
        for part in range(2):
            at = pl.ds(part * half, half)
            q = q_s[p, at].astype(f32)
            top = scores_of(p, q, at)

            def raise_two(jj, total):
                for t in range(2):
                    raised = jnp.exp(sc[2 * jj + t] - top)
                    sc[2 * jj + t] = raised
                    total = total + raised
                return total

            total = lax.fori_loop(0, pairs, raise_two, jnp.zeros((half, width), f32))
            factor = 1.0 / total

            def mix_two(jj, out):
                for t in range(2):
                    probs = (sc[2 * jj + t] * factor).astype(bf16).astype(f32)
                    out = out + probs * v_s[2 * jj + t, at].astype(f32)
                return out

            out = lax.fori_loop(0, pairs, mix_two, jnp.zeros((half, width), f32))
            mixed_s[p, at] = out.astype(bf16)

    def attend_back_one(p):
        pairs = p // 2 + 1
        for part in range(2):
            at = pl.ds(part * half, half)
            q = q_s[p, at].astype(f32)
            g = gmixed_s[at].astype(f32)
            top = scores_of(p, q, at)

            def raise_two(jj, carry):
                total, weighted = carry
                for t in range(2):
                    raised = jnp.exp(sc[2 * jj + t] - top)
                    sc[2 * jj + t] = raised
                    grad_probs = per_head(g * v_s[2 * jj + t, at].astype(f32))
                    dp[2 * jj + t] = grad_probs
                    total = total + raised
                    weighted = weighted + raised * grad_probs
                return total, weighted

            zero = jnp.zeros((half, width), f32)
            total, weighted = lax.fori_loop(0, pairs, raise_two, (zero, zero))
            factor = 1.0 / total
            centre = weighted * factor

            def back_two(jj, dq):
                for t in range(2):
                    j = 2 * jj + t
                    probs = sc[j] * factor
                    grad = (probs * (dp[j] - centre)).astype(bf16).astype(f32)
                    dq = dq + grad * k_s[j, at].astype(f32)
                    dk_s[j, at] = dk_s[j, at] + grad * q
                    dv_s[j, at] = dv_s[j, at] + probs.astype(bf16).astype(f32) * g
                return dq

            dq = lax.fori_loop(0, pairs, back_two, zero)
            gproj_s[0, at] = (dq * scale).astype(bf16)
        gproj_s[1] = dk_s[p].astype(bf16)
        gproj_s[2] = dv_s[p].astype(bf16)

    blocks = (ZN, YN, local, depth)
    grad_ffn = FramesSum(
        place, (gu_sent, dn_sent), (gu_kept, dn_kept), (gu_core, dn_core), (gu_x, dn_x), sem_grad_ffn, free, 0
    )
    grad_att = FramesSum(
        place, (iw_sent, ow_sent), (iw_kept, ow_kept), (iw_core, ow_core), (iw_x, ow_x), sem_grad_att, free, 1
    )
    ffn_outs, att_outs = (gu_hbm, dn_hbm), (iw_hbm, ow_hbm)
    gain_sum = GainSum(place, gain_pieces, gain_got, sem_gain.at[0], sem_gain.at[1])

    def out_copy(p):
        return pltpu.make_async_copy(stage.at[0], out_hbm.at[p], sem_local.at[14])

    def ingrad_copy(p):
        return pltpu.make_async_copy(stage.at[1], ingrad_hbm.at[p], sem_local.at[15])

    class Position:
        def __init__(self, i):
            self.i = i
            self.p = last - i
            self.par = lax.rem(i + 16, 2)
            self.ring = lax.rem(i + 16, 4)

        def gather(self, kind, g, number):
            par = self.par
            return kind(place, g.at[par], sem_gather.at[number, par], sem_gather_got.at[number, par])

        def reduce(self, kind, part, over, ups, downs, number):
            par = self.par
            return kind(
                place, part, over.at[par], ups.at[par], downs.at[par],
                sem_reduce.at[number, par], sem_reduce_got.at[number, par],
            )

        def AF(self):
            return self.gather(FFN_GATHER, g_ffn, 0)

        def AG(self):
            return self.gather(ATT_GATHER, g_att, 1)

        def RA(self):
            return self.reduce(ATTN_REDUCE, p_attn, over_attn, ups_attn, downs_attn, 0)

        def RG(self):
            return self.reduce(GIN_REDUCE, p_gin, over_gin, ups_gin, downs_gin, 1)

        def RF(self):
            return self.reduce(FFN_REDUCE, p_ffn.at[self.par], over_ffn, ups_ffn, downs_ffn, 2)

        def RB(self):
            return self.reduce(BACK_REDUCE, p_back.at[self.par], over_back, ups_back, downs_back, 3)

        def do_A(self):
            p = self.p
            attend_one(p)
            load_owa(p).wait()
            p_attn[...] = dot(mixed_s[p], owa_v[...], NN).astype(bf16).reshape(blocks)
            self.RA().t1()
            when(p > 0, lambda: load_owa(p - 1).start())

        def do_RA5(self):
            p, total = self.p, self.RA()
            total.done()
            hmid = x_ref[p].astype(f32) + mask * total.total()
            hmid_s[self.ring] = hmid
            g_ffn[self.par, 0, 0] = (hmid * inverse_rms(hmid) * gain_of(1, p)).astype(bf16)
            self.AF().t1()

        def do_C(self):
            p, par = self.p, self.par
            self.AF().done()
            load_gu(p).wait()
            load_dn(p).wait()
            load_cot(p).wait()
            x = g_ffn[par].reshape(rows, depth)
            g = cot_v[...].reshape(rows, depth)
            for h in range(2):
                at = slice(h * hidden // 2, (h + 1) * hidden // 2)
                gate = dot(x, gu_v[0, :, at], NN)
                up = dot(x, gu_v[1, :, at], NN)
                grad_act = dot(g, dn_v[at], NT)
                sigma = 1.0 / (1.0 + jnp.exp(-gate))
                silu = gate * sigma
                act_s[:, at] = (silu * up).astype(bf16)
                gg_s[:, at] = (grad_act * up * sigma * (1.0 + gate * (1.0 - sigma))).astype(bf16)
                gup_s[:, at] = (grad_act * silu).astype(bf16)
            back = dot(gg_s[...], gu_v[0], NT) + dot(gup_s[...], gu_v[1], NT)
            p_gin[...] = back.astype(bf16).reshape(blocks)
            self.RG().t1()
            gain_s[1, pl.ds(p, 1), :] = jnp.sum(back * x.astype(f32), axis=0, keepdims=True)
            p_ffn[par] = dot(act_s[...], dn_v[...], NN).astype(bf16).reshape(blocks)
            self.RF().t1()

            @pl.when(p > 0)
            def _():
                load_gu(p - 1).start()
                load_dn(p - 1).start()

        def do_Cg(self):
            p, par = self.p, self.par

            @pl.when(p < last)
            def _():
                grad_ffn.drained(ffn_outs, p + 1)

            for r in range(4):
                at = piece_at(r, f, quarter)
                gu_to, dn_to = (gu_kept, dn_kept) if r % 2 == 0 else (gu_sent, dn_sent)
                columns = g_ffn[par, :, :, :, at].reshape(rows, quarter)
                gu_to[r // 2, 0] = dot(columns, gg_s[...], TN).astype(bf16)
                gu_to[r // 2, 1] = dot(columns, gup_s[...], TN).astype(bf16)
                dn_to[r // 2] = dot(act_s[...], cot_v[:, :, :, at].reshape(rows, quarter), TN).astype(bf16)
            grad_ffn.start(p < last)
            when(p > 0, lambda: load_cot(p - 1).start())

        def do_Fm(self):
            grad_ffn.middle(self.p < last)

        def do_Ff(self):
            grad_ffn.finish(ffn_outs, self.p, self.p > 0)

        def do_RG5(self):
            p, total = self.p, self.RG()
            total.done()
            hmid = hmid_s[self.ring]
            factor = inverse_rms(hmid)
            grad = cot_ref[p].astype(f32) + norm_back(total.total(), hmid * factor, factor, gain_of(1, p))
            ghmid_s[self.ring] = grad
            g_att[self.par, 0, 0] = (mask * grad).astype(bf16)
            self.AG().t1()

        def do_RF5(self):
            p, total = self.p, self.RF()
            total.done()

            @pl.when(p < last)
            def _():
                out_copy(p + 1).wait()

            stage[0] = (hmid_s[self.ring] + mask * total.total()).astype(bf16)
            out_copy(p).start()

        def do_E(self):
            p, par = self.p, self.par
            self.AG().done()
            load_owe(p).wait()
            load_iw(p, 0).wait()
            load_rows(p, xb, 8).wait()
            gmixed_s[...] = dot(g_att[par].reshape(rows, depth), owe_v[...], NT).astype(bf16)
            attend_back_one(p)
            back = dot(gproj_s[0], iw_v[0, 0], NT)
            back = back + dot(gproj_s[1], iw_v[0, 1], NT)
            back = back + dot(gproj_s[2], iw_v[0, 2], NT)
            p_back[par] = back.astype(bf16).reshape(blocks)
            self.RB().t1()
            gain_s[0, pl.ds(p, 1), :] = jnp.sum(back * xb[...].reshape(rows, depth).astype(f32), axis=0, keepdims=True)

            @pl.when(p == 0)
            def _():
                for r in range(4):
                    gain_pieces[r % 2, r // 2] = gain_s[:, :, piece_at(r, f, quarter)]
                gain_sum.start()

            @pl.when(p > 0)
            def _():
                load_owe(p - 1).start()
                load_iw(p - 1, 0).start()

        def do_Eg(self):
            p, par = self.p, self.par

            @pl.when(p < last)
            def _():
                grad_att.drained(att_outs, p + 1)

            for r in range(4):
                at = piece_at(r, f, quarter)
                iw_to, ow_to = (iw_kept, ow_kept) if r % 2 == 0 else (iw_sent, ow_sent)
                columns = xb[:, :, :, at].reshape(rows, quarter)
                for j in range(3):
                    iw_to[r // 2, j] = dot(columns, gproj_s[j], TN).astype(bf16)
                ow_to[r // 2] = dot(mixed_s[p], g_att[par, :, :, :, at].reshape(rows, quarter), TN).astype(bf16)
            grad_att.start(p < last)
            when(p > 0, lambda: load_rows(p - 1, xb, 8).start())

        def do_Em(self):
            grad_att.middle(self.p < last)

        def do_Ef(self):
            grad_att.finish(att_outs, self.p, self.p > 0)

        def do_RB5(self):
            p, total = self.p, self.RB()
            total.done()
            when(p == 0, lambda: gain_sum.next(3))

            @pl.when(p < last)
            def _():
                ingrad_copy(p + 1).wait()

            residual = x_ref[p].astype(f32)
            factor = inverse_rms(residual)
            grad = norm_back(total.total(), residual * factor, factor, gain_of(0, p))
            stage[1] = (ghmid_s[self.ring] + grad).astype(bf16)
            ingrad_copy(p).start()

        def do_RB2(self):
            self.RB().t2()
            when(self.p == 0, lambda: gain_sum.next(0))

        def do_RB3(self):
            self.RB().t3()
            when(self.p == 0, lambda: gain_sum.next(1))

        def do_RB4(self):
            self.RB().t4()
            when(self.p == 0, lambda: gain_sum.next(2))

        def runs(self):
            ticks = {}
            for name, event in (
                ("RA", self.RA), ("RG", self.RG), ("RF", self.RF), ("AF", self.AF), ("AG", self.AG),
            ):
                ticks[name + "2"] = lambda event=event: event().t2()
                ticks[name + "3"] = lambda event=event: event().t3()
                ticks[name + "4"] = lambda event=event: event().t4()
            return ticks | {
                "A": self.do_A, "RA5": self.do_RA5, "C": self.do_C, "Cg": self.do_Cg, "Fm": self.do_Fm,
                "Ff": self.do_Ff, "RG5": self.do_RG5, "RF5": self.do_RF5, "E": self.do_E, "Eg": self.do_Eg,
                "Em": self.do_Em, "Ef": self.do_Ef, "RB2": self.do_RB2, "RB3": self.do_RB3, "RB4": self.do_RB4,
                "RB5": self.do_RB5,
            }

    def cot_runs(j):
        event = cot_gather(j, lax.rem(j + 16, 2))
        return {"AC1": event.t1, "AC2": event.t2, "AC3": event.t3, "AC4": event.t4, "AC5": event.done}

    def tell(number, way):
        pl.semaphore_signal(credits.at[number], inc=1, device_id=place.device(way), device_id_type=MESH)

    def tell_all():
        tell(0, "y")
        when(z < 3, lambda: tell(1, "up"))
        when(z > 0, lambda: tell(2, "down"))

    steps = positions + max(delay for name, delay in SCHEDULE if name[:2] != "AC")
    tell_all()

    def step(s, c):
        pl.semaphore_wait(credits.at[0], 1)
        when(z > 0, lambda: pl.semaphore_wait(credits.at[1], 1))
        when(z < 3, lambda: pl.semaphore_wait(credits.at[2], 1))
        for name, delay in SCHEDULE:
            if name == "K":
                when(s < steps - 1, tell_all)
            elif name[:2] == "AC":
                j = s + 1 - delay
                when((j >= 1) & (j < pairs_of), cot_runs(j)[name])
            else:
                when((s >= delay) & (s <= last + delay), Position(s - delay).runs()[name])
        return c

    lax.fori_loop(0, steps, step, 0)
    gain_sum.next(4)
    gain_out[...] = gain_pieces[0, 0] / gains_ref[:, :, piece_at(0, f, quarter)]
    grad_ffn.drained(ffn_outs, 0)
    grad_att.drained(att_outs, 0)
    out_copy(0).wait()
    ingrad_copy(0).wait()


def layer(x, cot, mask, gains, masked_cot, in_weight, out_weight, gate_up, down):
    positions, local, depth = x.shape
    width, hidden = out_weight.shape[1], down.shape[1]
    rows = ZN * YN * local
    quarter = depth // 4
    block = (local, depth)
    groups = positions // 4

    def vm(*shape, dtype=bf16):
        return pltpu.VMEM(shape, dtype)

    def hbm(*shape, dtype=bf16):
        return jax.ShapeDtypeStruct(shape, dtype)

    everything = (ZN, YN) + block
    scratch = (
        [vm(2, *everything)] * 2
        + [vm(*everything)] * 3
        + [vm(2, *everything)] * 2
        + [vm(2, ZN, *block), vm(2, ZN, *block), vm(2, *block), vm(2, ZN, *block)]
        + [vm(2, 3, *block), vm(2, 3, *block), vm(2, 3, YN, *block), vm(2, 3, *block)] * 2
        + [vm(positions, rows, width)] * 4
        + [vm(positions, rows, width, dtype=f32)] * 2
        + [vm(positions, rows // 2, width, dtype=f32)] * 2
        + [vm(2, depth, hidden), vm(hidden, depth), vm(width, depth), vm(width, depth)]
        + [vm(2, 3, depth, width), vm(*everything)]
        + [vm(rows, hidden)] * 3
        + [vm(rows, width), vm(3, rows, width)]
        + [vm(4, *block, dtype=f32)] * 2
        + [vm(2, *block)]
        + [vm(2, positions, depth, dtype=f32)]
        + [vm(2, 2, 2, positions, quarter, dtype=f32), vm(6, 2, positions, quarter, dtype=f32)]
        + [vm(2, 2, quarter, hidden)] * 3
        + [vm(2, quarter, hidden)]
        + [vm(2, hidden, quarter)] * 3
        + [vm(hidden, quarter)]
        + [vm(2, 3, quarter, width)] * 3
        + [vm(3, quarter, width)]
        + [vm(2, width, quarter)] * 3
        + [vm(width, quarter)]
        + [
            pltpu.SemaphoreType.DMA((groups, 10)),
            pltpu.SemaphoreType.DMA((groups, 8)),
            pltpu.SemaphoreType.DMA((3, 2, 10)),
            pltpu.SemaphoreType.DMA((3, 2, 8)),
            pltpu.SemaphoreType.DMA((4, 2, 10)),
            pltpu.SemaphoreType.DMA((4, 2, 11)),
            pltpu.SemaphoreType.DMA((5, 2)),
            pltpu.SemaphoreType.DMA((5, 2)),
            pltpu.SemaphoreType.DMA((2, 5)),
            pltpu.SemaphoreType.DMA((16 + positions // 2,)),
            pltpu.SemaphoreType.REGULAR((3,)),
            pltpu.SemaphoreType.REGULAR((4,)),
        ]
    )
    in_vmem = pl.BlockSpec(memory_space=pltpu.VMEM)
    anywhere = pl.BlockSpec(memory_space=pl.ANY)
    return pl.pallas_call(
        layer_kernel,
        in_specs=[in_vmem] * 4 + [anywhere] * 5,
        out_specs=[anywhere] * 6 + [in_vmem, anywhere, anywhere],
        out_shape=[
            hbm(positions, *block),
            hbm(positions, *block),
            hbm(positions, 2, quarter, hidden),
            hbm(positions, hidden, quarter),
            hbm(positions, 3, quarter, width),
            hbm(positions, width, quarter),
            hbm(2, positions, quarter, dtype=f32),
            hbm(groups, ZN, YN, 2, 2, *block),
            hbm(positions // 2, ZN, YN, 2, *block),
        ],
        scratch_shapes=scratch,
        compiler_params=pltpu.CompilerParams(
            collective_id=0, has_side_effects=True, vmem_limit_bytes=KERNEL_VMEM_BYTES
        ),
        name="layer",
    )(x, cot, mask, gains, masked_cot, in_weight, out_weight, gate_up, down)


def body_in_one(inputs, counts, norm_gains, in_weight, out_weight, gate_up, down_weight, cotangent):
    local, positions, depth = inputs.shape
    ids = lax.axis_index("mp") * local + jnp.arange(local)
    valid = ids < counts[0]
    masked = jnp.where(valid[:, None, None], cotangent, jnp.zeros_like(cotangent))
    output, input_grad, g_gu, g_dn, g_in, g_out, gain_sums, _, _ = layer(
        jnp.swapaxes(inputs, 0, 1),
        jnp.swapaxes(cotangent, 0, 1),
        valid.astype(f32)[:, None],
        norm_gains,
        jnp.swapaxes(masked, 0, 1).reshape(positions // 2, 2, local, depth),
        in_weight,
        out_weight,
        gate_up,
        down_weight,
    )
    return (
        jnp.swapaxes(output, 0, 1),
        jnp.swapaxes(input_grad, 0, 1),
        g_in.astype(f32),
        g_out.astype(f32),
        g_gu.astype(f32),
        g_dn.astype(f32),
        gain_sums,
    )


def solution(mesh):
    placed = (
        P(("frames", "mp"), None, None),
        P("frames"),
        P(),
        P(None, None, None, "mp"),
        P(None, "mp", None),
        P(None, None, None, "mp"),
        P(None, "mp", None),
        P(("frames", "mp"), None, None),
    )
    def local_body(*args):
        frames, group_size = lax.axis_size("frames"), lax.axis_size("mp")
        local, positions, depth = args[0].shape
        width, hidden = args[4].shape[1], args[6].shape[1]
        one = fits(frames, group_size, local, positions, depth, width, hidden)
        return (body_in_one if one else body)(*args)

    return jax.shard_map(
        local_body,
        mesh=mesh,
        in_specs=placed,
        out_specs=(
            P(("frames", "mp"), None, None),
            P(("frames", "mp"), None, None),
            P(None, None, "frames", "mp"),
            P(None, "mp", "frames"),
            P(None, None, "frames", "mp"),
            P(None, "mp", "frames"),
            P(None, None, "frames"),
        ),
        check_vma=False,
    )
```

```python
import functools
import math

import jax
import jax.numpy as jnp
from jax import lax
from jax.experimental import pallas as pl
from jax.experimental.pallas import tpu as pltpu
from jax.sharding import PartitionSpec as P

HDIM = 64
EPSILON = 1e-05
Z_CHIPS = 4
FRAME_BLOCK = 16
CHUNKS = 4
VMEM_BYTES = 56 * 1024 * 1024
KERNEL_VMEM_BYTES = 63 * 1024 * 1024

f32 = jnp.float32
bf16 = jnp.bfloat16


class Line:
    def __init__(self, total, n, stride):
        self.n = n
        self.stride = stride
        self.starts = [i for i in range(total) if (i // stride) % n == 0]

    def up(self, low, high):
        return [(s + i * self.stride, s + (i + 1) * self.stride) for s in self.starts for i in range(low, high)]

    def down(self, low, high):
        return [(s + (i + 1) * self.stride, s + i * self.stride) for s in self.starts for i in range(low, high)]

    def gather(self, own):
        n = self.n
        if n == 1:
            return [own]
        if n == 2:
            return [own, lax.ppermute(own, "mp", self.up(0, 1) + self.down(0, 1))]
        ups, downs = [own], [own]
        for k in range(1, n):
            ups.append(lax.ppermute(ups[-1], "mp", self.up(k - 1, n - 1)))
            downs.append(lax.ppermute(downs[-1], "mp", self.down(0, n - k)))
        return [own] + [ups[k] + downs[n - k] for k in range(1, n)]

    def reduce(self, term):
        n = self.n
        if n == 1:
            return [term(0)]
        if n == 2:
            return [term(0), lax.ppermute(term(1).astype(bf16), "mp", self.up(0, 1) + self.down(0, 1)).astype(f32)]
        up = down = None
        for s in range(1, n):
            send_up = term(s) if up is None else term(s) + up.astype(f32)
            send_down = term(n - s) if down is None else term(n - s) + down.astype(f32)
            up = lax.ppermute(send_up.astype(bf16), "mp", self.up(0, min(s, n - 1)))
            down = lax.ppermute(send_down.astype(bf16), "mp", self.down(n - 1 - s, n - 1))
        return [term(0), up.astype(f32), down.astype(f32)]


class Group:
    def __init__(self, size):
        self.nz = math.gcd(size, Z_CHIPS)
        self.ny = size // self.nz
        self.z = Line(size, self.nz, self.ny)
        self.y = Line(size, self.ny, 1)

    def gather(self, own, z_first):
        if z_first:
            column = jnp.stack(self.z.gather(own), axis=1)
            return jnp.stack(self.y.gather(column), axis=1)
        row = jnp.stack(self.y.gather(own), axis=1)
        return jnp.stack(self.z.gather(row), axis=2)

    def reduce(self, parts, z_first):
        if not z_first:
            if self.ny == 2:
                got = lax.ppermute(parts[1], "mp", self.y.up(0, 1) + self.y.down(0, 1))
                columns = [parts[0], got]

                def term(k):
                    return columns[0][:, k].astype(f32) + columns[1][:, k].astype(f32)

            else:
                terms = self.y.reduce(lambda k: parts[k].astype(f32))

                def term(k):
                    return sum(t[:, k] for t in terms)

            return sum(self.z.reduce(term))

        def row(k):
            return jnp.stack([part[:, k] for part in parts], axis=1).astype(f32)

        terms = self.z.reduce(row)
        return sum(self.y.reduce(lambda k: sum(t[:, k] for t in terms)))


def frames_sum(keep, send, size):
    step = 1
    while True:
        got = lax.ppermute(send, "frames", [(i, i ^ step) for i in range(size)])
        total = keep.astype(f32) + got.astype(f32)
        step *= 2
        if step == size:
            return total[:, 0]
        keep, send = total[:, 0::2], total[:, 1::2].astype(send.dtype)


def dot(a, b, dims):
    return lax.dot_general(a, b, (dims, ((), ())), preferred_element_type=f32)


NN = ((1,), (0,))
NT = ((1,), (1,))
TN = ((0,), (0,))


def params():
    return pltpu.CompilerParams(vmem_limit_bytes=VMEM_BYTES)


def cost(flops, nbytes):
    return pl.CostEstimate(flops=int(flops), bytes_accessed=int(nbytes), transcendentals=0)


def qkv_kernel(x_ref, w_ref, q_ref, k_ref, v_ref):
    x = x_ref[0]
    for c, out in enumerate((q_ref, k_ref, v_ref)):
        out[0] = dot(x, w_ref[0, c], NN).astype(bf16)


def qkv(x, weight, base):
    count, rows, depth = x.shape
    width = weight.shape[-1]
    out = jax.ShapeDtypeStruct((count, rows, width), bf16)
    return pl.pallas_call(
        qkv_kernel,
        grid=(count,),
        in_specs=[
            pl.BlockSpec((1, rows, depth), lambda i: (i, 0, 0)),
            pl.BlockSpec((1, 3, depth, width), lambda i: (base + i, 0, 0, 0)),
        ],
        out_specs=[pl.BlockSpec((1, rows, width), lambda i: (i, 0, 0))] * 3,
        out_shape=[out] * 3,
        compiler_params=params(),
        cost_estimate=cost(6 * count * rows * depth * width, 2 * count * depth * (rows + 3 * width)),
        name="qkv",
    )(x, weight)


def head_masks(rows, width):
    lane = lax.broadcasted_iota(jnp.int32, (rows, width), 1)
    return [(lane >= h * HDIM) & (lane < (h + 1) * HDIM) for h in range(width // HDIM)]


def attention_mask(count, base, columns):
    rows = count * FRAME_BLOCK
    row = lax.broadcasted_iota(jnp.int32, (rows, columns), 0)
    column = lax.broadcasted_iota(jnp.int32, (rows, columns), 1)
    same = (row % FRAME_BLOCK) == (column % FRAME_BLOCK)
    return same & (column // FRAME_BLOCK <= row // FRAME_BLOCK + base)


def block_of(refs, rows):
    pieces = [ref[:, rows, :] for ref in refs]
    pieces = [p.reshape(p.shape[0] * p.shape[1], p.shape[2]) for p in pieces]
    return pieces[0] if len(pieces) == 1 else jnp.concatenate(pieces, axis=0)


def softmax(scores):
    top = jnp.max(scores, axis=-1, keepdims=True)
    raised = jnp.exp(scores - top)
    return raised / jnp.sum(raised, axis=-1, keepdims=True)


def pick(masks, values):
    out = values[0]
    for mask, value in zip(masks[1:], values[1:]):
        out = jnp.where(mask, value, out)
    return out


def attend_kernel(base, n_kv, ny, q_ref, *refs):
    k_refs, v_refs = refs[:n_kv], refs[n_kv : 2 * n_kv]
    w_ref = refs[2 * n_kv]
    mixed_ref = refs[2 * n_kv + 1]
    part_refs = refs[2 * n_kv + 2 :]
    count, rows, width = q_ref.shape
    columns = sum(ref.shape[0] for ref in k_refs) * FRAME_BLOCK
    step = pl.program_id(0)

    @pl.when(step == 0)
    def _():
        heads = head_masks(count * FRAME_BLOCK, width)
        allowed = attention_mask(count, base, columns)

        def one(b):
            at = pl.ds(pl.multiple_of(b * FRAME_BLOCK, FRAME_BLOCK), FRAME_BLOCK)
            queries = block_of([q_ref], at) * HDIM ** (-0.5)
            keys, values = block_of(k_refs, at), block_of(v_refs, at)
            outs = []
            for head in heads:
                mine = jnp.where(head, queries, jnp.zeros_like(queries))
                scores = jnp.where(allowed, dot(mine, keys, NT), -1e30)
                outs.append(dot(softmax(scores).astype(bf16), values, NN))
            mixed_ref[:, at, :] = pick(heads, outs).astype(bf16).reshape(count, FRAME_BLOCK, width)

        lax.fori_loop(0, rows // FRAME_BLOCK, lambda b, c: (one(b), c)[1], 0, unroll=4)

    out = dot(mixed_ref[step], w_ref[0], NN)
    span = rows // ny
    for y, part in enumerate(part_refs):
        part[0] = out[y * span : (y + 1) * span].astype(bf16)


def attend(q, ks, vs, weight, base, ny):
    count, rows, width = q.shape
    depth = weight.shape[-1]
    whole = pl.BlockSpec((count, rows, width), lambda i: (0, 0, 0))
    part = jax.ShapeDtypeStruct((count, rows // ny, depth), bf16)
    n_kv = len(ks)
    return pl.pallas_call(
        functools.partial(attend_kernel, base, n_kv, ny),
        grid=(count,),
        in_specs=[whole] * (1 + 2 * n_kv) + [pl.BlockSpec((1, width, depth), lambda i: (base + i, 0, 0))],
        out_specs=[whole] + [pl.BlockSpec((1, rows // ny, depth), lambda i: (i, 0, 0))] * ny,
        out_shape=[jax.ShapeDtypeStruct(q.shape, bf16)] + [part] * ny,
        compiler_params=params(),
        cost_estimate=cost(4 * count * rows * depth * width, 2 * count * rows * (depth + (2 + 2 * n_kv) * width)),
        name="attend",
    )(q, *ks, *vs, weight)


def gradient_pieces(size, depth):
    return size if size > 1 and (depth // size) % 128 == 0 else 1


def piece_at(piece, mine, span):
    return pl.ds(pl.multiple_of((piece ^ mine) * span, span), span)


def ffn_kernel(ny, pieces, mine_ref, x_ref, g_ref, gu_ref, dn_ref, *refs):
    outs, backs = refs[:ny], refs[ny : 2 * ny]
    gain_ref = refs[2 * ny]
    grads = refs[2 * ny + 1 :]
    rows, depth = x_ref.shape[1:]
    span = rows // ny
    x, g = x_ref[0], g_ref[0]
    gate = dot(x, gu_ref[0, 0], NN)
    up = dot(x, gu_ref[0, 1], NN)
    grad_act = dot(g, dn_ref[0], NT)
    sigma = 1.0 / (1.0 + jnp.exp(-gate))
    silu = gate * sigma
    act = (silu * up).astype(bf16)
    grad_gate = (grad_act * up * sigma * (1.0 + gate * (1.0 - sigma))).astype(bf16)
    grad_up = (grad_act * silu).astype(bf16)
    out = dot(act, dn_ref[0], NN)
    for y in range(ny):
        outs[y][0] = out[y * span : (y + 1) * span].astype(bf16)
    back = dot(grad_gate, gu_ref[0, 0], NT) + dot(grad_up, gu_ref[0, 1], NT)
    for y in range(ny):
        backs[y][0] = back[y * span : (y + 1) * span].astype(bf16)
    gain_ref[0] = jnp.sum(back * x.astype(f32), axis=0, keepdims=True)
    if pieces == 1:
        grads[0][0, 0] = dot(x, grad_gate, TN).astype(bf16)
        grads[0][0, 1] = dot(x, grad_up, TN).astype(bf16)
        grads[1][0] = dot(act, g, TN).astype(bf16)
        return
    mine = mine_ref[0]
    width = depth // pieces
    for r in range(pieces):
        at = piece_at(r, mine, width)
        gu_out, dn_out = grads[r % 2], grads[2 + r % 2]
        columns = x_ref[0, :, at]
        gu_out[0, r // 2, 0] = dot(columns, grad_gate, TN).astype(bf16)
        gu_out[0, r // 2, 1] = dot(columns, grad_up, TN).astype(bf16)
        dn_out[0, r // 2] = dot(act, g_ref[0, :, at], TN).astype(bf16)


def split_specs(shape, pieces, axis):
    if pieces == 1:
        block = (1,) + shape[1:]
        return [pl.BlockSpec(block, lambda i: (i,) + (0,) * (len(block) - 1))], [jax.ShapeDtypeStruct(shape, bf16)]
    rest = list(shape[1:])
    rest[axis - 1] //= pieces
    block = (1, pieces // 2) + tuple(rest)
    spec = pl.BlockSpec(block, lambda i: (i,) + (0,) * (len(block) - 1))
    return [spec] * 2, [jax.ShapeDtypeStruct((shape[0],) + block[1:], bf16)] * 2


def ffn(x, g, gate_up, down, base, ny, frames, mine):
    count, rows, depth = x.shape
    width = down.shape[1]
    pieces = gradient_pieces(frames, depth)
    part = jax.ShapeDtypeStruct((count, rows // ny, depth), bf16)
    part_spec = pl.BlockSpec((1, rows // ny, depth), lambda i: (i, 0, 0))
    row_spec = pl.BlockSpec((1, rows, depth), lambda i: (i, 0, 0))
    gu_specs, gu_shapes = split_specs((count, 2, depth, width), pieces, 2)
    dn_specs, dn_shapes = split_specs((count, width, depth), pieces, 2)
    out = pl.pallas_call(
        functools.partial(ffn_kernel, ny, pieces),
        grid=(count,),
        in_specs=[
            pl.BlockSpec(memory_space=pltpu.SMEM),
            row_spec,
            row_spec,
            pl.BlockSpec((1, 2, depth, width), lambda i: (base + i, 0, 0, 0)),
            pl.BlockSpec((1, width, depth), lambda i: (base + i, 0, 0)),
        ],
        out_specs=[part_spec] * (2 * ny) + [pl.BlockSpec((1, 1, depth), lambda i: (i, 0, 0))] + gu_specs + dn_specs,
        out_shape=[part] * (2 * ny) + [jax.ShapeDtypeStruct((count, 1, depth), f32)] + gu_shapes + dn_shapes,
        compiler_params=params(),
        cost_estimate=cost(18 * count * rows * depth * width, 2 * count * depth * (4 * rows + 6 * width)),
        name="ffn",
    )(mine, x, g, gate_up, down)
    n = len(gu_specs)
    return out[:ny], out[ny : 2 * ny], out[2 * ny], out[2 * ny + 1 : 2 * ny + 1 + n], out[2 * ny + 1 + n :]


def attend_back_kernel(base, n_kv, first, ny, pieces, mine_ref, ga_ref, gp_ref, x_ref, q_ref, *refs):
    refs = list(refs)

    def take(n):
        got = refs[:n]
        del refs[:n]
        return got

    k_refs, v_refs = take(n_kv), take(n_kv)
    (mixed_ref, ow_all_ref, iw_ref) = take(3)
    dk_in = dv_in = ()
    if not first:
        dk_in, dv_in = take(n_kv), take(n_kv)
    part_refs = take(ny)
    (gain_ref,) = take(1)
    n_out = 1 if pieces == 1 else 2
    iw_grads, ow_grads = take(n_out), take(n_out)
    dk_out, dv_out = take(n_kv - 1), take(n_kv - 1)
    gmixed_ref, gproj_ref = take(2)
    count, rows, width = q_ref.shape
    columns = n_kv * count * FRAME_BLOCK
    block = count * FRAME_BLOCK
    step = pl.program_id(0)

    @pl.when(step == 0)
    def _():
        for p in range(count):
            gmixed_ref[p] = dot(ga_ref[p], ow_all_ref[p], NT).astype(bf16)
        heads = head_masks(block, width)
        allowed = attention_mask(count, base, columns)
        factor = HDIM ** (-0.5)

        def one(b):
            at = pl.ds(pl.multiple_of(b * FRAME_BLOCK, FRAME_BLOCK), FRAME_BLOCK)
            queries = block_of([q_ref], at) * factor
            grad_mixed = block_of([gmixed_ref], at)
            keys, values = block_of(k_refs, at), block_of(v_refs, at)
            dqs, dk, dv = [], None, None
            for head in heads:
                my_q = jnp.where(head, queries, jnp.zeros_like(queries))
                my_g = jnp.where(head, grad_mixed, jnp.zeros_like(grad_mixed))
                probs = softmax(jnp.where(allowed, dot(my_q, keys, NT), -1e30))
                grad_probs = dot(my_g, values, NT)
                weighted = probs * grad_probs
                grad_scores = (weighted - probs * jnp.sum(weighted, axis=-1, keepdims=True)).astype(bf16)
                dqs.append(dot(grad_scores, keys, NN))
                more_k = dot(grad_scores, my_q, TN)
                more_v = dot(probs.astype(bf16), my_g, TN)
                dk = more_k if dk is None else dk + more_k
                dv = more_v if dv is None else dv + more_v
            gproj_ref[:, 0, at, :] = (pick(heads, dqs) * factor).astype(bf16).reshape(count, FRAME_BLOCK, width)
            for c, total, earlier, later in ((1, dk, dk_in, dk_out), (2, dv, dv_in, dv_out)):
                for j in range(n_kv):
                    piece = total[j * block : (j + 1) * block].reshape(count, FRAME_BLOCK, width)
                    if not first:
                        piece = piece + earlier[j][:, at, :]
                    if j < n_kv - 1:
                        later[j][:, at, :] = piece
                    else:
                        gproj_ref[:, c, at, :] = piece.astype(bf16)

        lax.fori_loop(0, rows // FRAME_BLOCK, lambda b, c: (one(b), c)[1], 0, unroll=2)

    grads = [gproj_ref[step, c] for c in range(3)]
    back = dot(grads[0], iw_ref[0, 0], NT) + dot(grads[1], iw_ref[0, 1], NT) + dot(grads[2], iw_ref[0, 2], NT)
    span = rows // ny
    for y, part in enumerate(part_refs):
        part[0] = back[y * span : (y + 1) * span].astype(bf16)
    gain_ref[0] = jnp.sum(back * x_ref[0].astype(f32), axis=0, keepdims=True)
    mixed = mixed_ref[0]
    if pieces == 1:
        for c in range(3):
            iw_grads[0][0, c] = dot(x_ref[0], grads[c], TN).astype(bf16)
        ow_grads[0][0] = dot(mixed, gp_ref[0], TN).astype(bf16)
        return
    mine = mine_ref[0]
    depth = x_ref.shape[2]
    for r in range(pieces):
        at = piece_at(r, mine, depth // pieces)
        columns = x_ref[0, :, at]
        for c in range(3):
            iw_grads[r % 2][0, r // 2, c] = dot(columns, grads[c], TN).astype(bf16)
        ow_grads[r % 2][0, r // 2] = dot(mixed, gp_ref[0, :, at], TN).astype(bf16)


def attend_back(grad_rows, x, q, ks, vs, mixed, out_weight, in_weight, dks, dvs, base, ny, frames, mine):
    count, rows, depth = x.shape
    width = q.shape[-1]
    pieces = gradient_pieces(frames, depth)
    n_kv = len(ks)
    first = not dks
    whole = pl.BlockSpec((count, rows, width), lambda i: (0, 0, 0))
    row_spec = pl.BlockSpec((1, rows, depth), lambda i: (i, 0, 0))
    chunk = base // count
    part = jax.ShapeDtypeStruct((count, rows // ny, depth), bf16)
    part_spec = pl.BlockSpec((1, rows // ny, depth), lambda i: (i, 0, 0))
    iw_specs, iw_shapes = split_specs((count, 3, depth, width), pieces, 2)
    ow_specs, ow_shapes = split_specs((count, width, depth), pieces, 2)
    total = jax.ShapeDtypeStruct((count, rows, width), f32)
    out = pl.pallas_call(
        functools.partial(attend_back_kernel, base, n_kv, first, ny, pieces),
        grid=(count,),
        in_specs=[
            pl.BlockSpec(memory_space=pltpu.SMEM),
            pl.BlockSpec((count, rows, depth), lambda i: (0, 0, 0)),
            row_spec,
            row_spec,
        ]
        + [whole] * (1 + 2 * n_kv)
        + [
            pl.BlockSpec((1, rows, width), lambda i: (i, 0, 0)),
            pl.BlockSpec((count, width, depth), lambda i: (chunk, 0, 0)),
            pl.BlockSpec((1, 3, depth, width), lambda i: (base + i, 0, 0, 0)),
        ]
        + [whole] * (len(dks) + len(dvs)),
        out_specs=[part_spec] * ny
        + [pl.BlockSpec((1, 1, depth), lambda i: (i, 0, 0))]
        + iw_specs
        + ow_specs
        + [whole] * (2 * (n_kv - 1)),
        out_shape=[part] * ny
        + [jax.ShapeDtypeStruct((count, 1, depth), f32)]
        + iw_shapes
        + ow_shapes
        + [total] * (2 * (n_kv - 1)),
        scratch_shapes=[pltpu.VMEM((count, rows, width), bf16), pltpu.VMEM((count, 3, rows, width), bf16)],
        compiler_params=params(),
        cost_estimate=cost(16 * count * rows * depth * width, 2 * count * rows * (4 * depth + 8 * n_kv * width)),
        name="attend_back",
    )(mine, grad_rows, grad_rows, x, q, *ks, *vs, mixed, out_weight, in_weight, *dks, *dvs)
    out = list(out)
    n = len(iw_specs)
    parts, gain = out[:ny], out[ny]
    iw, ow = out[ny + 1 : ny + 1 + n], out[ny + 1 + n : ny + 1 + 2 * n]
    rest = out[ny + 1 + 2 * n :]
    return parts, gain, iw, ow, rest[: n_kv - 1], rest[n_kv - 1 :]


def inverse_rms(values):
    return lax.rsqrt(jnp.mean(values * values, axis=-1, keepdims=True) + EPSILON)


def norm_back(grad_normed, normed, factor, gain):
    scaled = grad_normed * gain
    return factor * (scaled - normed * jnp.mean(scaled * normed, axis=-1, keepdims=True))


def body(inputs, counts, norm_gains, in_weight, out_weight, gate_up, down_weight, cotangent):
    frames, group_size = lax.axis_size("frames"), lax.axis_size("mp")
    group = Group(group_size)
    ny, nz = group.ny, group.nz
    local, positions, depth = inputs.shape
    rows = local * group_size
    size = positions // CHUNKS
    ids = lax.axis_index("mp") * local + jnp.arange(local)
    mask = (ids < counts[0]).astype(f32)[None, :, None]
    mine = lax.axis_index("frames").astype(jnp.int32)[None]
    x_major = jnp.swapaxes(inputs, 0, 1)
    g_major = jnp.swapaxes(cotangent, 0, 1)
    gains = norm_gains[:, :, None, :]

    def at(c):
        return slice(c * size, (c + 1) * size)

    def gathered(own, z_first):
        return group.gather(own, z_first).reshape(size, rows, depth)

    def reduced(parts, z_first):
        return group.reduce([p.reshape(size, nz, local, depth) for p in parts], z_first)

    def summed(grads):
        if len(grads) == 1:
            return lax.psum_scatter(grads[0], "frames", scatter_dimension=grads[0].ndim - 1, tiled=True).astype(f32)
        return frames_sum(grads[0], grads[1], frames)

    def summed_middle(grads):
        if len(grads) == 1:
            return lax.psum_scatter(grads[0], "frames", scatter_dimension=2, tiled=True).astype(f32)
        return frames_sum(grads[0], grads[1], frames)

    order = list(range(CHUNKS))[::-1]
    attn_in, qs, ks, vs = {}, {}, {}, {}
    for c in order:
        residual = x_major[at(c)].astype(f32)
        own = (residual * inverse_rms(residual) * gains[0, at(c)]).astype(bf16)
        attn_in[c] = gathered(own, True)
        qs[c], ks[c], vs[c] = qkv(attn_in[c], in_weight, c * size)

    outputs, input_grads = {}, {}
    g_in, g_out, g_gu, g_dn, gain_terms = {}, {}, {}, {}, {}
    dks, dvs = [], []
    for c in order:
        base = c * size
        gain_first, gain_second = gains[0, at(c)], gains[1, at(c)]
        residual = x_major[at(c)].astype(f32)
        gy = g_major[at(c)].astype(f32)
        grad_rows = gathered((mask * gy).astype(bf16), c % 2 == 0)
        earlier_k, earlier_v = [ks[j] for j in range(c + 1)], [vs[j] for j in range(c + 1)]
        mixed, *parts = attend(qs[c], earlier_k, earlier_v, out_weight, base, ny)
        hmid = residual + mask * reduced(parts, False)
        scale_second = inverse_rms(hmid)
        normed_second = hmid * scale_second
        ffn_rows = gathered((normed_second * gain_second).astype(bf16), True)
        out_parts, back_parts, gain_back, grad_gu, grad_dn = ffn(
            ffn_rows, grad_rows, gate_up, down_weight, base, ny, frames, mine
        )
        grad_ffn_in = reduced(back_parts, False)
        grad_mid = gy + norm_back(grad_ffn_in, normed_second, scale_second, gain_second)
        grad_attn = gathered((mask * grad_mid).astype(bf16), True)
        outputs[c] = (hmid + mask * reduced(out_parts, True)).astype(bf16)
        back, gain_front, grad_iw, grad_ow, dks, dvs = attend_back(
            grad_attn, attn_in[c], qs[c], earlier_k, earlier_v, mixed, out_weight, in_weight,
            dks, dvs, base, ny, frames, mine,
        )
        grad_attn_in = reduced(back, c % 2 == 1)
        scale_first = inverse_rms(residual)
        input_grads[c] = (
            grad_mid + norm_back(grad_attn_in, residual * scale_first, scale_first, gain_first)
        ).astype(bf16)
        gain_terms[c] = jnp.stack([gain_front[:, 0] / norm_gains[0, at(c)], gain_back[:, 0] / norm_gains[1, at(c)]])
        g_gu[c], g_dn[c] = summed_middle(grad_gu), summed(grad_dn)
        g_in[c], g_out[c] = summed_middle(grad_iw), summed(grad_ow)

    def joined(pieces, axis=0):
        return jnp.concatenate([pieces[c] for c in range(CHUNKS)], axis=axis)

    terms = lax.psum_scatter(joined(gain_terms, 1), "frames", scatter_dimension=2, tiled=True)
    step = 1
    while step < group_size:
        terms = terms + lax.ppermute(terms, "mp", [(i, i ^ step) for i in range(group_size)])
        step *= 2
    return (
        jnp.swapaxes(joined(outputs), 0, 1),
        jnp.swapaxes(joined(input_grads), 0, 1),
        joined(g_in),
        joined(g_out),
        joined(g_gu),
        joined(g_dn),
        terms,
    )


MESH = pl.DeviceIdType.MESH
ZN, YN = 4, 2


def fits(frames, group_size, local, positions, depth, width, hidden):
    return (
        frames == 4
        and group_size == ZN * YN
        and local % 16 == 0
        and positions == 16
        and width % 128 == 0
        and (depth // frames) % 128 == 0
        and hidden % 128 == 0
    )


class Place:
    def __init__(self):
        self.m = lax.axis_index("mp")
        self.f = lax.axis_index("frames")
        self.z = self.m // YN
        self.ids = {
            "y": ("mp", self.m ^ 1),
            "up": ("mp", self.m + YN),
            "down": ("mp", self.m - YN),
            "core": ("frames", self.f ^ 1),
            "x": ("frames", self.f ^ 2),
            "pair": ("mp", self.m ^ YN),
            "far": ("mp", self.m ^ (2 * YN)),
        }

    def device(self, way):
        axis, index = self.ids[way]
        return {axis: index}

    def copy(self, src, dst, send, recv, way):
        return pltpu.make_async_remote_copy(
            src_ref=src, dst_ref=dst, send_sem=send, recv_sem=recv, device_id=self.device(way), device_id_type=MESH
        )


def when(condition, run):
    pl.when(condition)(run)


def wait_got(dst, send, recv, place):
    place.copy(dst, dst, send, recv, "y").wait_recv()


class GatherZ:
    def __init__(self, place, g, send, recv):
        self.place, self.g, self.send, self.recv = place, g, send, recv

    def site(self, number, way, src, dst):
        return self.place.copy(
            self.g.at[src[0], src[1]],
            self.g.at[dst[0], dst[1]],
            self.send.at[number],
            self.recv.at[dst[0] * 2 + dst[1]],
            way,
        )

    def up(self, k):
        return self.site(k - 1, "up", (k - 1, 0), (k, 0))

    def down(self, k):
        return self.site(2 + k, "down", ((5 - k) % 4, 0), (4 - k, 0))

    def across(self, k):
        return self.site(6 + k, "y", (k, 0), (k, 1))

    def got(self, k, y):
        wait_got(self.g.at[k, y], self.send.at[0], self.recv.at[k * 2 + y], self.place)

    def t1(self):
        z = self.place.z
        when(z < 3, lambda: self.up(1).start())
        when(z > 0, lambda: self.down(1).start())
        self.across(0).start()

    def t2(self):
        z = self.place.z

        def low():
            self.got(1, 0)
            when(z < 3, lambda: self.up(2).start())
            self.across(1).start()

        def high():
            self.got(3, 0)
            when(z > 0, lambda: self.down(2).start())
            self.across(3).start()

        when(z >= 1, low)
        when(z <= 2, high)

    def t3(self):
        z = self.place.z
        self.got(2, 0)
        when(z == 2, lambda: self.up(3).start())
        when(z == 1, lambda: self.down(3).start())
        self.across(2).start()

    def t4(self):
        z = self.place.z

        def bottom():
            self.got(1, 0)
            self.across(1).start()

        def top():
            self.got(3, 0)
            self.across(3).start()

        when(z == 0, bottom)
        when(z == 3, top)

    def done(self):
        z = self.place.z
        for k in range(4):
            self.got(k, 1)
        when(z < 3, lambda: self.up(1).wait_send())
        when(z > 0, lambda: self.down(1).wait_send())
        when((z >= 1) & (z < 3), lambda: self.up(2).wait_send())
        when((z >= 1) & (z < 3), lambda: self.down(2).wait_send())
        when(z == 2, lambda: self.up(3).wait_send())
        when(z == 1, lambda: self.down(3).wait_send())
        for k in range(4):
            self.across(k).wait_send()


class GatherY:
    def __init__(self, place, g, send, recv):
        self.place, self.g, self.send, self.recv = place, g, send, recv

    def site(self, number, way, src, dst):
        return self.place.copy(self.g.at[src], self.g.at[dst], self.send.at[number], self.recv.at[dst], way)

    def up(self, k):
        return self.site(k - 1, "up", k - 1, k)

    def down(self, k):
        return self.site(2 + k, "down", (5 - k) % 4, 4 - k)

    def across(self):
        return self.place.copy(self.g.at[0, 0], self.g.at[0, 1], self.send.at[6], self.recv.at[4], "y")

    def got(self, k):
        wait_got(self.g.at[k], self.send.at[0], self.recv.at[k], self.place)

    def t1(self):
        self.across().start()

    def t2(self):
        z = self.place.z
        wait_got(self.g.at[0, 1], self.send.at[0], self.recv.at[4], self.place)
        when(z < 3, lambda: self.up(1).start())
        when(z > 0, lambda: self.down(1).start())

    def t3(self):
        z = self.place.z

        def low():
            self.got(1)
            when(z < 3, lambda: self.up(2).start())

        def high():
            self.got(3)
            when(z > 0, lambda: self.down(2).start())

        when(z >= 1, low)
        when(z <= 2, high)

    def t4(self):
        z = self.place.z
        self.got(2)
        when(z == 2, lambda: self.up(3).start())
        when(z == 1, lambda: self.down(3).start())

    def done(self):
        z = self.place.z
        when(z == 0, lambda: self.got(1))
        when(z == 3, lambda: self.got(3))
        when(z < 3, lambda: self.up(1).wait_send())
        when(z > 0, lambda: self.down(1).wait_send())
        when((z >= 1) & (z < 3), lambda: self.up(2).wait_send())
        when((z >= 1) & (z < 3), lambda: self.down(2).wait_send())
        when(z == 2, lambda: self.up(3).wait_send())
        when(z == 1, lambda: self.down(3).wait_send())
        self.across().wait_send()


def up_to_f32(condition, ref):
    return jnp.where(condition, ref[...].astype(f32), 0.0)


class ReduceY:
    def __init__(self, place, part, over, ups, downs, send, recv):
        self.place, self.part, self.over, self.ups, self.downs = place, part, over, ups, downs
        self.send, self.recv = send, recv

    def across(self, k):
        return self.place.copy(self.part.at[k, 1], self.over.at[k], self.send.at[6 + k], self.recv.at[7 + k], "y")

    def up(self, s):
        return self.place.copy(
            self.part.at[s, 0], self.ups.at[s - 1], self.send.at[2 * s - 2], self.recv.at[s], "up"
        )

    def down(self, s):
        return self.place.copy(
            self.part.at[4 - s, 0], self.downs.at[s - 1], self.send.at[2 * s - 1], self.recv.at[3 + s], "down"
        )

    def got_over(self, k):
        wait_got(self.over.at[k], self.send.at[0], self.recv.at[7 + k], self.place)

    def got_up(self, s):
        wait_got(self.ups.at[s - 1], self.send.at[0], self.recv.at[s], self.place)

    def got_down(self, s):
        wait_got(self.downs.at[s - 1], self.send.at[0], self.recv.at[3 + s], self.place)

    def local(self, k):
        return self.part[k, 0].astype(f32) + self.over[k].astype(f32)

    def store(self, k, value):
        self.part[k, 0] = value.astype(bf16)

    def t1(self):
        for k in (1, 3, 2, 0):
            self.across(k).start()

    def t2(self):
        z = self.place.z

        def bottom():
            self.got_over(1)
            self.store(1, self.local(1))
            self.up(1).start()

        def top():
            self.got_over(3)
            self.store(3, self.local(3))
            self.down(1).start()

        when(z == 0, bottom)
        when(z == 3, top)

    def t3(self):
        z = self.place.z
        self.got_over(2)
        when(z == 1, lambda: self.got_up(1))
        when(z == 2, lambda: self.got_down(1))
        self.store(
            2, self.local(2) + up_to_f32(z == 1, self.ups.at[0]) + up_to_f32(z == 2, self.downs.at[0])
        )
        when(z <= 1, lambda: self.up(2).start())
        when(z >= 2, lambda: self.down(2).start())

    def t4(self):
        z = self.place.z

        def low():
            self.got_over(3)
            when(z >= 1, lambda: self.got_up(2))
            self.store(3, self.local(3) + up_to_f32(z >= 1, self.ups.at[1]))
            self.up(3).start()

        def high():
            self.got_over(1)
            when(z <= 2, lambda: self.got_down(2))
            self.store(1, self.local(1) + up_to_f32(z <= 2, self.downs.at[1]))
            self.down(3).start()

        when(z <= 2, low)
        when(z >= 1, high)

    def done(self):
        z = self.place.z
        self.got_over(0)
        when(z >= 1, lambda: self.got_up(3))
        when(z <= 2, lambda: self.got_down(3))
        when(z == 0, lambda: self.up(1).wait_send())
        when(z == 3, lambda: self.down(1).wait_send())
        when(z <= 1, lambda: self.up(2).wait_send())
        when(z >= 2, lambda: self.down(2).wait_send())
        when(z <= 2, lambda: self.up(3).wait_send())
        when(z >= 1, lambda: self.down(3).wait_send())
        for k in range(4):
            self.across(k).wait_send()

    def total(self):
        z = self.place.z
        return self.local(0) + up_to_f32(z >= 1, self.ups.at[2]) + up_to_f32(z <= 2, self.downs.at[2])


class ReduceZ:
    def __init__(self, place, part, over, ups, downs, send, recv):
        self.place, self.part, self.over, self.ups, self.downs = place, part, over, ups, downs
        self.send, self.recv = send, recv

    def across(self):
        return self.place.copy(self.part.at[0, 1], self.over, self.send.at[0], self.recv.at[0], "y")

    def up(self, s):
        return self.place.copy(self.part.at[s], self.ups.at[s - 1], self.send.at[2 * s - 1], self.recv.at[s], "up")

    def down(self, s):
        return self.place.copy(
            self.part.at[4 - s], self.downs.at[s - 1], self.send.at[2 * s], self.recv.at[3 + s], "down"
        )

    got_up = ReduceY.got_up
    got_down = ReduceY.got_down

    def add(self, k, *more):
        value = self.part[k].astype(f32)
        for term in more:
            value = value + term
        self.part[k] = value.astype(bf16)

    def t1(self):
        z = self.place.z
        when(z == 0, lambda: self.up(1).start())
        when(z == 3, lambda: self.down(1).start())

    def t2(self):
        z = self.place.z

        def low():
            self.got_up(1)
            self.add(2, self.ups[0].astype(f32))

        def high():
            self.got_down(1)
            self.add(2, self.downs[0].astype(f32))

        when(z == 1, low)
        when(z == 2, high)
        when(z <= 1, lambda: self.up(2).start())
        when(z >= 2, lambda: self.down(2).start())

    def t3(self):
        z = self.place.z

        def low():
            self.got_up(2)
            self.add(3, self.ups[1].astype(f32))

        def high():
            self.got_down(2)
            self.add(1, self.downs[1].astype(f32))

        when((z >= 1) & (z <= 2), low)
        when((z >= 1) & (z <= 2), high)
        when(z <= 2, lambda: self.up(3).start())
        when(z >= 1, lambda: self.down(3).start())

    def t4(self):
        z = self.place.z
        when(z >= 1, lambda: self.got_up(3))
        when(z <= 2, lambda: self.got_down(3))
        value = self.part[0, 1].astype(f32)
        value = value + up_to_f32(z >= 1, self.ups.at[2, 1]) + up_to_f32(z <= 2, self.downs.at[2, 1])
        self.part[0, 1] = value.astype(bf16)
        self.across().start()

    def done(self):
        wait_got(self.over, self.send.at[0], self.recv.at[0], self.place)
        z = self.place.z
        when(z == 0, lambda: self.up(1).wait_send())
        when(z == 3, lambda: self.down(1).wait_send())
        when(z <= 1, lambda: self.up(2).wait_send())
        when(z >= 2, lambda: self.down(2).wait_send())
        when(z <= 2, lambda: self.up(3).wait_send())
        when(z >= 1, lambda: self.down(3).wait_send())
        self.across().wait_send()

    def total(self):
        z = self.place.z
        value = self.part[0, 0].astype(f32) + self.over[...].astype(f32)
        return value + up_to_f32(z >= 1, self.ups.at[2, 0]) + up_to_f32(z <= 2, self.downs.at[2, 0])


class FramesSum:
    def __init__(self, place, sent, kept, from_core, from_x, sems, free, number):
        self.place, self.sent, self.kept, self.from_core, self.from_x = place, sent, kept, from_core, from_x
        self.sems, self.free, self.number = sems, free, number

    def core(self, j):
        return self.place.copy(self.sent[j], self.from_core[j], self.sems.at[0, j], self.sems.at[1, j], "core")

    def x(self, j):
        return self.place.copy(self.kept[j].at[1], self.from_x[j], self.sems.at[2, j], self.sems.at[3, j], "x")

    def out(self, j, outs, p):
        return pltpu.make_async_copy(self.kept[j].at[0], outs[j].at[p], self.sems.at[4, j])

    def start(self, later):
        def credit():
            pl.semaphore_wait(self.free.at[2 * self.number], 1)

        when(later, credit)
        for j in range(2):
            self.core(j).start()

    def middle(self, later):
        for j in range(2):
            self.core(j).wait_recv()

        def credit():
            pl.semaphore_wait(self.free.at[2 * self.number + 1], 1)

        when(later, credit)
        for j in range(2):
            kept, got = self.kept[j], self.from_core[j]
            kept[1] = (kept[1].astype(f32) + got[1].astype(f32)).astype(bf16)
            self.x(j).start()
        for j in range(2):
            self.core(j).wait_send()

    def finish(self, outs, p, more):
        for j in range(2):
            self.x(j).wait_recv()
            kept = self.kept[j]
            total = kept[0].astype(f32) + self.from_core[j][0].astype(f32) + self.from_x[j][...].astype(f32)
            kept[0] = total.astype(bf16)
            self.out(j, outs, p).start()

        def credit():
            for k, way in enumerate(("core", "x")):
                pl.semaphore_signal(
                    self.free.at[2 * self.number + k], inc=1, device_id=self.place.device(way), device_id_type=MESH
                )

        when(more, credit)
        for j in range(2):
            self.x(j).wait_send()

    def drained(self, outs, p):
        for j in range(2):
            self.out(j, outs, p).wait()


COT_GATHER = GatherZ
ATTN_REDUCE = ReduceY
GIN_REDUCE = ReduceY
BACK_REDUCE = ReduceY
Z_FIRST = (0, 1, 2, 3, 4, 5, 6)
FFN_Y_FIRST = (0, 1, 2, 3, 4, 5, 6, 7, 8, 9, 10, 11, 12, 13, 14, 15)
ATT_Y_FIRST = (0, 1, 2, 3, 4, 5, 6, 7, 8, 9, 10, 11, 12, 13, 14, 15)

SCHEDULE = (
    ("RA5", 1), ("RG5", 3), ("RB3", 5), ("AC1", 0), ("A", 0), ("RF3", 3), ("Ef", 5), ("AF2", 1),
    ("C", 2), ("RF4", 3), ("RB4", 5), ("RA2", 0), ("AC2", 0), ("AG2", 3), ("E", 4), ("AF3", 1),
    ("Eg", 4), ("RA3", 0), ("AC5", 1), ("AC3", 0), ("Ff", 3), ("RG2", 2), ("AG3", 3), ("Cg", 2),
    ("RG3", 2), ("RA4", 0), ("RB5", 5), ("Em", 4), ("AC4", 0), ("RF5", 3), ("K", 0), ("RG4", 2),
    ("RB2", 4), ("AF4", 1), ("AG4", 3), ("Fm", 2), ("RF2", 2),
)


class EitherGather:
    def __init__(self, place, g, send, recv):
        self.along_y = GatherY(place, g, send, recv)
        self.along_z = GatherZ(place, g, send, recv)

    def choose(self, i, y_first):
        self.y_first = i < 0
        for k in y_first:
            self.y_first = self.y_first | (i == k)
        return self

    def both(self, along_y, along_z):
        when(self.y_first, along_y)
        when(jnp.logical_not(self.y_first), along_z)

    def t1(self):
        self.both(self.along_y.t1, self.along_z.t1)

    def t2(self):
        self.both(self.along_y.t2, self.along_z.t2)

    def t3(self):
        self.both(self.along_y.t3, self.along_z.t3)

    def t4(self):
        self.both(self.along_y.t4, self.along_z.t4)

    def done(self):
        self.both(self.along_y.done, self.along_z.done)


class EitherReduce:
    def __init__(self, place, part, over, ups, downs, send, recv):
        self.along_z = ReduceZ(place, part, over.at[0], ups, downs, send, recv)
        self.along_y = ReduceY(place, part, over, ups.at[:, 0], downs.at[:, 0], send, recv)

    def choose(self, i):
        self.z_first = i < 0
        for k in Z_FIRST:
            self.z_first = self.z_first | (i == k)
        return self

    def both(self, along_z, along_y):
        when(self.z_first, along_z)
        when(jnp.logical_not(self.z_first), along_y)

    def t1(self):
        self.both(self.along_z.t1, self.along_y.t1)

    def t2(self):
        self.both(self.along_z.t2, self.along_y.t2)

    def t3(self):
        self.both(self.along_z.t3, self.along_y.t3)

    def t4(self):
        self.both(self.along_z.t4, self.along_y.t4)

    def done(self):
        self.both(self.along_z.done, self.along_y.done)

    def total(self):
        z = self.along_z.place.z
        value = self.along_y.local(0)
        return value + up_to_f32(z >= 1, self.along_y.ups.at[2]) + up_to_f32(z <= 2, self.along_y.downs.at[2])


class GainSum:
    def __init__(self, place, pieces, got, send, recv):
        self.place, self.pieces, self.got, self.send, self.recv = place, pieces, got, send, recv

    def hop(self, k):
        ways = ("core", "x", "y", "pair", "far")
        sources = (self.pieces.at[1], self.pieces.at[0].at[1], self.pieces.at[0].at[0])
        src = sources[min(k, 2)]
        if k == 0:
            dst = self.got.at[pl.ds(0, 2)]
        else:
            dst = self.got.at[k + 1]
        return self.place.copy(src, dst, self.send.at[k], self.recv.at[k], ways[k])

    def start(self):
        self.hop(0).start()

    def next(self, k):
        self.hop(k).wait()
        if k == 0:
            self.pieces[0] = self.pieces[0] + self.got[0:2]
        else:
            self.pieces[0, 0] = self.pieces[0, 0] + self.got[k + 1]
        if k < 4:
            self.hop(k + 1).start()


def layer_kernel(
    x_ref, cot_ref, mask_ref, gains_ref, masked_cot, in_w, out_w, gu_w, dn_w,
    out_hbm, ingrad_hbm, gu_hbm, dn_hbm, iw_hbm, ow_hbm, gain_out, rows_hbm, cot_hbm,
    g_ffn, g_att, cot_v, p_attn, p_gin, p_ffn, p_back,
    over_attn, over_gin, over_ffn, over_back, ups_attn, ups_gin, ups_ffn, ups_back,
    downs_attn, downs_gin, downs_ffn, downs_back,
    q_s, k_s, v_s, mixed_s, dk_s, dv_s, sc, dp,
    gu_v, dn_v, owa_v, owe_v, iw_v, xb,
    act_s, gg_s, gup_s, gmixed_s, gproj_s, hmid_s, ghmid_s, stage, gain_s, gain_pieces, gain_got,
    gu_sent, gu_kept, gu_core, gu_x, dn_sent, dn_kept, dn_core, dn_x,
    iw_sent, iw_kept, iw_core, iw_x, ow_sent, ow_kept, ow_core, ow_x,
    sem_first, sem_first_got, sem_gather, sem_gather_got, sem_reduce, sem_reduce_got,
    sem_grad_ffn, sem_grad_att, sem_gain, sem_local, credits, free,
):
    place = Place()
    z, f = place.z, place.f
    positions, local, depth = x_ref.shape
    rows = ZN * YN * local
    last = positions - 1
    width = q_s.shape[-1]
    hidden = dn_v.shape[0]
    half = rows // 2
    quarter = depth // 4
    mask = mask_ref[...]
    scale = HDIM ** (-0.5)
    pairs_of = positions // 2

    def load(src, dst, number):
        return pltpu.make_async_copy(src, dst, sem_local.at[number])

    def load_owa(p):
        return load(out_w.at[p], owa_v, 0)

    def load_owe(p):
        return load(out_w.at[p], owe_v, 1)

    def load_iw(p, slot):
        return load(in_w.at[p], iw_v.at[slot], 2 + slot)

    def load_gu(p):
        return load(gu_w.at[p], gu_v, 4)

    def load_dn(p):
        return load(dn_w.at[p], dn_v, 5)

    def load_rows(p, dst, number):
        return load(rows_hbm.at[p // 2, :, :, p % 2], dst, number)

    def load_cot(p):
        return load(cot_hbm.at[p // 2, :, :, p % 2], cot_v, 9)

    def own_cot(j):
        return load(masked_cot.at[j], cot_hbm.at[j, 0, 0], 16 + j)

    def own_rows(j):
        return load(g_att.at[j // 4, j % 4], rows_hbm.at[j, 0, 0], 16 + pairs_of + j)

    for j in range(pairs_of):
        own_cot(j).start()

    barrier = pltpu.get_barrier_semaphore()

    def greet(way):
        pl.semaphore_signal(barrier, inc=1, device_id=place.device(way), device_id_type=MESH)

    for way in ("y", "core", "x", "far"):
        greet(way)
    when(z < 3, lambda: greet("up"))
    when(z > 0, lambda: greet("down"))
    pl.semaphore_wait(barrier, 4 + (z < 3).astype(jnp.int32) + (z > 0).astype(jnp.int32))

    groups = pairs_of

    def gain_of(which, p):
        return gains_ref[which, pl.ds(p, 1), :]

    def normalise(p, c):
        residual = x_ref[p].astype(f32)
        value = residual * inverse_rms(residual) * gain_of(0, p)
        g_att[p // 8, (p % 8) // 2, p % 2] = value.astype(bf16)
        return c

    def first_kind(g):
        return GatherY if g == groups - 1 else GatherZ

    firsts = [
        first_kind(g)(place, rows_hbm.at[g], sem_first.at[g], sem_first_got.at[g]) for g in range(groups)
    ]

    def cot_gather(j, which):
        return COT_GATHER(place, cot_hbm.at[pairs_of - 1 - j], sem_gather.at[2, which], sem_gather_got.at[2, which])

    for g in range(groups):
        lax.fori_loop(2 * g, 2 * g + 2, normalise, 0)
        own_rows(g).start()
        own_rows(g).wait()
        firsts[g].t1()
    for j in range(pairs_of):
        own_cot(j).wait()
    load_owa(last).start()
    load_gu(last).start()
    load_dn(last).start()
    load_iw(0, 0).start()
    dk_s[...] = jnp.zeros_like(dk_s)
    dv_s[...] = jnp.zeros_like(dv_s)

    def project(p, c):
        slot = lax.rem(p, 2)
        load_rows(p, g_ffn.at[slot], 6 + slot).wait()
        load_iw(p, slot).wait()

        @pl.when(p < last)
        def _():
            load_iw(p + 1, 1 - slot).start()

        block = g_ffn[slot].reshape(rows, depth)
        q_s[p] = (dot(block, iw_v[slot, 0], NN).astype(bf16) * scale).astype(bf16)
        k_s[p] = dot(block, iw_v[slot, 1], NN).astype(bf16)
        v_s[p] = dot(block, iw_v[slot, 2], NN).astype(bf16)
        return c

    for g in range(groups):
        firsts[g].t2()
    for g in range(groups):
        firsts[g].t3()
    for g in range(groups):
        firsts[g].t4()
    for g in range(groups):
        firsts[g].done()
        load_rows(2 * g, g_ffn.at[0], 6).start()
        load_rows(2 * g + 1, g_ffn.at[1], 7).start()
        lax.fori_loop(2 * g, 2 * g + 2, project, 0)
    load_owe(last).start()
    load_iw(last, 0).start()
    load_rows(last, xb, 8).start()

    row = lax.broadcasted_iota(jnp.int32, (2 * width, width), 0)
    column = lax.broadcasted_iota(jnp.int32, (2 * width, width), 1)
    ones = jnp.where((row % width) // HDIM == column // HDIM, 1.0, 0.0).astype(bf16)

    def per_head(product):
        high = product.astype(bf16)
        low = (product - high.astype(f32)).astype(bf16)
        return dot(jnp.concatenate([high, low], axis=1), ones, NN)

    def scores_of(p, q, at):
        def two(jj, top):
            first = per_head(q * k_s[2 * jj, at].astype(f32))
            second = per_head(q * k_s[2 * jj + 1, at].astype(f32))
            second = jnp.where(2 * jj + 1 <= p, second, -1e30)
            sc[2 * jj], sc[2 * jj + 1] = first, second
            return jnp.maximum(top, jnp.maximum(first, second))

        return lax.fori_loop(0, p // 2 + 1, two, jnp.full((half, width), -1e30, f32))

    def attend_one(p):
        pairs = p // 2 + 1
        for part in range(2):
            at = pl.ds(part * half, half)
            q = q_s[p, at].astype(f32)
            top = scores_of(p, q, at)

            def raise_two(jj, total):
                for t in range(2):
                    raised = jnp.exp(sc[2 * jj + t] - top)
                    sc[2 * jj + t] = raised
                    total = total + raised
                return total

            total = lax.fori_loop(0, pairs, raise_two, jnp.zeros((half, width), f32))
            factor = 1.0 / total

            def mix_two(jj, out):
                for t in range(2):
                    probs = (sc[2 * jj + t] * factor).astype(bf16).astype(f32)
                    out = out + probs * v_s[2 * jj + t, at].astype(f32)
                return out

            out = lax.fori_loop(0, pairs, mix_two, jnp.zeros((half, width), f32))
            mixed_s[p, at] = out.astype(bf16)

    def attend_back_one(p):
        pairs = p // 2 + 1
        for part in range(2):
            at = pl.ds(part * half, half)
            q = q_s[p, at].astype(f32)
            g = gmixed_s[at].astype(f32)
            top = scores_of(p, q, at)

            def raise_two(jj, carry):
                total, weighted = carry
                for t in range(2):
                    raised = jnp.exp(sc[2 * jj + t] - top)
                    sc[2 * jj + t] = raised
                    grad_probs = per_head(g * v_s[2 * jj + t, at].astype(f32))
                    dp[2 * jj + t] = grad_probs
                    total = total + raised
                    weighted = weighted + raised * grad_probs
                return total, weighted

            zero = jnp.zeros((half, width), f32)
            total, weighted = lax.fori_loop(0, pairs, raise_two, (zero, zero))
            factor = 1.0 / total
            centre = weighted * factor

            def back_two(jj, dq):
                for t in range(2):
                    j = 2 * jj + t
                    probs = sc[j] * factor
                    grad = (probs * (dp[j] - centre)).astype(bf16).astype(f32)
                    dq = dq + grad * k_s[j, at].astype(f32)
                    dk_s[j, at] = dk_s[j, at] + grad * q
                    dv_s[j, at] = dv_s[j, at] + probs.astype(bf16).astype(f32) * g
                return dq

            dq = lax.fori_loop(0, pairs, back_two, zero)
            gproj_s[0, at] = (dq * scale).astype(bf16)
        gproj_s[1] = dk_s[p].astype(bf16)
        gproj_s[2] = dv_s[p].astype(bf16)

    blocks = (ZN, YN, local, depth)
    grad_ffn = FramesSum(
        place, (gu_sent, dn_sent), (gu_kept, dn_kept), (gu_core, dn_core), (gu_x, dn_x), sem_grad_ffn, free, 0
    )
    grad_att = FramesSum(
        place, (iw_sent, ow_sent), (iw_kept, ow_kept), (iw_core, ow_core), (iw_x, ow_x), sem_grad_att, free, 1
    )
    ffn_outs, att_outs = (gu_hbm, dn_hbm), (iw_hbm, ow_hbm)
    gain_sum = GainSum(place, gain_pieces, gain_got, sem_gain.at[0], sem_gain.at[1])

    def out_copy(p):
        return pltpu.make_async_copy(stage.at[0], out_hbm.at[p], sem_local.at[14])

    def ingrad_copy(p):
        return pltpu.make_async_copy(stage.at[1], ingrad_hbm.at[p], sem_local.at[15])

    class Position:
        def __init__(self, i):
            self.i = i
            self.p = last - i
            self.par = lax.rem(i + 16, 2)
            self.ring = lax.rem(i + 16, 4)

        def gather(self, kind, g, number):
            par = self.par
            return kind(place, g.at[par], sem_gather.at[number, par], sem_gather_got.at[number, par])

        def reduce(self, kind, part, over, ups, downs, number):
            par = self.par
            return kind(
                place, part, over.at[par], ups.at[par], downs.at[par],
                sem_reduce.at[number, par], sem_reduce_got.at[number, par],
            )

        def AF(self):
            return self.gather(EitherGather, g_ffn, 0).choose(self.i, FFN_Y_FIRST)

        def AG(self):
            return self.gather(EitherGather, g_att, 1).choose(self.i, ATT_Y_FIRST)

        def RA(self):
            return self.reduce(ATTN_REDUCE, p_attn, over_attn, ups_attn, downs_attn, 0)

        def RG(self):
            return self.reduce(GIN_REDUCE, p_gin, over_gin, ups_gin, downs_gin, 1)

        def RF(self):
            return self.reduce(EitherReduce, p_ffn.at[self.par], over_ffn, ups_ffn, downs_ffn, 2).choose(self.i)

        def RB(self):
            return self.reduce(BACK_REDUCE, p_back.at[self.par], over_back, ups_back, downs_back, 3)

        def do_A(self):
            p = self.p
            attend_one(p)
            load_owa(p).wait()
            p_attn[...] = dot(mixed_s[p], owa_v[...], NN).astype(bf16).reshape(blocks)
            self.RA().t1()
            when(p > 0, lambda: load_owa(p - 1).start())

        def do_RA5(self):
            p, total = self.p, self.RA()
            total.done()
            hmid = x_ref[p].astype(f32) + mask * total.total()
            hmid_s[self.ring] = hmid
            g_ffn[self.par, 0, 0] = (hmid * inverse_rms(hmid) * gain_of(1, p)).astype(bf16)
            self.AF().t1()

        def do_C(self):
            p, par = self.p, self.par
            self.AF().done()
            load_gu(p).wait()
            load_dn(p).wait()
            load_cot(p).wait()
            x = g_ffn[par].reshape(rows, depth)
            g = cot_v[...].reshape(rows, depth)
            for h in range(2):
                at = slice(h * hidden // 2, (h + 1) * hidden // 2)
                gate = dot(x, gu_v[0, :, at], NN)
                up = dot(x, gu_v[1, :, at], NN)
                grad_act = dot(g, dn_v[at], NT)
                sigma = 1.0 / (1.0 + jnp.exp(-gate))
                silu = gate * sigma
                act_s[:, at] = (silu * up).astype(bf16)
                gg_s[:, at] = (grad_act * up * sigma * (1.0 + gate * (1.0 - sigma))).astype(bf16)
                gup_s[:, at] = (grad_act * silu).astype(bf16)
            back = dot(gg_s[...], gu_v[0], NT) + dot(gup_s[...], gu_v[1], NT)
            p_gin[...] = back.astype(bf16).reshape(blocks)
            self.RG().t1()
            gain_s[1, pl.ds(p, 1), :] = jnp.sum(back * x.astype(f32), axis=0, keepdims=True)
            p_ffn[par] = dot(act_s[...], dn_v[...], NN).astype(bf16).reshape(blocks)
            self.RF().t1()

            @pl.when(p > 0)
            def _():
                load_gu(p - 1).start()
                load_dn(p - 1).start()

        def do_Cg(self):
            p, par = self.p, self.par

            @pl.when(p < last)
            def _():
                grad_ffn.drained(ffn_outs, p + 1)

            for r in range(4):
                at = piece_at(r, f, quarter)
                gu_to, dn_to = (gu_kept, dn_kept) if r % 2 == 0 else (gu_sent, dn_sent)
                columns = g_ffn[par, :, :, :, at].reshape(rows, quarter)
                gu_to[r // 2, 0] = dot(columns, gg_s[...], TN).astype(bf16)
                gu_to[r // 2, 1] = dot(columns, gup_s[...], TN).astype(bf16)
                dn_to[r // 2] = dot(act_s[...], cot_v[:, :, :, at].reshape(rows, quarter), TN).astype(bf16)
            grad_ffn.start(p < last)
            when(p > 0, lambda: load_cot(p - 1).start())

        def do_Fm(self):
            grad_ffn.middle(self.p < last)

        def do_Ff(self):
            grad_ffn.finish(ffn_outs, self.p, self.p > 0)

        def do_RG5(self):
            p, total = self.p, self.RG()
            total.done()
            hmid = hmid_s[self.ring]
            factor = inverse_rms(hmid)
            grad = cot_ref[p].astype(f32) + norm_back(total.total(), hmid * factor, factor, gain_of(1, p))
            ghmid_s[self.ring] = grad
            g_att[self.par, 0, 0] = (mask * grad).astype(bf16)
            self.AG().t1()

        def do_RF5(self):
            p, total = self.p, self.RF()
            total.done()

            @pl.when(p < last)
            def _():
                out_copy(p + 1).wait()

            stage[0] = (hmid_s[self.ring] + mask * total.total()).astype(bf16)
            out_copy(p).start()

        def do_E(self):
            p, par = self.p, self.par
            self.AG().done()
            load_owe(p).wait()
            load_iw(p, 0).wait()
            load_rows(p, xb, 8).wait()
            gmixed_s[...] = dot(g_att[par].reshape(rows, depth), owe_v[...], NT).astype(bf16)
            attend_back_one(p)
            back = dot(gproj_s[0], iw_v[0, 0], NT)
            back = back + dot(gproj_s[1], iw_v[0, 1], NT)
            back = back + dot(gproj_s[2], iw_v[0, 2], NT)
            p_back[par] = back.astype(bf16).reshape(blocks)
            self.RB().t1()
            gain_s[0, pl.ds(p, 1), :] = jnp.sum(back * xb[...].reshape(rows, depth).astype(f32), axis=0, keepdims=True)

            @pl.when(p == 0)
            def _():
                for r in range(4):
                    gain_pieces[r % 2, r // 2] = gain_s[:, :, piece_at(r, f, quarter)]
                gain_sum.start()

            @pl.when(p > 0)
            def _():
                load_owe(p - 1).start()
                load_iw(p - 1, 0).start()

        def do_Eg(self):
            p, par = self.p, self.par

            @pl.when(p < last)
            def _():
                grad_att.drained(att_outs, p + 1)

            for r in range(4):
                at = piece_at(r, f, quarter)
                iw_to, ow_to = (iw_kept, ow_kept) if r % 2 == 0 else (iw_sent, ow_sent)
                columns = xb[:, :, :, at].reshape(rows, quarter)
                for j in range(3):
                    iw_to[r // 2, j] = dot(columns, gproj_s[j], TN).astype(bf16)
                ow_to[r // 2] = dot(mixed_s[p], g_att[par, :, :, :, at].reshape(rows, quarter), TN).astype(bf16)
            grad_att.start(p < last)
            when(p > 0, lambda: load_rows(p - 1, xb, 8).start())

        def do_Em(self):
            grad_att.middle(self.p < last)

        def do_Ef(self):
            grad_att.finish(att_outs, self.p, self.p > 0)

        def do_RB5(self):
            p, total = self.p, self.RB()
            total.done()
            when(p == 0, lambda: gain_sum.next(3))

            @pl.when(p < last)
            def _():
                ingrad_copy(p + 1).wait()

            residual = x_ref[p].astype(f32)
            factor = inverse_rms(residual)
            grad = norm_back(total.total(), residual * factor, factor, gain_of(0, p))
            stage[1] = (ghmid_s[self.ring] + grad).astype(bf16)
            ingrad_copy(p).start()

        def do_RB2(self):
            self.RB().t2()
            when(self.p == 0, lambda: gain_sum.next(0))

        def do_RB3(self):
            self.RB().t3()
            when(self.p == 0, lambda: gain_sum.next(1))

        def do_RB4(self):
            self.RB().t4()
            when(self.p == 0, lambda: gain_sum.next(2))

        def runs(self):
            ticks = {}
            for name, event in (
                ("RA", self.RA), ("RG", self.RG), ("RF", self.RF), ("AF", self.AF), ("AG", self.AG),
            ):
                ticks[name + "2"] = lambda event=event: event().t2()
                ticks[name + "3"] = lambda event=event: event().t3()
                ticks[name + "4"] = lambda event=event: event().t4()
            return ticks | {
                "A": self.do_A, "RA5": self.do_RA5, "C": self.do_C, "Cg": self.do_Cg, "Fm": self.do_Fm,
                "Ff": self.do_Ff, "RG5": self.do_RG5, "RF5": self.do_RF5, "E": self.do_E, "Eg": self.do_Eg,
                "Em": self.do_Em, "Ef": self.do_Ef, "RB2": self.do_RB2, "RB3": self.do_RB3, "RB4": self.do_RB4,
                "RB5": self.do_RB5,
            }

    def cot_runs(j):
        event = cot_gather(j, lax.rem(j + 16, 2))

        def done():
            event.done()
            when(j == 0, lambda: load_cot(last).start())

        return {"AC1": event.t1, "AC2": event.t2, "AC3": event.t3, "AC4": event.t4, "AC5": done}

    def tell(number, way):
        pl.semaphore_signal(credits.at[number], inc=1, device_id=place.device(way), device_id_type=MESH)

    def tell_all():
        tell(0, "y")
        when(z < 3, lambda: tell(1, "up"))
        when(z > 0, lambda: tell(2, "down"))

    steps = positions + max(delay for name, delay in SCHEDULE if name[:2] != "AC")
    tell_all()

    def step(s, c):
        pl.semaphore_wait(credits.at[0], 1)
        when(z > 0, lambda: pl.semaphore_wait(credits.at[1], 1))
        when(z < 3, lambda: pl.semaphore_wait(credits.at[2], 1))
        for name, delay in SCHEDULE:
            if name == "K":
                when(s < steps - 1, tell_all)
            elif name[:2] == "AC":
                j = s - delay
                when((j >= 0) & (j < pairs_of), cot_runs(j)[name])
            else:
                when((s >= delay) & (s <= last + delay), Position(s - delay).runs()[name])
        return c

    lax.fori_loop(0, steps, step, 0)
    gain_sum.next(4)
    gain_out[...] = gain_pieces[0, 0] / gains_ref[:, :, piece_at(0, f, quarter)]
    grad_ffn.drained(ffn_outs, 0)
    grad_att.drained(att_outs, 0)
    out_copy(0).wait()
    ingrad_copy(0).wait()


def layer(x, cot, mask, gains, masked_cot, in_weight, out_weight, gate_up, down):
    positions, local, depth = x.shape
    width, hidden = out_weight.shape[1], down.shape[1]
    rows = ZN * YN * local
    quarter = depth // 4
    block = (local, depth)
    groups = positions // 2

    def vm(*shape, dtype=bf16):
        return pltpu.VMEM(shape, dtype)

    def hbm(*shape, dtype=bf16):
        return jax.ShapeDtypeStruct(shape, dtype)

    everything = (ZN, YN) + block
    scratch = (
        [vm(2, *everything)] * 2
        + [vm(*everything)] * 3
        + [vm(2, *everything)] * 2
        + [vm(2, ZN, *block), vm(2, ZN, *block), vm(2, ZN, *block), vm(2, ZN, *block)]
        + [vm(2, 3, *block), vm(2, 3, *block), vm(2, 3, YN, *block), vm(2, 3, *block)] * 2
        + [vm(positions, rows, width)] * 4
        + [vm(positions, rows, width, dtype=f32)] * 2
        + [vm(positions, rows // 2, width, dtype=f32)] * 2
        + [vm(2, depth, hidden), vm(hidden, depth), vm(width, depth), vm(width, depth)]
        + [vm(2, 3, depth, width), vm(*everything)]
        + [vm(rows, hidden)] * 3
        + [vm(rows, width), vm(3, rows, width)]
        + [vm(4, *block, dtype=f32)] * 2
        + [vm(2, *block)]
        + [vm(2, positions, depth, dtype=f32)]
        + [vm(2, 2, 2, positions, quarter, dtype=f32), vm(6, 2, positions, quarter, dtype=f32)]
        + [vm(2, 2, quarter, hidden)] * 3
        + [vm(2, quarter, hidden)]
        + [vm(2, hidden, quarter)] * 3
        + [vm(hidden, quarter)]
        + [vm(2, 3, quarter, width)] * 3
        + [vm(3, quarter, width)]
        + [vm(2, width, quarter)] * 3
        + [vm(width, quarter)]
        + [
            pltpu.SemaphoreType.DMA((groups, 10)),
            pltpu.SemaphoreType.DMA((groups, 8)),
            pltpu.SemaphoreType.DMA((3, 2, 10)),
            pltpu.SemaphoreType.DMA((3, 2, 8)),
            pltpu.SemaphoreType.DMA((4, 2, 10)),
            pltpu.SemaphoreType.DMA((4, 2, 11)),
            pltpu.SemaphoreType.DMA((5, 2)),
            pltpu.SemaphoreType.DMA((5, 2)),
            pltpu.SemaphoreType.DMA((2, 5)),
            pltpu.SemaphoreType.DMA((16 + positions,)),
            pltpu.SemaphoreType.REGULAR((3,)),
            pltpu.SemaphoreType.REGULAR((4,)),
        ]
    )
    in_vmem = pl.BlockSpec(memory_space=pltpu.VMEM)
    anywhere = pl.BlockSpec(memory_space=pl.ANY)
    return pl.pallas_call(
        layer_kernel,
        in_specs=[in_vmem] * 4 + [anywhere] * 5,
        out_specs=[anywhere] * 6 + [in_vmem, anywhere, anywhere],
        out_shape=[
            hbm(positions, *block),
            hbm(positions, *block),
            hbm(positions, 2, quarter, hidden),
            hbm(positions, hidden, quarter),
            hbm(positions, 3, quarter, width),
            hbm(positions, width, quarter),
            hbm(2, positions, quarter, dtype=f32),
            hbm(positions // 2, ZN, YN, 2, *block),
            hbm(positions // 2, ZN, YN, 2, *block),
        ],
        scratch_shapes=scratch,
        compiler_params=pltpu.CompilerParams(
            collective_id=0, has_side_effects=True, vmem_limit_bytes=KERNEL_VMEM_BYTES
        ),
        name="layer",
    )(x, cot, mask, gains, masked_cot, in_weight, out_weight, gate_up, down)


def body_in_one(inputs, counts, norm_gains, in_weight, out_weight, gate_up, down_weight, cotangent):
    local, positions, depth = inputs.shape
    ids = lax.axis_index("mp") * local + jnp.arange(local)
    valid = ids < counts[0]
    masked = jnp.where(valid[:, None, None], cotangent, jnp.zeros_like(cotangent))
    output, input_grad, g_gu, g_dn, g_in, g_out, gain_sums, _, _ = layer(
        jnp.swapaxes(inputs, 0, 1),
        jnp.swapaxes(cotangent, 0, 1),
        valid.astype(f32)[:, None],
        norm_gains,
        jnp.swapaxes(masked, 0, 1).reshape(positions // 2, 2, local, depth),
        in_weight,
        out_weight,
        gate_up,
        down_weight,
    )
    return (
        jnp.swapaxes(output, 0, 1),
        jnp.swapaxes(input_grad, 0, 1),
        g_in.astype(f32),
        g_out.astype(f32),
        g_gu.astype(f32),
        g_dn.astype(f32),
        gain_sums,
    )


def solution(mesh):
    placed = (
        P(("frames", "mp"), None, None),
        P("frames"),
        P(),
        P(None, None, None, "mp"),
        P(None, "mp", None),
        P(None, None, None, "mp"),
        P(None, "mp", None),
        P(("frames", "mp"), None, None),
    )
    def local_body(*args):
        frames, group_size = lax.axis_size("frames"), lax.axis_size("mp")
        local, positions, depth = args[0].shape
        width, hidden = args[4].shape[1], args[6].shape[1]
        one = fits(frames, group_size, local, positions, depth, width, hidden)
        return (body_in_one if one else body)(*args)

    return jax.shard_map(
        local_body,
        mesh=mesh,
        in_specs=placed,
        out_specs=(
            P(("frames", "mp"), None, None),
            P(("frames", "mp"), None, None),
            P(None, None, "frames", "mp"),
            P(None, "mp", "frames"),
            P(None, None, "frames", "mp"),
            P(None, "mp", "frames"),
            P(None, None, "frames"),
        ),
        check_vma=False,
    )
```

```python
import functools
import math

import jax
import jax.numpy as jnp
from jax import lax
from jax.experimental import pallas as pl
from jax.experimental.pallas import tpu as pltpu
from jax.sharding import PartitionSpec as P

HDIM = 64
EPSILON = 1e-05
Z_CHIPS = 4
FRAME_BLOCK = 16
CHUNKS = 4
VMEM_BYTES = 56 * 1024 * 1024
KERNEL_VMEM_BYTES = 63 * 1024 * 1024

f32 = jnp.float32
bf16 = jnp.bfloat16


class Line:
    def __init__(self, total, n, stride):
        self.n = n
        self.stride = stride
        self.starts = [i for i in range(total) if (i // stride) % n == 0]

    def up(self, low, high):
        return [(s + i * self.stride, s + (i + 1) * self.stride) for s in self.starts for i in range(low, high)]

    def down(self, low, high):
        return [(s + (i + 1) * self.stride, s + i * self.stride) for s in self.starts for i in range(low, high)]

    def gather(self, own):
        n = self.n
        if n == 1:
            return [own]
        if n == 2:
            return [own, lax.ppermute(own, "mp", self.up(0, 1) + self.down(0, 1))]
        ups, downs = [own], [own]
        for k in range(1, n):
            ups.append(lax.ppermute(ups[-1], "mp", self.up(k - 1, n - 1)))
            downs.append(lax.ppermute(downs[-1], "mp", self.down(0, n - k)))
        return [own] + [ups[k] + downs[n - k] for k in range(1, n)]

    def reduce(self, term):
        n = self.n
        if n == 1:
            return [term(0)]
        if n == 2:
            return [term(0), lax.ppermute(term(1).astype(bf16), "mp", self.up(0, 1) + self.down(0, 1)).astype(f32)]
        up = down = None
        for s in range(1, n):
            send_up = term(s) if up is None else term(s) + up.astype(f32)
            send_down = term(n - s) if down is None else term(n - s) + down.astype(f32)
            up = lax.ppermute(send_up.astype(bf16), "mp", self.up(0, min(s, n - 1)))
            down = lax.ppermute(send_down.astype(bf16), "mp", self.down(n - 1 - s, n - 1))
        return [term(0), up.astype(f32), down.astype(f32)]


class Group:
    def __init__(self, size):
        self.nz = math.gcd(size, Z_CHIPS)
        self.ny = size // self.nz
        self.z = Line(size, self.nz, self.ny)
        self.y = Line(size, self.ny, 1)

    def gather(self, own, z_first):
        if z_first:
            column = jnp.stack(self.z.gather(own), axis=1)
            return jnp.stack(self.y.gather(column), axis=1)
        row = jnp.stack(self.y.gather(own), axis=1)
        return jnp.stack(self.z.gather(row), axis=2)

    def reduce(self, parts, z_first):
        if not z_first:
            if self.ny == 2:
                got = lax.ppermute(parts[1], "mp", self.y.up(0, 1) + self.y.down(0, 1))
                columns = [parts[0], got]

                def term(k):
                    return columns[0][:, k].astype(f32) + columns[1][:, k].astype(f32)

            else:
                terms = self.y.reduce(lambda k: parts[k].astype(f32))

                def term(k):
                    return sum(t[:, k] for t in terms)

            return sum(self.z.reduce(term))

        def row(k):
            return jnp.stack([part[:, k] for part in parts], axis=1).astype(f32)

        terms = self.z.reduce(row)
        return sum(self.y.reduce(lambda k: sum(t[:, k] for t in terms)))


def frames_sum(keep, send, size):
    step = 1
    while True:
        got = lax.ppermute(send, "frames", [(i, i ^ step) for i in range(size)])
        total = keep.astype(f32) + got.astype(f32)
        step *= 2
        if step == size:
            return total[:, 0]
        keep, send = total[:, 0::2], total[:, 1::2].astype(send.dtype)


def dot(a, b, dims):
    return lax.dot_general(a, b, (dims, ((), ())), preferred_element_type=f32)


NN = ((1,), (0,))
NT = ((1,), (1,))
TN = ((0,), (0,))


def params():
    return pltpu.CompilerParams(vmem_limit_bytes=VMEM_BYTES)


def cost(flops, nbytes):
    return pl.CostEstimate(flops=int(flops), bytes_accessed=int(nbytes), transcendentals=0)


def qkv_kernel(x_ref, w_ref, q_ref, k_ref, v_ref):
    x = x_ref[0]
    for c, out in enumerate((q_ref, k_ref, v_ref)):
        out[0] = dot(x, w_ref[0, c], NN).astype(bf16)


def qkv(x, weight, base):
    count, rows, depth = x.shape
    width = weight.shape[-1]
    out = jax.ShapeDtypeStruct((count, rows, width), bf16)
    return pl.pallas_call(
        qkv_kernel,
        grid=(count,),
        in_specs=[
            pl.BlockSpec((1, rows, depth), lambda i: (i, 0, 0)),
            pl.BlockSpec((1, 3, depth, width), lambda i: (base + i, 0, 0, 0)),
        ],
        out_specs=[pl.BlockSpec((1, rows, width), lambda i: (i, 0, 0))] * 3,
        out_shape=[out] * 3,
        compiler_params=params(),
        cost_estimate=cost(6 * count * rows * depth * width, 2 * count * depth * (rows + 3 * width)),
        name="qkv",
    )(x, weight)


def head_masks(rows, width):
    lane = lax.broadcasted_iota(jnp.int32, (rows, width), 1)
    return [(lane >= h * HDIM) & (lane < (h + 1) * HDIM) for h in range(width // HDIM)]


def attention_mask(count, base, columns):
    rows = count * FRAME_BLOCK
    row = lax.broadcasted_iota(jnp.int32, (rows, columns), 0)
    column = lax.broadcasted_iota(jnp.int32, (rows, columns), 1)
    same = (row % FRAME_BLOCK) == (column % FRAME_BLOCK)
    return same & (column // FRAME_BLOCK <= row // FRAME_BLOCK + base)


def block_of(refs, rows):
    pieces = [ref[:, rows, :] for ref in refs]
    pieces = [p.reshape(p.shape[0] * p.shape[1], p.shape[2]) for p in pieces]
    return pieces[0] if len(pieces) == 1 else jnp.concatenate(pieces, axis=0)


def softmax(scores):
    top = jnp.max(scores, axis=-1, keepdims=True)
    raised = jnp.exp(scores - top)
    return raised / jnp.sum(raised, axis=-1, keepdims=True)


def pick(masks, values):
    out = values[0]
    for mask, value in zip(masks[1:], values[1:]):
        out = jnp.where(mask, value, out)
    return out


def attend_kernel(base, n_kv, ny, q_ref, *refs):
    k_refs, v_refs = refs[:n_kv], refs[n_kv : 2 * n_kv]
    w_ref = refs[2 * n_kv]
    mixed_ref = refs[2 * n_kv + 1]
    part_refs = refs[2 * n_kv + 2 :]
    count, rows, width = q_ref.shape
    columns = sum(ref.shape[0] for ref in k_refs) * FRAME_BLOCK
    step = pl.program_id(0)

    @pl.when(step == 0)
    def _():
        heads = head_masks(count * FRAME_BLOCK, width)
        allowed = attention_mask(count, base, columns)

        def one(b):
            at = pl.ds(pl.multiple_of(b * FRAME_BLOCK, FRAME_BLOCK), FRAME_BLOCK)
            queries = block_of([q_ref], at) * HDIM ** (-0.5)
            keys, values = block_of(k_refs, at), block_of(v_refs, at)
            outs = []
            for head in heads:
                mine = jnp.where(head, queries, jnp.zeros_like(queries))
                scores = jnp.where(allowed, dot(mine, keys, NT), -1e30)
                outs.append(dot(softmax(scores).astype(bf16), values, NN))
            mixed_ref[:, at, :] = pick(heads, outs).astype(bf16).reshape(count, FRAME_BLOCK, width)

        lax.fori_loop(0, rows // FRAME_BLOCK, lambda b, c: (one(b), c)[1], 0, unroll=4)

    out = dot(mixed_ref[step], w_ref[0], NN)
    span = rows // ny
    for y, part in enumerate(part_refs):
        part[0] = out[y * span : (y + 1) * span].astype(bf16)


def attend(q, ks, vs, weight, base, ny):
    count, rows, width = q.shape
    depth = weight.shape[-1]
    whole = pl.BlockSpec((count, rows, width), lambda i: (0, 0, 0))
    part = jax.ShapeDtypeStruct((count, rows // ny, depth), bf16)
    n_kv = len(ks)
    return pl.pallas_call(
        functools.partial(attend_kernel, base, n_kv, ny),
        grid=(count,),
        in_specs=[whole] * (1 + 2 * n_kv) + [pl.BlockSpec((1, width, depth), lambda i: (base + i, 0, 0))],
        out_specs=[whole] + [pl.BlockSpec((1, rows // ny, depth), lambda i: (i, 0, 0))] * ny,
        out_shape=[jax.ShapeDtypeStruct(q.shape, bf16)] + [part] * ny,
        compiler_params=params(),
        cost_estimate=cost(4 * count * rows * depth * width, 2 * count * rows * (depth + (2 + 2 * n_kv) * width)),
        name="attend",
    )(q, *ks, *vs, weight)


def gradient_pieces(size, depth):
    return size if size > 1 and (depth // size) % 128 == 0 else 1


def piece_at(piece, mine, span):
    return pl.ds(pl.multiple_of((piece ^ mine) * span, span), span)


def ffn_kernel(ny, pieces, mine_ref, x_ref, g_ref, gu_ref, dn_ref, *refs):
    outs, backs = refs[:ny], refs[ny : 2 * ny]
    gain_ref = refs[2 * ny]
    grads = refs[2 * ny + 1 :]
    rows, depth = x_ref.shape[1:]
    span = rows // ny
    x, g = x_ref[0], g_ref[0]
    gate = dot(x, gu_ref[0, 0], NN)
    up = dot(x, gu_ref[0, 1], NN)
    grad_act = dot(g, dn_ref[0], NT)
    sigma = 1.0 / (1.0 + jnp.exp(-gate))
    silu = gate * sigma
    act = (silu * up).astype(bf16)
    grad_gate = (grad_act * up * sigma * (1.0 + gate * (1.0 - sigma))).astype(bf16)
    grad_up = (grad_act * silu).astype(bf16)
    out = dot(act, dn_ref[0], NN)
    for y in range(ny):
        outs[y][0] = out[y * span : (y + 1) * span].astype(bf16)
    back = dot(grad_gate, gu_ref[0, 0], NT) + dot(grad_up, gu_ref[0, 1], NT)
    for y in range(ny):
        backs[y][0] = back[y * span : (y + 1) * span].astype(bf16)
    gain_ref[0] = jnp.sum(back * x.astype(f32), axis=0, keepdims=True)
    if pieces == 1:
        grads[0][0, 0] = dot(x, grad_gate, TN).astype(bf16)
        grads[0][0, 1] = dot(x, grad_up, TN).astype(bf16)
        grads[1][0] = dot(act, g, TN).astype(bf16)
        return
    mine = mine_ref[0]
    width = depth // pieces
    for r in range(pieces):
        at = piece_at(r, mine, width)
        gu_out, dn_out = grads[r % 2], grads[2 + r % 2]
        columns = x_ref[0, :, at]
        gu_out[0, r // 2, 0] = dot(columns, grad_gate, TN).astype(bf16)
        gu_out[0, r // 2, 1] = dot(columns, grad_up, TN).astype(bf16)
        dn_out[0, r // 2] = dot(act, g_ref[0, :, at], TN).astype(bf16)


def split_specs(shape, pieces, axis):
    if pieces == 1:
        block = (1,) + shape[1:]
        return [pl.BlockSpec(block, lambda i: (i,) + (0,) * (len(block) - 1))], [jax.ShapeDtypeStruct(shape, bf16)]
    rest = list(shape[1:])
    rest[axis - 1] //= pieces
    block = (1, pieces // 2) + tuple(rest)
    spec = pl.BlockSpec(block, lambda i: (i,) + (0,) * (len(block) - 1))
    return [spec] * 2, [jax.ShapeDtypeStruct((shape[0],) + block[1:], bf16)] * 2


def ffn(x, g, gate_up, down, base, ny, frames, mine):
    count, rows, depth = x.shape
    width = down.shape[1]
    pieces = gradient_pieces(frames, depth)
    part = jax.ShapeDtypeStruct((count, rows // ny, depth), bf16)
    part_spec = pl.BlockSpec((1, rows // ny, depth), lambda i: (i, 0, 0))
    row_spec = pl.BlockSpec((1, rows, depth), lambda i: (i, 0, 0))
    gu_specs, gu_shapes = split_specs((count, 2, depth, width), pieces, 2)
    dn_specs, dn_shapes = split_specs((count, width, depth), pieces, 2)
    out = pl.pallas_call(
        functools.partial(ffn_kernel, ny, pieces),
        grid=(count,),
        in_specs=[
            pl.BlockSpec(memory_space=pltpu.SMEM),
            row_spec,
            row_spec,
            pl.BlockSpec((1, 2, depth, width), lambda i: (base + i, 0, 0, 0)),
            pl.BlockSpec((1, width, depth), lambda i: (base + i, 0, 0)),
        ],
        out_specs=[part_spec] * (2 * ny) + [pl.BlockSpec((1, 1, depth), lambda i: (i, 0, 0))] + gu_specs + dn_specs,
        out_shape=[part] * (2 * ny) + [jax.ShapeDtypeStruct((count, 1, depth), f32)] + gu_shapes + dn_shapes,
        compiler_params=params(),
        cost_estimate=cost(18 * count * rows * depth * width, 2 * count * depth * (4 * rows + 6 * width)),
        name="ffn",
    )(mine, x, g, gate_up, down)
    n = len(gu_specs)
    return out[:ny], out[ny : 2 * ny], out[2 * ny], out[2 * ny + 1 : 2 * ny + 1 + n], out[2 * ny + 1 + n :]


def attend_back_kernel(base, n_kv, first, ny, pieces, mine_ref, ga_ref, gp_ref, x_ref, q_ref, *refs):
    refs = list(refs)

    def take(n):
        got = refs[:n]
        del refs[:n]
        return got

    k_refs, v_refs = take(n_kv), take(n_kv)
    (mixed_ref, ow_all_ref, iw_ref) = take(3)
    dk_in = dv_in = ()
    if not first:
        dk_in, dv_in = take(n_kv), take(n_kv)
    part_refs = take(ny)
    (gain_ref,) = take(1)
    n_out = 1 if pieces == 1 else 2
    iw_grads, ow_grads = take(n_out), take(n_out)
    dk_out, dv_out = take(n_kv - 1), take(n_kv - 1)
    gmixed_ref, gproj_ref = take(2)
    count, rows, width = q_ref.shape
    columns = n_kv * count * FRAME_BLOCK
    block = count * FRAME_BLOCK
    step = pl.program_id(0)

    @pl.when(step == 0)
    def _():
        for p in range(count):
            gmixed_ref[p] = dot(ga_ref[p], ow_all_ref[p], NT).astype(bf16)
        heads = head_masks(block, width)
        allowed = attention_mask(count, base, columns)
        factor = HDIM ** (-0.5)

        def one(b):
            at = pl.ds(pl.multiple_of(b * FRAME_BLOCK, FRAME_BLOCK), FRAME_BLOCK)
            queries = block_of([q_ref], at) * factor
            grad_mixed = block_of([gmixed_ref], at)
            keys, values = block_of(k_refs, at), block_of(v_refs, at)
            dqs, dk, dv = [], None, None
            for head in heads:
                my_q = jnp.where(head, queries, jnp.zeros_like(queries))
                my_g = jnp.where(head, grad_mixed, jnp.zeros_like(grad_mixed))
                probs = softmax(jnp.where(allowed, dot(my_q, keys, NT), -1e30))
                grad_probs = dot(my_g, values, NT)
                weighted = probs * grad_probs
                grad_scores = (weighted - probs * jnp.sum(weighted, axis=-1, keepdims=True)).astype(bf16)
                dqs.append(dot(grad_scores, keys, NN))
                more_k = dot(grad_scores, my_q, TN)
                more_v = dot(probs.astype(bf16), my_g, TN)
                dk = more_k if dk is None else dk + more_k
                dv = more_v if dv is None else dv + more_v
            gproj_ref[:, 0, at, :] = (pick(heads, dqs) * factor).astype(bf16).reshape(count, FRAME_BLOCK, width)
            for c, total, earlier, later in ((1, dk, dk_in, dk_out), (2, dv, dv_in, dv_out)):
                for j in range(n_kv):
                    piece = total[j * block : (j + 1) * block].reshape(count, FRAME_BLOCK, width)
                    if not first:
                        piece = piece + earlier[j][:, at, :]
                    if j < n_kv - 1:
                        later[j][:, at, :] = piece
                    else:
                        gproj_ref[:, c, at, :] = piece.astype(bf16)

        lax.fori_loop(0, rows // FRAME_BLOCK, lambda b, c: (one(b), c)[1], 0, unroll=2)

    grads = [gproj_ref[step, c] for c in range(3)]
    back = dot(grads[0], iw_ref[0, 0], NT) + dot(grads[1], iw_ref[0, 1], NT) + dot(grads[2], iw_ref[0, 2], NT)
    span = rows // ny
    for y, part in enumerate(part_refs):
        part[0] = back[y * span : (y + 1) * span].astype(bf16)
    gain_ref[0] = jnp.sum(back * x_ref[0].astype(f32), axis=0, keepdims=True)
    mixed = mixed_ref[0]
    if pieces == 1:
        for c in range(3):
            iw_grads[0][0, c] = dot(x_ref[0], grads[c], TN).astype(bf16)
        ow_grads[0][0] = dot(mixed, gp_ref[0], TN).astype(bf16)
        return
    mine = mine_ref[0]
    depth = x_ref.shape[2]
    for r in range(pieces):
        at = piece_at(r, mine, depth // pieces)
        columns = x_ref[0, :, at]
        for c in range(3):
            iw_grads[r % 2][0, r // 2, c] = dot(columns, grads[c], TN).astype(bf16)
        ow_grads[r % 2][0, r // 2] = dot(mixed, gp_ref[0, :, at], TN).astype(bf16)


def attend_back(grad_rows, x, q, ks, vs, mixed, out_weight, in_weight, dks, dvs, base, ny, frames, mine):
    count, rows, depth = x.shape
    width = q.shape[-1]
    pieces = gradient_pieces(frames, depth)
    n_kv = len(ks)
    first = not dks
    whole = pl.BlockSpec((count, rows, width), lambda i: (0, 0, 0))
    row_spec = pl.BlockSpec((1, rows, depth), lambda i: (i, 0, 0))
    chunk = base // count
    part = jax.ShapeDtypeStruct((count, rows // ny, depth), bf16)
    part_spec = pl.BlockSpec((1, rows // ny, depth), lambda i: (i, 0, 0))
    iw_specs, iw_shapes = split_specs((count, 3, depth, width), pieces, 2)
    ow_specs, ow_shapes = split_specs((count, width, depth), pieces, 2)
    total = jax.ShapeDtypeStruct((count, rows, width), f32)
    out = pl.pallas_call(
        functools.partial(attend_back_kernel, base, n_kv, first, ny, pieces),
        grid=(count,),
        in_specs=[
            pl.BlockSpec(memory_space=pltpu.SMEM),
            pl.BlockSpec((count, rows, depth), lambda i: (0, 0, 0)),
            row_spec,
            row_spec,
        ]
        + [whole] * (1 + 2 * n_kv)
        + [
            pl.BlockSpec((1, rows, width), lambda i: (i, 0, 0)),
            pl.BlockSpec((count, width, depth), lambda i: (chunk, 0, 0)),
            pl.BlockSpec((1, 3, depth, width), lambda i: (base + i, 0, 0, 0)),
        ]
        + [whole] * (len(dks) + len(dvs)),
        out_specs=[part_spec] * ny
        + [pl.BlockSpec((1, 1, depth), lambda i: (i, 0, 0))]
        + iw_specs
        + ow_specs
        + [whole] * (2 * (n_kv - 1)),
        out_shape=[part] * ny
        + [jax.ShapeDtypeStruct((count, 1, depth), f32)]
        + iw_shapes
        + ow_shapes
        + [total] * (2 * (n_kv - 1)),
        scratch_shapes=[pltpu.VMEM((count, rows, width), bf16), pltpu.VMEM((count, 3, rows, width), bf16)],
        compiler_params=params(),
        cost_estimate=cost(16 * count * rows * depth * width, 2 * count * rows * (4 * depth + 8 * n_kv * width)),
        name="attend_back",
    )(mine, grad_rows, grad_rows, x, q, *ks, *vs, mixed, out_weight, in_weight, *dks, *dvs)
    out = list(out)
    n = len(iw_specs)
    parts, gain = out[:ny], out[ny]
    iw, ow = out[ny + 1 : ny + 1 + n], out[ny + 1 + n : ny + 1 + 2 * n]
    rest = out[ny + 1 + 2 * n :]
    return parts, gain, iw, ow, rest[: n_kv - 1], rest[n_kv - 1 :]


def inverse_rms(values):
    return lax.rsqrt(jnp.mean(values * values, axis=-1, keepdims=True) + EPSILON)


def norm_back(grad_normed, normed, factor, gain):
    scaled = grad_normed * gain
    return factor * (scaled - normed * jnp.mean(scaled * normed, axis=-1, keepdims=True))


def body(inputs, counts, norm_gains, in_weight, out_weight, gate_up, down_weight, cotangent):
    frames, group_size = lax.axis_size("frames"), lax.axis_size("mp")
    group = Group(group_size)
    ny, nz = group.ny, group.nz
    local, positions, depth = inputs.shape
    rows = local * group_size
    size = positions // CHUNKS
    ids = lax.axis_index("mp") * local + jnp.arange(local)
    mask = (ids < counts[0]).astype(f32)[None, :, None]
    mine = lax.axis_index("frames").astype(jnp.int32)[None]
    x_major = jnp.swapaxes(inputs, 0, 1)
    g_major = jnp.swapaxes(cotangent, 0, 1)
    gains = norm_gains[:, :, None, :]

    def at(c):
        return slice(c * size, (c + 1) * size)

    def gathered(own, z_first):
        return group.gather(own, z_first).reshape(size, rows, depth)

    def reduced(parts, z_first):
        return group.reduce([p.reshape(size, nz, local, depth) for p in parts], z_first)

    def summed(grads):
        if len(grads) == 1:
            return lax.psum_scatter(grads[0], "frames", scatter_dimension=grads[0].ndim - 1, tiled=True).astype(f32)
        return frames_sum(grads[0], grads[1], frames)

    def summed_middle(grads):
        if len(grads) == 1:
            return lax.psum_scatter(grads[0], "frames", scatter_dimension=2, tiled=True).astype(f32)
        return frames_sum(grads[0], grads[1], frames)

    order = list(range(CHUNKS))[::-1]
    attn_in, qs, ks, vs = {}, {}, {}, {}
    for c in order:
        residual = x_major[at(c)].astype(f32)
        own = (residual * inverse_rms(residual) * gains[0, at(c)]).astype(bf16)
        attn_in[c] = gathered(own, True)
        qs[c], ks[c], vs[c] = qkv(attn_in[c], in_weight, c * size)

    outputs, input_grads = {}, {}
    g_in, g_out, g_gu, g_dn, gain_terms = {}, {}, {}, {}, {}
    dks, dvs = [], []
    for c in order:
        base = c * size
        gain_first, gain_second = gains[0, at(c)], gains[1, at(c)]
        residual = x_major[at(c)].astype(f32)
        gy = g_major[at(c)].astype(f32)
        grad_rows = gathered((mask * gy).astype(bf16), c % 2 == 0)
        earlier_k, earlier_v = [ks[j] for j in range(c + 1)], [vs[j] for j in range(c + 1)]
        mixed, *parts = attend(qs[c], earlier_k, earlier_v, out_weight, base, ny)
        hmid = residual + mask * reduced(parts, False)
        scale_second = inverse_rms(hmid)
        normed_second = hmid * scale_second
        ffn_rows = gathered((normed_second * gain_second).astype(bf16), True)
        out_parts, back_parts, gain_back, grad_gu, grad_dn = ffn(
            ffn_rows, grad_rows, gate_up, down_weight, base, ny, frames, mine
        )
        grad_ffn_in = reduced(back_parts, False)
        grad_mid = gy + norm_back(grad_ffn_in, normed_second, scale_second, gain_second)
        grad_attn = gathered((mask * grad_mid).astype(bf16), True)
        outputs[c] = (hmid + mask * reduced(out_parts, True)).astype(bf16)
        back, gain_front, grad_iw, grad_ow, dks, dvs = attend_back(
            grad_attn, attn_in[c], qs[c], earlier_k, earlier_v, mixed, out_weight, in_weight,
            dks, dvs, base, ny, frames, mine,
        )
        grad_attn_in = reduced(back, c % 2 == 1)
        scale_first = inverse_rms(residual)
        input_grads[c] = (
            grad_mid + norm_back(grad_attn_in, residual * scale_first, scale_first, gain_first)
        ).astype(bf16)
        gain_terms[c] = jnp.stack([gain_front[:, 0] / norm_gains[0, at(c)], gain_back[:, 0] / norm_gains[1, at(c)]])
        g_gu[c], g_dn[c] = summed_middle(grad_gu), summed(grad_dn)
        g_in[c], g_out[c] = summed_middle(grad_iw), summed(grad_ow)

    def joined(pieces, axis=0):
        return jnp.concatenate([pieces[c] for c in range(CHUNKS)], axis=axis)

    terms = lax.psum_scatter(joined(gain_terms, 1), "frames", scatter_dimension=2, tiled=True)
    step = 1
    while step < group_size:
        terms = terms + lax.ppermute(terms, "mp", [(i, i ^ step) for i in range(group_size)])
        step *= 2
    return (
        jnp.swapaxes(joined(outputs), 0, 1),
        jnp.swapaxes(joined(input_grads), 0, 1),
        joined(g_in),
        joined(g_out),
        joined(g_gu),
        joined(g_dn),
        terms,
    )


MESH = pl.DeviceIdType.MESH
ZN, YN = 4, 2


def fits(frames, group_size, local, positions, depth, width, hidden):
    return (
        frames == 4
        and group_size == ZN * YN
        and local == 48
        and positions == 16
        and width % 128 == 0
        and (depth // frames) % 128 == 0
        and hidden % 128 == 0
    )


class Place:
    def __init__(self):
        self.m = lax.axis_index("mp")
        self.f = lax.axis_index("frames")
        self.z = self.m // YN
        self.ids = {
            "y": ("mp", self.m ^ 1),
            "up": ("mp", self.m + YN),
            "down": ("mp", self.m - YN),
            "core": ("frames", self.f ^ 1),
            "x": ("frames", self.f ^ 2),
            "pair": ("mp", self.m ^ YN),
            "far": ("mp", self.m ^ (2 * YN)),
        }

    def device(self, way):
        axis, index = self.ids[way]
        return {axis: index}

    def copy(self, src, dst, send, recv, way):
        return pltpu.make_async_remote_copy(
            src_ref=src, dst_ref=dst, send_sem=send, recv_sem=recv, device_id=self.device(way), device_id_type=MESH
        )


def when(condition, run):
    pl.when(condition)(run)


def wait_got(dst, send, recv, place):
    place.copy(dst, dst, send, recv, "y").wait_recv()


class GatherZ:
    def __init__(self, place, g, send, recv):
        self.place, self.g, self.send, self.recv = place, g, send, recv

    def site(self, number, way, src, dst):
        return self.place.copy(
            self.g.at[src[0], src[1]],
            self.g.at[dst[0], dst[1]],
            self.send.at[number],
            self.recv.at[dst[0] * 2 + dst[1]],
            way,
        )

    def up(self, k):
        return self.site(k - 1, "up", (k - 1, 0), (k, 0))

    def down(self, k):
        return self.site(2 + k, "down", ((5 - k) % 4, 0), (4 - k, 0))

    def across(self, k):
        return self.site(6 + k, "y", (k, 0), (k, 1))

    def got(self, k, y):
        wait_got(self.g.at[k, y], self.send.at[0], self.recv.at[k * 2 + y], self.place)

    def t1(self):
        z = self.place.z
        when(z < 3, lambda: self.up(1).start())
        when(z > 0, lambda: self.down(1).start())
        self.across(0).start()

    def t2(self):
        z = self.place.z

        def low():
            self.got(1, 0)
            when(z < 3, lambda: self.up(2).start())
            self.across(1).start()

        def high():
            self.got(3, 0)
            when(z > 0, lambda: self.down(2).start())
            self.across(3).start()

        when(z >= 1, low)
        when(z <= 2, high)

    def t3(self):
        z = self.place.z
        self.got(2, 0)
        when(z == 2, lambda: self.up(3).start())
        when(z == 1, lambda: self.down(3).start())
        self.across(2).start()

    def t4(self):
        z = self.place.z

        def bottom():
            self.got(1, 0)
            self.across(1).start()

        def top():
            self.got(3, 0)
            self.across(3).start()

        when(z == 0, bottom)
        when(z == 3, top)

    def done(self):
        z = self.place.z
        for k in range(4):
            self.got(k, 1)
        when(z < 3, lambda: self.up(1).wait_send())
        when(z > 0, lambda: self.down(1).wait_send())
        when((z >= 1) & (z < 3), lambda: self.up(2).wait_send())
        when((z >= 1) & (z < 3), lambda: self.down(2).wait_send())
        when(z == 2, lambda: self.up(3).wait_send())
        when(z == 1, lambda: self.down(3).wait_send())
        for k in range(4):
            self.across(k).wait_send()


class GatherY:
    def __init__(self, place, g, send, recv):
        self.place, self.g, self.send, self.recv = place, g, send, recv

    def site(self, number, way, src, dst):
        return self.place.copy(self.g.at[src], self.g.at[dst], self.send.at[number], self.recv.at[dst], way)

    def up(self, k):
        return self.site(k - 1, "up", k - 1, k)

    def down(self, k):
        return self.site(2 + k, "down", (5 - k) % 4, 4 - k)

    def across(self):
        return self.place.copy(self.g.at[0, 0], self.g.at[0, 1], self.send.at[6], self.recv.at[4], "y")

    def got(self, k):
        wait_got(self.g.at[k], self.send.at[0], self.recv.at[k], self.place)

    def t1(self):
        self.across().start()

    def t2(self):
        z = self.place.z
        wait_got(self.g.at[0, 1], self.send.at[0], self.recv.at[4], self.place)
        when(z < 3, lambda: self.up(1).start())
        when(z > 0, lambda: self.down(1).start())

    def t3(self):
        z = self.place.z

        def low():
            self.got(1)
            when(z < 3, lambda: self.up(2).start())

        def high():
            self.got(3)
            when(z > 0, lambda: self.down(2).start())

        when(z >= 1, low)
        when(z <= 2, high)

    def t4(self):
        z = self.place.z
        self.got(2)
        when(z == 2, lambda: self.up(3).start())
        when(z == 1, lambda: self.down(3).start())

    def done(self):
        z = self.place.z
        when(z == 0, lambda: self.got(1))
        when(z == 3, lambda: self.got(3))
        when(z < 3, lambda: self.up(1).wait_send())
        when(z > 0, lambda: self.down(1).wait_send())
        when((z >= 1) & (z < 3), lambda: self.up(2).wait_send())
        when((z >= 1) & (z < 3), lambda: self.down(2).wait_send())
        when(z == 2, lambda: self.up(3).wait_send())
        when(z == 1, lambda: self.down(3).wait_send())
        self.across().wait_send()


def up_to_f32(condition, ref):
    return jnp.where(condition, ref[...].astype(f32), 0.0)


class ReduceY:
    def __init__(self, place, part, over, ups, downs, send, recv):
        self.place, self.part, self.over, self.ups, self.downs = place, part, over, ups, downs
        self.send, self.recv = send, recv

    def across(self, k):
        return self.place.copy(self.part.at[k, 1], self.over.at[k], self.send.at[6 + k], self.recv.at[7 + k], "y")

    def up(self, s):
        return self.place.copy(
            self.part.at[s, 0], self.ups.at[s - 1], self.send.at[2 * s - 2], self.recv.at[s], "up"
        )

    def down(self, s):
        return self.place.copy(
            self.part.at[4 - s, 0], self.downs.at[s - 1], self.send.at[2 * s - 1], self.recv.at[3 + s], "down"
        )

    def got_over(self, k):
        wait_got(self.over.at[k], self.send.at[0], self.recv.at[7 + k], self.place)

    def got_up(self, s):
        wait_got(self.ups.at[s - 1], self.send.at[0], self.recv.at[s], self.place)

    def got_down(self, s):
        wait_got(self.downs.at[s - 1], self.send.at[0], self.recv.at[3 + s], self.place)

    def local(self, k):
        return self.part[k, 0].astype(f32) + self.over[k].astype(f32)

    def store(self, k, value):
        self.part[k, 0] = value.astype(bf16)

    def t1(self):
        for k in (1, 3, 2, 0):
            self.across(k).start()

    def t2(self):
        z = self.place.z

        def bottom():
            self.got_over(1)
            self.store(1, self.local(1))
            self.up(1).start()

        def top():
            self.got_over(3)
            self.store(3, self.local(3))
            self.down(1).start()

        when(z == 0, bottom)
        when(z == 3, top)

    def t3(self):
        z = self.place.z
        self.got_over(2)
        when(z == 1, lambda: self.got_up(1))
        when(z == 2, lambda: self.got_down(1))
        self.store(
            2, self.local(2) + up_to_f32(z == 1, self.ups.at[0]) + up_to_f32(z == 2, self.downs.at[0])
        )
        when(z <= 1, lambda: self.up(2).start())
        when(z >= 2, lambda: self.down(2).start())

    def t4(self):
        z = self.place.z

        def low():
            self.got_over(3)
            when(z >= 1, lambda: self.got_up(2))
            self.store(3, self.local(3) + up_to_f32(z >= 1, self.ups.at[1]))
            self.up(3).start()

        def high():
            self.got_over(1)
            when(z <= 2, lambda: self.got_down(2))
            self.store(1, self.local(1) + up_to_f32(z <= 2, self.downs.at[1]))
            self.down(3).start()

        when(z <= 2, low)
        when(z >= 1, high)

    def done(self):
        z = self.place.z
        self.got_over(0)
        when(z >= 1, lambda: self.got_up(3))
        when(z <= 2, lambda: self.got_down(3))
        when(z == 0, lambda: self.up(1).wait_send())
        when(z == 3, lambda: self.down(1).wait_send())
        when(z <= 1, lambda: self.up(2).wait_send())
        when(z >= 2, lambda: self.down(2).wait_send())
        when(z <= 2, lambda: self.up(3).wait_send())
        when(z >= 1, lambda: self.down(3).wait_send())
        for k in range(4):
            self.across(k).wait_send()

    def total(self):
        z = self.place.z
        return self.local(0) + up_to_f32(z >= 1, self.ups.at[2]) + up_to_f32(z <= 2, self.downs.at[2])


class ReduceZ:
    def __init__(self, place, part, over, ups, downs, send, recv):
        self.place, self.part, self.over, self.ups, self.downs = place, part, over, ups, downs
        self.send, self.recv = send, recv

    def across(self):
        return self.place.copy(self.part.at[0, 1], self.over, self.send.at[0], self.recv.at[0], "y")

    def up(self, s):
        return self.place.copy(self.part.at[s], self.ups.at[s - 1], self.send.at[2 * s - 1], self.recv.at[s], "up")

    def down(self, s):
        return self.place.copy(
            self.part.at[4 - s], self.downs.at[s - 1], self.send.at[2 * s], self.recv.at[3 + s], "down"
        )

    got_up = ReduceY.got_up
    got_down = ReduceY.got_down

    def add(self, k, *more):
        value = self.part[k].astype(f32)
        for term in more:
            value = value + term
        self.part[k] = value.astype(bf16)

    def t1(self):
        z = self.place.z
        when(z == 0, lambda: self.up(1).start())
        when(z == 3, lambda: self.down(1).start())

    def t2(self):
        z = self.place.z

        def low():
            self.got_up(1)
            self.add(2, self.ups[0].astype(f32))

        def high():
            self.got_down(1)
            self.add(2, self.downs[0].astype(f32))

        when(z == 1, low)
        when(z == 2, high)
        when(z <= 1, lambda: self.up(2).start())
        when(z >= 2, lambda: self.down(2).start())

    def t3(self):
        z = self.place.z

        def low():
            self.got_up(2)
            self.add(3, self.ups[1].astype(f32))

        def high():
            self.got_down(2)
            self.add(1, self.downs[1].astype(f32))

        when((z >= 1) & (z <= 2), low)
        when((z >= 1) & (z <= 2), high)
        when(z <= 2, lambda: self.up(3).start())
        when(z >= 1, lambda: self.down(3).start())

    def t4(self):
        z = self.place.z
        when(z >= 1, lambda: self.got_up(3))
        when(z <= 2, lambda: self.got_down(3))
        value = self.part[0, 1].astype(f32)
        value = value + up_to_f32(z >= 1, self.ups.at[2, 1]) + up_to_f32(z <= 2, self.downs.at[2, 1])
        self.part[0, 1] = value.astype(bf16)
        self.across().start()

    def done(self):
        wait_got(self.over, self.send.at[0], self.recv.at[0], self.place)
        z = self.place.z
        when(z == 0, lambda: self.up(1).wait_send())
        when(z == 3, lambda: self.down(1).wait_send())
        when(z <= 1, lambda: self.up(2).wait_send())
        when(z >= 2, lambda: self.down(2).wait_send())
        when(z <= 2, lambda: self.up(3).wait_send())
        when(z >= 1, lambda: self.down(3).wait_send())
        self.across().wait_send()

    def total(self):
        z = self.place.z
        value = self.part[0, 0].astype(f32) + self.over[...].astype(f32)
        return value + up_to_f32(z >= 1, self.ups.at[2, 0]) + up_to_f32(z <= 2, self.downs.at[2, 0])


class FramesSum:
    def __init__(self, place, sent, kept, from_core, from_x, sems, free, number):
        self.place, self.sent, self.kept, self.from_core, self.from_x = place, sent, kept, from_core, from_x
        self.sems, self.free, self.number = sems, free, number

    def core(self, j):
        return self.place.copy(self.sent[j], self.from_core[j], self.sems.at[0, j], self.sems.at[1, j], "core")

    def x(self, j):
        return self.place.copy(self.kept[j].at[1], self.from_x[j], self.sems.at[2, j], self.sems.at[3, j], "x")

    def out(self, j, outs, p):
        return pltpu.make_async_copy(self.kept[j].at[0], outs[j].at[p], self.sems.at[4, j])

    def start(self, later):
        def credit():
            pl.semaphore_wait(self.free.at[2 * self.number], 1)

        when(later, credit)
        for j in range(2):
            self.core(j).start()

    def middle(self, later):
        for j in range(2):
            self.core(j).wait_recv()

        def credit():
            pl.semaphore_wait(self.free.at[2 * self.number + 1], 1)

        when(later, credit)
        for j in range(2):
            kept, got = self.kept[j], self.from_core[j]
            kept[1] = (kept[1].astype(f32) + got[1].astype(f32)).astype(bf16)
            self.x(j).start()
        for j in range(2):
            self.core(j).wait_send()

    def finish(self, outs, p, more):
        for j in range(2):
            self.x(j).wait_recv()
            kept = self.kept[j]
            total = kept[0].astype(f32) + self.from_core[j][0].astype(f32) + self.from_x[j][...].astype(f32)
            kept[0] = total.astype(bf16)
            self.out(j, outs, p).start()

        def credit():
            for k, way in enumerate(("core", "x")):
                pl.semaphore_signal(
                    self.free.at[2 * self.number + k], inc=1, device_id=self.place.device(way), device_id_type=MESH
                )

        when(more, credit)
        for j in range(2):
            self.x(j).wait_send()

    def drained(self, outs, p):
        for j in range(2):
            self.out(j, outs, p).wait()


ATTN_REDUCE = ReduceY
GIN_REDUCE = ReduceY
BACK_REDUCE = ReduceY
FIRST_Y_FIRST = (6,)
COT_Y_FIRST = (1, 4)
FFN_Y_FIRST = (1, 2, 4, 5, 6, 7, 8, 9, 10, 11, 12, 13, 14, 15)
ATT_Y_FIRST = (0, 2, 3, 4, 5, 6, 7, 8, 9, 10, 11, 12, 13, 14)
Z_ROWS = (48, 48, 48, 48, 48, 48, 16, 16, 16, 16, 16, 16, 16, 16, 0, 0)

SCHEDULES = (
    (
        ("AC1", 0), ("RA5", 1), ("RF3", 3), ("A", 0), ("Fm", 3), ("AG4", 4), ("RB3", 5), ("AC4", 1),
        ("RG5", 3), ("AF2", 1), ("AC2", 0), ("RA2", 0), ("C", 2), ("RB4", 5), ("Ef", 5), ("RF4", 3),
        ("RA3", 0), ("AG2", 3), ("E", 4), ("AF3", 1), ("Eg", 4), ("AC5", 1), ("RG2", 2), ("RA4", 0),
        ("Ff", 3), ("RB5", 5), ("Em", 4), ("AC3", 0), ("RG3", 2), ("RF2", 2), ("AG3", 3), ("Cg", 2),
        ("RF5", 3), ("K", 0), ("RG4", 2), ("AF4", 1), ("RB2", 4),
    ),
)
CHANGES = ()


class EitherGather:
    def __init__(self, place, g, send, recv):
        self.along_y = GatherY(place, g, send, recv)
        self.along_z = GatherZ(place, g, send, recv)

    def choose(self, i, y_first):
        self.y_first = i < 0
        for k in y_first:
            self.y_first = self.y_first | (i == k)
        return self

    def both(self, along_y, along_z):
        when(self.y_first, along_y)
        when(jnp.logical_not(self.y_first), along_z)

    def t1(self):
        self.both(self.along_y.t1, self.along_z.t1)

    def t2(self):
        self.both(self.along_y.t2, self.along_z.t2)

    def t3(self):
        self.both(self.along_y.t3, self.along_z.t3)

    def t4(self):
        self.both(self.along_y.t4, self.along_z.t4)

    def done(self):
        self.both(self.along_y.done, self.along_z.done)


class SplitReduce:
    def __init__(self, place, part, over, ups, downs, send, recv):
        self.place, self.part, self.over, self.ups, self.downs = place, part, over, ups, downs
        local = part.shape[2]

        def pair(count):
            first, rest = pl.ds(0, count), pl.ds(count, local - count)
            runs = []
            if count > 0:
                runs.append(
                    ReduceZ(
                        place, part.at[:, :, first], over.at[0, first], ups.at[:, :, first], downs.at[:, :, first],
                        send.at[0], recv.at[0],
                    )
                )
            if count < local:
                runs.append(
                    ReduceY(
                        place, part.at[:, :, rest], over.at[:, rest], ups.at[:, 0, rest], downs.at[:, 0, rest],
                        send.at[1], recv.at[1],
                    )
                )
            return runs

        self.pairs = {count: pair(count * local // 48) for count in sorted(set(Z_ROWS))}

    def choose(self, i):
        self.chosen = {}
        for count in self.pairs:
            chosen = i < 0
            for k in range(len(Z_ROWS)):
                if Z_ROWS[k] == count:
                    chosen = chosen | (i == k)
            self.chosen[count] = chosen
        return self

    def both(self, run):
        for count, pair in self.pairs.items():

            def each(pair=pair):
                for part in pair:
                    run(part)

            when(self.chosen[count], each)

    def t1(self):
        self.both(lambda part: part.t1())

    def t2(self):
        self.both(lambda part: part.t2())

    def t3(self):
        self.both(lambda part: part.t3())

    def t4(self):
        self.both(lambda part: part.t4())

    def done(self):
        self.both(lambda part: part.done())

    def total(self):
        z = self.place.z
        value = self.part[0, 0].astype(f32) + self.over[0].astype(f32)
        return value + up_to_f32(z >= 1, self.ups.at[2, 0]) + up_to_f32(z <= 2, self.downs.at[2, 0])


class GainSum:
    def __init__(self, place, pieces, got, send, recv):
        self.place, self.pieces, self.got, self.send, self.recv = place, pieces, got, send, recv

    def hop(self, k):
        ways = ("core", "x", "y", "pair", "far")
        sources = (self.pieces.at[1], self.pieces.at[0].at[1], self.pieces.at[0].at[0])
        src = sources[min(k, 2)]
        if k == 0:
            dst = self.got.at[pl.ds(0, 2)]
        else:
            dst = self.got.at[k + 1]
        return self.place.copy(src, dst, self.send.at[k], self.recv.at[k], ways[k])

    def start(self):
        self.hop(0).start()

    def next(self, k):
        self.hop(k).wait()
        if k == 0:
            self.pieces[0] = self.pieces[0] + self.got[0:2]
        else:
            self.pieces[0, 0] = self.pieces[0, 0] + self.got[k + 1]
        if k < 4:
            self.hop(k + 1).start()


def layer_kernel(
    x_ref, cot_ref, mask_ref, gains_ref, in_w, out_w, gu_w, dn_w,
    out_hbm, ingrad_hbm, gu_hbm, dn_hbm, iw_hbm, ow_hbm, gain_out, rows_hbm, cot_hbm,
    g_ffn, g_att, cot_v, p_attn, p_gin, p_ffn, p_back,
    over_attn, over_gin, over_ffn, over_back, ups_attn, ups_gin, ups_ffn, ups_back,
    downs_attn, downs_gin, downs_ffn, downs_back,
    q_s, k_s, v_s, mixed_s, dk_s, dv_s, sc, dp,
    gu_v, dn_v, owa_v, owe_v, iw_v, xb,
    act_s, gg_s, gup_s, gmixed_s, gproj_s, hmid_s, ghmid_s, stage, gain_s, gain_pieces, gain_got,
    gu_sent, gu_kept, gu_core, gu_x, dn_sent, dn_kept, dn_core, dn_x,
    iw_sent, iw_kept, iw_core, iw_x, ow_sent, ow_kept, ow_core, ow_x,
    sem_first, sem_first_got, sem_gather, sem_gather_got, sem_reduce, sem_reduce_got, sem_split, sem_split_got,
    sem_grad_ffn, sem_grad_att, sem_gain, sem_local, credits, free,
):
    place = Place()
    z, f = place.z, place.f
    positions, local, depth = x_ref.shape
    rows = ZN * YN * local
    last = positions - 1
    width = q_s.shape[-1]
    hidden = dn_v.shape[0]
    half = rows // 2
    quarter = depth // 4
    mask = mask_ref[...]
    scale = HDIM ** (-0.5)
    pairs_of = positions // 2

    def load(src, dst, number):
        return pltpu.make_async_copy(src, dst, sem_local.at[number])

    def load_owa(p):
        return load(out_w.at[p], owa_v, 0)

    def load_owe(p):
        return load(out_w.at[p], owe_v, 1)

    def load_iw(p, slot):
        return load(in_w.at[p], iw_v.at[slot], 2 + slot)

    def load_gu(p):
        return load(gu_w.at[p], gu_v, 4)

    def load_dn(p):
        return load(dn_w.at[p], dn_v, 5)

    def load_rows(p, dst, number):
        return load(rows_hbm.at[p // 2, :, :, p % 2], dst, number)

    def load_cot(p):
        return load(cot_hbm.at[p // 2, :, :, p % 2], cot_v, 9)

    def own_cot(j):
        return load(g_ffn.at[j // 4, j % 4], cot_hbm.at[j, 0, 0], 16 + j)

    def own_rows(j):
        return load(g_att.at[j // 4, j % 4], rows_hbm.at[j, 0, 0], 16 + pairs_of + j)

    barrier = pltpu.get_barrier_semaphore()

    def greet(way):
        pl.semaphore_signal(barrier, inc=1, device_id=place.device(way), device_id_type=MESH)

    for way in ("y", "core", "x", "far"):
        greet(way)
    when(z < 3, lambda: greet("up"))
    when(z > 0, lambda: greet("down"))
    pl.semaphore_wait(barrier, 4 + (z < 3).astype(jnp.int32) + (z > 0).astype(jnp.int32))

    groups = pairs_of

    def gain_of(which, p):
        return gains_ref[which, pl.ds(p, 1), :]

    def normalise(p, c):
        residual = x_ref[p].astype(f32)
        value = residual * inverse_rms(residual) * gain_of(0, p)
        g_att[p // 8, (p % 8) // 2, p % 2] = value.astype(bf16)
        return c

    def first_kind(g):
        return GatherY if g in FIRST_Y_FIRST else GatherZ

    firsts = [
        first_kind(g)(place, rows_hbm.at[g], sem_first.at[g], sem_first_got.at[g]) for g in range(groups)
    ]

    def cot_gather(j, which):
        sems = sem_gather.at[2, which], sem_gather_got.at[2, which]
        return EitherGather(place, cot_hbm.at[pairs_of - 1 - j], *sems).choose(j, COT_Y_FIRST)

    for g in range(groups):
        lax.fori_loop(2 * g, 2 * g + 2, normalise, 0)
        own_rows(g).start()
        own_rows(g).wait()
        firsts[g].t1()

    def masked(p, c):
        g_ffn[p // 8, (p % 8) // 2, p % 2] = (mask * cot_ref[p].astype(f32)).astype(bf16)
        return c

    lax.fori_loop(0, positions, masked, 0)
    for j in range(pairs_of):
        own_cot(j).start()
    load_owa(last).start()
    load_gu(last).start()
    load_dn(last).start()
    load_iw(0, 0).start()
    dk_s[...] = jnp.zeros_like(dk_s)
    dv_s[...] = jnp.zeros_like(dv_s)

    def project(p, c):
        slot = lax.rem(p, 2)
        load_rows(p, g_ffn.at[slot], 6 + slot).wait()
        load_iw(p, slot).wait()

        @pl.when(p < last)
        def _():
            load_iw(p + 1, 1 - slot).start()

        block = g_ffn[slot].reshape(rows, depth)
        q_s[p] = (dot(block, iw_v[slot, 0], NN).astype(bf16) * scale).astype(bf16)
        k_s[p] = dot(block, iw_v[slot, 1], NN).astype(bf16)
        v_s[p] = dot(block, iw_v[slot, 2], NN).astype(bf16)
        return c

    for g in range(groups):
        firsts[g].t2()
    for g in range(groups):
        firsts[g].t3()
    for g in range(groups):
        firsts[g].t4()
    for j in range(pairs_of):
        own_cot(j).wait()
    for g in range(groups):
        firsts[g].done()
        load_rows(2 * g, g_ffn.at[0], 6).start()
        load_rows(2 * g + 1, g_ffn.at[1], 7).start()
        lax.fori_loop(2 * g, 2 * g + 2, project, 0)
    load_owe(last).start()
    load_iw(last, 0).start()
    load_rows(last, xb, 8).start()

    row = lax.broadcasted_iota(jnp.int32, (2 * width, width), 0)
    column = lax.broadcasted_iota(jnp.int32, (2 * width, width), 1)
    ones = jnp.where((row % width) // HDIM == column // HDIM, 1.0, 0.0).astype(bf16)

    def per_head(product):
        high = product.astype(bf16)
        low = (product - high.astype(f32)).astype(bf16)
        return dot(jnp.concatenate([high, low], axis=1), ones, NN)

    def scores_of(p, q, at):
        def two(jj, top):
            first = per_head(q * k_s[2 * jj, at].astype(f32))
            second = per_head(q * k_s[2 * jj + 1, at].astype(f32))
            second = jnp.where(2 * jj + 1 <= p, second, -1e30)
            sc[2 * jj], sc[2 * jj + 1] = first, second
            return jnp.maximum(top, jnp.maximum(first, second))

        return lax.fori_loop(0, p // 2 + 1, two, jnp.full((half, width), -1e30, f32))

    def attend_one(p):
        pairs = p // 2 + 1
        for part in range(2):
            at = pl.ds(part * half, half)
            q = q_s[p, at].astype(f32)
            top = scores_of(p, q, at)

            def raise_two(jj, total):
                for t in range(2):
                    raised = jnp.exp(sc[2 * jj + t] - top)
                    sc[2 * jj + t] = raised
                    total = total + raised
                return total

            total = lax.fori_loop(0, pairs, raise_two, jnp.zeros((half, width), f32))
            factor = 1.0 / total

            def mix_two(jj, out):
                for t in range(2):
                    probs = (sc[2 * jj + t] * factor).astype(bf16).astype(f32)
                    out = out + probs * v_s[2 * jj + t, at].astype(f32)
                return out

            out = lax.fori_loop(0, pairs, mix_two, jnp.zeros((half, width), f32))
            mixed_s[p, at] = out.astype(bf16)

    def attend_back_one(p):
        pairs = p // 2 + 1
        for part in range(2):
            at = pl.ds(part * half, half)
            q = q_s[p, at].astype(f32)
            g = gmixed_s[at].astype(f32)
            top = scores_of(p, q, at)

            def raise_two(jj, carry):
                total, weighted = carry
                for t in range(2):
                    raised = jnp.exp(sc[2 * jj + t] - top)
                    sc[2 * jj + t] = raised
                    grad_probs = per_head(g * v_s[2 * jj + t, at].astype(f32))
                    dp[2 * jj + t] = grad_probs
                    total = total + raised
                    weighted = weighted + raised * grad_probs
                return total, weighted

            zero = jnp.zeros((half, width), f32)
            total, weighted = lax.fori_loop(0, pairs, raise_two, (zero, zero))
            factor = 1.0 / total
            centre = weighted * factor

            def back_two(jj, dq):
                for t in range(2):
                    j = 2 * jj + t
                    probs = sc[j] * factor
                    grad = (probs * (dp[j] - centre)).astype(bf16).astype(f32)
                    dq = dq + grad * k_s[j, at].astype(f32)
                    dk_s[j, at] = dk_s[j, at] + grad * q
                    dv_s[j, at] = dv_s[j, at] + probs.astype(bf16).astype(f32) * g
                return dq

            dq = lax.fori_loop(0, pairs, back_two, zero)
            gproj_s[0, at] = (dq * scale).astype(bf16)
        gproj_s[1] = dk_s[p].astype(bf16)
        gproj_s[2] = dv_s[p].astype(bf16)

    blocks = (ZN, YN, local, depth)
    grad_ffn = FramesSum(
        place, (gu_sent, dn_sent), (gu_kept, dn_kept), (gu_core, dn_core), (gu_x, dn_x), sem_grad_ffn, free, 0
    )
    grad_att = FramesSum(
        place, (iw_sent, ow_sent), (iw_kept, ow_kept), (iw_core, ow_core), (iw_x, ow_x), sem_grad_att, free, 1
    )
    ffn_outs, att_outs = (gu_hbm, dn_hbm), (iw_hbm, ow_hbm)
    gain_sum = GainSum(place, gain_pieces, gain_got, sem_gain.at[0], sem_gain.at[1])

    def out_copy(p):
        return pltpu.make_async_copy(stage.at[0], out_hbm.at[p], sem_local.at[14])

    def ingrad_copy(p):
        return pltpu.make_async_copy(stage.at[1], ingrad_hbm.at[p], sem_local.at[15])

    class Position:
        def __init__(self, i):
            self.i = i
            self.p = last - i
            self.par = lax.rem(i + 16, 2)
            self.ring = lax.rem(i + 16, 4)

        def gather(self, kind, g, number):
            par = self.par
            return kind(place, g.at[par], sem_gather.at[number, par], sem_gather_got.at[number, par])

        def reduce(self, kind, part, over, ups, downs, number):
            par = self.par
            return kind(
                place, part, over.at[par], ups.at[par], downs.at[par],
                sem_reduce.at[number, par], sem_reduce_got.at[number, par],
            )

        def AF(self):
            return self.gather(EitherGather, g_ffn, 0).choose(self.i, FFN_Y_FIRST)

        def AG(self):
            return self.gather(EitherGather, g_att, 1).choose(self.i, ATT_Y_FIRST)

        def RA(self):
            return self.reduce(ATTN_REDUCE, p_attn, over_attn, ups_attn, downs_attn, 0)

        def RG(self):
            return self.reduce(GIN_REDUCE, p_gin, over_gin, ups_gin, downs_gin, 1)

        def RF(self):
            par = self.par
            return SplitReduce(
                place, p_ffn.at[par], over_ffn.at[par], ups_ffn.at[par], downs_ffn.at[par],
                sem_split.at[par], sem_split_got.at[par],
            ).choose(self.i)

        def RB(self):
            return self.reduce(BACK_REDUCE, p_back.at[self.par], over_back, ups_back, downs_back, 3)

        def do_A(self):
            p = self.p
            attend_one(p)
            load_owa(p).wait()
            p_attn[...] = dot(mixed_s[p], owa_v[...], NN).astype(bf16).reshape(blocks)
            self.RA().t1()
            when(p > 0, lambda: load_owa(p - 1).start())

        def do_RA5(self):
            p, total = self.p, self.RA()
            total.done()
            hmid = x_ref[p].astype(f32) + mask * total.total()
            hmid_s[self.ring] = hmid
            g_ffn[self.par, 0, 0] = (hmid * inverse_rms(hmid) * gain_of(1, p)).astype(bf16)
            self.AF().t1()

        def do_C(self):
            p, par = self.p, self.par
            self.AF().done()
            load_gu(p).wait()
            load_dn(p).wait()
            load_cot(p).wait()
            x = g_ffn[par].reshape(rows, depth)
            g = cot_v[...].reshape(rows, depth)
            for h in range(2):
                at = slice(h * hidden // 2, (h + 1) * hidden // 2)
                gate = dot(x, gu_v[0, :, at], NN)
                up = dot(x, gu_v[1, :, at], NN)
                grad_act = dot(g, dn_v[at], NT)
                sigma = 1.0 / (1.0 + jnp.exp(-gate))
                silu = gate * sigma
                act_s[:, at] = (silu * up).astype(bf16)
                gg_s[:, at] = (grad_act * up * sigma * (1.0 + gate * (1.0 - sigma))).astype(bf16)
                gup_s[:, at] = (grad_act * silu).astype(bf16)
            back = dot(gg_s[...], gu_v[0], NT) + dot(gup_s[...], gu_v[1], NT)
            p_gin[...] = back.astype(bf16).reshape(blocks)
            self.RG().t1()
            gain_s[1, pl.ds(p, 1), :] = jnp.sum(back * x.astype(f32), axis=0, keepdims=True)
            p_ffn[par] = dot(act_s[...], dn_v[...], NN).astype(bf16).reshape(blocks)
            self.RF().t1()

            @pl.when(p > 0)
            def _():
                load_gu(p - 1).start()
                load_dn(p - 1).start()

        def do_Cg(self):
            p, par = self.p, self.par

            @pl.when(p < last)
            def _():
                grad_ffn.drained(ffn_outs, p + 1)

            for r in range(4):
                at = piece_at(r, f, quarter)
                gu_to, dn_to = (gu_kept, dn_kept) if r % 2 == 0 else (gu_sent, dn_sent)
                columns = g_ffn[par, :, :, :, at].reshape(rows, quarter)
                gu_to[r // 2, 0] = dot(columns, gg_s[...], TN).astype(bf16)
                gu_to[r // 2, 1] = dot(columns, gup_s[...], TN).astype(bf16)
                dn_to[r // 2] = dot(act_s[...], cot_v[:, :, :, at].reshape(rows, quarter), TN).astype(bf16)
            grad_ffn.start(p < last)
            when(p > 0, lambda: load_cot(p - 1).start())

        def do_Fm(self):
            grad_ffn.middle(self.p < last)

        def do_Ff(self):
            grad_ffn.finish(ffn_outs, self.p, self.p > 0)

        def do_RG5(self):
            p, total = self.p, self.RG()
            total.done()
            hmid = hmid_s[self.ring]
            factor = inverse_rms(hmid)
            grad = cot_ref[p].astype(f32) + norm_back(total.total(), hmid * factor, factor, gain_of(1, p))
            ghmid_s[self.ring] = grad
            g_att[self.par, 0, 0] = (mask * grad).astype(bf16)
            self.AG().t1()

        def do_RF5(self):
            p, total = self.p, self.RF()
            total.done()

            @pl.when(p < last)
            def _():
                out_copy(p + 1).wait()

            stage[0] = (hmid_s[self.ring] + mask * total.total()).astype(bf16)
            out_copy(p).start()

        def do_E(self):
            p, par = self.p, self.par
            self.AG().done()
            load_owe(p).wait()
            load_iw(p, 0).wait()
            load_rows(p, xb, 8).wait()
            gmixed_s[...] = dot(g_att[par].reshape(rows, depth), owe_v[...], NT).astype(bf16)
            attend_back_one(p)
            back = dot(gproj_s[0], iw_v[0, 0], NT)
            back = back + dot(gproj_s[1], iw_v[0, 1], NT)
            back = back + dot(gproj_s[2], iw_v[0, 2], NT)
            p_back[par] = back.astype(bf16).reshape(blocks)
            self.RB().t1()
            gain_s[0, pl.ds(p, 1), :] = jnp.sum(back * xb[...].reshape(rows, depth).astype(f32), axis=0, keepdims=True)

            @pl.when(p == 0)
            def _():
                for r in range(4):
                    gain_pieces[r % 2, r // 2] = gain_s[:, :, piece_at(r, f, quarter)]
                gain_sum.start()

            @pl.when(p > 0)
            def _():
                load_owe(p - 1).start()
                load_iw(p - 1, 0).start()

        def do_Eg(self):
            p, par = self.p, self.par

            @pl.when(p < last)
            def _():
                grad_att.drained(att_outs, p + 1)

            for r in range(4):
                at = piece_at(r, f, quarter)
                iw_to, ow_to = (iw_kept, ow_kept) if r % 2 == 0 else (iw_sent, ow_sent)
                columns = xb[:, :, :, at].reshape(rows, quarter)
                for j in range(3):
                    iw_to[r // 2, j] = dot(columns, gproj_s[j], TN).astype(bf16)
                ow_to[r // 2] = dot(mixed_s[p], g_att[par, :, :, :, at].reshape(rows, quarter), TN).astype(bf16)
            grad_att.start(p < last)
            when(p > 0, lambda: load_rows(p - 1, xb, 8).start())

        def do_Em(self):
            grad_att.middle(self.p < last)

        def do_Ef(self):
            grad_att.finish(att_outs, self.p, self.p > 0)

        def do_RB5(self):
            p, total = self.p, self.RB()
            total.done()
            when(p == 0, lambda: gain_sum.next(3))

            @pl.when(p < last)
            def _():
                ingrad_copy(p + 1).wait()

            residual = x_ref[p].astype(f32)
            factor = inverse_rms(residual)
            grad = norm_back(total.total(), residual * factor, factor, gain_of(0, p))
            stage[1] = (ghmid_s[self.ring] + grad).astype(bf16)
            ingrad_copy(p).start()

        def do_RB2(self):
            self.RB().t2()
            when(self.p == 0, lambda: gain_sum.next(0))

        def do_RB3(self):
            self.RB().t3()
            when(self.p == 0, lambda: gain_sum.next(1))

        def do_RB4(self):
            self.RB().t4()
            when(self.p == 0, lambda: gain_sum.next(2))

        def runs(self):
            ticks = {}
            for name, event in (
                ("RA", self.RA), ("RG", self.RG), ("RF", self.RF), ("AF", self.AF), ("AG", self.AG),
            ):
                ticks[name + "2"] = lambda event=event: event().t2()
                ticks[name + "3"] = lambda event=event: event().t3()
                ticks[name + "4"] = lambda event=event: event().t4()
            return ticks | {
                "A": self.do_A, "RA5": self.do_RA5, "C": self.do_C, "Cg": self.do_Cg, "Fm": self.do_Fm,
                "Ff": self.do_Ff, "RG5": self.do_RG5, "RF5": self.do_RF5, "E": self.do_E, "Eg": self.do_Eg,
                "Em": self.do_Em, "Ef": self.do_Ef, "RB2": self.do_RB2, "RB3": self.do_RB3, "RB4": self.do_RB4,
                "RB5": self.do_RB5,
            }

    def cot_runs(j):
        event = cot_gather(j, lax.rem(j + 16, 2))

        def done():
            event.done()
            when(j == 0, lambda: load_cot(last).start())

        return {"AC1": event.t1, "AC2": event.t2, "AC3": event.t3, "AC4": event.t4, "AC5": done}

    def tell(number, way):
        pl.semaphore_signal(credits.at[number], inc=1, device_id=place.device(way), device_id_type=MESH)

    def tell_all():
        tell(0, "y")
        when(z < 3, lambda: tell(1, "up"))
        when(z > 0, lambda: tell(2, "down"))

    steps = positions + max(delay for name, delay in SCHEDULES[0] if name[:2] != "AC")
    tell_all()

    def step(low, high, schedule, s, c):
        pl.semaphore_wait(credits.at[0], 1)
        when(z > 0, lambda: pl.semaphore_wait(credits.at[1], 1))
        when(z < 3, lambda: pl.semaphore_wait(credits.at[2], 1))
        for name, delay in schedule:
            if name == "K":
                when(s < steps - 1, tell_all)
            elif high <= delay or low >= delay + (pairs_of if name[:2] == "AC" else positions):
                continue
            elif name[:2] == "AC":
                j = s - delay
                when((j >= 0) & (j < pairs_of), cot_runs(j)[name])
            else:
                when((s >= delay) & (s <= last + delay), Position(s - delay).runs()[name])
        return c

    bounds = (0,) + CHANGES + (steps,)
    for low, high, schedule in zip(bounds, bounds[1:], SCHEDULES):
        lax.fori_loop(low, high, functools.partial(step, low, high, schedule), 0)
    gain_sum.next(4)
    gain_out[...] = gain_pieces[0, 0] / gains_ref[:, :, piece_at(0, f, quarter)]
    grad_ffn.drained(ffn_outs, 0)
    grad_att.drained(att_outs, 0)
    out_copy(0).wait()
    ingrad_copy(0).wait()


def layer(x, cot, mask, gains, in_weight, out_weight, gate_up, down):
    positions, local, depth = x.shape
    width, hidden = out_weight.shape[1], down.shape[1]
    rows = ZN * YN * local
    quarter = depth // 4
    block = (local, depth)
    groups = positions // 2

    def vm(*shape, dtype=bf16):
        return pltpu.VMEM(shape, dtype)

    def hbm(*shape, dtype=bf16):
        return jax.ShapeDtypeStruct(shape, dtype)

    everything = (ZN, YN) + block
    scratch = (
        [vm(2, *everything)] * 2
        + [vm(*everything)] * 3
        + [vm(2, *everything)] * 2
        + [vm(2, ZN, *block)] * 4
        + [vm(2, 3, *block), vm(2, 3, *block), vm(2, 3, YN, *block), vm(2, 3, *block)] * 2
        + [vm(positions, rows, width)] * 4
        + [vm(positions, rows, width, dtype=f32)] * 2
        + [vm(positions, rows // 2, width, dtype=f32)] * 2
        + [vm(2, depth, hidden), vm(hidden, depth), vm(width, depth), vm(width, depth)]
        + [vm(2, 3, depth, width), vm(*everything)]
        + [vm(rows, hidden)] * 3
        + [vm(rows, width), vm(3, rows, width)]
        + [vm(4, *block, dtype=f32)] * 2
        + [vm(2, *block)]
        + [vm(2, positions, depth, dtype=f32)]
        + [vm(2, 2, 2, positions, quarter, dtype=f32), vm(6, 2, positions, quarter, dtype=f32)]
        + [vm(2, 2, quarter, hidden)] * 3
        + [vm(2, quarter, hidden)]
        + [vm(2, hidden, quarter)] * 3
        + [vm(hidden, quarter)]
        + [vm(2, 3, quarter, width)] * 3
        + [vm(3, quarter, width)]
        + [vm(2, width, quarter)] * 3
        + [vm(width, quarter)]
        + [
            pltpu.SemaphoreType.DMA((groups, 10)),
            pltpu.SemaphoreType.DMA((groups, 8)),
            pltpu.SemaphoreType.DMA((3, 2, 10)),
            pltpu.SemaphoreType.DMA((3, 2, 8)),
            pltpu.SemaphoreType.DMA((4, 2, 10)),
            pltpu.SemaphoreType.DMA((4, 2, 11)),
            pltpu.SemaphoreType.DMA((2, 2, 10)),
            pltpu.SemaphoreType.DMA((2, 2, 11)),
            pltpu.SemaphoreType.DMA((5, 2)),
            pltpu.SemaphoreType.DMA((5, 2)),
            pltpu.SemaphoreType.DMA((2, 5)),
            pltpu.SemaphoreType.DMA((16 + positions,)),
            pltpu.SemaphoreType.REGULAR((3,)),
            pltpu.SemaphoreType.REGULAR((4,)),
        ]
    )
    in_vmem = pl.BlockSpec(memory_space=pltpu.VMEM)
    anywhere = pl.BlockSpec(memory_space=pl.ANY)
    return pl.pallas_call(
        layer_kernel,
        in_specs=[in_vmem] * 4 + [anywhere] * 4,
        out_specs=[anywhere] * 6 + [in_vmem, anywhere, anywhere],
        out_shape=[
            hbm(positions, *block),
            hbm(positions, *block),
            hbm(positions, 2, quarter, hidden),
            hbm(positions, hidden, quarter),
            hbm(positions, 3, quarter, width),
            hbm(positions, width, quarter),
            hbm(2, positions, quarter, dtype=f32),
            hbm(positions // 2, ZN, YN, 2, *block),
            hbm(positions // 2, ZN, YN, 2, *block),
        ],
        scratch_shapes=scratch,
        compiler_params=pltpu.CompilerParams(
            collective_id=0, has_side_effects=True, vmem_limit_bytes=KERNEL_VMEM_BYTES
        ),
        name="layer",
    )(x, cot, mask, gains, in_weight, out_weight, gate_up, down)


def widen_kernel(*refs):
    half = len(refs) // 2
    for narrow, wide in zip(refs[:half], refs[half:]):
        wide[...] = narrow[...].astype(f32)


def widened(*arrays):
    def spec(a):
        rank = a.ndim
        return pl.BlockSpec((1,) + a.shape[1:], lambda i: (i,) + (0,) * (rank - 1))

    return pl.pallas_call(
        widen_kernel,
        grid=(arrays[0].shape[0],),
        in_specs=[spec(a) for a in arrays],
        out_specs=[spec(a) for a in arrays],
        out_shape=[jax.ShapeDtypeStruct(a.shape, f32) for a in arrays],
        compiler_params=pltpu.CompilerParams(vmem_limit_bytes=32 * 1024 * 1024),
        name="widen",
    )(*arrays)


def body_in_one(inputs, counts, norm_gains, in_weight, out_weight, gate_up, down_weight, cotangent):
    local = inputs.shape[0]
    ids = lax.axis_index("mp") * local + jnp.arange(local)
    valid = ids < counts[0]
    output, input_grad, g_gu, g_dn, g_in, g_out, gain_sums, _, _ = layer(
        jnp.swapaxes(inputs, 0, 1),
        jnp.swapaxes(cotangent, 0, 1),
        valid.astype(f32)[:, None],
        norm_gains,
        in_weight,
        out_weight,
        gate_up,
        down_weight,
    )
    return (
        jnp.swapaxes(output, 0, 1),
        jnp.swapaxes(input_grad, 0, 1),
        *widened(g_in, g_out, g_gu, g_dn),
        gain_sums,
    )


def solution(mesh):
    placed = (
        P(("frames", "mp"), None, None),
        P("frames"),
        P(),
        P(None, None, None, "mp"),
        P(None, "mp", None),
        P(None, None, None, "mp"),
        P(None, "mp", None),
        P(("frames", "mp"), None, None),
    )
    def local_body(*args):
        frames, group_size = lax.axis_size("frames"), lax.axis_size("mp")
        local, positions, depth = args[0].shape
        width, hidden = args[4].shape[1], args[6].shape[1]
        one = fits(frames, group_size, local, positions, depth, width, hidden)
        return (body_in_one if one else body)(*args)

    return jax.shard_map(
        local_body,
        mesh=mesh,
        in_specs=placed,
        out_specs=(
            P(("frames", "mp"), None, None),
            P(("frames", "mp"), None, None),
            P(None, None, "frames", "mp"),
            P(None, "mp", "frames"),
            P(None, None, "frames", "mp"),
            P(None, "mp", "frames"),
            P(None, None, "frames"),
        ),
        check_vma=False,
    )
```

```python
import functools
import math

import jax
import jax.numpy as jnp
from jax import lax
from jax.experimental import pallas as pl
from jax.experimental.pallas import tpu as pltpu
from jax.sharding import PartitionSpec as P

HDIM = 64
EPSILON = 1e-05
Z_CHIPS = 4
FRAME_BLOCK = 16
CHUNKS = 4
VMEM_BYTES = 56 * 1024 * 1024
KERNEL_VMEM_BYTES = 63 * 1024 * 1024

f32 = jnp.float32
bf16 = jnp.bfloat16


class Line:
    def __init__(self, total, n, stride):
        self.n = n
        self.stride = stride
        self.starts = [i for i in range(total) if (i // stride) % n == 0]

    def up(self, low, high):
        return [(s + i * self.stride, s + (i + 1) * self.stride) for s in self.starts for i in range(low, high)]

    def down(self, low, high):
        return [(s + (i + 1) * self.stride, s + i * self.stride) for s in self.starts for i in range(low, high)]

    def gather(self, own):
        n = self.n
        if n == 1:
            return [own]
        if n == 2:
            return [own, lax.ppermute(own, "mp", self.up(0, 1) + self.down(0, 1))]
        ups, downs = [own], [own]
        for k in range(1, n):
            ups.append(lax.ppermute(ups[-1], "mp", self.up(k - 1, n - 1)))
            downs.append(lax.ppermute(downs[-1], "mp", self.down(0, n - k)))
        return [own] + [ups[k] + downs[n - k] for k in range(1, n)]

    def reduce(self, term):
        n = self.n
        if n == 1:
            return [term(0)]
        if n == 2:
            return [term(0), lax.ppermute(term(1).astype(bf16), "mp", self.up(0, 1) + self.down(0, 1)).astype(f32)]
        up = down = None
        for s in range(1, n):
            send_up = term(s) if up is None else term(s) + up.astype(f32)
            send_down = term(n - s) if down is None else term(n - s) + down.astype(f32)
            up = lax.ppermute(send_up.astype(bf16), "mp", self.up(0, min(s, n - 1)))
            down = lax.ppermute(send_down.astype(bf16), "mp", self.down(n - 1 - s, n - 1))
        return [term(0), up.astype(f32), down.astype(f32)]


class Group:
    def __init__(self, size):
        self.nz = math.gcd(size, Z_CHIPS)
        self.ny = size // self.nz
        self.z = Line(size, self.nz, self.ny)
        self.y = Line(size, self.ny, 1)

    def gather(self, own, z_first):
        if z_first:
            column = jnp.stack(self.z.gather(own), axis=1)
            return jnp.stack(self.y.gather(column), axis=1)
        row = jnp.stack(self.y.gather(own), axis=1)
        return jnp.stack(self.z.gather(row), axis=2)

    def reduce(self, parts, z_first):
        if not z_first:
            if self.ny == 2:
                got = lax.ppermute(parts[1], "mp", self.y.up(0, 1) + self.y.down(0, 1))
                columns = [parts[0], got]

                def term(k):
                    return columns[0][:, k].astype(f32) + columns[1][:, k].astype(f32)

            else:
                terms = self.y.reduce(lambda k: parts[k].astype(f32))

                def term(k):
                    return sum(t[:, k] for t in terms)

            return sum(self.z.reduce(term))

        def row(k):
            return jnp.stack([part[:, k] for part in parts], axis=1).astype(f32)

        terms = self.z.reduce(row)
        return sum(self.y.reduce(lambda k: sum(t[:, k] for t in terms)))


def frames_sum(keep, send, size):
    step = 1
    while True:
        got = lax.ppermute(send, "frames", [(i, i ^ step) for i in range(size)])
        total = keep.astype(f32) + got.astype(f32)
        step *= 2
        if step == size:
            return total[:, 0]
        keep, send = total[:, 0::2], total[:, 1::2].astype(send.dtype)


def dot(a, b, dims):
    return lax.dot_general(a, b, (dims, ((), ())), preferred_element_type=f32)


NN = ((1,), (0,))
NT = ((1,), (1,))
TN = ((0,), (0,))


def params():
    return pltpu.CompilerParams(vmem_limit_bytes=VMEM_BYTES)


def cost(flops, nbytes):
    return pl.CostEstimate(flops=int(flops), bytes_accessed=int(nbytes), transcendentals=0)


def qkv_kernel(x_ref, w_ref, q_ref, k_ref, v_ref):
    x = x_ref[0]
    for c, out in enumerate((q_ref, k_ref, v_ref)):
        out[0] = dot(x, w_ref[0, c], NN).astype(bf16)


def qkv(x, weight, base):
    count, rows, depth = x.shape
    width = weight.shape[-1]
    out = jax.ShapeDtypeStruct((count, rows, width), bf16)
    return pl.pallas_call(
        qkv_kernel,
        grid=(count,),
        in_specs=[
            pl.BlockSpec((1, rows, depth), lambda i: (i, 0, 0)),
            pl.BlockSpec((1, 3, depth, width), lambda i: (base + i, 0, 0, 0)),
        ],
        out_specs=[pl.BlockSpec((1, rows, width), lambda i: (i, 0, 0))] * 3,
        out_shape=[out] * 3,
        compiler_params=params(),
        cost_estimate=cost(6 * count * rows * depth * width, 2 * count * depth * (rows + 3 * width)),
        name="qkv",
    )(x, weight)


def head_masks(rows, width):
    lane = lax.broadcasted_iota(jnp.int32, (rows, width), 1)
    return [(lane >= h * HDIM) & (lane < (h + 1) * HDIM) for h in range(width // HDIM)]


def attention_mask(count, base, columns):
    rows = count * FRAME_BLOCK
    row = lax.broadcasted_iota(jnp.int32, (rows, columns), 0)
    column = lax.broadcasted_iota(jnp.int32, (rows, columns), 1)
    same = (row % FRAME_BLOCK) == (column % FRAME_BLOCK)
    return same & (column // FRAME_BLOCK <= row // FRAME_BLOCK + base)


def block_of(refs, rows):
    pieces = [ref[:, rows, :] for ref in refs]
    pieces = [p.reshape(p.shape[0] * p.shape[1], p.shape[2]) for p in pieces]
    return pieces[0] if len(pieces) == 1 else jnp.concatenate(pieces, axis=0)


def softmax(scores):
    top = jnp.max(scores, axis=-1, keepdims=True)
    raised = jnp.exp(scores - top)
    return raised / jnp.sum(raised, axis=-1, keepdims=True)


def pick(masks, values):
    out = values[0]
    for mask, value in zip(masks[1:], values[1:]):
        out = jnp.where(mask, value, out)
    return out


def attend_kernel(base, n_kv, ny, q_ref, *refs):
    k_refs, v_refs = refs[:n_kv], refs[n_kv : 2 * n_kv]
    w_ref = refs[2 * n_kv]
    mixed_ref = refs[2 * n_kv + 1]
    part_refs = refs[2 * n_kv + 2 :]
    count, rows, width = q_ref.shape
    columns = sum(ref.shape[0] for ref in k_refs) * FRAME_BLOCK
    step = pl.program_id(0)

    @pl.when(step == 0)
    def _():
        heads = head_masks(count * FRAME_BLOCK, width)
        allowed = attention_mask(count, base, columns)

        def one(b):
            at = pl.ds(pl.multiple_of(b * FRAME_BLOCK, FRAME_BLOCK), FRAME_BLOCK)
            queries = block_of([q_ref], at) * HDIM ** (-0.5)
            keys, values = block_of(k_refs, at), block_of(v_refs, at)
            outs = []
            for head in heads:
                mine = jnp.where(head, queries, jnp.zeros_like(queries))
                scores = jnp.where(allowed, dot(mine, keys, NT), -1e30)
                outs.append(dot(softmax(scores).astype(bf16), values, NN))
            mixed_ref[:, at, :] = pick(heads, outs).astype(bf16).reshape(count, FRAME_BLOCK, width)

        lax.fori_loop(0, rows // FRAME_BLOCK, lambda b, c: (one(b), c)[1], 0, unroll=4)

    out = dot(mixed_ref[step], w_ref[0], NN)
    span = rows // ny
    for y, part in enumerate(part_refs):
        part[0] = out[y * span : (y + 1) * span].astype(bf16)


def attend(q, ks, vs, weight, base, ny):
    count, rows, width = q.shape
    depth = weight.shape[-1]
    whole = pl.BlockSpec((count, rows, width), lambda i: (0, 0, 0))
    part = jax.ShapeDtypeStruct((count, rows // ny, depth), bf16)
    n_kv = len(ks)
    return pl.pallas_call(
        functools.partial(attend_kernel, base, n_kv, ny),
        grid=(count,),
        in_specs=[whole] * (1 + 2 * n_kv) + [pl.BlockSpec((1, width, depth), lambda i: (base + i, 0, 0))],
        out_specs=[whole] + [pl.BlockSpec((1, rows // ny, depth), lambda i: (i, 0, 0))] * ny,
        out_shape=[jax.ShapeDtypeStruct(q.shape, bf16)] + [part] * ny,
        compiler_params=params(),
        cost_estimate=cost(4 * count * rows * depth * width, 2 * count * rows * (depth + (2 + 2 * n_kv) * width)),
        name="attend",
    )(q, *ks, *vs, weight)


def gradient_pieces(size, depth):
    return size if size > 1 and (depth // size) % 128 == 0 else 1


def piece_at(piece, mine, span):
    return pl.ds(pl.multiple_of((piece ^ mine) * span, span), span)


def ffn_kernel(ny, pieces, mine_ref, x_ref, g_ref, gu_ref, dn_ref, *refs):
    outs, backs = refs[:ny], refs[ny : 2 * ny]
    gain_ref = refs[2 * ny]
    grads = refs[2 * ny + 1 :]
    rows, depth = x_ref.shape[1:]
    span = rows // ny
    x, g = x_ref[0], g_ref[0]
    gate = dot(x, gu_ref[0, 0], NN)
    up = dot(x, gu_ref[0, 1], NN)
    grad_act = dot(g, dn_ref[0], NT)
    sigma = 1.0 / (1.0 + jnp.exp(-gate))
    silu = gate * sigma
    act = (silu * up).astype(bf16)
    grad_gate = (grad_act * up * sigma * (1.0 + gate * (1.0 - sigma))).astype(bf16)
    grad_up = (grad_act * silu).astype(bf16)
    out = dot(act, dn_ref[0], NN)
    for y in range(ny):
        outs[y][0] = out[y * span : (y + 1) * span].astype(bf16)
    back = dot(grad_gate, gu_ref[0, 0], NT) + dot(grad_up, gu_ref[0, 1], NT)
    for y in range(ny):
        backs[y][0] = back[y * span : (y + 1) * span].astype(bf16)
    gain_ref[0] = jnp.sum(back * x.astype(f32), axis=0, keepdims=True)
    if pieces == 1:
        grads[0][0, 0] = dot(x, grad_gate, TN).astype(bf16)
        grads[0][0, 1] = dot(x, grad_up, TN).astype(bf16)
        grads[1][0] = dot(act, g, TN).astype(bf16)
        return
    mine = mine_ref[0]
    width = depth // pieces
    for r in range(pieces):
        at = piece_at(r, mine, width)
        gu_out, dn_out = grads[r % 2], grads[2 + r % 2]
        columns = x_ref[0, :, at]
        gu_out[0, r // 2, 0] = dot(columns, grad_gate, TN).astype(bf16)
        gu_out[0, r // 2, 1] = dot(columns, grad_up, TN).astype(bf16)
        dn_out[0, r // 2] = dot(act, g_ref[0, :, at], TN).astype(bf16)


def split_specs(shape, pieces, axis):
    if pieces == 1:
        block = (1,) + shape[1:]
        return [pl.BlockSpec(block, lambda i: (i,) + (0,) * (len(block) - 1))], [jax.ShapeDtypeStruct(shape, bf16)]
    rest = list(shape[1:])
    rest[axis - 1] //= pieces
    block = (1, pieces // 2) + tuple(rest)
    spec = pl.BlockSpec(block, lambda i: (i,) + (0,) * (len(block) - 1))
    return [spec] * 2, [jax.ShapeDtypeStruct((shape[0],) + block[1:], bf16)] * 2


def ffn(x, g, gate_up, down, base, ny, frames, mine):
    count, rows, depth = x.shape
    width = down.shape[1]
    pieces = gradient_pieces(frames, depth)
    part = jax.ShapeDtypeStruct((count, rows // ny, depth), bf16)
    part_spec = pl.BlockSpec((1, rows // ny, depth), lambda i: (i, 0, 0))
    row_spec = pl.BlockSpec((1, rows, depth), lambda i: (i, 0, 0))
    gu_specs, gu_shapes = split_specs((count, 2, depth, width), pieces, 2)
    dn_specs, dn_shapes = split_specs((count, width, depth), pieces, 2)
    out = pl.pallas_call(
        functools.partial(ffn_kernel, ny, pieces),
        grid=(count,),
        in_specs=[
            pl.BlockSpec(memory_space=pltpu.SMEM),
            row_spec,
            row_spec,
            pl.BlockSpec((1, 2, depth, width), lambda i: (base + i, 0, 0, 0)),
            pl.BlockSpec((1, width, depth), lambda i: (base + i, 0, 0)),
        ],
        out_specs=[part_spec] * (2 * ny) + [pl.BlockSpec((1, 1, depth), lambda i: (i, 0, 0))] + gu_specs + dn_specs,
        out_shape=[part] * (2 * ny) + [jax.ShapeDtypeStruct((count, 1, depth), f32)] + gu_shapes + dn_shapes,
        compiler_params=params(),
        cost_estimate=cost(18 * count * rows * depth * width, 2 * count * depth * (4 * rows + 6 * width)),
        name="ffn",
    )(mine, x, g, gate_up, down)
    n = len(gu_specs)
    return out[:ny], out[ny : 2 * ny], out[2 * ny], out[2 * ny + 1 : 2 * ny + 1 + n], out[2 * ny + 1 + n :]


def attend_back_kernel(base, n_kv, first, ny, pieces, mine_ref, ga_ref, gp_ref, x_ref, q_ref, *refs):
    refs = list(refs)

    def take(n):
        got = refs[:n]
        del refs[:n]
        return got

    k_refs, v_refs = take(n_kv), take(n_kv)
    (mixed_ref, ow_all_ref, iw_ref) = take(3)
    dk_in = dv_in = ()
    if not first:
        dk_in, dv_in = take(n_kv), take(n_kv)
    part_refs = take(ny)
    (gain_ref,) = take(1)
    n_out = 1 if pieces == 1 else 2
    iw_grads, ow_grads = take(n_out), take(n_out)
    dk_out, dv_out = take(n_kv - 1), take(n_kv - 1)
    gmixed_ref, gproj_ref = take(2)
    count, rows, width = q_ref.shape
    columns = n_kv * count * FRAME_BLOCK
    block = count * FRAME_BLOCK
    step = pl.program_id(0)

    @pl.when(step == 0)
    def _():
        for p in range(count):
            gmixed_ref[p] = dot(ga_ref[p], ow_all_ref[p], NT).astype(bf16)
        heads = head_masks(block, width)
        allowed = attention_mask(count, base, columns)
        factor = HDIM ** (-0.5)

        def one(b):
            at = pl.ds(pl.multiple_of(b * FRAME_BLOCK, FRAME_BLOCK), FRAME_BLOCK)
            queries = block_of([q_ref], at) * factor
            grad_mixed = block_of([gmixed_ref], at)
            keys, values = block_of(k_refs, at), block_of(v_refs, at)
            dqs, dk, dv = [], None, None
            for head in heads:
                my_q = jnp.where(head, queries, jnp.zeros_like(queries))
                my_g = jnp.where(head, grad_mixed, jnp.zeros_like(grad_mixed))
                probs = softmax(jnp.where(allowed, dot(my_q, keys, NT), -1e30))
                grad_probs = dot(my_g, values, NT)
                weighted = probs * grad_probs
                grad_scores = (weighted - probs * jnp.sum(weighted, axis=-1, keepdims=True)).astype(bf16)
                dqs.append(dot(grad_scores, keys, NN))
                more_k = dot(grad_scores, my_q, TN)
                more_v = dot(probs.astype(bf16), my_g, TN)
                dk = more_k if dk is None else dk + more_k
                dv = more_v if dv is None else dv + more_v
            gproj_ref[:, 0, at, :] = (pick(heads, dqs) * factor).astype(bf16).reshape(count, FRAME_BLOCK, width)
            for c, total, earlier, later in ((1, dk, dk_in, dk_out), (2, dv, dv_in, dv_out)):
                for j in range(n_kv):
                    piece = total[j * block : (j + 1) * block].reshape(count, FRAME_BLOCK, width)
                    if not first:
                        piece = piece + earlier[j][:, at, :]
                    if j < n_kv - 1:
                        later[j][:, at, :] = piece
                    else:
                        gproj_ref[:, c, at, :] = piece.astype(bf16)

        lax.fori_loop(0, rows // FRAME_BLOCK, lambda b, c: (one(b), c)[1], 0, unroll=2)

    grads = [gproj_ref[step, c] for c in range(3)]
    back = dot(grads[0], iw_ref[0, 0], NT) + dot(grads[1], iw_ref[0, 1], NT) + dot(grads[2], iw_ref[0, 2], NT)
    span = rows // ny
    for y, part in enumerate(part_refs):
        part[0] = back[y * span : (y + 1) * span].astype(bf16)
    gain_ref[0] = jnp.sum(back * x_ref[0].astype(f32), axis=0, keepdims=True)
    mixed = mixed_ref[0]
    if pieces == 1:
        for c in range(3):
            iw_grads[0][0, c] = dot(x_ref[0], grads[c], TN).astype(bf16)
        ow_grads[0][0] = dot(mixed, gp_ref[0], TN).astype(bf16)
        return
    mine = mine_ref[0]
    depth = x_ref.shape[2]
    for r in range(pieces):
        at = piece_at(r, mine, depth // pieces)
        columns = x_ref[0, :, at]
        for c in range(3):
            iw_grads[r % 2][0, r // 2, c] = dot(columns, grads[c], TN).astype(bf16)
        ow_grads[r % 2][0, r // 2] = dot(mixed, gp_ref[0, :, at], TN).astype(bf16)


def attend_back(grad_rows, x, q, ks, vs, mixed, out_weight, in_weight, dks, dvs, base, ny, frames, mine):
    count, rows, depth = x.shape
    width = q.shape[-1]
    pieces = gradient_pieces(frames, depth)
    n_kv = len(ks)
    first = not dks
    whole = pl.BlockSpec((count, rows, width), lambda i: (0, 0, 0))
    row_spec = pl.BlockSpec((1, rows, depth), lambda i: (i, 0, 0))
    chunk = base // count
    part = jax.ShapeDtypeStruct((count, rows // ny, depth), bf16)
    part_spec = pl.BlockSpec((1, rows // ny, depth), lambda i: (i, 0, 0))
    iw_specs, iw_shapes = split_specs((count, 3, depth, width), pieces, 2)
    ow_specs, ow_shapes = split_specs((count, width, depth), pieces, 2)
    total = jax.ShapeDtypeStruct((count, rows, width), f32)
    out = pl.pallas_call(
        functools.partial(attend_back_kernel, base, n_kv, first, ny, pieces),
        grid=(count,),
        in_specs=[
            pl.BlockSpec(memory_space=pltpu.SMEM),
            pl.BlockSpec((count, rows, depth), lambda i: (0, 0, 0)),
            row_spec,
            row_spec,
        ]
        + [whole] * (1 + 2 * n_kv)
        + [
            pl.BlockSpec((1, rows, width), lambda i: (i, 0, 0)),
            pl.BlockSpec((count, width, depth), lambda i: (chunk, 0, 0)),
            pl.BlockSpec((1, 3, depth, width), lambda i: (base + i, 0, 0, 0)),
        ]
        + [whole] * (len(dks) + len(dvs)),
        out_specs=[part_spec] * ny
        + [pl.BlockSpec((1, 1, depth), lambda i: (i, 0, 0))]
        + iw_specs
        + ow_specs
        + [whole] * (2 * (n_kv - 1)),
        out_shape=[part] * ny
        + [jax.ShapeDtypeStruct((count, 1, depth), f32)]
        + iw_shapes
        + ow_shapes
        + [total] * (2 * (n_kv - 1)),
        scratch_shapes=[pltpu.VMEM((count, rows, width), bf16), pltpu.VMEM((count, 3, rows, width), bf16)],
        compiler_params=params(),
        cost_estimate=cost(16 * count * rows * depth * width, 2 * count * rows * (4 * depth + 8 * n_kv * width)),
        name="attend_back",
    )(mine, grad_rows, grad_rows, x, q, *ks, *vs, mixed, out_weight, in_weight, *dks, *dvs)
    out = list(out)
    n = len(iw_specs)
    parts, gain = out[:ny], out[ny]
    iw, ow = out[ny + 1 : ny + 1 + n], out[ny + 1 + n : ny + 1 + 2 * n]
    rest = out[ny + 1 + 2 * n :]
    return parts, gain, iw, ow, rest[: n_kv - 1], rest[n_kv - 1 :]


def inverse_rms(values):
    return lax.rsqrt(jnp.mean(values * values, axis=-1, keepdims=True) + EPSILON)


def norm_back(grad_normed, normed, factor, gain):
    scaled = grad_normed * gain
    return factor * (scaled - normed * jnp.mean(scaled * normed, axis=-1, keepdims=True))


def body(inputs, counts, norm_gains, in_weight, out_weight, gate_up, down_weight, cotangent):
    frames, group_size = lax.axis_size("frames"), lax.axis_size("mp")
    group = Group(group_size)
    ny, nz = group.ny, group.nz
    local, positions, depth = inputs.shape
    rows = local * group_size
    size = positions // CHUNKS
    ids = lax.axis_index("mp") * local + jnp.arange(local)
    mask = (ids < counts[0]).astype(f32)[None, :, None]
    mine = lax.axis_index("frames").astype(jnp.int32)[None]
    x_major = jnp.swapaxes(inputs, 0, 1)
    g_major = jnp.swapaxes(cotangent, 0, 1)
    gains = norm_gains[:, :, None, :]

    def at(c):
        return slice(c * size, (c + 1) * size)

    def gathered(own, z_first):
        return group.gather(own, z_first).reshape(size, rows, depth)

    def reduced(parts, z_first):
        return group.reduce([p.reshape(size, nz, local, depth) for p in parts], z_first)

    def summed(grads):
        if len(grads) == 1:
            return lax.psum_scatter(grads[0], "frames", scatter_dimension=grads[0].ndim - 1, tiled=True).astype(f32)
        return frames_sum(grads[0], grads[1], frames)

    def summed_middle(grads):
        if len(grads) == 1:
            return lax.psum_scatter(grads[0], "frames", scatter_dimension=2, tiled=True).astype(f32)
        return frames_sum(grads[0], grads[1], frames)

    order = list(range(CHUNKS))[::-1]
    attn_in, qs, ks, vs = {}, {}, {}, {}
    for c in order:
        residual = x_major[at(c)].astype(f32)
        own = (residual * inverse_rms(residual) * gains[0, at(c)]).astype(bf16)
        attn_in[c] = gathered(own, True)
        qs[c], ks[c], vs[c] = qkv(attn_in[c], in_weight, c * size)

    outputs, input_grads = {}, {}
    g_in, g_out, g_gu, g_dn, gain_terms = {}, {}, {}, {}, {}
    dks, dvs = [], []
    for c in order:
        base = c * size
        gain_first, gain_second = gains[0, at(c)], gains[1, at(c)]
        residual = x_major[at(c)].astype(f32)
        gy = g_major[at(c)].astype(f32)
        grad_rows = gathered((mask * gy).astype(bf16), c % 2 == 0)
        earlier_k, earlier_v = [ks[j] for j in range(c + 1)], [vs[j] for j in range(c + 1)]
        mixed, *parts = attend(qs[c], earlier_k, earlier_v, out_weight, base, ny)
        hmid = residual + mask * reduced(parts, False)
        scale_second = inverse_rms(hmid)
        normed_second = hmid * scale_second
        ffn_rows = gathered((normed_second * gain_second).astype(bf16), True)
        out_parts, back_parts, gain_back, grad_gu, grad_dn = ffn(
            ffn_rows, grad_rows, gate_up, down_weight, base, ny, frames, mine
        )
        grad_ffn_in = reduced(back_parts, False)
        grad_mid = gy + norm_back(grad_ffn_in, normed_second, scale_second, gain_second)
        grad_attn = gathered((mask * grad_mid).astype(bf16), True)
        outputs[c] = (hmid + mask * reduced(out_parts, True)).astype(bf16)
        back, gain_front, grad_iw, grad_ow, dks, dvs = attend_back(
            grad_attn, attn_in[c], qs[c], earlier_k, earlier_v, mixed, out_weight, in_weight,
            dks, dvs, base, ny, frames, mine,
        )
        grad_attn_in = reduced(back, c % 2 == 1)
        scale_first = inverse_rms(residual)
        input_grads[c] = (
            grad_mid + norm_back(grad_attn_in, residual * scale_first, scale_first, gain_first)
        ).astype(bf16)
        gain_terms[c] = jnp.stack([gain_front[:, 0] / norm_gains[0, at(c)], gain_back[:, 0] / norm_gains[1, at(c)]])
        g_gu[c], g_dn[c] = summed_middle(grad_gu), summed(grad_dn)
        g_in[c], g_out[c] = summed_middle(grad_iw), summed(grad_ow)

    def joined(pieces, axis=0):
        return jnp.concatenate([pieces[c] for c in range(CHUNKS)], axis=axis)

    terms = lax.psum_scatter(joined(gain_terms, 1), "frames", scatter_dimension=2, tiled=True)
    step = 1
    while step < group_size:
        terms = terms + lax.ppermute(terms, "mp", [(i, i ^ step) for i in range(group_size)])
        step *= 2
    return (
        jnp.swapaxes(joined(outputs), 0, 1),
        jnp.swapaxes(joined(input_grads), 0, 1),
        joined(g_in),
        joined(g_out),
        joined(g_gu),
        joined(g_dn),
        terms,
    )


MESH = pl.DeviceIdType.MESH
ZN, YN = 4, 2


def fits(frames, group_size, local, positions, depth, width, hidden):
    return (
        frames == 4
        and group_size == ZN * YN
        and local == 48
        and positions == 16
        and width % 128 == 0
        and (depth // frames) % 128 == 0
        and hidden % 128 == 0
    )


class Place:
    def __init__(self):
        self.m = lax.axis_index("mp")
        self.f = lax.axis_index("frames")
        self.z = self.m // YN
        self.ids = {
            "y": ("mp", self.m ^ 1),
            "up": ("mp", self.m + YN),
            "down": ("mp", self.m - YN),
            "core": ("frames", self.f ^ 1),
            "x": ("frames", self.f ^ 2),
            "pair": ("mp", self.m ^ YN),
            "far": ("mp", self.m ^ (2 * YN)),
        }

    def device(self, way):
        axis, index = self.ids[way]
        return {axis: index}

    def copy(self, src, dst, send, recv, way):
        return pltpu.make_async_remote_copy(
            src_ref=src, dst_ref=dst, send_sem=send, recv_sem=recv, device_id=self.device(way), device_id_type=MESH
        )


def when(condition, run):
    pl.when(condition)(run)


def wait_got(dst, send, recv, place):
    place.copy(dst, dst, send, recv, "y").wait_recv()


class GatherZ:
    def __init__(self, place, g, send, recv):
        self.place, self.g, self.send, self.recv = place, g, send, recv

    def site(self, number, way, src, dst):
        return self.place.copy(
            self.g.at[src[0], src[1]],
            self.g.at[dst[0], dst[1]],
            self.send.at[number],
            self.recv.at[dst[0] * 2 + dst[1]],
            way,
        )

    def up(self, k):
        return self.site(k - 1, "up", (k - 1, 0), (k, 0))

    def down(self, k):
        return self.site(2 + k, "down", ((5 - k) % 4, 0), (4 - k, 0))

    def across(self, k):
        return self.site(6 + k, "y", (k, 0), (k, 1))

    def got(self, k, y):
        wait_got(self.g.at[k, y], self.send.at[0], self.recv.at[k * 2 + y], self.place)

    def t1(self):
        z = self.place.z
        when(z < 3, lambda: self.up(1).start())
        when(z > 0, lambda: self.down(1).start())
        self.across(0).start()

    def t2(self):
        z = self.place.z

        def low():
            self.got(1, 0)
            when(z < 3, lambda: self.up(2).start())
            self.across(1).start()

        def high():
            self.got(3, 0)
            when(z > 0, lambda: self.down(2).start())
            self.across(3).start()

        when(z >= 1, low)
        when(z <= 2, high)

    def t3(self):
        z = self.place.z
        self.got(2, 0)
        when(z == 2, lambda: self.up(3).start())
        when(z == 1, lambda: self.down(3).start())
        self.across(2).start()

    def t4(self):
        z = self.place.z

        def bottom():
            self.got(1, 0)
            self.across(1).start()

        def top():
            self.got(3, 0)
            self.across(3).start()

        when(z == 0, bottom)
        when(z == 3, top)

    def done(self):
        z = self.place.z
        for k in range(4):
            self.got(k, 1)
        when(z < 3, lambda: self.up(1).wait_send())
        when(z > 0, lambda: self.down(1).wait_send())
        when((z >= 1) & (z < 3), lambda: self.up(2).wait_send())
        when((z >= 1) & (z < 3), lambda: self.down(2).wait_send())
        when(z == 2, lambda: self.up(3).wait_send())
        when(z == 1, lambda: self.down(3).wait_send())
        for k in range(4):
            self.across(k).wait_send()


class GatherY:
    def __init__(self, place, g, send, recv):
        self.place, self.g, self.send, self.recv = place, g, send, recv

    def site(self, number, way, src, dst):
        return self.place.copy(self.g.at[src], self.g.at[dst], self.send.at[number], self.recv.at[dst], way)

    def up(self, k):
        return self.site(k - 1, "up", k - 1, k)

    def down(self, k):
        return self.site(2 + k, "down", (5 - k) % 4, 4 - k)

    def across(self):
        return self.place.copy(self.g.at[0, 0], self.g.at[0, 1], self.send.at[6], self.recv.at[4], "y")

    def got(self, k):
        wait_got(self.g.at[k], self.send.at[0], self.recv.at[k], self.place)

    def t1(self):
        self.across().start()

    def t2(self):
        z = self.place.z
        wait_got(self.g.at[0, 1], self.send.at[0], self.recv.at[4], self.place)
        when(z < 3, lambda: self.up(1).start())
        when(z > 0, lambda: self.down(1).start())

    def t3(self):
        z = self.place.z

        def low():
            self.got(1)
            when(z < 3, lambda: self.up(2).start())

        def high():
            self.got(3)
            when(z > 0, lambda: self.down(2).start())

        when(z >= 1, low)
        when(z <= 2, high)

    def t4(self):
        z = self.place.z
        self.got(2)
        when(z == 2, lambda: self.up(3).start())
        when(z == 1, lambda: self.down(3).start())

    def done(self):
        z = self.place.z
        when(z == 0, lambda: self.got(1))
        when(z == 3, lambda: self.got(3))
        when(z < 3, lambda: self.up(1).wait_send())
        when(z > 0, lambda: self.down(1).wait_send())
        when((z >= 1) & (z < 3), lambda: self.up(2).wait_send())
        when((z >= 1) & (z < 3), lambda: self.down(2).wait_send())
        when(z == 2, lambda: self.up(3).wait_send())
        when(z == 1, lambda: self.down(3).wait_send())
        self.across().wait_send()


def up_to_f32(condition, ref):
    return jnp.where(condition, ref[...].astype(f32), 0.0)


class ReduceY:
    def __init__(self, place, part, over, ups, downs, send, recv):
        self.place, self.part, self.over, self.ups, self.downs = place, part, over, ups, downs
        self.send, self.recv = send, recv

    def across(self, k):
        return self.place.copy(self.part.at[k, 1], self.over.at[k], self.send.at[6 + k], self.recv.at[7 + k], "y")

    def up(self, s):
        return self.place.copy(
            self.part.at[s, 0], self.ups.at[s - 1], self.send.at[2 * s - 2], self.recv.at[s], "up"
        )

    def down(self, s):
        return self.place.copy(
            self.part.at[4 - s, 0], self.downs.at[s - 1], self.send.at[2 * s - 1], self.recv.at[3 + s], "down"
        )

    def got_over(self, k):
        wait_got(self.over.at[k], self.send.at[0], self.recv.at[7 + k], self.place)

    def got_up(self, s):
        wait_got(self.ups.at[s - 1], self.send.at[0], self.recv.at[s], self.place)

    def got_down(self, s):
        wait_got(self.downs.at[s - 1], self.send.at[0], self.recv.at[3 + s], self.place)

    def local(self, k):
        return self.part[k, 0].astype(f32) + self.over[k].astype(f32)

    def store(self, k, value):
        self.part[k, 0] = value.astype(bf16)

    def t1(self):
        for k in (1, 3, 2, 0):
            self.across(k).start()

    def t2(self):
        z = self.place.z

        def bottom():
            self.got_over(1)
            self.store(1, self.local(1))
            self.up(1).start()

        def top():
            self.got_over(3)
            self.store(3, self.local(3))
            self.down(1).start()

        when(z == 0, bottom)
        when(z == 3, top)

    def t3(self):
        z = self.place.z
        self.got_over(2)
        when(z == 1, lambda: self.got_up(1))
        when(z == 2, lambda: self.got_down(1))
        self.store(
            2, self.local(2) + up_to_f32(z == 1, self.ups.at[0]) + up_to_f32(z == 2, self.downs.at[0])
        )
        when(z <= 1, lambda: self.up(2).start())
        when(z >= 2, lambda: self.down(2).start())

    def t4(self):
        z = self.place.z

        def low():
            self.got_over(3)
            when(z >= 1, lambda: self.got_up(2))
            self.store(3, self.local(3) + up_to_f32(z >= 1, self.ups.at[1]))
            self.up(3).start()

        def high():
            self.got_over(1)
            when(z <= 2, lambda: self.got_down(2))
            self.store(1, self.local(1) + up_to_f32(z <= 2, self.downs.at[1]))
            self.down(3).start()

        when(z <= 2, low)
        when(z >= 1, high)

    def done(self):
        z = self.place.z
        self.got_over(0)
        when(z >= 1, lambda: self.got_up(3))
        when(z <= 2, lambda: self.got_down(3))
        when(z == 0, lambda: self.up(1).wait_send())
        when(z == 3, lambda: self.down(1).wait_send())
        when(z <= 1, lambda: self.up(2).wait_send())
        when(z >= 2, lambda: self.down(2).wait_send())
        when(z <= 2, lambda: self.up(3).wait_send())
        when(z >= 1, lambda: self.down(3).wait_send())
        for k in range(4):
            self.across(k).wait_send()

    def total(self):
        z = self.place.z
        return self.local(0) + up_to_f32(z >= 1, self.ups.at[2]) + up_to_f32(z <= 2, self.downs.at[2])


class ReduceZ:
    def __init__(self, place, part, over, ups, downs, send, recv):
        self.place, self.part, self.over, self.ups, self.downs = place, part, over, ups, downs
        self.send, self.recv = send, recv

    def across(self):
        return self.place.copy(self.part.at[0, 1], self.over, self.send.at[0], self.recv.at[0], "y")

    def up(self, s):
        return self.place.copy(self.part.at[s], self.ups.at[s - 1], self.send.at[2 * s - 1], self.recv.at[s], "up")

    def down(self, s):
        return self.place.copy(
            self.part.at[4 - s], self.downs.at[s - 1], self.send.at[2 * s], self.recv.at[3 + s], "down"
        )

    got_up = ReduceY.got_up
    got_down = ReduceY.got_down

    def add(self, k, *more):
        value = self.part[k].astype(f32)
        for term in more:
            value = value + term
        self.part[k] = value.astype(bf16)

    def t1(self):
        z = self.place.z
        when(z == 0, lambda: self.up(1).start())
        when(z == 3, lambda: self.down(1).start())

    def t2(self):
        z = self.place.z

        def low():
            self.got_up(1)
            self.add(2, self.ups[0].astype(f32))

        def high():
            self.got_down(1)
            self.add(2, self.downs[0].astype(f32))

        when(z == 1, low)
        when(z == 2, high)
        when(z <= 1, lambda: self.up(2).start())
        when(z >= 2, lambda: self.down(2).start())

    def t3(self):
        z = self.place.z

        def low():
            self.got_up(2)
            self.add(3, self.ups[1].astype(f32))

        def high():
            self.got_down(2)
            self.add(1, self.downs[1].astype(f32))

        when((z >= 1) & (z <= 2), low)
        when((z >= 1) & (z <= 2), high)
        when(z <= 2, lambda: self.up(3).start())
        when(z >= 1, lambda: self.down(3).start())

    def t4(self):
        z = self.place.z
        when(z >= 1, lambda: self.got_up(3))
        when(z <= 2, lambda: self.got_down(3))
        value = self.part[0, 1].astype(f32)
        value = value + up_to_f32(z >= 1, self.ups.at[2, 1]) + up_to_f32(z <= 2, self.downs.at[2, 1])
        self.part[0, 1] = value.astype(bf16)
        self.across().start()

    def done(self):
        wait_got(self.over, self.send.at[0], self.recv.at[0], self.place)
        z = self.place.z
        when(z == 0, lambda: self.up(1).wait_send())
        when(z == 3, lambda: self.down(1).wait_send())
        when(z <= 1, lambda: self.up(2).wait_send())
        when(z >= 2, lambda: self.down(2).wait_send())
        when(z <= 2, lambda: self.up(3).wait_send())
        when(z >= 1, lambda: self.down(3).wait_send())
        self.across().wait_send()

    def total(self):
        z = self.place.z
        value = self.part[0, 0].astype(f32) + self.over[...].astype(f32)
        return value + up_to_f32(z >= 1, self.ups.at[2, 0]) + up_to_f32(z <= 2, self.downs.at[2, 0])


class FramesSum:
    def __init__(self, place, sent, kept, from_core, from_x, sems, free, number):
        self.place, self.sent, self.kept, self.from_core, self.from_x = place, sent, kept, from_core, from_x
        self.sems, self.free, self.number = sems, free, number

    def core(self, j):
        return self.place.copy(self.sent[j], self.from_core[j], self.sems.at[0, j], self.sems.at[1, j], "core")

    def x(self, j):
        return self.place.copy(self.kept[j].at[1], self.from_x[j], self.sems.at[2, j], self.sems.at[3, j], "x")

    def out(self, j, outs, p):
        return pltpu.make_async_copy(self.kept[j].at[0], outs[j].at[p], self.sems.at[4, j])

    def start(self, later):
        def credit():
            pl.semaphore_wait(self.free.at[2 * self.number], 1)

        when(later, credit)
        for j in range(2):
            self.core(j).start()

    def middle(self, later):
        for j in range(2):
            self.core(j).wait_recv()

        def credit():
            pl.semaphore_wait(self.free.at[2 * self.number + 1], 1)

        when(later, credit)
        for j in range(2):
            kept, got = self.kept[j], self.from_core[j]
            kept[1] = (kept[1].astype(f32) + got[1].astype(f32)).astype(bf16)
            self.x(j).start()
        for j in range(2):
            self.core(j).wait_send()

    def finish(self, outs, p, more):
        for j in range(2):
            self.x(j).wait_recv()
            kept = self.kept[j]
            total = kept[0].astype(f32) + self.from_core[j][0].astype(f32) + self.from_x[j][...].astype(f32)
            kept[0] = total.astype(bf16)
            self.out(j, outs, p).start()

        def credit():
            for k, way in enumerate(("core", "x")):
                pl.semaphore_signal(
                    self.free.at[2 * self.number + k], inc=1, device_id=self.place.device(way), device_id_type=MESH
                )

        when(more, credit)
        for j in range(2):
            self.x(j).wait_send()

    def drained(self, outs, p):
        for j in range(2):
            self.out(j, outs, p).wait()


GIN_REDUCE = ReduceY
BACK_REDUCE = ReduceY
FIRST_Y_ROWS = (0, 0, 0, 0, 0, 0, 16, 16)
COT_Y_ROWS = (16, 16, 0, 0, 0, 0, 0, 16)
FFN_Y_ROWS = (0, 48, 32, 48, 32, 48, 32, 48, 48, 48, 48, 48, 48, 48, 48, 16)
ATT_Y_ROWS = (48, 48, 32, 48, 48, 48, 48, 48, 48, 48, 48, 48, 48, 48, 0, 0)
FFN_Z_ROWS = (32, 16, 16, 32, 16, 16, 16, 16, 16, 16, 16, 16, 16, 0, 16, 48)
ATTN_Z_ROWS = (0, 0, 48, 48, 48, 48, 48, 48, 0, 0, 0, 0, 0, 0, 0, 0)

SCHEDULES = (
    (
        ("AC1", 0), ("RA5", 1), ("A", 0), ("RF3", 3), ("AC4", 1), ("Fm", 3), ("AG4", 4), ("RB3", 5),
        ("RG5", 3), ("AC2", 0), ("RA2", 0), ("AF2", 1), ("RF4", 3), ("C", 2), ("RB4", 5), ("Ef", 5),
        ("RA3", 0), ("AG2", 3), ("E", 4), ("RG2", 2), ("AF3", 1), ("Eg", 4), ("RB5", 5), ("Ff", 3),
        ("RA4", 0), ("AC5", 1), ("AC3", 0), ("RF5", 3), ("RG3", 2), ("RF2", 2), ("AG3", 3), ("Cg", 2),
        ("K", 0), ("Em", 4), ("AF4", 1), ("RG4", 2), ("RB2", 4),
    ),
)
CHANGES = ()


class Split:
    def choose(self, i, table):
        self.chosen = {}
        for count in self.pairs:
            chosen = i < 0
            for k in range(len(table)):
                if table[k] == count:
                    chosen = chosen | (i == k)
            self.chosen[count] = chosen
        return self

    def both(self, run):
        for count, pair in self.pairs.items():

            def each(pair=pair):
                for part in pair:
                    run(part)

            when(self.chosen[count], each)

    def t1(self):
        self.both(lambda part: part.t1())

    def t2(self):
        self.both(lambda part: part.t2())

    def t3(self):
        self.both(lambda part: part.t3())

    def t4(self):
        self.both(lambda part: part.t4())

    def done(self):
        self.both(lambda part: part.done())


class SplitGather(Split):
    def __init__(self, place, g, send, recv, table, rows=0):
        def cut(start, size):
            return g.at[(slice(None), slice(None)) + (slice(None),) * rows + (pl.ds(start, size),)]

        def pair(count, local):
            runs = []
            if count > 0:
                runs.append(GatherY(place, cut(0, count), send.at[0], recv.at[0]))
            if count < local:
                runs.append(GatherZ(place, cut(count, local - count), send.at[1], recv.at[1]))
            return runs

        self.pairs = {count: pair(count, g.shape[2 + rows]) for count in sorted(set(table))}


class SplitReduce(Split):
    def __init__(self, place, part, over, ups, downs, send, recv, table):
        self.place, self.part, self.over, self.ups, self.downs = place, part, over, ups, downs
        local = part.shape[2]

        def pair(count):
            first, rest = pl.ds(0, count), pl.ds(count, local - count)
            runs = []
            if count > 0:
                runs.append(
                    ReduceZ(
                        place, part.at[:, :, first], over.at[0, first], ups.at[:, :, first], downs.at[:, :, first],
                        send.at[0], recv.at[0],
                    )
                )
            if count < local:
                runs.append(
                    ReduceY(
                        place, part.at[:, :, rest], over.at[:, rest], ups.at[:, 0, rest], downs.at[:, 0, rest],
                        send.at[1], recv.at[1],
                    )
                )
            return runs

        self.pairs = {count: pair(count) for count in sorted(set(table))}

    def total(self):
        z = self.place.z
        value = self.part[0, 0].astype(f32) + self.over[0].astype(f32)
        return value + up_to_f32(z >= 1, self.ups.at[2, 0]) + up_to_f32(z <= 2, self.downs.at[2, 0])


class GainSum:
    def __init__(self, place, pieces, got, send, recv):
        self.place, self.pieces, self.got, self.send, self.recv = place, pieces, got, send, recv

    def hop(self, k):
        ways = ("core", "x", "y", "pair", "far")
        sources = (self.pieces.at[1], self.pieces.at[0].at[1], self.pieces.at[0].at[0])
        src = sources[min(k, 2)]
        if k == 0:
            dst = self.got.at[pl.ds(0, 2)]
        else:
            dst = self.got.at[k + 1]
        return self.place.copy(src, dst, self.send.at[k], self.recv.at[k], ways[k])

    def start(self):
        self.hop(0).start()

    def next(self, k):
        self.hop(k).wait()
        if k == 0:
            self.pieces[0] = self.pieces[0] + self.got[0:2]
        else:
            self.pieces[0, 0] = self.pieces[0, 0] + self.got[k + 1]
        if k < 4:
            self.hop(k + 1).start()


def layer_kernel(
    x_ref, cot_ref, mask_ref, gains_ref, in_w, out_w, gu_w, dn_w,
    out_hbm, ingrad_hbm, gu_hbm, dn_hbm, iw_hbm, ow_hbm, gain_out, rows_hbm, cot_hbm,
    g_ffn, g_att, cot_v, p_attn, p_gin, p_ffn, p_back,
    over_attn, over_gin, over_ffn, over_back, ups_attn, ups_gin, ups_ffn, ups_back,
    downs_attn, downs_gin, downs_ffn, downs_back,
    q_s, k_s, v_s, mixed_s, dk_s, dv_s, sc, dp,
    gu_v, dn_v, owa_v, owe_v, iw_v, xb,
    act_s, gg_s, gup_s, gmixed_s, gproj_s, hmid_s, ghmid_s, stage, gain_s, gain_pieces, gain_got,
    gu_sent, gu_kept, gu_core, gu_x, dn_sent, dn_kept, dn_core, dn_x,
    iw_sent, iw_kept, iw_core, iw_x, ow_sent, ow_kept, ow_core, ow_x,
    sem_first, sem_first_got, sem_gather, sem_gather_got, sem_reduce, sem_reduce_got, sem_split, sem_split_got,
    sem_grad_ffn, sem_grad_att, sem_gain, sem_local, credits, free,
):
    place = Place()
    z, f = place.z, place.f
    positions, local, depth = x_ref.shape
    rows = ZN * YN * local
    last = positions - 1
    width = q_s.shape[-1]
    hidden = dn_v.shape[0]
    half = rows // 2
    quarter = depth // 4
    mask = mask_ref[...]
    scale = HDIM ** (-0.5)
    pairs_of = positions // 2

    def load(src, dst, number):
        return pltpu.make_async_copy(src, dst, sem_local.at[number])

    def load_owa(p):
        return load(out_w.at[p], owa_v, 0)

    def load_owe(p):
        return load(out_w.at[p], owe_v, 1)

    def load_iw(p, slot):
        return load(in_w.at[p], iw_v.at[slot], 2 + slot)

    def load_gu(p):
        return load(gu_w.at[p], gu_v, 4)

    def load_dn(p):
        return load(dn_w.at[p], dn_v, 5)

    def load_rows(p, dst, number):
        return load(rows_hbm.at[p // 2, :, :, p % 2], dst, number)

    def load_cot(p):
        return load(cot_hbm.at[p // 2, :, :, p % 2], cot_v, 9)

    def own_cot(j):
        return load(g_ffn.at[j // 4, j % 4], cot_hbm.at[j, 0, 0], 16 + j)

    def own_rows(j):
        return load(g_att.at[j // 4, j % 4], rows_hbm.at[j, 0, 0], 16 + pairs_of + j)

    barrier = pltpu.get_barrier_semaphore()

    def greet(way):
        pl.semaphore_signal(barrier, inc=1, device_id=place.device(way), device_id_type=MESH)

    for way in ("y", "core", "x", "far"):
        greet(way)
    when(z < 3, lambda: greet("up"))
    when(z > 0, lambda: greet("down"))
    pl.semaphore_wait(barrier, 4 + (z < 3).astype(jnp.int32) + (z > 0).astype(jnp.int32))

    groups = pairs_of

    def gain_of(which, p):
        return gains_ref[which, pl.ds(p, 1), :]

    def normalise(p, c):
        residual = x_ref[p].astype(f32)
        value = residual * inverse_rms(residual) * gain_of(0, p)
        g_att[p // 8, (p % 8) // 2, p % 2] = value.astype(bf16)
        return c

    firsts = [
        SplitGather(place, rows_hbm.at[g], sem_first.at[g], sem_first_got.at[g], FIRST_Y_ROWS[g : g + 1], 1).choose(
            g, FIRST_Y_ROWS
        )
        for g in range(groups)
    ]

    def cot_gather(j, which):
        sems = sem_gather.at[2, which], sem_gather_got.at[2, which]
        return SplitGather(place, cot_hbm.at[pairs_of - 1 - j], *sems, COT_Y_ROWS, 1).choose(j, COT_Y_ROWS)

    for g in range(groups):
        lax.fori_loop(2 * g, 2 * g + 2, normalise, 0)
        own_rows(g).start()
        own_rows(g).wait()
        firsts[g].t1()

    def masked(p, c):
        g_ffn[p // 8, (p % 8) // 2, p % 2] = (mask * cot_ref[p].astype(f32)).astype(bf16)
        return c

    lax.fori_loop(0, positions, masked, 0)
    for j in range(pairs_of):
        own_cot(j).start()
    load_owa(last).start()
    load_gu(last).start()
    load_dn(last).start()
    load_iw(0, 0).start()
    dk_s[...] = jnp.zeros_like(dk_s)
    dv_s[...] = jnp.zeros_like(dv_s)

    def project(p, c):
        slot = lax.rem(p, 2)
        load_rows(p, g_ffn.at[slot], 6 + slot).wait()
        load_iw(p, slot).wait()

        @pl.when(p < last)
        def _():
            load_iw(p + 1, 1 - slot).start()

        block = g_ffn[slot].reshape(rows, depth)
        q_s[p] = (dot(block, iw_v[slot, 0], NN).astype(bf16) * scale).astype(bf16)
        k_s[p] = dot(block, iw_v[slot, 1], NN).astype(bf16)
        v_s[p] = dot(block, iw_v[slot, 2], NN).astype(bf16)
        return c

    for g in range(groups):
        firsts[g].t2()
    for g in range(groups):
        firsts[g].t3()
    for g in range(groups):
        firsts[g].t4()
    for j in range(pairs_of):
        own_cot(j).wait()
    for g in range(groups):
        firsts[g].done()
        load_rows(2 * g, g_ffn.at[0], 6).start()
        load_rows(2 * g + 1, g_ffn.at[1], 7).start()
        lax.fori_loop(2 * g, 2 * g + 2, project, 0)
    load_owe(last).start()
    load_iw(last, 0).start()
    load_rows(last, xb, 8).start()

    row = lax.broadcasted_iota(jnp.int32, (2 * width, width), 0)
    column = lax.broadcasted_iota(jnp.int32, (2 * width, width), 1)
    ones = jnp.where((row % width) // HDIM == column // HDIM, 1.0, 0.0).astype(bf16)

    def per_head(product):
        high = product.astype(bf16)
        low = (product - high.astype(f32)).astype(bf16)
        return dot(jnp.concatenate([high, low], axis=1), ones, NN)

    def scores_of(p, q, at):
        def two(jj, top):
            first = per_head(q * k_s[2 * jj, at].astype(f32))
            second = per_head(q * k_s[2 * jj + 1, at].astype(f32))
            second = jnp.where(2 * jj + 1 <= p, second, -1e30)
            sc[2 * jj], sc[2 * jj + 1] = first, second
            return jnp.maximum(top, jnp.maximum(first, second))

        return lax.fori_loop(0, p // 2 + 1, two, jnp.full((half, width), -1e30, f32))

    def attend_one(p):
        pairs = p // 2 + 1
        for part in range(2):
            at = pl.ds(part * half, half)
            q = q_s[p, at].astype(f32)
            top = scores_of(p, q, at)

            def raise_two(jj, total):
                for t in range(2):
                    raised = jnp.exp(sc[2 * jj + t] - top)
                    sc[2 * jj + t] = raised
                    total = total + raised
                return total

            total = lax.fori_loop(0, pairs, raise_two, jnp.zeros((half, width), f32))
            factor = 1.0 / total

            def mix_two(jj, out):
                for t in range(2):
                    probs = (sc[2 * jj + t] * factor).astype(bf16).astype(f32)
                    out = out + probs * v_s[2 * jj + t, at].astype(f32)
                return out

            out = lax.fori_loop(0, pairs, mix_two, jnp.zeros((half, width), f32))
            mixed_s[p, at] = out.astype(bf16)

    def attend_back_one(p):
        pairs = p // 2 + 1
        for part in range(2):
            at = pl.ds(part * half, half)
            q = q_s[p, at].astype(f32)
            g = gmixed_s[at].astype(f32)
            top = scores_of(p, q, at)

            def raise_two(jj, carry):
                total, weighted = carry
                for t in range(2):
                    raised = jnp.exp(sc[2 * jj + t] - top)
                    sc[2 * jj + t] = raised
                    grad_probs = per_head(g * v_s[2 * jj + t, at].astype(f32))
                    dp[2 * jj + t] = grad_probs
                    total = total + raised
                    weighted = weighted + raised * grad_probs
                return total, weighted

            zero = jnp.zeros((half, width), f32)
            total, weighted = lax.fori_loop(0, pairs, raise_two, (zero, zero))
            factor = 1.0 / total
            centre = weighted * factor

            def back_two(jj, dq):
                for t in range(2):
                    j = 2 * jj + t
                    probs = sc[j] * factor
                    grad = (probs * (dp[j] - centre)).astype(bf16).astype(f32)
                    dq = dq + grad * k_s[j, at].astype(f32)
                    dk_s[j, at] = dk_s[j, at] + grad * q
                    dv_s[j, at] = dv_s[j, at] + probs.astype(bf16).astype(f32) * g
                return dq

            dq = lax.fori_loop(0, pairs, back_two, zero)
            gproj_s[0, at] = (dq * scale).astype(bf16)
        gproj_s[1] = dk_s[p].astype(bf16)
        gproj_s[2] = dv_s[p].astype(bf16)

    blocks = (ZN, YN, local, depth)
    grad_ffn = FramesSum(
        place, (gu_sent, dn_sent), (gu_kept, dn_kept), (gu_core, dn_core), (gu_x, dn_x), sem_grad_ffn, free, 0
    )
    grad_att = FramesSum(
        place, (iw_sent, ow_sent), (iw_kept, ow_kept), (iw_core, ow_core), (iw_x, ow_x), sem_grad_att, free, 1
    )
    ffn_outs, att_outs = (gu_hbm, dn_hbm), (iw_hbm, ow_hbm)
    gain_sum = GainSum(place, gain_pieces, gain_got, sem_gain.at[0], sem_gain.at[1])

    def out_copy(p):
        return pltpu.make_async_copy(stage.at[0], out_hbm.at[p], sem_local.at[14])

    def ingrad_copy(p):
        return pltpu.make_async_copy(stage.at[1], ingrad_hbm.at[p], sem_local.at[15])

    class Position:
        def __init__(self, i):
            self.i = i
            self.p = last - i
            self.par = lax.rem(i + 16, 2)
            self.ring = lax.rem(i + 16, 4)

        def gather(self, g, number, table):
            par = self.par
            sems = sem_gather.at[number, par], sem_gather_got.at[number, par]
            return SplitGather(place, g.at[par], *sems, table).choose(self.i, table)

        def reduce(self, kind, part, over, ups, downs, number):
            par = self.par
            return kind(
                place, part, over.at[par], ups.at[par], downs.at[par],
                sem_reduce.at[number, par], sem_reduce_got.at[number, par],
            )

        def AF(self):
            return self.gather(g_ffn, 0, FFN_Y_ROWS)

        def AG(self):
            return self.gather(g_att, 1, ATT_Y_ROWS)

        def split(self, part, over, ups, downs, number, table):
            par = self.par
            event = SplitReduce(
                place, part, over.at[par], ups.at[par], downs.at[par],
                sem_split.at[number, par], sem_split_got.at[number, par], table,
            )
            return event.choose(self.i, table)

        def RA(self):
            return self.split(p_attn, over_attn, ups_attn, downs_attn, 1, ATTN_Z_ROWS)

        def RG(self):
            return self.reduce(GIN_REDUCE, p_gin, over_gin, ups_gin, downs_gin, 1)

        def RF(self):
            return self.split(p_ffn.at[self.par], over_ffn, ups_ffn, downs_ffn, 0, FFN_Z_ROWS)

        def RB(self):
            return self.reduce(BACK_REDUCE, p_back.at[self.par], over_back, ups_back, downs_back, 3)

        def do_A(self):
            p = self.p
            attend_one(p)
            load_owa(p).wait()
            p_attn[...] = dot(mixed_s[p], owa_v[...], NN).astype(bf16).reshape(blocks)
            self.RA().t1()
            when(p > 0, lambda: load_owa(p - 1).start())

        def do_RA5(self):
            p, total = self.p, self.RA()
            total.done()
            hmid = x_ref[p].astype(f32) + mask * total.total()
            hmid_s[self.ring] = hmid
            g_ffn[self.par, 0, 0] = (hmid * inverse_rms(hmid) * gain_of(1, p)).astype(bf16)
            self.AF().t1()

        def do_C(self):
            p, par = self.p, self.par
            self.AF().done()
            load_gu(p).wait()
            load_dn(p).wait()
            load_cot(p).wait()
            x = g_ffn[par].reshape(rows, depth)
            g = cot_v[...].reshape(rows, depth)
            for h in range(2):
                at = slice(h * hidden // 2, (h + 1) * hidden // 2)
                gate = dot(x, gu_v[0, :, at], NN)
                up = dot(x, gu_v[1, :, at], NN)
                grad_act = dot(g, dn_v[at], NT)
                sigma = 1.0 / (1.0 + jnp.exp(-gate))
                silu = gate * sigma
                act_s[:, at] = (silu * up).astype(bf16)
                gg_s[:, at] = (grad_act * up * sigma * (1.0 + gate * (1.0 - sigma))).astype(bf16)
                gup_s[:, at] = (grad_act * silu).astype(bf16)
            back = dot(gg_s[...], gu_v[0], NT) + dot(gup_s[...], gu_v[1], NT)
            p_gin[...] = back.astype(bf16).reshape(blocks)
            self.RG().t1()
            gain_s[1, pl.ds(p, 1), :] = jnp.sum(back * x.astype(f32), axis=0, keepdims=True)
            p_ffn[par] = dot(act_s[...], dn_v[...], NN).astype(bf16).reshape(blocks)
            self.RF().t1()

            @pl.when(p > 0)
            def _():
                load_gu(p - 1).start()
                load_dn(p - 1).start()

        def do_Cg(self):
            p, par = self.p, self.par

            @pl.when(p < last)
            def _():
                grad_ffn.drained(ffn_outs, p + 1)

            for r in range(4):
                at = piece_at(r, f, quarter)
                gu_to, dn_to = (gu_kept, dn_kept) if r % 2 == 0 else (gu_sent, dn_sent)
                columns = g_ffn[par, :, :, :, at].reshape(rows, quarter)
                gu_to[r // 2, 0] = dot(columns, gg_s[...], TN).astype(bf16)
                gu_to[r // 2, 1] = dot(columns, gup_s[...], TN).astype(bf16)
                dn_to[r // 2] = dot(act_s[...], cot_v[:, :, :, at].reshape(rows, quarter), TN).astype(bf16)
            grad_ffn.start(p < last)
            when(p > 0, lambda: load_cot(p - 1).start())

        def do_Fm(self):
            grad_ffn.middle(self.p < last)

        def do_Ff(self):
            grad_ffn.finish(ffn_outs, self.p, self.p > 0)

        def do_RG5(self):
            p, total = self.p, self.RG()
            total.done()
            hmid = hmid_s[self.ring]
            factor = inverse_rms(hmid)
            grad = cot_ref[p].astype(f32) + norm_back(total.total(), hmid * factor, factor, gain_of(1, p))
            ghmid_s[self.ring] = grad
            g_att[self.par, 0, 0] = (mask * grad).astype(bf16)
            self.AG().t1()

        def do_RF5(self):
            p, total = self.p, self.RF()
            total.done()

            @pl.when(p < last)
            def _():
                out_copy(p + 1).wait()

            stage[0] = (hmid_s[self.ring] + mask * total.total()).astype(bf16)
            out_copy(p).start()

        def do_E(self):
            p, par = self.p, self.par
            self.AG().done()
            load_owe(p).wait()
            load_iw(p, 0).wait()
            load_rows(p, xb, 8).wait()
            gmixed_s[...] = dot(g_att[par].reshape(rows, depth), owe_v[...], NT).astype(bf16)
            attend_back_one(p)
            back = dot(gproj_s[0], iw_v[0, 0], NT)
            back = back + dot(gproj_s[1], iw_v[0, 1], NT)
            back = back + dot(gproj_s[2], iw_v[0, 2], NT)
            p_back[par] = back.astype(bf16).reshape(blocks)
            self.RB().t1()
            gain_s[0, pl.ds(p, 1), :] = jnp.sum(back * xb[...].reshape(rows, depth).astype(f32), axis=0, keepdims=True)

            @pl.when(p == 0)
            def _():
                for r in range(4):
                    gain_pieces[r % 2, r // 2] = gain_s[:, :, piece_at(r, f, quarter)]
                gain_sum.start()

            @pl.when(p > 0)
            def _():
                load_owe(p - 1).start()
                load_iw(p - 1, 0).start()

        def do_Eg(self):
            p, par = self.p, self.par

            @pl.when(p < last)
            def _():
                grad_att.drained(att_outs, p + 1)

            for r in range(4):
                at = piece_at(r, f, quarter)
                iw_to, ow_to = (iw_kept, ow_kept) if r % 2 == 0 else (iw_sent, ow_sent)
                columns = xb[:, :, :, at].reshape(rows, quarter)
                for j in range(3):
                    iw_to[r // 2, j] = dot(columns, gproj_s[j], TN).astype(bf16)
                ow_to[r // 2] = dot(mixed_s[p], g_att[par, :, :, :, at].reshape(rows, quarter), TN).astype(bf16)
            grad_att.start(p < last)
            when(p > 0, lambda: load_rows(p - 1, xb, 8).start())

        def do_Em(self):
            grad_att.middle(self.p < last)

        def do_Ef(self):
            grad_att.finish(att_outs, self.p, self.p > 0)

        def do_RB5(self):
            p, total = self.p, self.RB()
            total.done()
            when(p == 0, lambda: gain_sum.next(3))

            @pl.when(p < last)
            def _():
                ingrad_copy(p + 1).wait()

            residual = x_ref[p].astype(f32)
            factor = inverse_rms(residual)
            grad = norm_back(total.total(), residual * factor, factor, gain_of(0, p))
            stage[1] = (ghmid_s[self.ring] + grad).astype(bf16)
            ingrad_copy(p).start()

        def do_RB2(self):
            self.RB().t2()
            when(self.p == 0, lambda: gain_sum.next(0))

        def do_RB3(self):
            self.RB().t3()
            when(self.p == 0, lambda: gain_sum.next(1))

        def do_RB4(self):
            self.RB().t4()
            when(self.p == 0, lambda: gain_sum.next(2))

        def runs(self):
            ticks = {}
            for name, event in (
                ("RA", self.RA), ("RG", self.RG), ("RF", self.RF), ("AF", self.AF), ("AG", self.AG),
            ):
                ticks[name + "2"] = lambda event=event: event().t2()
                ticks[name + "3"] = lambda event=event: event().t3()
                ticks[name + "4"] = lambda event=event: event().t4()
            return ticks | {
                "A": self.do_A, "RA5": self.do_RA5, "C": self.do_C, "Cg": self.do_Cg, "Fm": self.do_Fm,
                "Ff": self.do_Ff, "RG5": self.do_RG5, "RF5": self.do_RF5, "E": self.do_E, "Eg": self.do_Eg,
                "Em": self.do_Em, "Ef": self.do_Ef, "RB2": self.do_RB2, "RB3": self.do_RB3, "RB4": self.do_RB4,
                "RB5": self.do_RB5,
            }

    def cot_runs(j):
        event = cot_gather(j, lax.rem(j + 16, 2))

        def done():
            event.done()
            when(j == 0, lambda: load_cot(last).start())

        return {"AC1": event.t1, "AC2": event.t2, "AC3": event.t3, "AC4": event.t4, "AC5": done}

    def tell(number, way):
        pl.semaphore_signal(credits.at[number], inc=1, device_id=place.device(way), device_id_type=MESH)

    def tell_all():
        tell(0, "y")
        when(z < 3, lambda: tell(1, "up"))
        when(z > 0, lambda: tell(2, "down"))

    steps = positions + max(delay for name, delay in SCHEDULES[0] if name[:2] != "AC")
    tell_all()

    def step(low, high, schedule, s, c):
        pl.semaphore_wait(credits.at[0], 1)
        when(z > 0, lambda: pl.semaphore_wait(credits.at[1], 1))
        when(z < 3, lambda: pl.semaphore_wait(credits.at[2], 1))
        for name, delay in schedule:
            if name == "K":
                when(s < steps - 1, tell_all)
            elif high <= delay or low >= delay + (pairs_of if name[:2] == "AC" else positions):
                continue
            elif name[:2] == "AC":
                j = s - delay
                when((j >= 0) & (j < pairs_of), cot_runs(j)[name])
            else:
                when((s >= delay) & (s <= last + delay), Position(s - delay).runs()[name])
        return c

    bounds = (0,) + CHANGES + (steps,)
    for low, high, schedule in zip(bounds, bounds[1:], SCHEDULES):
        lax.fori_loop(low, high, functools.partial(step, low, high, schedule), 0)
    gain_sum.next(4)
    gain_out[...] = gain_pieces[0, 0] / gains_ref[:, :, piece_at(0, f, quarter)]
    grad_ffn.drained(ffn_outs, 0)
    grad_att.drained(att_outs, 0)
    out_copy(0).wait()
    ingrad_copy(0).wait()


def layer(x, cot, mask, gains, in_weight, out_weight, gate_up, down):
    positions, local, depth = x.shape
    width, hidden = out_weight.shape[1], down.shape[1]
    rows = ZN * YN * local
    quarter = depth // 4
    block = (local, depth)
    groups = positions // 2

    def vm(*shape, dtype=bf16):
        return pltpu.VMEM(shape, dtype)

    def hbm(*shape, dtype=bf16):
        return jax.ShapeDtypeStruct(shape, dtype)

    everything = (ZN, YN) + block
    scratch = (
        [vm(2, *everything)] * 2
        + [vm(*everything)] * 3
        + [vm(2, *everything)] * 2
        + [vm(2, ZN, *block)] * 4
        + [vm(2, 3, YN, *block), vm(2, 3, *block), vm(2, 3, YN, *block), vm(2, 3, *block)] * 2
        + [vm(positions, rows, width)] * 4
        + [vm(positions, rows, width, dtype=f32)] * 2
        + [vm(positions, rows // 2, width, dtype=f32)] * 2
        + [vm(2, depth, hidden), vm(hidden, depth), vm(width, depth), vm(width, depth)]
        + [vm(2, 3, depth, width), vm(*everything)]
        + [vm(rows, hidden)] * 3
        + [vm(rows, width), vm(3, rows, width)]
        + [vm(4, *block, dtype=f32)] * 2
        + [vm(2, *block)]
        + [vm(2, positions, depth, dtype=f32)]
        + [vm(2, 2, 2, positions, quarter, dtype=f32), vm(6, 2, positions, quarter, dtype=f32)]
        + [vm(2, 2, quarter, hidden)] * 3
        + [vm(2, quarter, hidden)]
        + [vm(2, hidden, quarter)] * 3
        + [vm(hidden, quarter)]
        + [vm(2, 3, quarter, width)] * 3
        + [vm(3, quarter, width)]
        + [vm(2, width, quarter)] * 3
        + [vm(width, quarter)]
        + [
            pltpu.SemaphoreType.DMA((groups, 2, 10)),
            pltpu.SemaphoreType.DMA((groups, 2, 8)),
            pltpu.SemaphoreType.DMA((3, 2, 2, 10)),
            pltpu.SemaphoreType.DMA((3, 2, 2, 8)),
            pltpu.SemaphoreType.DMA((4, 2, 10)),
            pltpu.SemaphoreType.DMA((4, 2, 11)),
            pltpu.SemaphoreType.DMA((2, 2, 2, 10)),
            pltpu.SemaphoreType.DMA((2, 2, 2, 11)),
            pltpu.SemaphoreType.DMA((5, 2)),
            pltpu.SemaphoreType.DMA((5, 2)),
            pltpu.SemaphoreType.DMA((2, 5)),
            pltpu.SemaphoreType.DMA((16 + positions,)),
            pltpu.SemaphoreType.REGULAR((3,)),
            pltpu.SemaphoreType.REGULAR((4,)),
        ]
    )
    in_vmem = pl.BlockSpec(memory_space=pltpu.VMEM)
    anywhere = pl.BlockSpec(memory_space=pl.ANY)
    return pl.pallas_call(
        layer_kernel,
        in_specs=[in_vmem] * 4 + [anywhere] * 4,
        out_specs=[anywhere] * 6 + [in_vmem, anywhere, anywhere],
        out_shape=[
            hbm(positions, *block),
            hbm(positions, *block),
            hbm(positions, 2, quarter, hidden),
            hbm(positions, hidden, quarter),
            hbm(positions, 3, quarter, width),
            hbm(positions, width, quarter),
            hbm(2, positions, quarter, dtype=f32),
            hbm(positions // 2, ZN, YN, 2, *block),
            hbm(positions // 2, ZN, YN, 2, *block),
        ],
        scratch_shapes=scratch,
        compiler_params=pltpu.CompilerParams(
            collective_id=0, has_side_effects=True, vmem_limit_bytes=KERNEL_VMEM_BYTES
        ),
        name="layer",
    )(x, cot, mask, gains, in_weight, out_weight, gate_up, down)


def widen_kernel(*refs):
    half = len(refs) // 2
    for narrow, wide in zip(refs[:half], refs[half:]):
        wide[...] = narrow[...].astype(f32)


def widened(*arrays):
    def spec(a):
        rank = a.ndim
        return pl.BlockSpec((1,) + a.shape[1:], lambda i: (i,) + (0,) * (rank - 1))

    return pl.pallas_call(
        widen_kernel,
        grid=(arrays[0].shape[0],),
        in_specs=[spec(a) for a in arrays],
        out_specs=[spec(a) for a in arrays],
        out_shape=[jax.ShapeDtypeStruct(a.shape, f32) for a in arrays],
        compiler_params=pltpu.CompilerParams(vmem_limit_bytes=KERNEL_VMEM_BYTES),
        name="widen",
    )(*arrays)


def body_in_one(inputs, counts, norm_gains, in_weight, out_weight, gate_up, down_weight, cotangent):
    local = inputs.shape[0]
    ids = lax.axis_index("mp") * local + jnp.arange(local)
    valid = ids < counts[0]
    output, input_grad, g_gu, g_dn, g_in, g_out, gain_sums, _, _ = layer(
        jnp.swapaxes(inputs, 0, 1),
        jnp.swapaxes(cotangent, 0, 1),
        valid.astype(f32)[:, None],
        norm_gains,
        in_weight,
        out_weight,
        gate_up,
        down_weight,
    )
    return (
        jnp.swapaxes(output, 0, 1),
        jnp.swapaxes(input_grad, 0, 1),
        *widened(g_in, g_out, g_gu, g_dn),
        gain_sums,
    )


def solution(mesh):
    placed = (
        P(("frames", "mp"), None, None),
        P("frames"),
        P(),
        P(None, None, None, "mp"),
        P(None, "mp", None),
        P(None, None, None, "mp"),
        P(None, "mp", None),
        P(("frames", "mp"), None, None),
    )
    def local_body(*args):
        frames, group_size = lax.axis_size("frames"), lax.axis_size("mp")
        local, positions, depth = args[0].shape
        width, hidden = args[4].shape[1], args[6].shape[1]
        one = fits(frames, group_size, local, positions, depth, width, hidden)
        return (body_in_one if one else body)(*args)

    return jax.shard_map(
        local_body,
        mesh=mesh,
        in_specs=placed,
        out_specs=(
            P(("frames", "mp"), None, None),
            P(("frames", "mp"), None, None),
            P(None, None, "frames", "mp"),
            P(None, "mp", "frames"),
            P(None, None, "frames", "mp"),
            P(None, "mp", "frames"),
            P(None, None, "frames"),
        ),
        check_vma=False,
    )
```

```python
import functools
import math

import jax
import jax.numpy as jnp
from jax import lax
from jax.experimental import pallas as pl
from jax.experimental.pallas import tpu as pltpu
from jax.sharding import PartitionSpec as P

HDIM = 64
EPSILON = 1e-05
Z_CHIPS = 4
FRAME_BLOCK = 16
CHUNKS = 4
VMEM_BYTES = 56 * 1024 * 1024
KERNEL_VMEM_BYTES = 63 * 1024 * 1024

f32 = jnp.float32
bf16 = jnp.bfloat16


class Line:
    def __init__(self, total, n, stride):
        self.n = n
        self.stride = stride
        self.starts = [i for i in range(total) if (i // stride) % n == 0]

    def up(self, low, high):
        return [(s + i * self.stride, s + (i + 1) * self.stride) for s in self.starts for i in range(low, high)]

    def down(self, low, high):
        return [(s + (i + 1) * self.stride, s + i * self.stride) for s in self.starts for i in range(low, high)]

    def gather(self, own):
        n = self.n
        if n == 1:
            return [own]
        if n == 2:
            return [own, lax.ppermute(own, "mp", self.up(0, 1) + self.down(0, 1))]
        ups, downs = [own], [own]
        for k in range(1, n):
            ups.append(lax.ppermute(ups[-1], "mp", self.up(k - 1, n - 1)))
            downs.append(lax.ppermute(downs[-1], "mp", self.down(0, n - k)))
        return [own] + [ups[k] + downs[n - k] for k in range(1, n)]

    def reduce(self, term):
        n = self.n
        if n == 1:
            return [term(0)]
        if n == 2:
            return [term(0), lax.ppermute(term(1).astype(bf16), "mp", self.up(0, 1) + self.down(0, 1)).astype(f32)]
        up = down = None
        for s in range(1, n):
            send_up = term(s) if up is None else term(s) + up.astype(f32)
            send_down = term(n - s) if down is None else term(n - s) + down.astype(f32)
            up = lax.ppermute(send_up.astype(bf16), "mp", self.up(0, min(s, n - 1)))
            down = lax.ppermute(send_down.astype(bf16), "mp", self.down(n - 1 - s, n - 1))
        return [term(0), up.astype(f32), down.astype(f32)]


class Group:
    def __init__(self, size):
        self.nz = math.gcd(size, Z_CHIPS)
        self.ny = size // self.nz
        self.z = Line(size, self.nz, self.ny)
        self.y = Line(size, self.ny, 1)

    def gather(self, own, z_first):
        if z_first:
            column = jnp.stack(self.z.gather(own), axis=1)
            return jnp.stack(self.y.gather(column), axis=1)
        row = jnp.stack(self.y.gather(own), axis=1)
        return jnp.stack(self.z.gather(row), axis=2)

    def reduce(self, parts, z_first):
        if not z_first:
            if self.ny == 2:
                got = lax.ppermute(parts[1], "mp", self.y.up(0, 1) + self.y.down(0, 1))
                columns = [parts[0], got]

                def term(k):
                    return columns[0][:, k].astype(f32) + columns[1][:, k].astype(f32)

            else:
                terms = self.y.reduce(lambda k: parts[k].astype(f32))

                def term(k):
                    return sum(t[:, k] for t in terms)

            return sum(self.z.reduce(term))

        def row(k):
            return jnp.stack([part[:, k] for part in parts], axis=1).astype(f32)

        terms = self.z.reduce(row)
        return sum(self.y.reduce(lambda k: sum(t[:, k] for t in terms)))


def frames_sum(keep, send, size):
    step = 1
    while True:
        got = lax.ppermute(send, "frames", [(i, i ^ step) for i in range(size)])
        total = keep.astype(f32) + got.astype(f32)
        step *= 2
        if step == size:
            return total[:, 0]
        keep, send = total[:, 0::2], total[:, 1::2].astype(send.dtype)


def dot(a, b, dims):
    return lax.dot_general(a, b, (dims, ((), ())), preferred_element_type=f32)


NN = ((1,), (0,))
NT = ((1,), (1,))
TN = ((0,), (0,))


def params():
    return pltpu.CompilerParams(vmem_limit_bytes=VMEM_BYTES)


def cost(flops, nbytes):
    return pl.CostEstimate(flops=int(flops), bytes_accessed=int(nbytes), transcendentals=0)


def qkv_kernel(x_ref, w_ref, q_ref, k_ref, v_ref):
    x = x_ref[0]
    for c, out in enumerate((q_ref, k_ref, v_ref)):
        out[0] = dot(x, w_ref[0, c], NN).astype(bf16)


def qkv(x, weight, base):
    count, rows, depth = x.shape
    width = weight.shape[-1]
    out = jax.ShapeDtypeStruct((count, rows, width), bf16)
    return pl.pallas_call(
        qkv_kernel,
        grid=(count,),
        in_specs=[
            pl.BlockSpec((1, rows, depth), lambda i: (i, 0, 0)),
            pl.BlockSpec((1, 3, depth, width), lambda i: (base + i, 0, 0, 0)),
        ],
        out_specs=[pl.BlockSpec((1, rows, width), lambda i: (i, 0, 0))] * 3,
        out_shape=[out] * 3,
        compiler_params=params(),
        cost_estimate=cost(6 * count * rows * depth * width, 2 * count * depth * (rows + 3 * width)),
        name="qkv",
    )(x, weight)


def head_masks(rows, width):
    lane = lax.broadcasted_iota(jnp.int32, (rows, width), 1)
    return [(lane >= h * HDIM) & (lane < (h + 1) * HDIM) for h in range(width // HDIM)]


def attention_mask(count, base, columns):
    rows = count * FRAME_BLOCK
    row = lax.broadcasted_iota(jnp.int32, (rows, columns), 0)
    column = lax.broadcasted_iota(jnp.int32, (rows, columns), 1)
    same = (row % FRAME_BLOCK) == (column % FRAME_BLOCK)
    return same & (column // FRAME_BLOCK <= row // FRAME_BLOCK + base)


def block_of(refs, rows):
    pieces = [ref[:, rows, :] for ref in refs]
    pieces = [p.reshape(p.shape[0] * p.shape[1], p.shape[2]) for p in pieces]
    return pieces[0] if len(pieces) == 1 else jnp.concatenate(pieces, axis=0)


def softmax(scores):
    top = jnp.max(scores, axis=-1, keepdims=True)
    raised = jnp.exp(scores - top)
    return raised / jnp.sum(raised, axis=-1, keepdims=True)


def pick(masks, values):
    out = values[0]
    for mask, value in zip(masks[1:], values[1:]):
        out = jnp.where(mask, value, out)
    return out


def attend_kernel(base, n_kv, ny, q_ref, *refs):
    k_refs, v_refs = refs[:n_kv], refs[n_kv : 2 * n_kv]
    w_ref = refs[2 * n_kv]
    mixed_ref = refs[2 * n_kv + 1]
    part_refs = refs[2 * n_kv + 2 :]
    count, rows, width = q_ref.shape
    columns = sum(ref.shape[0] for ref in k_refs) * FRAME_BLOCK
    step = pl.program_id(0)

    @pl.when(step == 0)
    def _():
        heads = head_masks(count * FRAME_BLOCK, width)
        allowed = attention_mask(count, base, columns)

        def one(b):
            at = pl.ds(pl.multiple_of(b * FRAME_BLOCK, FRAME_BLOCK), FRAME_BLOCK)
            queries = block_of([q_ref], at) * HDIM ** (-0.5)
            keys, values = block_of(k_refs, at), block_of(v_refs, at)
            outs = []
            for head in heads:
                mine = jnp.where(head, queries, jnp.zeros_like(queries))
                scores = jnp.where(allowed, dot(mine, keys, NT), -1e30)
                outs.append(dot(softmax(scores).astype(bf16), values, NN))
            mixed_ref[:, at, :] = pick(heads, outs).astype(bf16).reshape(count, FRAME_BLOCK, width)

        lax.fori_loop(0, rows // FRAME_BLOCK, lambda b, c: (one(b), c)[1], 0, unroll=4)

    out = dot(mixed_ref[step], w_ref[0], NN)
    span = rows // ny
    for y, part in enumerate(part_refs):
        part[0] = out[y * span : (y + 1) * span].astype(bf16)


def attend(q, ks, vs, weight, base, ny):
    count, rows, width = q.shape
    depth = weight.shape[-1]
    whole = pl.BlockSpec((count, rows, width), lambda i: (0, 0, 0))
    part = jax.ShapeDtypeStruct((count, rows // ny, depth), bf16)
    n_kv = len(ks)
    return pl.pallas_call(
        functools.partial(attend_kernel, base, n_kv, ny),
        grid=(count,),
        in_specs=[whole] * (1 + 2 * n_kv) + [pl.BlockSpec((1, width, depth), lambda i: (base + i, 0, 0))],
        out_specs=[whole] + [pl.BlockSpec((1, rows // ny, depth), lambda i: (i, 0, 0))] * ny,
        out_shape=[jax.ShapeDtypeStruct(q.shape, bf16)] + [part] * ny,
        compiler_params=params(),
        cost_estimate=cost(4 * count * rows * depth * width, 2 * count * rows * (depth + (2 + 2 * n_kv) * width)),
        name="attend",
    )(q, *ks, *vs, weight)


def gradient_pieces(size, depth):
    return size if size > 1 and (depth // size) % 128 == 0 else 1


def piece_at(piece, mine, span):
    return pl.ds(pl.multiple_of((piece ^ mine) * span, span), span)


def ffn_kernel(ny, pieces, mine_ref, x_ref, g_ref, gu_ref, dn_ref, *refs):
    outs, backs = refs[:ny], refs[ny : 2 * ny]
    gain_ref = refs[2 * ny]
    grads = refs[2 * ny + 1 :]
    rows, depth = x_ref.shape[1:]
    span = rows // ny
    x, g = x_ref[0], g_ref[0]
    gate = dot(x, gu_ref[0, 0], NN)
    up = dot(x, gu_ref[0, 1], NN)
    grad_act = dot(g, dn_ref[0], NT)
    sigma = 1.0 / (1.0 + jnp.exp(-gate))
    silu = gate * sigma
    act = (silu * up).astype(bf16)
    grad_gate = (grad_act * up * sigma * (1.0 + gate * (1.0 - sigma))).astype(bf16)
    grad_up = (grad_act * silu).astype(bf16)
    out = dot(act, dn_ref[0], NN)
    for y in range(ny):
        outs[y][0] = out[y * span : (y + 1) * span].astype(bf16)
    back = dot(grad_gate, gu_ref[0, 0], NT) + dot(grad_up, gu_ref[0, 1], NT)
    for y in range(ny):
        backs[y][0] = back[y * span : (y + 1) * span].astype(bf16)
    gain_ref[0] = jnp.sum(back * x.astype(f32), axis=0, keepdims=True)
    if pieces == 1:
        grads[0][0, 0] = dot(x, grad_gate, TN).astype(bf16)
        grads[0][0, 1] = dot(x, grad_up, TN).astype(bf16)
        grads[1][0] = dot(act, g, TN).astype(bf16)
        return
    mine = mine_ref[0]
    width = depth // pieces
    for r in range(pieces):
        at = piece_at(r, mine, width)
        gu_out, dn_out = grads[r % 2], grads[2 + r % 2]
        columns = x_ref[0, :, at]
        gu_out[0, r // 2, 0] = dot(columns, grad_gate, TN).astype(bf16)
        gu_out[0, r // 2, 1] = dot(columns, grad_up, TN).astype(bf16)
        dn_out[0, r // 2] = dot(act, g_ref[0, :, at], TN).astype(bf16)


def split_specs(shape, pieces, axis):
    if pieces == 1:
        block = (1,) + shape[1:]
        return [pl.BlockSpec(block, lambda i: (i,) + (0,) * (len(block) - 1))], [jax.ShapeDtypeStruct(shape, bf16)]
    rest = list(shape[1:])
    rest[axis - 1] //= pieces
    block = (1, pieces // 2) + tuple(rest)
    spec = pl.BlockSpec(block, lambda i: (i,) + (0,) * (len(block) - 1))
    return [spec] * 2, [jax.ShapeDtypeStruct((shape[0],) + block[1:], bf16)] * 2


def ffn(x, g, gate_up, down, base, ny, frames, mine):
    count, rows, depth = x.shape
    width = down.shape[1]
    pieces = gradient_pieces(frames, depth)
    part = jax.ShapeDtypeStruct((count, rows // ny, depth), bf16)
    part_spec = pl.BlockSpec((1, rows // ny, depth), lambda i: (i, 0, 0))
    row_spec = pl.BlockSpec((1, rows, depth), lambda i: (i, 0, 0))
    gu_specs, gu_shapes = split_specs((count, 2, depth, width), pieces, 2)
    dn_specs, dn_shapes = split_specs((count, width, depth), pieces, 2)
    out = pl.pallas_call(
        functools.partial(ffn_kernel, ny, pieces),
        grid=(count,),
        in_specs=[
            pl.BlockSpec(memory_space=pltpu.SMEM),
            row_spec,
            row_spec,
            pl.BlockSpec((1, 2, depth, width), lambda i: (base + i, 0, 0, 0)),
            pl.BlockSpec((1, width, depth), lambda i: (base + i, 0, 0)),
        ],
        out_specs=[part_spec] * (2 * ny) + [pl.BlockSpec((1, 1, depth), lambda i: (i, 0, 0))] + gu_specs + dn_specs,
        out_shape=[part] * (2 * ny) + [jax.ShapeDtypeStruct((count, 1, depth), f32)] + gu_shapes + dn_shapes,
        compiler_params=params(),
        cost_estimate=cost(18 * count * rows * depth * width, 2 * count * depth * (4 * rows + 6 * width)),
        name="ffn",
    )(mine, x, g, gate_up, down)
    n = len(gu_specs)
    return out[:ny], out[ny : 2 * ny], out[2 * ny], out[2 * ny + 1 : 2 * ny + 1 + n], out[2 * ny + 1 + n :]


def attend_back_kernel(base, n_kv, first, ny, pieces, mine_ref, ga_ref, gp_ref, x_ref, q_ref, *refs):
    refs = list(refs)

    def take(n):
        got = refs[:n]
        del refs[:n]
        return got

    k_refs, v_refs = take(n_kv), take(n_kv)
    (mixed_ref, ow_all_ref, iw_ref) = take(3)
    dk_in = dv_in = ()
    if not first:
        dk_in, dv_in = take(n_kv), take(n_kv)
    part_refs = take(ny)
    (gain_ref,) = take(1)
    n_out = 1 if pieces == 1 else 2
    iw_grads, ow_grads = take(n_out), take(n_out)
    dk_out, dv_out = take(n_kv - 1), take(n_kv - 1)
    gmixed_ref, gproj_ref = take(2)
    count, rows, width = q_ref.shape
    columns = n_kv * count * FRAME_BLOCK
    block = count * FRAME_BLOCK
    step = pl.program_id(0)

    @pl.when(step == 0)
    def _():
        for p in range(count):
            gmixed_ref[p] = dot(ga_ref[p], ow_all_ref[p], NT).astype(bf16)
        heads = head_masks(block, width)
        allowed = attention_mask(count, base, columns)
        factor = HDIM ** (-0.5)

        def one(b):
            at = pl.ds(pl.multiple_of(b * FRAME_BLOCK, FRAME_BLOCK), FRAME_BLOCK)
            queries = block_of([q_ref], at) * factor
            grad_mixed = block_of([gmixed_ref], at)
            keys, values = block_of(k_refs, at), block_of(v_refs, at)
            dqs, dk, dv = [], None, None
            for head in heads:
                my_q = jnp.where(head, queries, jnp.zeros_like(queries))
                my_g = jnp.where(head, grad_mixed, jnp.zeros_like(grad_mixed))
                probs = softmax(jnp.where(allowed, dot(my_q, keys, NT), -1e30))
                grad_probs = dot(my_g, values, NT)
                weighted = probs * grad_probs
                grad_scores = (weighted - probs * jnp.sum(weighted, axis=-1, keepdims=True)).astype(bf16)
                dqs.append(dot(grad_scores, keys, NN))
                more_k = dot(grad_scores, my_q, TN)
                more_v = dot(probs.astype(bf16), my_g, TN)
                dk = more_k if dk is None else dk + more_k
                dv = more_v if dv is None else dv + more_v
            gproj_ref[:, 0, at, :] = (pick(heads, dqs) * factor).astype(bf16).reshape(count, FRAME_BLOCK, width)
            for c, total, earlier, later in ((1, dk, dk_in, dk_out), (2, dv, dv_in, dv_out)):
                for j in range(n_kv):
                    piece = total[j * block : (j + 1) * block].reshape(count, FRAME_BLOCK, width)
                    if not first:
                        piece = piece + earlier[j][:, at, :]
                    if j < n_kv - 1:
                        later[j][:, at, :] = piece
                    else:
                        gproj_ref[:, c, at, :] = piece.astype(bf16)

        lax.fori_loop(0, rows // FRAME_BLOCK, lambda b, c: (one(b), c)[1], 0, unroll=2)

    grads = [gproj_ref[step, c] for c in range(3)]
    back = dot(grads[0], iw_ref[0, 0], NT) + dot(grads[1], iw_ref[0, 1], NT) + dot(grads[2], iw_ref[0, 2], NT)
    span = rows // ny
    for y, part in enumerate(part_refs):
        part[0] = back[y * span : (y + 1) * span].astype(bf16)
    gain_ref[0] = jnp.sum(back * x_ref[0].astype(f32), axis=0, keepdims=True)
    mixed = mixed_ref[0]
    if pieces == 1:
        for c in range(3):
            iw_grads[0][0, c] = dot(x_ref[0], grads[c], TN).astype(bf16)
        ow_grads[0][0] = dot(mixed, gp_ref[0], TN).astype(bf16)
        return
    mine = mine_ref[0]
    depth = x_ref.shape[2]
    for r in range(pieces):
        at = piece_at(r, mine, depth // pieces)
        columns = x_ref[0, :, at]
        for c in range(3):
            iw_grads[r % 2][0, r // 2, c] = dot(columns, grads[c], TN).astype(bf16)
        ow_grads[r % 2][0, r // 2] = dot(mixed, gp_ref[0, :, at], TN).astype(bf16)


def attend_back(grad_rows, x, q, ks, vs, mixed, out_weight, in_weight, dks, dvs, base, ny, frames, mine):
    count, rows, depth = x.shape
    width = q.shape[-1]
    pieces = gradient_pieces(frames, depth)
    n_kv = len(ks)
    first = not dks
    whole = pl.BlockSpec((count, rows, width), lambda i: (0, 0, 0))
    row_spec = pl.BlockSpec((1, rows, depth), lambda i: (i, 0, 0))
    chunk = base // count
    part = jax.ShapeDtypeStruct((count, rows // ny, depth), bf16)
    part_spec = pl.BlockSpec((1, rows // ny, depth), lambda i: (i, 0, 0))
    iw_specs, iw_shapes = split_specs((count, 3, depth, width), pieces, 2)
    ow_specs, ow_shapes = split_specs((count, width, depth), pieces, 2)
    total = jax.ShapeDtypeStruct((count, rows, width), f32)
    out = pl.pallas_call(
        functools.partial(attend_back_kernel, base, n_kv, first, ny, pieces),
        grid=(count,),
        in_specs=[
            pl.BlockSpec(memory_space=pltpu.SMEM),
            pl.BlockSpec((count, rows, depth), lambda i: (0, 0, 0)),
            row_spec,
            row_spec,
        ]
        + [whole] * (1 + 2 * n_kv)
        + [
            pl.BlockSpec((1, rows, width), lambda i: (i, 0, 0)),
            pl.BlockSpec((count, width, depth), lambda i: (chunk, 0, 0)),
            pl.BlockSpec((1, 3, depth, width), lambda i: (base + i, 0, 0, 0)),
        ]
        + [whole] * (len(dks) + len(dvs)),
        out_specs=[part_spec] * ny
        + [pl.BlockSpec((1, 1, depth), lambda i: (i, 0, 0))]
        + iw_specs
        + ow_specs
        + [whole] * (2 * (n_kv - 1)),
        out_shape=[part] * ny
        + [jax.ShapeDtypeStruct((count, 1, depth), f32)]
        + iw_shapes
        + ow_shapes
        + [total] * (2 * (n_kv - 1)),
        scratch_shapes=[pltpu.VMEM((count, rows, width), bf16), pltpu.VMEM((count, 3, rows, width), bf16)],
        compiler_params=params(),
        cost_estimate=cost(16 * count * rows * depth * width, 2 * count * rows * (4 * depth + 8 * n_kv * width)),
        name="attend_back",
    )(mine, grad_rows, grad_rows, x, q, *ks, *vs, mixed, out_weight, in_weight, *dks, *dvs)
    out = list(out)
    n = len(iw_specs)
    parts, gain = out[:ny], out[ny]
    iw, ow = out[ny + 1 : ny + 1 + n], out[ny + 1 + n : ny + 1 + 2 * n]
    rest = out[ny + 1 + 2 * n :]
    return parts, gain, iw, ow, rest[: n_kv - 1], rest[n_kv - 1 :]


def inverse_rms(values):
    return lax.rsqrt(jnp.mean(values * values, axis=-1, keepdims=True) + EPSILON)


def norm_back(grad_normed, normed, factor, gain):
    scaled = grad_normed * gain
    return factor * (scaled - normed * jnp.mean(scaled * normed, axis=-1, keepdims=True))


def body(inputs, counts, norm_gains, in_weight, out_weight, gate_up, down_weight, cotangent):
    frames, group_size = lax.axis_size("frames"), lax.axis_size("mp")
    group = Group(group_size)
    ny, nz = group.ny, group.nz
    local, positions, depth = inputs.shape
    rows = local * group_size
    size = positions // CHUNKS
    ids = lax.axis_index("mp") * local + jnp.arange(local)
    mask = (ids < counts[0]).astype(f32)[None, :, None]
    mine = lax.axis_index("frames").astype(jnp.int32)[None]
    x_major = jnp.swapaxes(inputs, 0, 1)
    g_major = jnp.swapaxes(cotangent, 0, 1)
    gains = norm_gains[:, :, None, :]

    def at(c):
        return slice(c * size, (c + 1) * size)

    def gathered(own, z_first):
        return group.gather(own, z_first).reshape(size, rows, depth)

    def reduced(parts, z_first):
        return group.reduce([p.reshape(size, nz, local, depth) for p in parts], z_first)

    def summed(grads):
        if len(grads) == 1:
            return lax.psum_scatter(grads[0], "frames", scatter_dimension=grads[0].ndim - 1, tiled=True).astype(f32)
        return frames_sum(grads[0], grads[1], frames)

    def summed_middle(grads):
        if len(grads) == 1:
            return lax.psum_scatter(grads[0], "frames", scatter_dimension=2, tiled=True).astype(f32)
        return frames_sum(grads[0], grads[1], frames)

    order = list(range(CHUNKS))[::-1]
    attn_in, qs, ks, vs = {}, {}, {}, {}
    for c in order:
        residual = x_major[at(c)].astype(f32)
        own = (residual * inverse_rms(residual) * gains[0, at(c)]).astype(bf16)
        attn_in[c] = gathered(own, True)
        qs[c], ks[c], vs[c] = qkv(attn_in[c], in_weight, c * size)

    outputs, input_grads = {}, {}
    g_in, g_out, g_gu, g_dn, gain_terms = {}, {}, {}, {}, {}
    dks, dvs = [], []
    for c in order:
        base = c * size
        gain_first, gain_second = gains[0, at(c)], gains[1, at(c)]
        residual = x_major[at(c)].astype(f32)
        gy = g_major[at(c)].astype(f32)
        grad_rows = gathered((mask * gy).astype(bf16), c % 2 == 0)
        earlier_k, earlier_v = [ks[j] for j in range(c + 1)], [vs[j] for j in range(c + 1)]
        mixed, *parts = attend(qs[c], earlier_k, earlier_v, out_weight, base, ny)
        hmid = residual + mask * reduced(parts, False)
        scale_second = inverse_rms(hmid)
        normed_second = hmid * scale_second
        ffn_rows = gathered((normed_second * gain_second).astype(bf16), True)
        out_parts, back_parts, gain_back, grad_gu, grad_dn = ffn(
            ffn_rows, grad_rows, gate_up, down_weight, base, ny, frames, mine
        )
        grad_ffn_in = reduced(back_parts, False)
        grad_mid = gy + norm_back(grad_ffn_in, normed_second, scale_second, gain_second)
        grad_attn = gathered((mask * grad_mid).astype(bf16), True)
        outputs[c] = (hmid + mask * reduced(out_parts, True)).astype(bf16)
        back, gain_front, grad_iw, grad_ow, dks, dvs = attend_back(
            grad_attn, attn_in[c], qs[c], earlier_k, earlier_v, mixed, out_weight, in_weight,
            dks, dvs, base, ny, frames, mine,
        )
        grad_attn_in = reduced(back, c % 2 == 1)
        scale_first = inverse_rms(residual)
        input_grads[c] = (
            grad_mid + norm_back(grad_attn_in, residual * scale_first, scale_first, gain_first)
        ).astype(bf16)
        gain_terms[c] = jnp.stack([gain_front[:, 0] / norm_gains[0, at(c)], gain_back[:, 0] / norm_gains[1, at(c)]])
        g_gu[c], g_dn[c] = summed_middle(grad_gu), summed(grad_dn)
        g_in[c], g_out[c] = summed_middle(grad_iw), summed(grad_ow)

    def joined(pieces, axis=0):
        return jnp.concatenate([pieces[c] for c in range(CHUNKS)], axis=axis)

    terms = lax.psum_scatter(joined(gain_terms, 1), "frames", scatter_dimension=2, tiled=True)
    step = 1
    while step < group_size:
        terms = terms + lax.ppermute(terms, "mp", [(i, i ^ step) for i in range(group_size)])
        step *= 2
    return (
        jnp.swapaxes(joined(outputs), 0, 1),
        jnp.swapaxes(joined(input_grads), 0, 1),
        joined(g_in),
        joined(g_out),
        joined(g_gu),
        joined(g_dn),
        terms,
    )


MESH = pl.DeviceIdType.MESH
ZN, YN = 4, 2


def fits(frames, group_size, local, positions, depth, width, hidden):
    return (
        frames == 4
        and group_size == ZN * YN
        and local == 48
        and positions == 16
        and width % 128 == 0
        and (depth // frames) % 128 == 0
        and hidden % 128 == 0
    )


class Place:
    def __init__(self):
        self.m = lax.axis_index("mp")
        self.f = lax.axis_index("frames")
        self.z = self.m // YN
        self.ids = {
            "y": ("mp", self.m ^ 1),
            "up": ("mp", self.m + YN),
            "down": ("mp", self.m - YN),
            "core": ("frames", self.f ^ 1),
            "x": ("frames", self.f ^ 2),
            "pair": ("mp", self.m ^ YN),
            "far": ("mp", self.m ^ (2 * YN)),
        }

    def device(self, way):
        axis, index = self.ids[way]
        return {axis: index}

    def copy(self, src, dst, send, recv, way):
        return pltpu.make_async_remote_copy(
            src_ref=src, dst_ref=dst, send_sem=send, recv_sem=recv, device_id=self.device(way), device_id_type=MESH
        )


def when(condition, run):
    pl.when(condition)(run)


def wait_got(dst, send, recv, place):
    place.copy(dst, dst, send, recv, "y").wait_recv()


class GatherZ:
    def __init__(self, place, g, send, recv):
        self.place, self.g, self.send, self.recv = place, g, send, recv

    def site(self, number, way, src, dst):
        return self.place.copy(
            self.g.at[src[0], src[1]],
            self.g.at[dst[0], dst[1]],
            self.send.at[number],
            self.recv.at[dst[0] * 2 + dst[1]],
            way,
        )

    def up(self, k):
        return self.site(k - 1, "up", (k - 1, 0), (k, 0))

    def down(self, k):
        return self.site(2 + k, "down", ((5 - k) % 4, 0), (4 - k, 0))

    def across(self, k):
        return self.site(6 + k, "y", (k, 0), (k, 1))

    def got(self, k, y):
        wait_got(self.g.at[k, y], self.send.at[0], self.recv.at[k * 2 + y], self.place)

    def t1(self):
        z = self.place.z
        when(z < 3, lambda: self.up(1).start())
        when(z > 0, lambda: self.down(1).start())
        self.across(0).start()

    def t2(self):
        z = self.place.z

        def low():
            self.got(1, 0)
            when(z < 3, lambda: self.up(2).start())
            self.across(1).start()

        def high():
            self.got(3, 0)
            when(z > 0, lambda: self.down(2).start())
            self.across(3).start()

        when(z >= 1, low)
        when(z <= 2, high)

    def t3(self):
        z = self.place.z
        self.got(2, 0)
        when(z == 2, lambda: self.up(3).start())
        when(z == 1, lambda: self.down(3).start())
        self.across(2).start()

    def t4(self):
        z = self.place.z

        def bottom():
            self.got(1, 0)
            self.across(1).start()

        def top():
            self.got(3, 0)
            self.across(3).start()

        when(z == 0, bottom)
        when(z == 3, top)

    def done(self):
        z = self.place.z
        for k in range(4):
            self.got(k, 1)
        when(z < 3, lambda: self.up(1).wait_send())
        when(z > 0, lambda: self.down(1).wait_send())
        when((z >= 1) & (z < 3), lambda: self.up(2).wait_send())
        when((z >= 1) & (z < 3), lambda: self.down(2).wait_send())
        when(z == 2, lambda: self.up(3).wait_send())
        when(z == 1, lambda: self.down(3).wait_send())
        for k in range(4):
            self.across(k).wait_send()


class GatherY:
    def __init__(self, place, g, send, recv):
        self.place, self.g, self.send, self.recv = place, g, send, recv

    def site(self, number, way, src, dst):
        return self.place.copy(self.g.at[src], self.g.at[dst], self.send.at[number], self.recv.at[dst], way)

    def up(self, k):
        return self.site(k - 1, "up", k - 1, k)

    def down(self, k):
        return self.site(2 + k, "down", (5 - k) % 4, 4 - k)

    def across(self):
        return self.place.copy(self.g.at[0, 0], self.g.at[0, 1], self.send.at[6], self.recv.at[4], "y")

    def got(self, k):
        wait_got(self.g.at[k], self.send.at[0], self.recv.at[k], self.place)

    def t1(self):
        self.across().start()

    def t2(self):
        z = self.place.z
        wait_got(self.g.at[0, 1], self.send.at[0], self.recv.at[4], self.place)
        when(z < 3, lambda: self.up(1).start())
        when(z > 0, lambda: self.down(1).start())

    def t3(self):
        z = self.place.z

        def low():
            self.got(1)
            when(z < 3, lambda: self.up(2).start())

        def high():
            self.got(3)
            when(z > 0, lambda: self.down(2).start())

        when(z >= 1, low)
        when(z <= 2, high)

    def t4(self):
        z = self.place.z
        self.got(2)
        when(z == 2, lambda: self.up(3).start())
        when(z == 1, lambda: self.down(3).start())

    def done(self):
        z = self.place.z
        when(z == 0, lambda: self.got(1))
        when(z == 3, lambda: self.got(3))
        when(z < 3, lambda: self.up(1).wait_send())
        when(z > 0, lambda: self.down(1).wait_send())
        when((z >= 1) & (z < 3), lambda: self.up(2).wait_send())
        when((z >= 1) & (z < 3), lambda: self.down(2).wait_send())
        when(z == 2, lambda: self.up(3).wait_send())
        when(z == 1, lambda: self.down(3).wait_send())
        self.across().wait_send()


def up_to_f32(condition, ref):
    return jnp.where(condition, ref[...].astype(f32), 0.0)


class ReduceY:
    def __init__(self, place, part, over, ups, downs, send, recv):
        self.place, self.part, self.over, self.ups, self.downs = place, part, over, ups, downs
        self.send, self.recv = send, recv

    def across(self, k):
        return self.place.copy(self.part.at[k, 1], self.over.at[k], self.send.at[6 + k], self.recv.at[7 + k], "y")

    def up(self, s):
        return self.place.copy(
            self.part.at[s, 0], self.ups.at[s - 1], self.send.at[2 * s - 2], self.recv.at[s], "up"
        )

    def down(self, s):
        return self.place.copy(
            self.part.at[4 - s, 0], self.downs.at[s - 1], self.send.at[2 * s - 1], self.recv.at[3 + s], "down"
        )

    def got_over(self, k):
        wait_got(self.over.at[k], self.send.at[0], self.recv.at[7 + k], self.place)

    def got_up(self, s):
        wait_got(self.ups.at[s - 1], self.send.at[0], self.recv.at[s], self.place)

    def got_down(self, s):
        wait_got(self.downs.at[s - 1], self.send.at[0], self.recv.at[3 + s], self.place)

    def local(self, k):
        return self.part[k, 0].astype(f32) + self.over[k].astype(f32)

    def store(self, k, value):
        self.part[k, 0] = value.astype(bf16)

    def t1(self):
        for k in (1, 3, 2, 0):
            self.across(k).start()

    def t2(self):
        z = self.place.z

        def bottom():
            self.got_over(1)
            self.store(1, self.local(1))
            self.up(1).start()

        def top():
            self.got_over(3)
            self.store(3, self.local(3))
            self.down(1).start()

        when(z == 0, bottom)
        when(z == 3, top)

    def t3(self):
        z = self.place.z
        self.got_over(2)
        when(z == 1, lambda: self.got_up(1))
        when(z == 2, lambda: self.got_down(1))
        self.store(
            2, self.local(2) + up_to_f32(z == 1, self.ups.at[0]) + up_to_f32(z == 2, self.downs.at[0])
        )
        when(z <= 1, lambda: self.up(2).start())
        when(z >= 2, lambda: self.down(2).start())

    def t4(self):
        z = self.place.z

        def low():
            self.got_over(3)
            when(z >= 1, lambda: self.got_up(2))
            self.store(3, self.local(3) + up_to_f32(z >= 1, self.ups.at[1]))
            self.up(3).start()

        def high():
            self.got_over(1)
            when(z <= 2, lambda: self.got_down(2))
            self.store(1, self.local(1) + up_to_f32(z <= 2, self.downs.at[1]))
            self.down(3).start()

        when(z <= 2, low)
        when(z >= 1, high)

    def done(self):
        z = self.place.z
        self.got_over(0)
        when(z >= 1, lambda: self.got_up(3))
        when(z <= 2, lambda: self.got_down(3))
        when(z == 0, lambda: self.up(1).wait_send())
        when(z == 3, lambda: self.down(1).wait_send())
        when(z <= 1, lambda: self.up(2).wait_send())
        when(z >= 2, lambda: self.down(2).wait_send())
        when(z <= 2, lambda: self.up(3).wait_send())
        when(z >= 1, lambda: self.down(3).wait_send())
        for k in range(4):
            self.across(k).wait_send()

    def total(self):
        z = self.place.z
        return self.local(0) + up_to_f32(z >= 1, self.ups.at[2]) + up_to_f32(z <= 2, self.downs.at[2])


class ReduceZ:
    def __init__(self, place, part, over, ups, downs, send, recv):
        self.place, self.part, self.over, self.ups, self.downs = place, part, over, ups, downs
        self.send, self.recv = send, recv

    def across(self):
        return self.place.copy(self.part.at[0, 1], self.over, self.send.at[0], self.recv.at[0], "y")

    def up(self, s):
        return self.place.copy(self.part.at[s], self.ups.at[s - 1], self.send.at[2 * s - 1], self.recv.at[s], "up")

    def down(self, s):
        return self.place.copy(
            self.part.at[4 - s], self.downs.at[s - 1], self.send.at[2 * s], self.recv.at[3 + s], "down"
        )

    got_up = ReduceY.got_up
    got_down = ReduceY.got_down

    def add(self, k, *more):
        value = self.part[k].astype(f32)
        for term in more:
            value = value + term
        self.part[k] = value.astype(bf16)

    def t1(self):
        z = self.place.z
        when(z == 0, lambda: self.up(1).start())
        when(z == 3, lambda: self.down(1).start())

    def t2(self):
        z = self.place.z

        def low():
            self.got_up(1)
            self.add(2, self.ups[0].astype(f32))

        def high():
            self.got_down(1)
            self.add(2, self.downs[0].astype(f32))

        when(z == 1, low)
        when(z == 2, high)
        when(z <= 1, lambda: self.up(2).start())
        when(z >= 2, lambda: self.down(2).start())

    def t3(self):
        z = self.place.z

        def low():
            self.got_up(2)
            self.add(3, self.ups[1].astype(f32))

        def high():
            self.got_down(2)
            self.add(1, self.downs[1].astype(f32))

        when((z >= 1) & (z <= 2), low)
        when((z >= 1) & (z <= 2), high)
        when(z <= 2, lambda: self.up(3).start())
        when(z >= 1, lambda: self.down(3).start())

    def t4(self):
        z = self.place.z
        when(z >= 1, lambda: self.got_up(3))
        when(z <= 2, lambda: self.got_down(3))
        value = self.part[0, 1].astype(f32)
        value = value + up_to_f32(z >= 1, self.ups.at[2, 1]) + up_to_f32(z <= 2, self.downs.at[2, 1])
        self.part[0, 1] = value.astype(bf16)
        self.across().start()

    def done(self):
        wait_got(self.over, self.send.at[0], self.recv.at[0], self.place)
        z = self.place.z
        when(z == 0, lambda: self.up(1).wait_send())
        when(z == 3, lambda: self.down(1).wait_send())
        when(z <= 1, lambda: self.up(2).wait_send())
        when(z >= 2, lambda: self.down(2).wait_send())
        when(z <= 2, lambda: self.up(3).wait_send())
        when(z >= 1, lambda: self.down(3).wait_send())
        self.across().wait_send()

    def total(self):
        z = self.place.z
        value = self.part[0, 0].astype(f32) + self.over[...].astype(f32)
        return value + up_to_f32(z >= 1, self.ups.at[2, 0]) + up_to_f32(z <= 2, self.downs.at[2, 0])


class FramesSum:
    def __init__(self, place, sent, kept, from_core, from_x, sems, free, number):
        self.place, self.sent, self.kept, self.from_core, self.from_x = place, sent, kept, from_core, from_x
        self.sems, self.free, self.number = sems, free, number

    def core(self, j):
        return self.place.copy(self.sent[j], self.from_core[j], self.sems.at[0, j], self.sems.at[1, j], "core")

    def x(self, j):
        return self.place.copy(self.kept[j].at[1], self.from_x[j], self.sems.at[2, j], self.sems.at[3, j], "x")

    def out(self, j, outs, p):
        return pltpu.make_async_copy(self.kept[j].at[0], outs[j].at[p], self.sems.at[4, j])

    def start(self, later):
        def credit():
            pl.semaphore_wait(self.free.at[2 * self.number], 1)

        when(later, credit)
        for j in range(2):
            self.core(j).start()

    def middle(self, later):
        for j in range(2):
            self.core(j).wait_recv()

        def credit():
            pl.semaphore_wait(self.free.at[2 * self.number + 1], 1)

        when(later, credit)
        for j in range(2):
            kept, got = self.kept[j], self.from_core[j]
            kept[1] = (kept[1].astype(f32) + got[1].astype(f32)).astype(bf16)
            self.x(j).start()
        for j in range(2):
            self.core(j).wait_send()

    def finish(self, outs, p, more):
        for j in range(2):
            self.x(j).wait_recv()
            kept = self.kept[j]
            total = kept[0].astype(f32) + self.from_core[j][0].astype(f32) + self.from_x[j][...].astype(f32)
            kept[0] = total.astype(bf16)
            self.out(j, outs, p).start()

        def credit():
            for k, way in enumerate(("core", "x")):
                pl.semaphore_signal(
                    self.free.at[2 * self.number + k], inc=1, device_id=self.place.device(way), device_id_type=MESH
                )

        when(more, credit)
        for j in range(2):
            self.x(j).wait_send()

    def drained(self, outs, p):
        for j in range(2):
            self.out(j, outs, p).wait()


GIN_REDUCE = ReduceY
BACK_REDUCE = ReduceY
FIRST_Y_ROWS = (0, 0, 0, 16, 16, 0, 0, 0)
COT_Y_ROWS = (16, 32, 16, 16, 16, 16, 16, 16)
FFN_Y_ROWS = (0, 0, 16, 0, 0, 16, 0, 32, 48, 48, 48, 48, 48, 48, 48, 0)
ATT_Y_ROWS = (16, 48, 48, 32, 48, 48, 48, 48, 48, 48, 48, 48, 48, 16, 0, 16)
FFN_Z_ROWS = (32, 32, 32, 32, 32, 32, 16, 16, 16, 16, 16, 16, 16, 0, 48, 48)
ATTN_Z_ROWS = (0, 0, 48, 48, 48, 48, 48, 48, 48, 0, 0, 0, 0, 0, 0, 0)

SCHEDULES = (
    (
        ("AC1", 0), ("AC3", 1), ("Fm", 3), ("RF3", 3), ("RA5", 1), ("A", 0), ("AG4", 4), ("RG5", 3),
        ("RB3", 5), ("AC2", 0), ("C", 2), ("RF4", 3), ("RA2", 0), ("AC4", 1), ("AG2", 3), ("AF2", 1),
        ("E", 4), ("RG2", 2), ("Ef", 5), ("Ff", 3), ("RA3", 0), ("Eg", 4), ("RB4", 5), ("Cg", 2),
        ("RG3", 2), ("RF5", 3), ("AF3", 1), ("RF2", 2), ("AG3", 3), ("RB2", 4), ("AC5", 1), ("Em", 4),
        ("RA4", 0), ("RB5", 5), ("K", 0), ("RG4", 2), ("AF4", 1),
    ),
    (
        ("RA5", 1), ("A", 0), ("AC3", 1), ("RF3", 3), ("Fm", 3), ("AF2", 1), ("Ef", 5), ("AG4", 4),
        ("RG5", 3), ("AC4", 1), ("RA2", 0), ("RB3", 5), ("RF4", 3), ("C", 2), ("AF3", 1), ("RA3", 0),
        ("AG2", 3), ("E", 4), ("RG2", 2), ("RB4", 5), ("AC1", 0), ("RA4", 0), ("AC5", 1), ("AC2", 0),
        ("AF4", 1), ("Ff", 3), ("RF5", 3), ("Eg", 4), ("RG3", 2), ("RF2", 2), ("Cg", 2), ("Em", 4),
        ("AG3", 3), ("RB5", 5), ("K", 0), ("RG4", 2), ("RB2", 4),
    ),
    (
        ("Fm", 3), ("RF3", 3), ("RA5", 1), ("AC1", 0), ("AG4", 4), ("A", 0), ("RA2", 0), ("RG5", 3),
        ("C", 2), ("RB3", 5), ("Ef", 5), ("RF4", 3), ("AF2", 1), ("E", 4), ("AC2", 0), ("Eg", 4),
        ("AF3", 1), ("AC3", 1), ("RG2", 2), ("RB4", 5), ("AG2", 3), ("Em", 4), ("Ff", 3), ("AC4", 1),
        ("RA3", 0), ("RG3", 2), ("RF2", 2), ("Cg", 2), ("AF4", 1), ("AG3", 3), ("RG4", 2), ("RA4", 0),
        ("RF5", 3), ("RB2", 4), ("AC5", 1), ("RB5", 5), ("K", 0),
    ),
)
CHANGES = (9, 16)


class Split:
    def choose(self, i, table):
        self.chosen = {}
        for count in self.pairs:
            chosen = i < 0
            for k in range(len(table)):
                if table[k] == count:
                    chosen = chosen | (i == k)
            self.chosen[count] = chosen
        return self

    def both(self, run):
        for count, pair in self.pairs.items():

            def each(pair=pair):
                for part in pair:
                    run(part)

            when(self.chosen[count], each)

    def t1(self):
        self.both(lambda part: part.t1())

    def t2(self):
        self.both(lambda part: part.t2())

    def t3(self):
        self.both(lambda part: part.t3())

    def t4(self):
        self.both(lambda part: part.t4())

    def done(self):
        self.both(lambda part: part.done())


class SplitGather(Split):
    def __init__(self, place, g, send, recv, table, rows=0):
        def cut(start, size):
            return g.at[(slice(None), slice(None)) + (slice(None),) * rows + (pl.ds(start, size),)]

        def pair(count, local):
            runs = []
            if count > 0:
                runs.append(GatherY(place, cut(0, count), send.at[0], recv.at[0]))
            if count < local:
                runs.append(GatherZ(place, cut(count, local - count), send.at[1], recv.at[1]))
            return runs

        self.pairs = {count: pair(count, g.shape[2 + rows]) for count in sorted(set(table))}


class SplitReduce(Split):
    def __init__(self, place, part, over, ups, downs, send, recv, table):
        self.place, self.part, self.over, self.ups, self.downs = place, part, over, ups, downs
        local = part.shape[2]

        def pair(count):
            first, rest = pl.ds(0, count), pl.ds(count, local - count)
            runs = []
            if count > 0:
                runs.append(
                    ReduceZ(
                        place, part.at[:, :, first], over.at[0, first], ups.at[:, :, first], downs.at[:, :, first],
                        send.at[0], recv.at[0],
                    )
                )
            if count < local:
                runs.append(
                    ReduceY(
                        place, part.at[:, :, rest], over.at[:, rest], ups.at[:, 0, rest], downs.at[:, 0, rest],
                        send.at[1], recv.at[1],
                    )
                )
            return runs

        self.pairs = {count: pair(count) for count in sorted(set(table))}

    def total(self):
        z = self.place.z
        value = self.part[0, 0].astype(f32) + self.over[0].astype(f32)
        return value + up_to_f32(z >= 1, self.ups.at[2, 0]) + up_to_f32(z <= 2, self.downs.at[2, 0])


class GainSum:
    def __init__(self, place, pieces, got, send, recv):
        self.place, self.pieces, self.got, self.send, self.recv = place, pieces, got, send, recv

    def hop(self, k):
        ways = ("core", "x", "y", "pair", "far")
        sources = (self.pieces.at[1], self.pieces.at[0].at[1], self.pieces.at[0].at[0])
        src = sources[min(k, 2)]
        if k == 0:
            dst = self.got.at[pl.ds(0, 2)]
        else:
            dst = self.got.at[k + 1]
        return self.place.copy(src, dst, self.send.at[k], self.recv.at[k], ways[k])

    def start(self):
        self.hop(0).start()

    def next(self, k):
        self.hop(k).wait()
        if k == 0:
            self.pieces[0] = self.pieces[0] + self.got[0:2]
        else:
            self.pieces[0, 0] = self.pieces[0, 0] + self.got[k + 1]
        if k < 4:
            self.hop(k + 1).start()


def layer_kernel(
    x_ref, cot_ref, mask_ref, gains_ref, in_w, out_w, gu_w, dn_w,
    out_hbm, ingrad_hbm, gu_hbm, dn_hbm, iw_hbm, ow_hbm, gain_out, rows_hbm, cot_hbm,
    g_ffn, g_att, cot_v, p_attn, p_gin, p_ffn, p_back,
    over_attn, over_gin, over_ffn, over_back, ups_attn, ups_gin, ups_ffn, ups_back,
    downs_attn, downs_gin, downs_ffn, downs_back,
    q_s, k_s, v_s, mixed_s, dk_s, dv_s, sc, dp,
    gu_v, dn_v, owa_v, owe_v, iw_v, xb,
    act_s, gg_s, gup_s, gmixed_s, gproj_s, hmid_s, ghmid_s, stage, gain_s, gain_pieces, gain_got,
    gu_sent, gu_kept, gu_core, gu_x, dn_sent, dn_kept, dn_core, dn_x,
    iw_sent, iw_kept, iw_core, iw_x, ow_sent, ow_kept, ow_core, ow_x,
    sem_first, sem_first_got, sem_gather, sem_gather_got, sem_reduce, sem_reduce_got, sem_split, sem_split_got,
    sem_grad_ffn, sem_grad_att, sem_gain, sem_local, credits, free,
):
    place = Place()
    z, f = place.z, place.f
    positions, local, depth = x_ref.shape
    rows = ZN * YN * local
    last = positions - 1
    width = q_s.shape[-1]
    hidden = dn_v.shape[0]
    half = rows // 2
    quarter = depth // 4
    mask = mask_ref[...]
    scale = HDIM ** (-0.5)
    pairs_of = positions // 2

    def load(src, dst, number):
        return pltpu.make_async_copy(src, dst, sem_local.at[number])

    def load_owa(p):
        return load(out_w.at[p], owa_v, 0)

    def load_owe(p):
        return load(out_w.at[p], owe_v, 1)

    def load_iw(p, slot):
        return load(in_w.at[p], iw_v.at[slot], 2 + slot)

    def load_gu(p):
        return load(gu_w.at[p], gu_v, 4)

    def load_dn(p):
        return load(dn_w.at[p], dn_v, 5)

    def load_rows(p, dst, number):
        return load(rows_hbm.at[p // 2, :, :, p % 2], dst, number)

    def load_cot(p):
        return load(cot_hbm.at[p // 2, :, :, p % 2], cot_v, 9)

    def own_cot(j):
        return load(g_ffn.at[j // 4, j % 4], cot_hbm.at[j, 0, 0], 16 + j)

    def own_rows(j):
        return load(g_att.at[j // 4, j % 4], rows_hbm.at[j, 0, 0], 16 + pairs_of + j)

    barrier = pltpu.get_barrier_semaphore()

    def greet(way):
        pl.semaphore_signal(barrier, inc=1, device_id=place.device(way), device_id_type=MESH)

    for way in ("y", "core", "x", "far"):
        greet(way)
    when(z < 3, lambda: greet("up"))
    when(z > 0, lambda: greet("down"))
    pl.semaphore_wait(barrier, 4 + (z < 3).astype(jnp.int32) + (z > 0).astype(jnp.int32))

    groups = pairs_of

    def gain_of(which, p):
        return gains_ref[which, pl.ds(p, 1), :]

    def normalise(p, c):
        residual = x_ref[p].astype(f32)
        value = residual * inverse_rms(residual) * gain_of(0, p)
        g_att[p // 8, (p % 8) // 2, p % 2] = value.astype(bf16)
        return c

    firsts = [
        SplitGather(place, rows_hbm.at[g], sem_first.at[g], sem_first_got.at[g], FIRST_Y_ROWS[g : g + 1], 1).choose(
            g, FIRST_Y_ROWS
        )
        for g in range(groups)
    ]

    def cot_gather(j, which):
        sems = sem_gather.at[2, which], sem_gather_got.at[2, which]
        return SplitGather(place, cot_hbm.at[pairs_of - 1 - j], *sems, COT_Y_ROWS, 1).choose(j, COT_Y_ROWS)

    for g in range(groups):
        lax.fori_loop(2 * g, 2 * g + 2, normalise, 0)
        own_rows(g).start()
        own_rows(g).wait()
        firsts[g].t1()

    def masked(p, c):
        g_ffn[p // 8, (p % 8) // 2, p % 2] = (mask * cot_ref[p].astype(f32)).astype(bf16)
        return c

    lax.fori_loop(0, positions, masked, 0)
    for j in range(pairs_of):
        own_cot(j).start()
    load_owa(last).start()
    load_gu(last).start()
    load_dn(last).start()
    load_iw(0, 0).start()
    dk_s[...] = jnp.zeros_like(dk_s)
    dv_s[...] = jnp.zeros_like(dv_s)

    def project(p, c):
        slot = lax.rem(p, 2)
        load_rows(p, g_ffn.at[slot], 6 + slot).wait()
        load_iw(p, slot).wait()

        @pl.when(p < last)
        def _():
            load_iw(p + 1, 1 - slot).start()

        block = g_ffn[slot].reshape(rows, depth)
        q_s[p] = (dot(block, iw_v[slot, 0], NN).astype(bf16) * scale).astype(bf16)
        k_s[p] = dot(block, iw_v[slot, 1], NN).astype(bf16)
        v_s[p] = dot(block, iw_v[slot, 2], NN).astype(bf16)
        return c

    for g in range(groups):
        firsts[g].t2()
    for g in range(groups):
        firsts[g].t3()
    for g in range(groups):
        firsts[g].t4()
    for j in range(pairs_of):
        own_cot(j).wait()
    for g in range(groups):
        firsts[g].done()
        load_rows(2 * g, g_ffn.at[0], 6).start()
        load_rows(2 * g + 1, g_ffn.at[1], 7).start()
        lax.fori_loop(2 * g, 2 * g + 2, project, 0)
    load_owe(last).start()
    load_iw(last, 0).start()
    load_rows(last, xb, 8).start()

    row = lax.broadcasted_iota(jnp.int32, (2 * width, width), 0)
    column = lax.broadcasted_iota(jnp.int32, (2 * width, width), 1)
    ones = jnp.where((row % width) // HDIM == column // HDIM, 1.0, 0.0).astype(bf16)

    def per_head(product):
        high = product.astype(bf16)
        low = (product - high.astype(f32)).astype(bf16)
        return dot(jnp.concatenate([high, low], axis=1), ones, NN)

    def scores_of(p, q, at):
        def two(jj, top):
            first = per_head(q * k_s[2 * jj, at].astype(f32))
            second = per_head(q * k_s[2 * jj + 1, at].astype(f32))
            second = jnp.where(2 * jj + 1 <= p, second, -1e30)
            sc[2 * jj], sc[2 * jj + 1] = first, second
            return jnp.maximum(top, jnp.maximum(first, second))

        return lax.fori_loop(0, p // 2 + 1, two, jnp.full((half, width), -1e30, f32))

    def attend_one(p):
        pairs = p // 2 + 1
        for part in range(2):
            at = pl.ds(part * half, half)
            q = q_s[p, at].astype(f32)
            top = scores_of(p, q, at)

            def raise_two(jj, total):
                for t in range(2):
                    raised = jnp.exp(sc[2 * jj + t] - top)
                    sc[2 * jj + t] = raised
                    total = total + raised
                return total

            total = lax.fori_loop(0, pairs, raise_two, jnp.zeros((half, width), f32))
            factor = 1.0 / total

            def mix_two(jj, out):
                for t in range(2):
                    probs = (sc[2 * jj + t] * factor).astype(bf16).astype(f32)
                    out = out + probs * v_s[2 * jj + t, at].astype(f32)
                return out

            out = lax.fori_loop(0, pairs, mix_two, jnp.zeros((half, width), f32))
            mixed_s[p, at] = out.astype(bf16)

    def attend_back_one(p):
        pairs = p // 2 + 1
        for part in range(2):
            at = pl.ds(part * half, half)
            q = q_s[p, at].astype(f32)
            g = gmixed_s[at].astype(f32)
            top = scores_of(p, q, at)

            def raise_two(jj, carry):
                total, weighted = carry
                for t in range(2):
                    raised = jnp.exp(sc[2 * jj + t] - top)
                    sc[2 * jj + t] = raised
                    grad_probs = per_head(g * v_s[2 * jj + t, at].astype(f32))
                    dp[2 * jj + t] = grad_probs
                    total = total + raised
                    weighted = weighted + raised * grad_probs
                return total, weighted

            zero = jnp.zeros((half, width), f32)
            total, weighted = lax.fori_loop(0, pairs, raise_two, (zero, zero))
            factor = 1.0 / total
            centre = weighted * factor

            def back_two(jj, dq):
                for t in range(2):
                    j = 2 * jj + t
                    probs = sc[j] * factor
                    grad = (probs * (dp[j] - centre)).astype(bf16).astype(f32)
                    dq = dq + grad * k_s[j, at].astype(f32)
                    dk_s[j, at] = dk_s[j, at] + grad * q
                    dv_s[j, at] = dv_s[j, at] + probs.astype(bf16).astype(f32) * g
                return dq

            dq = lax.fori_loop(0, pairs, back_two, zero)
            gproj_s[0, at] = (dq * scale).astype(bf16)
        gproj_s[1] = dk_s[p].astype(bf16)
        gproj_s[2] = dv_s[p].astype(bf16)

    blocks = (ZN, YN, local, depth)
    grad_ffn = FramesSum(
        place, (gu_sent, dn_sent), (gu_kept, dn_kept), (gu_core, dn_core), (gu_x, dn_x), sem_grad_ffn, free, 0
    )
    grad_att = FramesSum(
        place, (iw_sent, ow_sent), (iw_kept, ow_kept), (iw_core, ow_core), (iw_x, ow_x), sem_grad_att, free, 1
    )
    ffn_outs, att_outs = (gu_hbm, dn_hbm), (iw_hbm, ow_hbm)
    gain_sum = GainSum(place, gain_pieces, gain_got, sem_gain.at[0], sem_gain.at[1])

    def out_copy(p):
        return pltpu.make_async_copy(stage.at[0], out_hbm.at[p], sem_local.at[14])

    def ingrad_copy(p):
        return pltpu.make_async_copy(stage.at[1], ingrad_hbm.at[p], sem_local.at[15])

    class Position:
        def __init__(self, i):
            self.i = i
            self.p = last - i
            self.par = lax.rem(i + 16, 2)
            self.ring = lax.rem(i + 16, 4)

        def gather(self, g, number, table):
            par = self.par
            sems = sem_gather.at[number, par], sem_gather_got.at[number, par]
            return SplitGather(place, g.at[par], *sems, table).choose(self.i, table)

        def reduce(self, kind, part, over, ups, downs, number):
            par = self.par
            return kind(
                place, part, over.at[par], ups.at[par], downs.at[par],
                sem_reduce.at[number, par], sem_reduce_got.at[number, par],
            )

        def AF(self):
            return self.gather(g_ffn, 0, FFN_Y_ROWS)

        def AG(self):
            return self.gather(g_att, 1, ATT_Y_ROWS)

        def split(self, part, over, ups, downs, number, table):
            par = self.par
            event = SplitReduce(
                place, part, over.at[par], ups.at[par], downs.at[par],
                sem_split.at[number, par], sem_split_got.at[number, par], table,
            )
            return event.choose(self.i, table)

        def RA(self):
            return self.split(p_attn, over_attn, ups_attn, downs_attn, 1, ATTN_Z_ROWS)

        def RG(self):
            return self.reduce(GIN_REDUCE, p_gin, over_gin, ups_gin, downs_gin, 1)

        def RF(self):
            return self.split(p_ffn.at[self.par], over_ffn, ups_ffn, downs_ffn, 0, FFN_Z_ROWS)

        def RB(self):
            return self.reduce(BACK_REDUCE, p_back.at[self.par], over_back, ups_back, downs_back, 3)

        def do_A(self):
            p = self.p
            attend_one(p)
            load_owa(p).wait()
            p_attn[...] = dot(mixed_s[p], owa_v[...], NN).astype(bf16).reshape(blocks)
            self.RA().t1()
            when(p > 0, lambda: load_owa(p - 1).start())

        def do_RA5(self):
            p, total = self.p, self.RA()
            total.done()
            hmid = x_ref[p].astype(f32) + mask * total.total()
            hmid_s[self.ring] = hmid
            g_ffn[self.par, 0, 0] = (hmid * inverse_rms(hmid) * gain_of(1, p)).astype(bf16)
            self.AF().t1()

        def do_C(self):
            p, par = self.p, self.par
            self.AF().done()
            load_gu(p).wait()
            load_dn(p).wait()
            load_cot(p).wait()
            x = g_ffn[par].reshape(rows, depth)
            g = cot_v[...].reshape(rows, depth)
            for h in range(2):
                at = slice(h * hidden // 2, (h + 1) * hidden // 2)
                gate = dot(x, gu_v[0, :, at], NN)
                up = dot(x, gu_v[1, :, at], NN)
                grad_act = dot(g, dn_v[at], NT)
                sigma = 1.0 / (1.0 + jnp.exp(-gate))
                silu = gate * sigma
                act_s[:, at] = (silu * up).astype(bf16)
                gg_s[:, at] = (grad_act * up * sigma * (1.0 + gate * (1.0 - sigma))).astype(bf16)
                gup_s[:, at] = (grad_act * silu).astype(bf16)
            back = dot(gg_s[...], gu_v[0], NT) + dot(gup_s[...], gu_v[1], NT)
            p_gin[...] = back.astype(bf16).reshape(blocks)
            self.RG().t1()
            gain_s[1, pl.ds(p, 1), :] = jnp.sum(back * x.astype(f32), axis=0, keepdims=True)
            p_ffn[par] = dot(act_s[...], dn_v[...], NN).astype(bf16).reshape(blocks)
            self.RF().t1()

            @pl.when(p > 0)
            def _():
                load_gu(p - 1).start()
                load_dn(p - 1).start()

        def do_Cg(self):
            p, par = self.p, self.par

            @pl.when(p < last)
            def _():
                grad_ffn.drained(ffn_outs, p + 1)

            for r in range(4):
                at = piece_at(r, f, quarter)
                gu_to, dn_to = (gu_kept, dn_kept) if r % 2 == 0 else (gu_sent, dn_sent)
                columns = g_ffn[par, :, :, :, at].reshape(rows, quarter)
                gu_to[r // 2, 0] = dot(columns, gg_s[...], TN).astype(bf16)
                gu_to[r // 2, 1] = dot(columns, gup_s[...], TN).astype(bf16)
                dn_to[r // 2] = dot(act_s[...], cot_v[:, :, :, at].reshape(rows, quarter), TN).astype(bf16)
            grad_ffn.start(p < last)
            when(p > 0, lambda: load_cot(p - 1).start())

        def do_Fm(self):
            grad_ffn.middle(self.p < last)

        def do_Ff(self):
            grad_ffn.finish(ffn_outs, self.p, self.p > 0)

        def do_RG5(self):
            p, total = self.p, self.RG()
            total.done()
            hmid = hmid_s[self.ring]
            factor = inverse_rms(hmid)
            grad = cot_ref[p].astype(f32) + norm_back(total.total(), hmid * factor, factor, gain_of(1, p))
            ghmid_s[self.ring] = grad
            g_att[self.par, 0, 0] = (mask * grad).astype(bf16)
            self.AG().t1()

        def do_RF5(self):
            p, total = self.p, self.RF()
            total.done()

            @pl.when(p < last)
            def _():
                out_copy(p + 1).wait()

            stage[0] = (hmid_s[self.ring] + mask * total.total()).astype(bf16)
            out_copy(p).start()

        def do_E(self):
            p, par = self.p, self.par
            self.AG().done()
            load_owe(p).wait()
            load_iw(p, 0).wait()
            load_rows(p, xb, 8).wait()
            gmixed_s[...] = dot(g_att[par].reshape(rows, depth), owe_v[...], NT).astype(bf16)
            attend_back_one(p)
            back = dot(gproj_s[0], iw_v[0, 0], NT)
            back = back + dot(gproj_s[1], iw_v[0, 1], NT)
            back = back + dot(gproj_s[2], iw_v[0, 2], NT)
            p_back[par] = back.astype(bf16).reshape(blocks)
            self.RB().t1()
            gain_s[0, pl.ds(p, 1), :] = jnp.sum(back * xb[...].reshape(rows, depth).astype(f32), axis=0, keepdims=True)

            @pl.when(p == 0)
            def _():
                for r in range(4):
                    gain_pieces[r % 2, r // 2] = gain_s[:, :, piece_at(r, f, quarter)]
                gain_sum.start()

            @pl.when(p > 0)
            def _():
                load_owe(p - 1).start()
                load_iw(p - 1, 0).start()

        def do_Eg(self):
            p, par = self.p, self.par

            @pl.when(p < last)
            def _():
                grad_att.drained(att_outs, p + 1)

            for r in range(4):
                at = piece_at(r, f, quarter)
                iw_to, ow_to = (iw_kept, ow_kept) if r % 2 == 0 else (iw_sent, ow_sent)
                columns = xb[:, :, :, at].reshape(rows, quarter)
                for j in range(3):
                    iw_to[r // 2, j] = dot(columns, gproj_s[j], TN).astype(bf16)
                ow_to[r // 2] = dot(mixed_s[p], g_att[par, :, :, :, at].reshape(rows, quarter), TN).astype(bf16)
            grad_att.start(p < last)
            when(p > 0, lambda: load_rows(p - 1, xb, 8).start())

        def do_Em(self):
            grad_att.middle(self.p < last)

        def do_Ef(self):
            grad_att.finish(att_outs, self.p, self.p > 0)

        def do_RB5(self):
            p, total = self.p, self.RB()
            total.done()
            when(p == 0, lambda: gain_sum.next(3))

            @pl.when(p < last)
            def _():
                ingrad_copy(p + 1).wait()

            residual = x_ref[p].astype(f32)
            factor = inverse_rms(residual)
            grad = norm_back(total.total(), residual * factor, factor, gain_of(0, p))
            stage[1] = (ghmid_s[self.ring] + grad).astype(bf16)
            ingrad_copy(p).start()

        def do_RB2(self):
            self.RB().t2()
            when(self.p == 0, lambda: gain_sum.next(0))

        def do_RB3(self):
            self.RB().t3()
            when(self.p == 0, lambda: gain_sum.next(1))

        def do_RB4(self):
            self.RB().t4()
            when(self.p == 0, lambda: gain_sum.next(2))

        def runs(self):
            ticks = {}
            for name, event in (
                ("RA", self.RA), ("RG", self.RG), ("RF", self.RF), ("AF", self.AF), ("AG", self.AG),
            ):
                ticks[name + "2"] = lambda event=event: event().t2()
                ticks[name + "3"] = lambda event=event: event().t3()
                ticks[name + "4"] = lambda event=event: event().t4()
            return ticks | {
                "A": self.do_A, "RA5": self.do_RA5, "C": self.do_C, "Cg": self.do_Cg, "Fm": self.do_Fm,
                "Ff": self.do_Ff, "RG5": self.do_RG5, "RF5": self.do_RF5, "E": self.do_E, "Eg": self.do_Eg,
                "Em": self.do_Em, "Ef": self.do_Ef, "RB2": self.do_RB2, "RB3": self.do_RB3, "RB4": self.do_RB4,
                "RB5": self.do_RB5,
            }

    def cot_runs(j):
        event = cot_gather(j, lax.rem(j + 16, 2))

        def done():
            event.done()
            when(j == 0, lambda: load_cot(last).start())

        return {"AC1": event.t1, "AC2": event.t2, "AC3": event.t3, "AC4": event.t4, "AC5": done}

    def tell(number, way):
        pl.semaphore_signal(credits.at[number], inc=1, device_id=place.device(way), device_id_type=MESH)

    def tell_all():
        tell(0, "y")
        when(z < 3, lambda: tell(1, "up"))
        when(z > 0, lambda: tell(2, "down"))

    steps = positions + max(delay for name, delay in SCHEDULES[0] if name[:2] != "AC")
    tell_all()

    def step(low, high, schedule, s, c):
        pl.semaphore_wait(credits.at[0], 1)
        when(z > 0, lambda: pl.semaphore_wait(credits.at[1], 1))
        when(z < 3, lambda: pl.semaphore_wait(credits.at[2], 1))
        for name, delay in schedule:
            if name == "K":
                when(s < steps - 1, tell_all)
            elif high <= delay or low >= delay + (pairs_of if name[:2] == "AC" else positions):
                continue
            elif name[:2] == "AC":
                j = s - delay
                when((j >= 0) & (j < pairs_of), cot_runs(j)[name])
            else:
                when((s >= delay) & (s <= last + delay), Position(s - delay).runs()[name])
        return c

    bounds = (0,) + CHANGES + (steps,)
    for low, high, schedule in zip(bounds, bounds[1:], SCHEDULES):
        lax.fori_loop(low, high, functools.partial(step, low, high, schedule), 0)
    gain_sum.next(4)
    gain_out[...] = gain_pieces[0, 0] / gains_ref[:, :, piece_at(0, f, quarter)]
    grad_ffn.drained(ffn_outs, 0)
    grad_att.drained(att_outs, 0)
    out_copy(0).wait()
    ingrad_copy(0).wait()


def layer(x, cot, mask, gains, in_weight, out_weight, gate_up, down):
    positions, local, depth = x.shape
    width, hidden = out_weight.shape[1], down.shape[1]
    rows = ZN * YN * local
    quarter = depth // 4
    block = (local, depth)
    groups = positions // 2

    def vm(*shape, dtype=bf16):
        return pltpu.VMEM(shape, dtype)

    def hbm(*shape, dtype=bf16):
        return jax.ShapeDtypeStruct(shape, dtype)

    everything = (ZN, YN) + block
    scratch = (
        [vm(2, *everything)] * 2
        + [vm(*everything)] * 3
        + [vm(2, *everything)] * 2
        + [vm(2, ZN, *block)] * 4
        + [vm(2, 3, YN, *block), vm(2, 3, *block), vm(2, 3, YN, *block), vm(2, 3, *block)] * 2
        + [vm(positions, rows, width)] * 4
        + [vm(positions, rows, width, dtype=f32)] * 2
        + [vm(positions, rows // 2, width, dtype=f32)] * 2
        + [vm(2, depth, hidden), vm(hidden, depth), vm(width, depth), vm(width, depth)]
        + [vm(2, 3, depth, width), vm(*everything)]
        + [vm(rows, hidden)] * 3
        + [vm(rows, width), vm(3, rows, width)]
        + [vm(4, *block, dtype=f32)] * 2
        + [vm(2, *block)]
        + [vm(2, positions, depth, dtype=f32)]
        + [vm(2, 2, 2, positions, quarter, dtype=f32), vm(6, 2, positions, quarter, dtype=f32)]
        + [vm(2, 2, quarter, hidden)] * 3
        + [vm(2, quarter, hidden)]
        + [vm(2, hidden, quarter)] * 3
        + [vm(hidden, quarter)]
        + [vm(2, 3, quarter, width)] * 3
        + [vm(3, quarter, width)]
        + [vm(2, width, quarter)] * 3
        + [vm(width, quarter)]
        + [
            pltpu.SemaphoreType.DMA((groups, 2, 10)),
            pltpu.SemaphoreType.DMA((groups, 2, 8)),
            pltpu.SemaphoreType.DMA((3, 2, 2, 10)),
            pltpu.SemaphoreType.DMA((3, 2, 2, 8)),
            pltpu.SemaphoreType.DMA((4, 2, 10)),
            pltpu.SemaphoreType.DMA((4, 2, 11)),
            pltpu.SemaphoreType.DMA((2, 2, 2, 10)),
            pltpu.SemaphoreType.DMA((2, 2, 2, 11)),
            pltpu.SemaphoreType.DMA((5, 2)),
            pltpu.SemaphoreType.DMA((5, 2)),
            pltpu.SemaphoreType.DMA((2, 5)),
            pltpu.SemaphoreType.DMA((16 + positions,)),
            pltpu.SemaphoreType.REGULAR((3,)),
            pltpu.SemaphoreType.REGULAR((4,)),
        ]
    )
    in_vmem = pl.BlockSpec(memory_space=pltpu.VMEM)
    anywhere = pl.BlockSpec(memory_space=pl.ANY)
    return pl.pallas_call(
        layer_kernel,
        in_specs=[in_vmem] * 4 + [anywhere] * 4,
        out_specs=[anywhere] * 6 + [in_vmem, anywhere, anywhere],
        out_shape=[
            hbm(positions, *block),
            hbm(positions, *block),
            hbm(positions, 2, quarter, hidden),
            hbm(positions, hidden, quarter),
            hbm(positions, 3, quarter, width),
            hbm(positions, width, quarter),
            hbm(2, positions, quarter, dtype=f32),
            hbm(positions // 2, ZN, YN, 2, *block),
            hbm(positions // 2, ZN, YN, 2, *block),
        ],
        scratch_shapes=scratch,
        compiler_params=pltpu.CompilerParams(
            collective_id=0, has_side_effects=True, vmem_limit_bytes=KERNEL_VMEM_BYTES
        ),
        name="layer",
    )(x, cot, mask, gains, in_weight, out_weight, gate_up, down)


def widen_kernel(*refs):
    half = len(refs) // 2
    for narrow, wide in zip(refs[:half], refs[half:]):
        wide[...] = narrow[...].astype(f32)


def widened(*arrays):
    def spec(a):
        rank = a.ndim
        return pl.BlockSpec((1,) + a.shape[1:], lambda i: (i,) + (0,) * (rank - 1))

    return pl.pallas_call(
        widen_kernel,
        grid=(arrays[0].shape[0],),
        in_specs=[spec(a) for a in arrays],
        out_specs=[spec(a) for a in arrays],
        out_shape=[jax.ShapeDtypeStruct(a.shape, f32) for a in arrays],
        compiler_params=pltpu.CompilerParams(vmem_limit_bytes=KERNEL_VMEM_BYTES),
        name="widen",
    )(*arrays)


def body_in_one(inputs, counts, norm_gains, in_weight, out_weight, gate_up, down_weight, cotangent):
    local = inputs.shape[0]
    ids = lax.axis_index("mp") * local + jnp.arange(local)
    valid = ids < counts[0]
    output, input_grad, g_gu, g_dn, g_in, g_out, gain_sums, _, _ = layer(
        jnp.swapaxes(inputs, 0, 1),
        jnp.swapaxes(cotangent, 0, 1),
        valid.astype(f32)[:, None],
        norm_gains,
        in_weight,
        out_weight,
        gate_up,
        down_weight,
    )
    return (
        jnp.swapaxes(output, 0, 1),
        jnp.swapaxes(input_grad, 0, 1),
        *widened(g_in, g_out, g_gu, g_dn),
        gain_sums,
    )


def solution(mesh):
    placed = (
        P(("frames", "mp"), None, None),
        P("frames"),
        P(),
        P(None, None, None, "mp"),
        P(None, "mp", None),
        P(None, None, None, "mp"),
        P(None, "mp", None),
        P(("frames", "mp"), None, None),
    )
    def local_body(*args):
        frames, group_size = lax.axis_size("frames"), lax.axis_size("mp")
        local, positions, depth = args[0].shape
        width, hidden = args[4].shape[1], args[6].shape[1]
        one = fits(frames, group_size, local, positions, depth, width, hidden)
        return (body_in_one if one else body)(*args)

    return jax.shard_map(
        local_body,
        mesh=mesh,
        in_specs=placed,
        out_specs=(
            P(("frames", "mp"), None, None),
            P(("frames", "mp"), None, None),
            P(None, None, "frames", "mp"),
            P(None, "mp", "frames"),
            P(None, None, "frames", "mp"),
            P(None, "mp", "frames"),
            P(None, None, "frames"),
        ),
        check_vma=False,
    )
```

```python
import functools
import math

import jax
import jax.numpy as jnp
from jax import lax
from jax.experimental import pallas as pl
from jax.experimental.pallas import tpu as pltpu
from jax.sharding import PartitionSpec as P

HDIM = 64
EPSILON = 1e-05
Z_CHIPS = 4
FRAME_BLOCK = 16
CHUNKS = 4
VMEM_BYTES = 56 * 1024 * 1024
KERNEL_VMEM_BYTES = 63 * 1024 * 1024

f32 = jnp.float32
bf16 = jnp.bfloat16


class Line:
    def __init__(self, total, n, stride):
        self.n = n
        self.stride = stride
        self.starts = [i for i in range(total) if (i // stride) % n == 0]

    def up(self, low, high):
        return [(s + i * self.stride, s + (i + 1) * self.stride) for s in self.starts for i in range(low, high)]

    def down(self, low, high):
        return [(s + (i + 1) * self.stride, s + i * self.stride) for s in self.starts for i in range(low, high)]

    def gather(self, own):
        n = self.n
        if n == 1:
            return [own]
        if n == 2:
            return [own, lax.ppermute(own, "mp", self.up(0, 1) + self.down(0, 1))]
        ups, downs = [own], [own]
        for k in range(1, n):
            ups.append(lax.ppermute(ups[-1], "mp", self.up(k - 1, n - 1)))
            downs.append(lax.ppermute(downs[-1], "mp", self.down(0, n - k)))
        return [own] + [ups[k] + downs[n - k] for k in range(1, n)]

    def reduce(self, term):
        n = self.n
        if n == 1:
            return [term(0)]
        if n == 2:
            return [term(0), lax.ppermute(term(1).astype(bf16), "mp", self.up(0, 1) + self.down(0, 1)).astype(f32)]
        up = down = None
        for s in range(1, n):
            send_up = term(s) if up is None else term(s) + up.astype(f32)
            send_down = term(n - s) if down is None else term(n - s) + down.astype(f32)
            up = lax.ppermute(send_up.astype(bf16), "mp", self.up(0, min(s, n - 1)))
            down = lax.ppermute(send_down.astype(bf16), "mp", self.down(n - 1 - s, n - 1))
        return [term(0), up.astype(f32), down.astype(f32)]


class Group:
    def __init__(self, size):
        self.nz = math.gcd(size, Z_CHIPS)
        self.ny = size // self.nz
        self.z = Line(size, self.nz, self.ny)
        self.y = Line(size, self.ny, 1)

    def gather(self, own, z_first):
        if z_first:
            column = jnp.stack(self.z.gather(own), axis=1)
            return jnp.stack(self.y.gather(column), axis=1)
        row = jnp.stack(self.y.gather(own), axis=1)
        return jnp.stack(self.z.gather(row), axis=2)

    def reduce(self, parts, z_first):
        if not z_first:
            if self.ny == 2:
                got = lax.ppermute(parts[1], "mp", self.y.up(0, 1) + self.y.down(0, 1))
                columns = [parts[0], got]

                def term(k):
                    return columns[0][:, k].astype(f32) + columns[1][:, k].astype(f32)

            else:
                terms = self.y.reduce(lambda k: parts[k].astype(f32))

                def term(k):
                    return sum(t[:, k] for t in terms)

            return sum(self.z.reduce(term))

        def row(k):
            return jnp.stack([part[:, k] for part in parts], axis=1).astype(f32)

        terms = self.z.reduce(row)
        return sum(self.y.reduce(lambda k: sum(t[:, k] for t in terms)))


def frames_sum(keep, send, size):
    step = 1
    while True:
        got = lax.ppermute(send, "frames", [(i, i ^ step) for i in range(size)])
        total = keep.astype(f32) + got.astype(f32)
        step *= 2
        if step == size:
            return total[:, 0]
        keep, send = total[:, 0::2], total[:, 1::2].astype(send.dtype)


def dot(a, b, dims):
    return lax.dot_general(a, b, (dims, ((), ())), preferred_element_type=f32)


NN = ((1,), (0,))
NT = ((1,), (1,))
TN = ((0,), (0,))


def params():
    return pltpu.CompilerParams(vmem_limit_bytes=VMEM_BYTES)


def cost(flops, nbytes):
    return pl.CostEstimate(flops=int(flops), bytes_accessed=int(nbytes), transcendentals=0)


def qkv_kernel(x_ref, w_ref, q_ref, k_ref, v_ref):
    x = x_ref[0]
    for c, out in enumerate((q_ref, k_ref, v_ref)):
        out[0] = dot(x, w_ref[0, c], NN).astype(bf16)


def qkv(x, weight, base):
    count, rows, depth = x.shape
    width = weight.shape[-1]
    out = jax.ShapeDtypeStruct((count, rows, width), bf16)
    return pl.pallas_call(
        qkv_kernel,
        grid=(count,),
        in_specs=[
            pl.BlockSpec((1, rows, depth), lambda i: (i, 0, 0)),
            pl.BlockSpec((1, 3, depth, width), lambda i: (base + i, 0, 0, 0)),
        ],
        out_specs=[pl.BlockSpec((1, rows, width), lambda i: (i, 0, 0))] * 3,
        out_shape=[out] * 3,
        compiler_params=params(),
        cost_estimate=cost(6 * count * rows * depth * width, 2 * count * depth * (rows + 3 * width)),
        name="qkv",
    )(x, weight)


def head_masks(rows, width):
    lane = lax.broadcasted_iota(jnp.int32, (rows, width), 1)
    return [(lane >= h * HDIM) & (lane < (h + 1) * HDIM) for h in range(width // HDIM)]


def attention_mask(count, base, columns):
    rows = count * FRAME_BLOCK
    row = lax.broadcasted_iota(jnp.int32, (rows, columns), 0)
    column = lax.broadcasted_iota(jnp.int32, (rows, columns), 1)
    same = (row % FRAME_BLOCK) == (column % FRAME_BLOCK)
    return same & (column // FRAME_BLOCK <= row // FRAME_BLOCK + base)


def block_of(refs, rows):
    pieces = [ref[:, rows, :] for ref in refs]
    pieces = [p.reshape(p.shape[0] * p.shape[1], p.shape[2]) for p in pieces]
    return pieces[0] if len(pieces) == 1 else jnp.concatenate(pieces, axis=0)


def softmax(scores):
    top = jnp.max(scores, axis=-1, keepdims=True)
    raised = jnp.exp(scores - top)
    return raised / jnp.sum(raised, axis=-1, keepdims=True)


def pick(masks, values):
    out = values[0]
    for mask, value in zip(masks[1:], values[1:]):
        out = jnp.where(mask, value, out)
    return out


def attend_kernel(base, n_kv, ny, q_ref, *refs):
    k_refs, v_refs = refs[:n_kv], refs[n_kv : 2 * n_kv]
    w_ref = refs[2 * n_kv]
    mixed_ref = refs[2 * n_kv + 1]
    part_refs = refs[2 * n_kv + 2 :]
    count, rows, width = q_ref.shape
    columns = sum(ref.shape[0] for ref in k_refs) * FRAME_BLOCK
    step = pl.program_id(0)

    @pl.when(step == 0)
    def _():
        heads = head_masks(count * FRAME_BLOCK, width)
        allowed = attention_mask(count, base, columns)

        def one(b):
            at = pl.ds(pl.multiple_of(b * FRAME_BLOCK, FRAME_BLOCK), FRAME_BLOCK)
            queries = block_of([q_ref], at) * HDIM ** (-0.5)
            keys, values = block_of(k_refs, at), block_of(v_refs, at)
            outs = []
            for head in heads:
                mine = jnp.where(head, queries, jnp.zeros_like(queries))
                scores = jnp.where(allowed, dot(mine, keys, NT), -1e30)
                outs.append(dot(softmax(scores).astype(bf16), values, NN))
            mixed_ref[:, at, :] = pick(heads, outs).astype(bf16).reshape(count, FRAME_BLOCK, width)

        lax.fori_loop(0, rows // FRAME_BLOCK, lambda b, c: (one(b), c)[1], 0, unroll=4)

    out = dot(mixed_ref[step], w_ref[0], NN)
    span = rows // ny
    for y, part in enumerate(part_refs):
        part[0] = out[y * span : (y + 1) * span].astype(bf16)


def attend(q, ks, vs, weight, base, ny):
    count, rows, width = q.shape
    depth = weight.shape[-1]
    whole = pl.BlockSpec((count, rows, width), lambda i: (0, 0, 0))
    part = jax.ShapeDtypeStruct((count, rows // ny, depth), bf16)
    n_kv = len(ks)
    return pl.pallas_call(
        functools.partial(attend_kernel, base, n_kv, ny),
        grid=(count,),
        in_specs=[whole] * (1 + 2 * n_kv) + [pl.BlockSpec((1, width, depth), lambda i: (base + i, 0, 0))],
        out_specs=[whole] + [pl.BlockSpec((1, rows // ny, depth), lambda i: (i, 0, 0))] * ny,
        out_shape=[jax.ShapeDtypeStruct(q.shape, bf16)] + [part] * ny,
        compiler_params=params(),
        cost_estimate=cost(4 * count * rows * depth * width, 2 * count * rows * (depth + (2 + 2 * n_kv) * width)),
        name="attend",
    )(q, *ks, *vs, weight)


def gradient_pieces(size, depth):
    return size if size > 1 and (depth // size) % 128 == 0 else 1


def piece_at(piece, mine, span):
    return pl.ds(pl.multiple_of((piece ^ mine) * span, span), span)


def ffn_kernel(ny, pieces, mine_ref, x_ref, g_ref, gu_ref, dn_ref, *refs):
    outs, backs = refs[:ny], refs[ny : 2 * ny]
    gain_ref = refs[2 * ny]
    grads = refs[2 * ny + 1 :]
    rows, depth = x_ref.shape[1:]
    span = rows // ny
    x, g = x_ref[0], g_ref[0]
    gate = dot(x, gu_ref[0, 0], NN)
    up = dot(x, gu_ref[0, 1], NN)
    grad_act = dot(g, dn_ref[0], NT)
    sigma = 1.0 / (1.0 + jnp.exp(-gate))
    silu = gate * sigma
    act = (silu * up).astype(bf16)
    grad_gate = (grad_act * up * sigma * (1.0 + gate * (1.0 - sigma))).astype(bf16)
    grad_up = (grad_act * silu).astype(bf16)
    out = dot(act, dn_ref[0], NN)
    for y in range(ny):
        outs[y][0] = out[y * span : (y + 1) * span].astype(bf16)
    back = dot(grad_gate, gu_ref[0, 0], NT) + dot(grad_up, gu_ref[0, 1], NT)
    for y in range(ny):
        backs[y][0] = back[y * span : (y + 1) * span].astype(bf16)
    gain_ref[0] = jnp.sum(back * x.astype(f32), axis=0, keepdims=True)
    if pieces == 1:
        grads[0][0, 0] = dot(x, grad_gate, TN).astype(bf16)
        grads[0][0, 1] = dot(x, grad_up, TN).astype(bf16)
        grads[1][0] = dot(act, g, TN).astype(bf16)
        return
    mine = mine_ref[0]
    width = depth // pieces
    for r in range(pieces):
        at = piece_at(r, mine, width)
        gu_out, dn_out = grads[r % 2], grads[2 + r % 2]
        columns = x_ref[0, :, at]
        gu_out[0, r // 2, 0] = dot(columns, grad_gate, TN).astype(bf16)
        gu_out[0, r // 2, 1] = dot(columns, grad_up, TN).astype(bf16)
        dn_out[0, r // 2] = dot(act, g_ref[0, :, at], TN).astype(bf16)


def split_specs(shape, pieces, axis):
    if pieces == 1:
        block = (1,) + shape[1:]
        return [pl.BlockSpec(block, lambda i: (i,) + (0,) * (len(block) - 1))], [jax.ShapeDtypeStruct(shape, bf16)]
    rest = list(shape[1:])
    rest[axis - 1] //= pieces
    block = (1, pieces // 2) + tuple(rest)
    spec = pl.BlockSpec(block, lambda i: (i,) + (0,) * (len(block) - 1))
    return [spec] * 2, [jax.ShapeDtypeStruct((shape[0],) + block[1:], bf16)] * 2


def ffn(x, g, gate_up, down, base, ny, frames, mine):
    count, rows, depth = x.shape
    width = down.shape[1]
    pieces = gradient_pieces(frames, depth)
    part = jax.ShapeDtypeStruct((count, rows // ny, depth), bf16)
    part_spec = pl.BlockSpec((1, rows // ny, depth), lambda i: (i, 0, 0))
    row_spec = pl.BlockSpec((1, rows, depth), lambda i: (i, 0, 0))
    gu_specs, gu_shapes = split_specs((count, 2, depth, width), pieces, 2)
    dn_specs, dn_shapes = split_specs((count, width, depth), pieces, 2)
    out = pl.pallas_call(
        functools.partial(ffn_kernel, ny, pieces),
        grid=(count,),
        in_specs=[
            pl.BlockSpec(memory_space=pltpu.SMEM),
            row_spec,
            row_spec,
            pl.BlockSpec((1, 2, depth, width), lambda i: (base + i, 0, 0, 0)),
            pl.BlockSpec((1, width, depth), lambda i: (base + i, 0, 0)),
        ],
        out_specs=[part_spec] * (2 * ny) + [pl.BlockSpec((1, 1, depth), lambda i: (i, 0, 0))] + gu_specs + dn_specs,
        out_shape=[part] * (2 * ny) + [jax.ShapeDtypeStruct((count, 1, depth), f32)] + gu_shapes + dn_shapes,
        compiler_params=params(),
        cost_estimate=cost(18 * count * rows * depth * width, 2 * count * depth * (4 * rows + 6 * width)),
        name="ffn",
    )(mine, x, g, gate_up, down)
    n = len(gu_specs)
    return out[:ny], out[ny : 2 * ny], out[2 * ny], out[2 * ny + 1 : 2 * ny + 1 + n], out[2 * ny + 1 + n :]


def attend_back_kernel(base, n_kv, first, ny, pieces, mine_ref, ga_ref, gp_ref, x_ref, q_ref, *refs):
    refs = list(refs)

    def take(n):
        got = refs[:n]
        del refs[:n]
        return got

    k_refs, v_refs = take(n_kv), take(n_kv)
    (mixed_ref, ow_all_ref, iw_ref) = take(3)
    dk_in = dv_in = ()
    if not first:
        dk_in, dv_in = take(n_kv), take(n_kv)
    part_refs = take(ny)
    (gain_ref,) = take(1)
    n_out = 1 if pieces == 1 else 2
    iw_grads, ow_grads = take(n_out), take(n_out)
    dk_out, dv_out = take(n_kv - 1), take(n_kv - 1)
    gmixed_ref, gproj_ref = take(2)
    count, rows, width = q_ref.shape
    columns = n_kv * count * FRAME_BLOCK
    block = count * FRAME_BLOCK
    step = pl.program_id(0)

    @pl.when(step == 0)
    def _():
        for p in range(count):
            gmixed_ref[p] = dot(ga_ref[p], ow_all_ref[p], NT).astype(bf16)
        heads = head_masks(block, width)
        allowed = attention_mask(count, base, columns)
        factor = HDIM ** (-0.5)

        def one(b):
            at = pl.ds(pl.multiple_of(b * FRAME_BLOCK, FRAME_BLOCK), FRAME_BLOCK)
            queries = block_of([q_ref], at) * factor
            grad_mixed = block_of([gmixed_ref], at)
            keys, values = block_of(k_refs, at), block_of(v_refs, at)
            dqs, dk, dv = [], None, None
            for head in heads:
                my_q = jnp.where(head, queries, jnp.zeros_like(queries))
                my_g = jnp.where(head, grad_mixed, jnp.zeros_like(grad_mixed))
                probs = softmax(jnp.where(allowed, dot(my_q, keys, NT), -1e30))
                grad_probs = dot(my_g, values, NT)
                weighted = probs * grad_probs
                grad_scores = (weighted - probs * jnp.sum(weighted, axis=-1, keepdims=True)).astype(bf16)
                dqs.append(dot(grad_scores, keys, NN))
                more_k = dot(grad_scores, my_q, TN)
                more_v = dot(probs.astype(bf16), my_g, TN)
                dk = more_k if dk is None else dk + more_k
                dv = more_v if dv is None else dv + more_v
            gproj_ref[:, 0, at, :] = (pick(heads, dqs) * factor).astype(bf16).reshape(count, FRAME_BLOCK, width)
            for c, total, earlier, later in ((1, dk, dk_in, dk_out), (2, dv, dv_in, dv_out)):
                for j in range(n_kv):
                    piece = total[j * block : (j + 1) * block].reshape(count, FRAME_BLOCK, width)
                    if not first:
                        piece = piece + earlier[j][:, at, :]
                    if j < n_kv - 1:
                        later[j][:, at, :] = piece
                    else:
                        gproj_ref[:, c, at, :] = piece.astype(bf16)

        lax.fori_loop(0, rows // FRAME_BLOCK, lambda b, c: (one(b), c)[1], 0, unroll=2)

    grads = [gproj_ref[step, c] for c in range(3)]
    back = dot(grads[0], iw_ref[0, 0], NT) + dot(grads[1], iw_ref[0, 1], NT) + dot(grads[2], iw_ref[0, 2], NT)
    span = rows // ny
    for y, part in enumerate(part_refs):
        part[0] = back[y * span : (y + 1) * span].astype(bf16)
    gain_ref[0] = jnp.sum(back * x_ref[0].astype(f32), axis=0, keepdims=True)
    mixed = mixed_ref[0]
    if pieces == 1:
        for c in range(3):
            iw_grads[0][0, c] = dot(x_ref[0], grads[c], TN).astype(bf16)
        ow_grads[0][0] = dot(mixed, gp_ref[0], TN).astype(bf16)
        return
    mine = mine_ref[0]
    depth = x_ref.shape[2]
    for r in range(pieces):
        at = piece_at(r, mine, depth // pieces)
        columns = x_ref[0, :, at]
        for c in range(3):
            iw_grads[r % 2][0, r // 2, c] = dot(columns, grads[c], TN).astype(bf16)
        ow_grads[r % 2][0, r // 2] = dot(mixed, gp_ref[0, :, at], TN).astype(bf16)


def attend_back(grad_rows, x, q, ks, vs, mixed, out_weight, in_weight, dks, dvs, base, ny, frames, mine):
    count, rows, depth = x.shape
    width = q.shape[-1]
    pieces = gradient_pieces(frames, depth)
    n_kv = len(ks)
    first = not dks
    whole = pl.BlockSpec((count, rows, width), lambda i: (0, 0, 0))
    row_spec = pl.BlockSpec((1, rows, depth), lambda i: (i, 0, 0))
    chunk = base // count
    part = jax.ShapeDtypeStruct((count, rows // ny, depth), bf16)
    part_spec = pl.BlockSpec((1, rows // ny, depth), lambda i: (i, 0, 0))
    iw_specs, iw_shapes = split_specs((count, 3, depth, width), pieces, 2)
    ow_specs, ow_shapes = split_specs((count, width, depth), pieces, 2)
    total = jax.ShapeDtypeStruct((count, rows, width), f32)
    out = pl.pallas_call(
        functools.partial(attend_back_kernel, base, n_kv, first, ny, pieces),
        grid=(count,),
        in_specs=[
            pl.BlockSpec(memory_space=pltpu.SMEM),
            pl.BlockSpec((count, rows, depth), lambda i: (0, 0, 0)),
            row_spec,
            row_spec,
        ]
        + [whole] * (1 + 2 * n_kv)
        + [
            pl.BlockSpec((1, rows, width), lambda i: (i, 0, 0)),
            pl.BlockSpec((count, width, depth), lambda i: (chunk, 0, 0)),
            pl.BlockSpec((1, 3, depth, width), lambda i: (base + i, 0, 0, 0)),
        ]
        + [whole] * (len(dks) + len(dvs)),
        out_specs=[part_spec] * ny
        + [pl.BlockSpec((1, 1, depth), lambda i: (i, 0, 0))]
        + iw_specs
        + ow_specs
        + [whole] * (2 * (n_kv - 1)),
        out_shape=[part] * ny
        + [jax.ShapeDtypeStruct((count, 1, depth), f32)]
        + iw_shapes
        + ow_shapes
        + [total] * (2 * (n_kv - 1)),
        scratch_shapes=[pltpu.VMEM((count, rows, width), bf16), pltpu.VMEM((count, 3, rows, width), bf16)],
        compiler_params=params(),
        cost_estimate=cost(16 * count * rows * depth * width, 2 * count * rows * (4 * depth + 8 * n_kv * width)),
        name="attend_back",
    )(mine, grad_rows, grad_rows, x, q, *ks, *vs, mixed, out_weight, in_weight, *dks, *dvs)
    out = list(out)
    n = len(iw_specs)
    parts, gain = out[:ny], out[ny]
    iw, ow = out[ny + 1 : ny + 1 + n], out[ny + 1 + n : ny + 1 + 2 * n]
    rest = out[ny + 1 + 2 * n :]
    return parts, gain, iw, ow, rest[: n_kv - 1], rest[n_kv - 1 :]


def inverse_rms(values):
    return lax.rsqrt(jnp.mean(values * values, axis=-1, keepdims=True) + EPSILON)


def norm_back(grad_normed, normed, factor, gain):
    scaled = grad_normed * gain
    return factor * (scaled - normed * jnp.mean(scaled * normed, axis=-1, keepdims=True))


def body(inputs, counts, norm_gains, in_weight, out_weight, gate_up, down_weight, cotangent):
    frames, group_size = lax.axis_size("frames"), lax.axis_size("mp")
    group = Group(group_size)
    ny, nz = group.ny, group.nz
    local, positions, depth = inputs.shape
    rows = local * group_size
    size = positions // CHUNKS
    ids = lax.axis_index("mp") * local + jnp.arange(local)
    mask = (ids < counts[0]).astype(f32)[None, :, None]
    mine = lax.axis_index("frames").astype(jnp.int32)[None]
    x_major = jnp.swapaxes(inputs, 0, 1)
    g_major = jnp.swapaxes(cotangent, 0, 1)
    gains = norm_gains[:, :, None, :]

    def at(c):
        return slice(c * size, (c + 1) * size)

    def gathered(own, z_first):
        return group.gather(own, z_first).reshape(size, rows, depth)

    def reduced(parts, z_first):
        return group.reduce([p.reshape(size, nz, local, depth) for p in parts], z_first)

    def summed(grads):
        if len(grads) == 1:
            return lax.psum_scatter(grads[0], "frames", scatter_dimension=grads[0].ndim - 1, tiled=True).astype(f32)
        return frames_sum(grads[0], grads[1], frames)

    def summed_middle(grads):
        if len(grads) == 1:
            return lax.psum_scatter(grads[0], "frames", scatter_dimension=2, tiled=True).astype(f32)
        return frames_sum(grads[0], grads[1], frames)

    order = list(range(CHUNKS))[::-1]
    attn_in, qs, ks, vs = {}, {}, {}, {}
    for c in order:
        residual = x_major[at(c)].astype(f32)
        own = (residual * inverse_rms(residual) * gains[0, at(c)]).astype(bf16)
        attn_in[c] = gathered(own, True)
        qs[c], ks[c], vs[c] = qkv(attn_in[c], in_weight, c * size)

    outputs, input_grads = {}, {}
    g_in, g_out, g_gu, g_dn, gain_terms = {}, {}, {}, {}, {}
    dks, dvs = [], []
    for c in order:
        base = c * size
        gain_first, gain_second = gains[0, at(c)], gains[1, at(c)]
        residual = x_major[at(c)].astype(f32)
        gy = g_major[at(c)].astype(f32)
        grad_rows = gathered((mask * gy).astype(bf16), c % 2 == 0)
        earlier_k, earlier_v = [ks[j] for j in range(c + 1)], [vs[j] for j in range(c + 1)]
        mixed, *parts = attend(qs[c], earlier_k, earlier_v, out_weight, base, ny)
        hmid = residual + mask * reduced(parts, False)
        scale_second = inverse_rms(hmid)
        normed_second = hmid * scale_second
        ffn_rows = gathered((normed_second * gain_second).astype(bf16), True)
        out_parts, back_parts, gain_back, grad_gu, grad_dn = ffn(
            ffn_rows, grad_rows, gate_up, down_weight, base, ny, frames, mine
        )
        grad_ffn_in = reduced(back_parts, False)
        grad_mid = gy + norm_back(grad_ffn_in, normed_second, scale_second, gain_second)
        grad_attn = gathered((mask * grad_mid).astype(bf16), True)
        outputs[c] = (hmid + mask * reduced(out_parts, True)).astype(bf16)
        back, gain_front, grad_iw, grad_ow, dks, dvs = attend_back(
            grad_attn, attn_in[c], qs[c], earlier_k, earlier_v, mixed, out_weight, in_weight,
            dks, dvs, base, ny, frames, mine,
        )
        grad_attn_in = reduced(back, c % 2 == 1)
        scale_first = inverse_rms(residual)
        input_grads[c] = (
            grad_mid + norm_back(grad_attn_in, residual * scale_first, scale_first, gain_first)
        ).astype(bf16)
        gain_terms[c] = jnp.stack([gain_front[:, 0] / norm_gains[0, at(c)], gain_back[:, 0] / norm_gains[1, at(c)]])
        g_gu[c], g_dn[c] = summed_middle(grad_gu), summed(grad_dn)
        g_in[c], g_out[c] = summed_middle(grad_iw), summed(grad_ow)

    def joined(pieces, axis=0):
        return jnp.concatenate([pieces[c] for c in range(CHUNKS)], axis=axis)

    terms = lax.psum_scatter(joined(gain_terms, 1), "frames", scatter_dimension=2, tiled=True)
    step = 1
    while step < group_size:
        terms = terms + lax.ppermute(terms, "mp", [(i, i ^ step) for i in range(group_size)])
        step *= 2
    return (
        jnp.swapaxes(joined(outputs), 0, 1),
        jnp.swapaxes(joined(input_grads), 0, 1),
        joined(g_in),
        joined(g_out),
        joined(g_gu),
        joined(g_dn),
        terms,
    )


MESH = pl.DeviceIdType.MESH
ZN, YN = 4, 2


def fits(frames, group_size, local, positions, depth, width, hidden):
    return (
        frames == 4
        and group_size == ZN * YN
        and local == 48
        and positions == 16
        and width % 128 == 0
        and (depth // frames) % 128 == 0
        and hidden % 128 == 0
    )


class Place:
    def __init__(self):
        self.m = lax.axis_index("mp")
        self.f = lax.axis_index("frames")
        self.z = self.m // YN
        self.ids = {
            "y": ("mp", self.m ^ 1),
            "up": ("mp", self.m + YN),
            "down": ("mp", self.m - YN),
            "core": ("frames", self.f ^ 1),
            "x": ("frames", self.f ^ 2),
            "pair": ("mp", self.m ^ YN),
            "far": ("mp", self.m ^ (2 * YN)),
        }

    def device(self, way):
        axis, index = self.ids[way]
        return {axis: index}

    def copy(self, src, dst, send, recv, way):
        return pltpu.make_async_remote_copy(
            src_ref=src, dst_ref=dst, send_sem=send, recv_sem=recv, device_id=self.device(way), device_id_type=MESH
        )


def when(condition, run):
    pl.when(condition)(run)


def wait_got(dst, send, recv, place):
    place.copy(dst, dst, send, recv, "y").wait_recv()


class GatherZ:
    def __init__(self, place, g, send, recv):
        self.place, self.g, self.send, self.recv = place, g, send, recv

    def site(self, number, way, src, dst):
        return self.place.copy(
            self.g.at[src[0], src[1]],
            self.g.at[dst[0], dst[1]],
            self.send.at[number],
            self.recv.at[dst[0] * 2 + dst[1]],
            way,
        )

    def up(self, k):
        return self.site(k - 1, "up", (k - 1, 0), (k, 0))

    def down(self, k):
        return self.site(2 + k, "down", ((5 - k) % 4, 0), (4 - k, 0))

    def across(self, k):
        return self.site(6 + k, "y", (k, 0), (k, 1))

    def got(self, k, y):
        wait_got(self.g.at[k, y], self.send.at[0], self.recv.at[k * 2 + y], self.place)

    def t1(self):
        z = self.place.z
        when(z < 3, lambda: self.up(1).start())
        when(z > 0, lambda: self.down(1).start())
        self.across(0).start()

    def t2(self):
        z = self.place.z

        def low():
            self.got(1, 0)
            when(z < 3, lambda: self.up(2).start())
            self.across(1).start()

        def high():
            self.got(3, 0)
            when(z > 0, lambda: self.down(2).start())
            self.across(3).start()

        when(z >= 1, low)
        when(z <= 2, high)

    def t3(self):
        z = self.place.z
        self.got(2, 0)
        when(z == 2, lambda: self.up(3).start())
        when(z == 1, lambda: self.down(3).start())
        self.across(2).start()

    def t4(self):
        z = self.place.z

        def bottom():
            self.got(1, 0)
            self.across(1).start()

        def top():
            self.got(3, 0)
            self.across(3).start()

        when(z == 0, bottom)
        when(z == 3, top)

    def done(self):
        z = self.place.z
        for k in range(4):
            self.got(k, 1)
        when(z < 3, lambda: self.up(1).wait_send())
        when(z > 0, lambda: self.down(1).wait_send())
        when((z >= 1) & (z < 3), lambda: self.up(2).wait_send())
        when((z >= 1) & (z < 3), lambda: self.down(2).wait_send())
        when(z == 2, lambda: self.up(3).wait_send())
        when(z == 1, lambda: self.down(3).wait_send())
        for k in range(4):
            self.across(k).wait_send()


class GatherY:
    def __init__(self, place, g, send, recv):
        self.place, self.g, self.send, self.recv = place, g, send, recv

    def site(self, number, way, src, dst):
        return self.place.copy(self.g.at[src], self.g.at[dst], self.send.at[number], self.recv.at[dst], way)

    def up(self, k):
        return self.site(k - 1, "up", k - 1, k)

    def down(self, k):
        return self.site(2 + k, "down", (5 - k) % 4, 4 - k)

    def across(self):
        return self.place.copy(self.g.at[0, 0], self.g.at[0, 1], self.send.at[6], self.recv.at[4], "y")

    def got(self, k):
        wait_got(self.g.at[k], self.send.at[0], self.recv.at[k], self.place)

    def t1(self):
        self.across().start()

    def t2(self):
        z = self.place.z
        wait_got(self.g.at[0, 1], self.send.at[0], self.recv.at[4], self.place)
        when(z < 3, lambda: self.up(1).start())
        when(z > 0, lambda: self.down(1).start())

    def t3(self):
        z = self.place.z

        def low():
            self.got(1)
            when(z < 3, lambda: self.up(2).start())

        def high():
            self.got(3)
            when(z > 0, lambda: self.down(2).start())

        when(z >= 1, low)
        when(z <= 2, high)

    def t4(self):
        z = self.place.z
        self.got(2)
        when(z == 2, lambda: self.up(3).start())
        when(z == 1, lambda: self.down(3).start())

    def done(self):
        z = self.place.z
        when(z == 0, lambda: self.got(1))
        when(z == 3, lambda: self.got(3))
        when(z < 3, lambda: self.up(1).wait_send())
        when(z > 0, lambda: self.down(1).wait_send())
        when((z >= 1) & (z < 3), lambda: self.up(2).wait_send())
        when((z >= 1) & (z < 3), lambda: self.down(2).wait_send())
        when(z == 2, lambda: self.up(3).wait_send())
        when(z == 1, lambda: self.down(3).wait_send())
        self.across().wait_send()


def up_to_f32(condition, ref):
    return jnp.where(condition, ref[...].astype(f32), 0.0)


class ReduceY:
    def __init__(self, place, part, over, ups, downs, send, recv):
        self.place, self.part, self.over, self.ups, self.downs = place, part, over, ups, downs
        self.send, self.recv = send, recv

    def across(self, k):
        return self.place.copy(self.part.at[k, 1], self.over.at[k], self.send.at[6 + k], self.recv.at[7 + k], "y")

    def up(self, s):
        return self.place.copy(
            self.part.at[s, 0], self.ups.at[s - 1], self.send.at[2 * s - 2], self.recv.at[s], "up"
        )

    def down(self, s):
        return self.place.copy(
            self.part.at[4 - s, 0], self.downs.at[s - 1], self.send.at[2 * s - 1], self.recv.at[3 + s], "down"
        )

    def got_over(self, k):
        wait_got(self.over.at[k], self.send.at[0], self.recv.at[7 + k], self.place)

    def got_up(self, s):
        wait_got(self.ups.at[s - 1], self.send.at[0], self.recv.at[s], self.place)

    def got_down(self, s):
        wait_got(self.downs.at[s - 1], self.send.at[0], self.recv.at[3 + s], self.place)

    def local(self, k):
        return self.part[k, 0].astype(f32) + self.over[k].astype(f32)

    def store(self, k, value):
        self.part[k, 0] = value.astype(bf16)

    def t1(self):
        for k in (1, 3, 2, 0):
            self.across(k).start()

    def t2(self):
        z = self.place.z

        def bottom():
            self.got_over(1)
            self.store(1, self.local(1))
            self.up(1).start()

        def top():
            self.got_over(3)
            self.store(3, self.local(3))
            self.down(1).start()

        when(z == 0, bottom)
        when(z == 3, top)

    def t3(self):
        z = self.place.z
        self.got_over(2)
        when(z == 1, lambda: self.got_up(1))
        when(z == 2, lambda: self.got_down(1))
        self.store(
            2, self.local(2) + up_to_f32(z == 1, self.ups.at[0]) + up_to_f32(z == 2, self.downs.at[0])
        )
        when(z <= 1, lambda: self.up(2).start())
        when(z >= 2, lambda: self.down(2).start())

    def t4(self):
        z = self.place.z

        def low():
            self.got_over(3)
            when(z >= 1, lambda: self.got_up(2))
            self.store(3, self.local(3) + up_to_f32(z >= 1, self.ups.at[1]))
            self.up(3).start()

        def high():
            self.got_over(1)
            when(z <= 2, lambda: self.got_down(2))
            self.store(1, self.local(1) + up_to_f32(z <= 2, self.downs.at[1]))
            self.down(3).start()

        when(z <= 2, low)
        when(z >= 1, high)

    def done(self):
        z = self.place.z
        self.got_over(0)
        when(z >= 1, lambda: self.got_up(3))
        when(z <= 2, lambda: self.got_down(3))
        when(z == 0, lambda: self.up(1).wait_send())
        when(z == 3, lambda: self.down(1).wait_send())
        when(z <= 1, lambda: self.up(2).wait_send())
        when(z >= 2, lambda: self.down(2).wait_send())
        when(z <= 2, lambda: self.up(3).wait_send())
        when(z >= 1, lambda: self.down(3).wait_send())
        for k in range(4):
            self.across(k).wait_send()

    def total(self):
        z = self.place.z
        return self.local(0) + up_to_f32(z >= 1, self.ups.at[2]) + up_to_f32(z <= 2, self.downs.at[2])


class ReduceZ:
    def __init__(self, place, part, over, ups, downs, send, recv):
        self.place, self.part, self.over, self.ups, self.downs = place, part, over, ups, downs
        self.send, self.recv = send, recv

    def across(self):
        return self.place.copy(self.part.at[0, 1], self.over, self.send.at[0], self.recv.at[0], "y")

    def up(self, s):
        return self.place.copy(self.part.at[s], self.ups.at[s - 1], self.send.at[2 * s - 1], self.recv.at[s], "up")

    def down(self, s):
        return self.place.copy(
            self.part.at[4 - s], self.downs.at[s - 1], self.send.at[2 * s], self.recv.at[3 + s], "down"
        )

    got_up = ReduceY.got_up
    got_down = ReduceY.got_down

    def add(self, k, *more):
        value = self.part[k].astype(f32)
        for term in more:
            value = value + term
        self.part[k] = value.astype(bf16)

    def t1(self):
        z = self.place.z
        when(z == 0, lambda: self.up(1).start())
        when(z == 3, lambda: self.down(1).start())

    def t2(self):
        z = self.place.z

        def low():
            self.got_up(1)
            self.add(2, self.ups[0].astype(f32))

        def high():
            self.got_down(1)
            self.add(2, self.downs[0].astype(f32))

        when(z == 1, low)
        when(z == 2, high)
        when(z <= 1, lambda: self.up(2).start())
        when(z >= 2, lambda: self.down(2).start())

    def t3(self):
        z = self.place.z

        def low():
            self.got_up(2)
            self.add(3, self.ups[1].astype(f32))

        def high():
            self.got_down(2)
            self.add(1, self.downs[1].astype(f32))

        when((z >= 1) & (z <= 2), low)
        when((z >= 1) & (z <= 2), high)
        when(z <= 2, lambda: self.up(3).start())
        when(z >= 1, lambda: self.down(3).start())

    def t4(self):
        z = self.place.z
        when(z >= 1, lambda: self.got_up(3))
        when(z <= 2, lambda: self.got_down(3))
        value = self.part[0, 1].astype(f32)
        value = value + up_to_f32(z >= 1, self.ups.at[2, 1]) + up_to_f32(z <= 2, self.downs.at[2, 1])
        self.part[0, 1] = value.astype(bf16)
        self.across().start()

    def done(self):
        wait_got(self.over, self.send.at[0], self.recv.at[0], self.place)
        z = self.place.z
        when(z == 0, lambda: self.up(1).wait_send())
        when(z == 3, lambda: self.down(1).wait_send())
        when(z <= 1, lambda: self.up(2).wait_send())
        when(z >= 2, lambda: self.down(2).wait_send())
        when(z <= 2, lambda: self.up(3).wait_send())
        when(z >= 1, lambda: self.down(3).wait_send())
        self.across().wait_send()

    def total(self):
        z = self.place.z
        value = self.part[0, 0].astype(f32) + self.over[...].astype(f32)
        return value + up_to_f32(z >= 1, self.ups.at[2, 0]) + up_to_f32(z <= 2, self.downs.at[2, 0])


class FramesSum:
    def __init__(self, place, sent, kept, from_core, from_x, sems, free, number):
        self.place, self.sent, self.kept, self.from_core, self.from_x = place, sent, kept, from_core, from_x
        self.sems, self.free, self.number = sems, free, number

    def core(self, j):
        return self.place.copy(self.sent[j], self.from_core[j], self.sems.at[0, j], self.sems.at[1, j], "core")

    def x(self, j):
        return self.place.copy(self.kept[j].at[1], self.from_x[j], self.sems.at[2, j], self.sems.at[3, j], "x")

    def out(self, j, outs, p):
        return pltpu.make_async_copy(self.kept[j].at[0], outs[j].at[p], self.sems.at[4, j])

    def start(self, later):
        def credit():
            pl.semaphore_wait(self.free.at[2 * self.number], 1)

        when(later, credit)
        for j in range(2):
            self.core(j).start()

    def middle(self, later):
        for j in range(2):
            self.core(j).wait_recv()

        def credit():
            pl.semaphore_wait(self.free.at[2 * self.number + 1], 1)

        when(later, credit)
        for j in range(2):
            kept, got = self.kept[j], self.from_core[j]
            kept[1] = (kept[1].astype(f32) + got[1].astype(f32)).astype(bf16)
            self.x(j).start()
        for j in range(2):
            self.core(j).wait_send()

    def finish(self, outs, p, more):
        for j in range(2):
            self.x(j).wait_recv()
            kept = self.kept[j]
            total = kept[0].astype(f32) + self.from_core[j][0].astype(f32) + self.from_x[j][...].astype(f32)
            kept[0] = total.astype(bf16)
            self.out(j, outs, p).start()

        def credit():
            for k, way in enumerate(("core", "x")):
                pl.semaphore_signal(
                    self.free.at[2 * self.number + k], inc=1, device_id=self.place.device(way), device_id_type=MESH
                )

        when(more, credit)
        for j in range(2):
            self.x(j).wait_send()

    def drained(self, outs, p):
        for j in range(2):
            self.out(j, outs, p).wait()


GIN_REDUCE = ReduceY
BACK_REDUCE = ReduceY
FIRST_Y_ROWS = (0, 16, 16, 0, 0, 0, 0, 0)
COT_Y_ROWS = (16, 16, 0, 0, 0, 0, 0, 16)
FFN_Y_ROWS = (0, 48, 32, 48, 48, 48, 48, 48, 48, 48, 48, 48, 48, 48, 32, 0)
ATT_Y_ROWS = (16, 48, 32, 32, 32, 48, 48, 48, 48, 48, 48, 48, 32, 16, 0, 0)
FFN_Z_ROWS = (32, 32, 32, 32, 32, 48, 32, 16, 16, 16, 16, 16, 16, 16, 48, 48)
ATTN_Z_ROWS = (0, 0, 48, 48, 48, 48, 48, 0, 0, 0, 0, 0, 0, 0, 0, 0)

SCHEDULES = (
    (
        ("AC1", 0), ("RA5", 1), ("A", 0), ("RF3", 3), ("Fm", 3), ("RB3", 5), ("RG5", 3), ("AG4", 4),
        ("AC4", 1), ("AC2", 0), ("RA2", 0), ("AF2", 1), ("C", 2), ("RB4", 5), ("Ef", 5), ("RF4", 3),
        ("AG2", 3), ("RA3", 0), ("E", 4), ("AF3", 1), ("Eg", 4), ("RG2", 2), ("RB5", 5), ("Ff", 3),
        ("RA4", 0), ("AC3", 0), ("Em", 4), ("AC5", 1), ("RG3", 2), ("RF2", 2), ("AG3", 3), ("Cg", 2),
        ("RF5", 3), ("K", 0), ("RG4", 2), ("RB2", 4), ("AF4", 1),
    ),
)
CHANGES = ()


class Split:
    def choose(self, i, table):
        self.chosen = {}
        for count in self.pairs:
            places = sum(1 << k for k in range(len(table)) if table[k] == count)
            self.chosen[count] = (places >> (i % 16)) % 2 == 1
        return self

    def both(self, run):
        for count, pair in self.pairs.items():

            def each(pair=pair):
                for part in pair:
                    run(part)

            when(self.chosen[count], each)

    def t1(self):
        self.both(lambda part: part.t1())

    def t2(self):
        self.both(lambda part: part.t2())

    def t3(self):
        self.both(lambda part: part.t3())

    def t4(self):
        self.both(lambda part: part.t4())

    def done(self):
        self.both(lambda part: part.done())


class SplitGather(Split):
    def __init__(self, place, g, send, recv, table, rows=0):
        def cut(start, size):
            return g.at[(slice(None), slice(None)) + (slice(None),) * rows + (pl.ds(start, size),)]

        def pair(count, local):
            runs = []
            if count > 0:
                runs.append(GatherY(place, cut(0, count), send.at[0], recv.at[0]))
            if count < local:
                runs.append(GatherZ(place, cut(count, local - count), send.at[1], recv.at[1]))
            return runs

        self.pairs = {count: pair(count, g.shape[2 + rows]) for count in sorted(set(table))}


class SplitReduce(Split):
    def __init__(self, place, part, over, ups, downs, send, recv, table):
        self.place, self.part, self.over, self.ups, self.downs = place, part, over, ups, downs
        local = part.shape[2]

        def pair(count):
            first, rest = pl.ds(0, count), pl.ds(count, local - count)
            runs = []
            if count > 0:
                runs.append(
                    ReduceZ(
                        place, part.at[:, :, first], over.at[0, first], ups.at[:, :, first], downs.at[:, :, first],
                        send.at[0], recv.at[0],
                    )
                )
            if count < local:
                runs.append(
                    ReduceY(
                        place, part.at[:, :, rest], over.at[:, rest], ups.at[:, 0, rest], downs.at[:, 0, rest],
                        send.at[1], recv.at[1],
                    )
                )
            return runs

        self.pairs = {count: pair(count) for count in sorted(set(table))}

    def total(self):
        z = self.place.z
        value = self.part[0, 0].astype(f32) + self.over[0].astype(f32)
        return value + up_to_f32(z >= 1, self.ups.at[2, 0]) + up_to_f32(z <= 2, self.downs.at[2, 0])


class GainSum:
    def __init__(self, place, pieces, got, send, recv):
        self.place, self.pieces, self.got, self.send, self.recv = place, pieces, got, send, recv

    def hop(self, k):
        ways = ("core", "x", "y", "pair", "far")
        sources = (self.pieces.at[1], self.pieces.at[0].at[1], self.pieces.at[0].at[0])
        src = sources[min(k, 2)]
        if k == 0:
            dst = self.got.at[pl.ds(0, 2)]
        else:
            dst = self.got.at[k + 1]
        return self.place.copy(src, dst, self.send.at[k], self.recv.at[k], ways[k])

    def start(self):
        self.hop(0).start()

    def next(self, k):
        self.hop(k).wait()
        if k == 0:
            self.pieces[0] = self.pieces[0] + self.got[0:2]
        else:
            self.pieces[0, 0] = self.pieces[0, 0] + self.got[k + 1]
        if k < 4:
            self.hop(k + 1).start()


def layer_kernel(
    x_ref, cot_ref, mask_ref, gains_ref, in_w, out_w, gu_w, dn_w,
    out_hbm, ingrad_hbm, gu_hbm, dn_hbm, iw_hbm, ow_hbm, gain_out, rows_hbm, cot_hbm,
    g_ffn, g_att, cot_v, p_attn, p_gin, p_ffn, p_back,
    over_attn, over_gin, over_ffn, over_back, ups_attn, ups_gin, ups_ffn, ups_back,
    downs_attn, downs_gin, downs_ffn, downs_back,
    q_s, k_s, v_s, mixed_s, dk_s, dv_s, sc, dp,
    gu_v, dn_v, owa_v, owe_v, iw_v, xb,
    act_s, gg_s, gup_s, gmixed_s, gproj_s, hmid_s, ghmid_s, stage, gain_s, gain_pieces, gain_got,
    gu_sent, gu_kept, gu_core, gu_x, dn_sent, dn_kept, dn_core, dn_x,
    iw_sent, iw_kept, iw_core, iw_x, ow_sent, ow_kept, ow_core, ow_x,
    sem_first, sem_first_got, sem_gather, sem_gather_got, sem_reduce, sem_reduce_got, sem_split, sem_split_got,
    sem_grad_ffn, sem_grad_att, sem_gain, sem_local, credits, free,
):
    place = Place()
    z, f = place.z, place.f
    positions, local, depth = x_ref.shape
    rows = ZN * YN * local
    last = positions - 1
    width = q_s.shape[-1]
    hidden = dn_v.shape[0]
    half = rows // 2
    quarter = depth // 4
    mask = mask_ref[...]
    scale = HDIM ** (-0.5)
    pairs_of = positions // 2

    def load(src, dst, number):
        return pltpu.make_async_copy(src, dst, sem_local.at[number])

    def load_owa(p):
        return load(out_w.at[p], owa_v, 0)

    def load_owe(p):
        return load(out_w.at[p], owe_v, 1)

    def load_iw(p, slot):
        return load(in_w.at[p], iw_v.at[slot], 2 + slot)

    def load_gu(p):
        return load(gu_w.at[p], gu_v, 4)

    def load_dn(p):
        return load(dn_w.at[p], dn_v, 5)

    def load_rows(p, dst, number):
        return load(rows_hbm.at[p // 2, :, :, p % 2], dst, number)

    def load_cot(p):
        return load(cot_hbm.at[p // 2, :, :, p % 2], cot_v, 9)

    def own_cot(j):
        return load(g_ffn.at[j // 4, j % 4], cot_hbm.at[j, 0, 0], 16 + j)

    def own_rows(j):
        return load(g_att.at[j // 4, j % 4], rows_hbm.at[j, 0, 0], 16 + pairs_of + j)

    barrier = pltpu.get_barrier_semaphore()

    def greet(way):
        pl.semaphore_signal(barrier, inc=1, device_id=place.device(way), device_id_type=MESH)

    for way in ("y", "core", "x", "far"):
        greet(way)
    when(z < 3, lambda: greet("up"))
    when(z > 0, lambda: greet("down"))
    pl.semaphore_wait(barrier, 4 + (z < 3).astype(jnp.int32) + (z > 0).astype(jnp.int32))

    groups = pairs_of

    tile_row = lax.broadcasted_iota(jnp.int32, (8, depth), 0)

    def tile_of(p):
        return pl.ds(pl.multiple_of((p // 8) * 8, 8), 8)

    def gain_of(which, p):
        return jnp.sum(jnp.where(tile_row == p % 8, gains_ref[which, tile_of(p)], 0.0), axis=0, keepdims=True)

    def set_gain_sum(which, p, value):
        gain_s[which, tile_of(p)] = jnp.where(tile_row == p % 8, value, gain_s[which, tile_of(p)])

    def normalise(p, c):
        residual = x_ref[p].astype(f32)
        value = residual * inverse_rms(residual) * gain_of(0, p)
        g_att[p // 8, (p % 8) // 2, p % 2] = value.astype(bf16)
        return c

    firsts = [
        SplitGather(place, rows_hbm.at[g], sem_first.at[g], sem_first_got.at[g], FIRST_Y_ROWS[g : g + 1], 1).choose(
            g, FIRST_Y_ROWS
        )
        for g in range(groups)
    ]

    def cot_gather(j, which):
        sems = sem_gather.at[2, which], sem_gather_got.at[2, which]
        return SplitGather(place, cot_hbm.at[pairs_of - 1 - j], *sems, COT_Y_ROWS, 1).choose(j, COT_Y_ROWS)

    for g in range(groups):
        lax.fori_loop(2 * g, 2 * g + 2, normalise, 0)
        own_rows(g).start()
        own_rows(g).wait()
        firsts[g].t1()

    def masked(p, c):
        g_ffn[p // 8, (p % 8) // 2, p % 2] = (mask * cot_ref[p].astype(f32)).astype(bf16)
        return c

    lax.fori_loop(0, positions, masked, 0)
    for j in range(pairs_of):
        own_cot(j).start()
    load_owa(last).start()
    load_gu(last).start()
    load_dn(last).start()
    load_iw(0, 0).start()
    dk_s[...] = jnp.zeros_like(dk_s)
    dv_s[...] = jnp.zeros_like(dv_s)

    def project(p, c):
        slot = lax.rem(p, 2)
        load_rows(p, g_ffn.at[slot], 6 + slot).wait()
        load_iw(p, slot).wait()

        @pl.when(p < last)
        def _():
            load_iw(p + 1, 1 - slot).start()

        block = g_ffn[slot].reshape(rows, depth)
        q_s[p] = (dot(block, iw_v[slot, 0], NN).astype(bf16) * scale).astype(bf16)
        k_s[p] = dot(block, iw_v[slot, 1], NN).astype(bf16)
        v_s[p] = dot(block, iw_v[slot, 2], NN).astype(bf16)
        return c

    for g in range(groups):
        firsts[g].t2()
    for g in range(groups):
        firsts[g].t3()
    for g in range(groups):
        firsts[g].t4()
    for j in range(pairs_of):
        own_cot(j).wait()
    for g in range(groups):
        firsts[g].done()
        load_rows(2 * g, g_ffn.at[0], 6).start()
        load_rows(2 * g + 1, g_ffn.at[1], 7).start()
        lax.fori_loop(2 * g, 2 * g + 2, project, 0)
    load_owe(last).start()
    load_iw(last, 0).start()
    load_rows(last, xb, 8).start()

    row = lax.broadcasted_iota(jnp.int32, (2 * width, width), 0)
    column = lax.broadcasted_iota(jnp.int32, (2 * width, width), 1)
    ones = jnp.where((row % width) // HDIM == column // HDIM, 1.0, 0.0).astype(bf16)

    def per_head(product):
        high = product.astype(bf16)
        low = (product - high.astype(f32)).astype(bf16)
        return dot(jnp.concatenate([high, low], axis=1), ones, NN)

    def scores_of(p, q, at):
        def two(jj, top):
            first = per_head(q * k_s[2 * jj, at].astype(f32))
            second = per_head(q * k_s[2 * jj + 1, at].astype(f32))
            second = jnp.where(2 * jj + 1 <= p, second, -1e30)
            sc[2 * jj], sc[2 * jj + 1] = first, second
            return jnp.maximum(top, jnp.maximum(first, second))

        return lax.fori_loop(0, p // 2 + 1, two, jnp.full((half, width), -1e30, f32))

    def attend_one(p):
        pairs = p // 2 + 1
        for part in range(2):
            at = pl.ds(part * half, half)
            q = q_s[p, at].astype(f32)
            top = scores_of(p, q, at)

            def raise_two(jj, total):
                for t in range(2):
                    raised = jnp.exp(sc[2 * jj + t] - top)
                    sc[2 * jj + t] = raised
                    total = total + raised
                return total

            total = lax.fori_loop(0, pairs, raise_two, jnp.zeros((half, width), f32))
            factor = 1.0 / total

            def mix_two(jj, out):
                for t in range(2):
                    probs = (sc[2 * jj + t] * factor).astype(bf16).astype(f32)
                    out = out + probs * v_s[2 * jj + t, at].astype(f32)
                return out

            out = lax.fori_loop(0, pairs, mix_two, jnp.zeros((half, width), f32))
            mixed_s[p, at] = out.astype(bf16)

    def attend_back_one(p):
        pairs = p // 2 + 1
        for part in range(2):
            at = pl.ds(part * half, half)
            q = q_s[p, at].astype(f32)
            g = gmixed_s[at].astype(f32)
            top = scores_of(p, q, at)

            def raise_two(jj, carry):
                total, weighted = carry
                for t in range(2):
                    raised = jnp.exp(sc[2 * jj + t] - top)
                    sc[2 * jj + t] = raised
                    grad_probs = per_head(g * v_s[2 * jj + t, at].astype(f32))
                    dp[2 * jj + t] = grad_probs
                    total = total + raised
                    weighted = weighted + raised * grad_probs
                return total, weighted

            zero = jnp.zeros((half, width), f32)
            total, weighted = lax.fori_loop(0, pairs, raise_two, (zero, zero))
            factor = 1.0 / total
            centre = weighted * factor

            def back_two(jj, dq):
                for t in range(2):
                    j = 2 * jj + t
                    probs = sc[j] * factor
                    grad = (probs * (dp[j] - centre)).astype(bf16).astype(f32)
                    dq = dq + grad * k_s[j, at].astype(f32)
                    dk_s[j, at] = dk_s[j, at] + grad * q
                    dv_s[j, at] = dv_s[j, at] + probs.astype(bf16).astype(f32) * g
                return dq

            dq = lax.fori_loop(0, pairs, back_two, zero)
            gproj_s[0, at] = (dq * scale).astype(bf16)
        gproj_s[1] = dk_s[p].astype(bf16)
        gproj_s[2] = dv_s[p].astype(bf16)

    blocks = (ZN, YN, local, depth)
    grad_ffn = FramesSum(
        place, (gu_sent, dn_sent), (gu_kept, dn_kept), (gu_core, dn_core), (gu_x, dn_x), sem_grad_ffn, free, 0
    )
    grad_att = FramesSum(
        place, (iw_sent, ow_sent), (iw_kept, ow_kept), (iw_core, ow_core), (iw_x, ow_x), sem_grad_att, free, 1
    )
    ffn_outs, att_outs = (gu_hbm, dn_hbm), (iw_hbm, ow_hbm)
    gain_sum = GainSum(place, gain_pieces, gain_got, sem_gain.at[0], sem_gain.at[1])

    def out_copy(p):
        return pltpu.make_async_copy(stage.at[0], out_hbm.at[p], sem_local.at[14])

    def ingrad_copy(p):
        return pltpu.make_async_copy(stage.at[1], ingrad_hbm.at[p], sem_local.at[15])

    class Position:
        def __init__(self, i):
            self.i = i
            self.p = last - i
            self.par = lax.rem(i + 16, 2)
            self.ring = lax.rem(i + 16, 4)

        def gather(self, g, number, table):
            par = self.par
            sems = sem_gather.at[number, par], sem_gather_got.at[number, par]
            return SplitGather(place, g.at[par], *sems, table).choose(self.i, table)

        def reduce(self, kind, part, over, ups, downs, number):
            par = self.par
            return kind(
                place, part, over.at[par], ups.at[par], downs.at[par],
                sem_reduce.at[number, par], sem_reduce_got.at[number, par],
            )

        def AF(self):
            return self.gather(g_ffn, 0, FFN_Y_ROWS)

        def AG(self):
            return self.gather(g_att, 1, ATT_Y_ROWS)

        def split(self, part, over, ups, downs, number, table):
            par = self.par
            event = SplitReduce(
                place, part, over.at[par], ups.at[par], downs.at[par],
                sem_split.at[number, par], sem_split_got.at[number, par], table,
            )
            return event.choose(self.i, table)

        def RA(self):
            return self.split(p_attn, over_attn, ups_attn, downs_attn, 1, ATTN_Z_ROWS)

        def RG(self):
            return self.reduce(GIN_REDUCE, p_gin, over_gin, ups_gin, downs_gin, 1)

        def RF(self):
            return self.split(p_ffn.at[self.par], over_ffn, ups_ffn, downs_ffn, 0, FFN_Z_ROWS)

        def RB(self):
            return self.reduce(BACK_REDUCE, p_back.at[self.par], over_back, ups_back, downs_back, 3)

        def do_A(self):
            p = self.p
            attend_one(p)
            load_owa(p).wait()
            p_attn[...] = dot(mixed_s[p], owa_v[...], NN).astype(bf16).reshape(blocks)
            self.RA().t1()
            when(p > 0, lambda: load_owa(p - 1).start())

        def do_RA5(self):
            p, total = self.p, self.RA()
            total.done()
            hmid = x_ref[p].astype(f32) + mask * total.total()
            hmid_s[self.ring] = hmid
            g_ffn[self.par, 0, 0] = (hmid * inverse_rms(hmid) * gain_of(1, p)).astype(bf16)
            self.AF().t1()

        def do_C(self):
            p, par = self.p, self.par
            self.AF().done()
            load_gu(p).wait()
            load_dn(p).wait()
            load_cot(p).wait()
            x = g_ffn[par].reshape(rows, depth)
            g = cot_v[...].reshape(rows, depth)
            for h in range(2):
                at = slice(h * hidden // 2, (h + 1) * hidden // 2)
                gate = dot(x, gu_v[0, :, at], NN)
                up = dot(x, gu_v[1, :, at], NN)
                grad_act = dot(g, dn_v[at], NT)
                sigma = 1.0 / (1.0 + jnp.exp(-gate))
                silu = gate * sigma
                act_s[:, at] = (silu * up).astype(bf16)
                gg_s[:, at] = (grad_act * up * sigma * (1.0 + gate * (1.0 - sigma))).astype(bf16)
                gup_s[:, at] = (grad_act * silu).astype(bf16)
            back = dot(gg_s[...], gu_v[0], NT) + dot(gup_s[...], gu_v[1], NT)
            p_gin[...] = back.astype(bf16).reshape(blocks)
            self.RG().t1()
            set_gain_sum(1, p, jnp.sum(back * x.astype(f32), axis=0, keepdims=True))
            p_ffn[par] = dot(act_s[...], dn_v[...], NN).astype(bf16).reshape(blocks)
            self.RF().t1()

            @pl.when(p > 0)
            def _():
                load_gu(p - 1).start()
                load_dn(p - 1).start()

        def do_Cg(self):
            p, par = self.p, self.par

            @pl.when(p < last)
            def _():
                grad_ffn.drained(ffn_outs, p + 1)

            for r in range(4):
                at = piece_at(r, f, quarter)
                gu_to, dn_to = (gu_kept, dn_kept) if r % 2 == 0 else (gu_sent, dn_sent)
                columns = g_ffn[par, :, :, :, at].reshape(rows, quarter)
                gu_to[r // 2, 0] = dot(columns, gg_s[...], TN).astype(bf16)
                gu_to[r // 2, 1] = dot(columns, gup_s[...], TN).astype(bf16)
                dn_to[r // 2] = dot(act_s[...], cot_v[:, :, :, at].reshape(rows, quarter), TN).astype(bf16)
            grad_ffn.start(p < last)
            when(p > 0, lambda: load_cot(p - 1).start())

        def do_Fm(self):
            grad_ffn.middle(self.p < last)

        def do_Ff(self):
            grad_ffn.finish(ffn_outs, self.p, self.p > 0)

        def do_RG5(self):
            p, total = self.p, self.RG()
            total.done()
            hmid = hmid_s[self.ring]
            factor = inverse_rms(hmid)
            grad = cot_ref[p].astype(f32) + norm_back(total.total(), hmid * factor, factor, gain_of(1, p))
            ghmid_s[self.ring] = grad
            g_att[self.par, 0, 0] = (mask * grad).astype(bf16)
            self.AG().t1()

        def do_RF5(self):
            p, total = self.p, self.RF()
            total.done()

            @pl.when(p < last)
            def _():
                out_copy(p + 1).wait()

            stage[0] = (hmid_s[self.ring] + mask * total.total()).astype(bf16)
            out_copy(p).start()

        def do_E(self):
            p, par = self.p, self.par
            self.AG().done()
            load_owe(p).wait()
            load_iw(p, 0).wait()
            load_rows(p, xb, 8).wait()
            gmixed_s[...] = dot(g_att[par].reshape(rows, depth), owe_v[...], NT).astype(bf16)
            attend_back_one(p)
            back = dot(gproj_s[0], iw_v[0, 0], NT)
            back = back + dot(gproj_s[1], iw_v[0, 1], NT)
            back = back + dot(gproj_s[2], iw_v[0, 2], NT)
            p_back[par] = back.astype(bf16).reshape(blocks)
            self.RB().t1()
            set_gain_sum(0, p, jnp.sum(back * xb[...].reshape(rows, depth).astype(f32), axis=0, keepdims=True))

            @pl.when(p == 0)
            def _():
                for r in range(4):
                    gain_pieces[r % 2, r // 2] = gain_s[:, :, piece_at(r, f, quarter)]
                gain_sum.start()

            @pl.when(p > 0)
            def _():
                load_owe(p - 1).start()
                load_iw(p - 1, 0).start()

        def do_Eg(self):
            p, par = self.p, self.par

            @pl.when(p < last)
            def _():
                grad_att.drained(att_outs, p + 1)

            for r in range(4):
                at = piece_at(r, f, quarter)
                iw_to, ow_to = (iw_kept, ow_kept) if r % 2 == 0 else (iw_sent, ow_sent)
                columns = xb[:, :, :, at].reshape(rows, quarter)
                for j in range(3):
                    iw_to[r // 2, j] = dot(columns, gproj_s[j], TN).astype(bf16)
                ow_to[r // 2] = dot(mixed_s[p], g_att[par, :, :, :, at].reshape(rows, quarter), TN).astype(bf16)
            grad_att.start(p < last)
            when(p > 0, lambda: load_rows(p - 1, xb, 8).start())

        def do_Em(self):
            grad_att.middle(self.p < last)

        def do_Ef(self):
            grad_att.finish(att_outs, self.p, self.p > 0)

        def do_RB5(self):
            p, total = self.p, self.RB()
            total.done()
            when(p == 0, lambda: gain_sum.next(3))

            @pl.when(p < last)
            def _():
                ingrad_copy(p + 1).wait()

            residual = x_ref[p].astype(f32)
            factor = inverse_rms(residual)
            grad = norm_back(total.total(), residual * factor, factor, gain_of(0, p))
            stage[1] = (ghmid_s[self.ring] + grad).astype(bf16)
            ingrad_copy(p).start()

        def do_RB2(self):
            self.RB().t2()
            when(self.p == 0, lambda: gain_sum.next(0))

        def do_RB3(self):
            self.RB().t3()
            when(self.p == 0, lambda: gain_sum.next(1))

        def do_RB4(self):
            self.RB().t4()
            when(self.p == 0, lambda: gain_sum.next(2))

        def runs(self):
            ticks = {}
            for name, event in (
                ("RA", self.RA), ("RG", self.RG), ("RF", self.RF), ("AF", self.AF), ("AG", self.AG),
            ):
                ticks[name + "2"] = lambda event=event: event().t2()
                ticks[name + "3"] = lambda event=event: event().t3()
                ticks[name + "4"] = lambda event=event: event().t4()
            return ticks | {
                "A": self.do_A, "RA5": self.do_RA5, "C": self.do_C, "Cg": self.do_Cg, "Fm": self.do_Fm,
                "Ff": self.do_Ff, "RG5": self.do_RG5, "RF5": self.do_RF5, "E": self.do_E, "Eg": self.do_Eg,
                "Em": self.do_Em, "Ef": self.do_Ef, "RB2": self.do_RB2, "RB3": self.do_RB3, "RB4": self.do_RB4,
                "RB5": self.do_RB5,
            }

    def cot_runs(j):
        event = cot_gather(j, lax.rem(j + 16, 2))

        def done():
            event.done()
            when(j == 0, lambda: load_cot(last).start())

        return {"AC1": event.t1, "AC2": event.t2, "AC3": event.t3, "AC4": event.t4, "AC5": done}

    def tell(number, way):
        pl.semaphore_signal(credits.at[number], inc=1, device_id=place.device(way), device_id_type=MESH)

    def tell_all():
        tell(0, "y")
        when(z < 3, lambda: tell(1, "up"))
        when(z > 0, lambda: tell(2, "down"))

    steps = positions + max(delay for name, delay in SCHEDULES[0] if name[:2] != "AC")
    tell_all()

    def step(low, high, schedule, s, c):
        pl.semaphore_wait(credits.at[0], 1)
        when(z > 0, lambda: pl.semaphore_wait(credits.at[1], 1))
        when(z < 3, lambda: pl.semaphore_wait(credits.at[2], 1))
        for name, delay in schedule:
            if name == "K":
                when(s < steps - 1, tell_all)
            elif high <= delay or low >= delay + (pairs_of if name[:2] == "AC" else positions):
                continue
            elif name[:2] == "AC":
                j = s - delay
                when((j >= 0) & (j < pairs_of), cot_runs(j)[name])
            else:
                when((s >= delay) & (s <= last + delay), Position(s - delay).runs()[name])
        return c

    bounds = (0,) + CHANGES + (steps,)
    for low, high, schedule in zip(bounds, bounds[1:], SCHEDULES):
        lax.fori_loop(low, high, functools.partial(step, low, high, schedule), 0)
    gain_sum.next(4)
    gain_out[...] = gain_pieces[0, 0] / gains_ref[:, :, piece_at(0, f, quarter)]
    grad_ffn.drained(ffn_outs, 0)
    grad_att.drained(att_outs, 0)
    out_copy(0).wait()
    ingrad_copy(0).wait()


def layer(x, cot, mask, gains, in_weight, out_weight, gate_up, down):
    positions, local, depth = x.shape
    width, hidden = out_weight.shape[1], down.shape[1]
    rows = ZN * YN * local
    quarter = depth // 4
    block = (local, depth)
    groups = positions // 2

    def vm(*shape, dtype=bf16):
        return pltpu.VMEM(shape, dtype)

    def hbm(*shape, dtype=bf16):
        return jax.ShapeDtypeStruct(shape, dtype)

    everything = (ZN, YN) + block
    scratch = (
        [vm(2, *everything)] * 2
        + [vm(*everything)] * 3
        + [vm(2, *everything)] * 2
        + [vm(2, ZN, *block)] * 4
        + [vm(2, 3, YN, *block), vm(2, 3, *block), vm(2, 3, YN, *block), vm(2, 3, *block)] * 2
        + [vm(positions, rows, width)] * 4
        + [vm(positions, rows, width, dtype=f32)] * 2
        + [vm(positions, rows // 2, width, dtype=f32)] * 2
        + [vm(2, depth, hidden), vm(hidden, depth), vm(width, depth), vm(width, depth)]
        + [vm(2, 3, depth, width), vm(*everything)]
        + [vm(rows, hidden)] * 3
        + [vm(rows, width), vm(3, rows, width)]
        + [vm(4, *block, dtype=f32)] * 2
        + [vm(2, *block)]
        + [vm(2, positions, depth, dtype=f32)]
        + [vm(2, 2, 2, positions, quarter, dtype=f32), vm(6, 2, positions, quarter, dtype=f32)]
        + [vm(2, 2, quarter, hidden)] * 3
        + [vm(2, quarter, hidden)]
        + [vm(2, hidden, quarter)] * 3
        + [vm(hidden, quarter)]
        + [vm(2, 3, quarter, width)] * 3
        + [vm(3, quarter, width)]
        + [vm(2, width, quarter)] * 3
        + [vm(width, quarter)]
        + [
            pltpu.SemaphoreType.DMA((groups, 2, 10)),
            pltpu.SemaphoreType.DMA((groups, 2, 8)),
            pltpu.SemaphoreType.DMA((3, 2, 2, 10)),
            pltpu.SemaphoreType.DMA((3, 2, 2, 8)),
            pltpu.SemaphoreType.DMA((4, 2, 10)),
            pltpu.SemaphoreType.DMA((4, 2, 11)),
            pltpu.SemaphoreType.DMA((2, 2, 2, 10)),
            pltpu.SemaphoreType.DMA((2, 2, 2, 11)),
            pltpu.SemaphoreType.DMA((5, 2)),
            pltpu.SemaphoreType.DMA((5, 2)),
            pltpu.SemaphoreType.DMA((2, 5)),
            pltpu.SemaphoreType.DMA((16 + positions,)),
            pltpu.SemaphoreType.REGULAR((3,)),
            pltpu.SemaphoreType.REGULAR((4,)),
        ]
    )
    in_vmem = pl.BlockSpec(memory_space=pltpu.VMEM)
    anywhere = pl.BlockSpec(memory_space=pl.ANY)
    return pl.pallas_call(
        layer_kernel,
        in_specs=[in_vmem] * 4 + [anywhere] * 4,
        out_specs=[anywhere] * 6 + [in_vmem, anywhere, anywhere],
        out_shape=[
            hbm(positions, *block),
            hbm(positions, *block),
            hbm(positions, 2, quarter, hidden),
            hbm(positions, hidden, quarter),
            hbm(positions, 3, quarter, width),
            hbm(positions, width, quarter),
            hbm(2, positions, quarter, dtype=f32),
            hbm(positions // 2, ZN, YN, 2, *block),
            hbm(positions // 2, ZN, YN, 2, *block),
        ],
        scratch_shapes=scratch,
        compiler_params=pltpu.CompilerParams(
            collective_id=0, has_side_effects=True, vmem_limit_bytes=KERNEL_VMEM_BYTES
        ),
        name="layer",
    )(x, cot, mask, gains, in_weight, out_weight, gate_up, down)


def widen_kernel(*refs):
    half = len(refs) // 2
    for narrow, wide in zip(refs[:half], refs[half:]):
        wide[...] = narrow[...].astype(f32)


def widened(*arrays):
    def spec(a):
        rank = a.ndim
        return pl.BlockSpec((2,) + a.shape[1:], lambda i: (i,) + (0,) * (rank - 1))

    return pl.pallas_call(
        widen_kernel,
        grid=(arrays[0].shape[0] // 2,),
        in_specs=[spec(a) for a in arrays],
        out_specs=[spec(a) for a in arrays],
        out_shape=[jax.ShapeDtypeStruct(a.shape, f32) for a in arrays],
        compiler_params=pltpu.CompilerParams(vmem_limit_bytes=KERNEL_VMEM_BYTES),
        name="widen",
    )(*arrays)


def body_in_one(inputs, counts, norm_gains, in_weight, out_weight, gate_up, down_weight, cotangent):
    local = inputs.shape[0]
    ids = lax.axis_index("mp") * local + jnp.arange(local)
    valid = ids < counts[0]
    output, input_grad, g_gu, g_dn, g_in, g_out, gain_sums, _, _ = layer(
        jnp.swapaxes(inputs, 0, 1),
        jnp.swapaxes(cotangent, 0, 1),
        valid.astype(f32)[:, None],
        norm_gains,
        in_weight,
        out_weight,
        gate_up,
        down_weight,
    )
    return (
        jnp.swapaxes(output, 0, 1),
        jnp.swapaxes(input_grad, 0, 1),
        *widened(g_in, g_out, g_gu, g_dn),
        gain_sums,
    )


def solution(mesh):
    placed = (
        P(("frames", "mp"), None, None),
        P("frames"),
        P(),
        P(None, None, None, "mp"),
        P(None, "mp", None),
        P(None, None, None, "mp"),
        P(None, "mp", None),
        P(("frames", "mp"), None, None),
    )
    def local_body(*args):
        frames, group_size = lax.axis_size("frames"), lax.axis_size("mp")
        local, positions, depth = args[0].shape
        width, hidden = args[4].shape[1], args[6].shape[1]
        one = fits(frames, group_size, local, positions, depth, width, hidden)
        return (body_in_one if one else body)(*args)

    return jax.shard_map(
        local_body,
        mesh=mesh,
        in_specs=placed,
        out_specs=(
            P(("frames", "mp"), None, None),
            P(("frames", "mp"), None, None),
            P(None, None, "frames", "mp"),
            P(None, "mp", "frames"),
            P(None, None, "frames", "mp"),
            P(None, "mp", "frames"),
            P(None, None, "frames"),
        ),
        check_vma=False,
    )
```
